32 devices in a mesh: grp: 2 (over y), feat: 4 (over z), pos: 2 (over x), rep: 2 (over core).
Axes of the slice: x: 2, y: 2, z: 4, core: 2. Of those that a mesh axis runs over, the one named last changes fastest.
Arguments:
- active_ids: int32 [4, 16, 28], P(('grp', 'pos'), 'feat'), parts along dimension 0, may hold values from 0 to 4095, as said below
- active_vals: float32 [4, 16, 28], P(('grp', 'pos'), 'feat'), parts along dimension 0, may hold values from 0.1 to 10
- block_pattern: int32 [4, 4, 4], P(('grp', 'pos')), parts along dimension 0, may hold values from 0 to 1, as said below
- target_slots: int32 [4, 128], P(('grp', 'pos')), parts along dimension 0, may hold values from 0 to 447
- encoder: bfloat16 [4096, 2304], P(('feat', 'pos'), 'rep'), may hold values from -0.125 to 0.125
- decoder: bfloat16 [4096, 3, 2304], P(('feat', 'pos'), None, 'rep'), may hold values from -6 to 6
Outputs:
- edges: bfloat16 [4, 448, 448], P(('grp', 'pos'), ('feat', 'rep')), parts along dimension 0
- influence: float32 [4, 448, 128], P(('grp', 'pos'), ('feat', 'rep')), parts along dimension 0
The draws below stay inside these ranges and needn't reach their ends.
There are 2 independent parts, one for each index of `grp`. The reference program is written for one: setup_inputs(seed, part) draws one part's arguments, and reference() takes and returns one part's arrays. A program takes and returns all parts, laid end to end along the dimension named above; an argument that names none is the same for every part. Nothing has to cross between parts.
Inputs may be any that keep to these rules, and one draw needn't show every extreme that they name: `active_ids`: feature f is held by index f // 512 of feat+pos. In each prompt's aligned blocks of 4 positions (112 slots), at most 20 features belong to one holder, and in each prompt one holder has exactly 20 in every block. `block_pattern`: for each prompt: 1 on the diagonal, 0 above it, 0 or 1 below it.
All inputs are finite; a program needn't handle non-finite values.
Results may differ from the reference program's by a relative error of at most 0.006.
Values may be sent and summed in bfloat16 or wider, within the bound.
No kernel may reach another device: no remote copies, remote signals or barrier semaphores. Data moves between devices by JAX's collectives and lax.ppermute only.
A program may use at most 64 MiB of HBM per device.

```python
import math
import jax
import jax.numpy as jnp
from jax import lax

D = 2304
FEAT_DEV = 512
POS_DEV = 4
K = 28
LAYERS = 4
ITERS = 3
TGT = 128
PROMPTS = 2
PLEN = 16
SLOTS = 448
FEATS = 4096
CAP = 20


def draw_active_ids(key, part):
    key = jax.random.fold_in(key, 11)
    holders = FEATS // FEAT_DEV
    blocks = PLEN // POS_DEV
    block_rows = POS_DEV * K
    spare = block_rows - CAP
    key_hot, key_rest, key_local = jax.random.split(key, 3)
    hottest = jax.random.randint(key_hot, (PROMPTS,), 0, holders)
    offsets = jnp.repeat(jnp.arange(1, holders, dtype=jnp.int32), CAP)

    def one_block(block_key, hot_owner):
        first_key, second_key = jax.random.split(block_key)
        picked = jax.random.permutation(first_key, offsets)[:spare]
        shifts = jnp.concatenate([jnp.zeros((CAP,), jnp.int32), picked])
        shifts = jax.random.permutation(second_key, shifts)
        return (shifts + hot_owner) % holders
    block_keys = jax.random.split(key_rest, PROMPTS * blocks)
    block_hot = jnp.repeat(hottest, blocks)
    owners = jax.vmap(one_block)(block_keys, block_hot).reshape(PROMPTS, PLEN, K)
    local_rows = jax.random.randint(key_local, (PROMPTS, PLEN, K), 0, FEAT_DEV)
    return (owners * FEAT_DEV + local_rows).astype(jnp.int32)


def draw_block_pattern(key, part):
    key = jax.random.fold_in(key, 23)
    blocks = PLEN // POS_DEV
    coins = (jax.random.randint(key, (PROMPTS, blocks, blocks), 0, 5) < 3).astype(jnp.int32)
    rows = jnp.arange(blocks)[:, None]
    cols = jnp.arange(blocks)[None, :]
    lower = jnp.where(cols < rows, coins, 0)
    return jnp.where(rows == cols, 1, lower).astype(jnp.int32)


def set_ends(drawn, key, least, high):
    place = [jax.random.randint(jax.random.fold_in(key, axis), (), 0, length) for axis, length in enumerate(drawn.shape)]
    main_axis = drawn.shape.index(max(drawn.shape))
    neighbour = place[:main_axis] + [(place[main_axis] + 1) % drawn.shape[main_axis]] + place[main_axis + 1:]
    return drawn.at[tuple(place)].set(least).at[tuple(neighbour)].set(high)


def levels(stream_key, shape, cuts, smallest, largest):
    level = 1.0
    for dim, shards_of in cuts:
        draws = jax.random.uniform(jax.random.fold_in(jax.random.fold_in(stream_key, 6), dim), (shards_of,), jnp.float32, smallest / len(cuts), largest / len(cuts))
        level = level * jnp.repeat(jnp.exp(draws), shape[dim] // shards_of).reshape((-1,) + (1,) * (len(shape) - 1 - dim))
    return level


def noise(key, extent, deviation, limit, shards=(), kind=jnp.bfloat16):
    values = jax.random.normal(key, extent, jnp.float32) * deviation
    if len(shards) > 0:
        values = levels(key, extent, shards, -0.22, 0.18) * values
    return jnp.clip(values, min=-limit, max=limit).astype(kind)


def setup_inputs(seed: int = 0, part: int = 0) -> dict:
    key_list = jax.random.split(jax.random.key(seed), 7)
    part_splits = jax.random.split(jax.random.fold_in(key_list[6], part), 7)
    return {
        "active_ids": draw_active_ids(jax.random.fold_in(jax.random.fold_in(key_list[6], part), 71), part),
        "active_vals": jnp.clip(jnp.exp(math.log(10.0) - 4.6051702 * jax.random.uniform(part_splits[1], (PROMPTS, PLEN, K), jnp.float32) ** levels(part_splits[1], (PROMPTS, PLEN, K), ((0, 2), (1, 4)), -0.2, 0.2)), 0.1, 10.0),
        "block_pattern": draw_block_pattern(jax.random.fold_in(jax.random.fold_in(key_list[6], part), 71), part),
        "target_slots": set_ends(jax.random.randint(part_splits[3], (PROMPTS, TGT), 0, SLOTS), jax.random.fold_in(part_splits[3], 1), 0, SLOTS - 1).astype(jnp.int32),
        "encoder": noise(key_list[4], (FEATS, D), D ** -0.5, 0.125, ((0, 8), (1, 2))),
        "decoder": noise(key_list[5], (FEATS, LAYERS - 1, D), 1.0, 6.0, ((0, 8), (2, 2))),
    }


def reference(active_ids, active_vals, block_pattern, target_slots, encoder, decoder):
    block_rows = POS_DEV * K

    def one_prompt(inputs):
        prompt_ids, prompt_vals, pattern, chosen_slots = inputs
        entry_ids = prompt_ids.reshape(SLOTS)
        entry_vals = prompt_vals.reshape(SLOTS)
        layer = entry_ids % LAYERS
        depth = jnp.arange(LAYERS - 1)
        keep = (layer[:, None] <= depth[None, :]).astype(jnp.float32) * entry_vals[:, None]
        scaled = (decoder[entry_ids].astype(jnp.float32) * keep[:, :, None]).astype(jnp.bfloat16)
        chosen = (layer[:, None] == depth[None, :] + 1).astype(jnp.bfloat16)
        placed = encoder[entry_ids][:, None, :] * chosen[:, :, None]
        raw = jnp.dot(placed.reshape(SLOTS, (LAYERS - 1) * D), scaled.reshape(SLOTS, (LAYERS - 1) * D).T,
                      preferred_element_type=jnp.float32)
        slot = jnp.arange(SLOTS)
        position = slot // K
        block = slot // block_rows
        allowed = (pattern[block][:, block] > 0) & (position[None, :] <= position[:, None])
        edges = jnp.where(allowed, raw, 0.0).astype(jnp.bfloat16)
        magnitude = jnp.abs(edges.astype(jnp.float32))
        weights = magnitude / jnp.maximum(jnp.sum(magnitude, axis=1, keepdims=True), 1.0)
        current = (slot[:, None] == chosen_slots[None, :]).astype(jnp.float32)
        accum = jnp.zeros_like(current)
        for sweep in range(ITERS):
            current = jnp.dot(weights.T, current, precision=lax.Precision.HIGHEST,
                              preferred_element_type=jnp.float32)
            accum = accum + current
        return edges, accum * float(SLOTS)

    edges, influence = lax.map(one_prompt, (active_ids, active_vals, block_pattern, target_slots))
    return edges, influence
```

```python
import jax
import jax.numpy as jnp
from jax import lax
from jax.experimental import pallas as pl
from jax.experimental.pallas import tpu as pltpu
from jax.sharding import PartitionSpec as P

ITERS = 3
F32 = jnp.float32
BF16 = jnp.bfloat16
NN = (((1,), (0,)), ((), ()))
NT = (((1,), (1,)), ((), ()))
TILE = 8
KERNEL_SLOTS = 1024
DIRECT = 16


def dot(a, b, dims=NN):
    return lax.dot_general(a, b, dims, preferred_element_type=F32)


def dot_exact(a, b):
    return lax.dot_general(a, b, NN, precision=lax.Precision.HIGHEST, preferred_element_type=F32)


def iota(shape, dim):
    return lax.broadcasted_iota(jnp.int32, shape, dim).astype(F32)


def floor_div(x, n):
    return jnp.floor((x + 0.5) * (1.0 / n))


def on_core(fn, scalars, args, outs, kernel=True):
    if not kernel:
        return fn(scalars, *args)
    count = len(args)

    def body(scalar_ref, *refs):
        values = [ref[...] for ref in refs[:count]]
        results = fn([scalar_ref[i] for i in range(len(scalars))], *values)
        for ref, value in zip(refs[count:], results):
            ref[...] = value

    return pl.pallas_call(
        body,
        out_shape=outs,
        in_specs=[pl.BlockSpec(memory_space=pltpu.SMEM)]
        + [pl.BlockSpec(memory_space=pltpu.VMEM)] * count,
        out_specs=[pl.BlockSpec(memory_space=pltpu.VMEM)] * len(outs),
        compiler_params=pltpu.CompilerParams(vmem_limit_bytes=56 * 1024 * 1024),
    )(jnp.stack(scalars).astype(jnp.int32), *args)


def rotate(x, axis, step):
    count = lax.axis_size(axis)
    return lax.ppermute(x, axis, [(i, (i + step) % count) for i in range(count)])


def shape(*dims, dtype=F32):
    return jax.ShapeDtypeStruct(dims, dtype)


def per_device(active_ids, active_vals, block_pattern, target_slots, encoder, decoder):
    feats = lax.axis_size("feat")
    poses = lax.axis_size("pos")
    reps = lax.axis_size("rep")
    holders = feats * poses
    feat = lax.axis_index("feat")
    pos = lax.axis_index("pos")
    rep = lax.axis_index("rep")
    scalars = [feat, pos, rep]
    table_rows, width = encoder.shape
    depth = decoder.shape[1]
    layers = depth + 1
    positions, kslots = active_ids.shape[1:]
    block_rows = positions * kslots
    slots = block_rows * feats
    capacity = max(2, (10 * block_rows + 7 * holders - 1) // (7 * holders))
    listed = capacity * feats
    column = poses * listed
    half = column // reps
    result_rows = block_rows // reps
    panel = target_slots.shape[1]
    tiles = -(-positions // TILE) * TILE
    small = slots <= KERNEL_SLOTS

    def pack(_, ids, vals):
        pad = jnp.zeros((tiles - positions, kslots), F32)
        return (jnp.concatenate([ids[0].astype(F32), pad, vals[0], pad], axis=0)[None],)

    (packed,) = on_core(pack, scalars, [active_ids, active_vals], [shape(1, 2 * tiles, kslots)])
    if holders <= DIRECT:
        pieces = [packed] + [rotate(packed, ("feat", "pos"), m) for m in range(1, holders)]
    else:
        pieces = [lax.all_gather(packed, ("feat", "pos"), axis=0, tiled=True)]

    def block_of(values, own, feat_of, pos_of):
        wanted = feat_of * poses + pos_of
        if len(values) == 1:
            return lax.dynamic_index_in_dim(values[0], wanted, 0, keepdims=False)
        shift = lax.rem(own - wanted + holders, holders)
        picked = values[0][0]
        for m in range(1, holders):
            picked = jnp.where(shift == m, values[m][0], picked)
        return picked

    def list_row(slot):
        place = floor_div(slot, kslots)
        block = floor_div(place, positions)
        return block * tiles + place - block * positions

    def slot_entry(slot):
        return slot - floor_div(slot, kslots) * kslots

    def as_row(table):
        spread = (iota((kslots, slots), 0) == slot_entry(iota((kslots, slots), 1))).astype(F32)
        mine = iota((table.shape[0], slots), 0) == list_row(iota((table.shape[0], slots), 1))
        return jnp.sum(jnp.where(mine, dot_exact(table, spread), 0.0), axis=0, keepdims=True)

    def as_col(table):
        spread = (list_row(iota((slots, table.shape[0]), 0)) == iota((slots, table.shape[0]), 1))
        mine = slot_entry(iota((slots, kslots), 0)) == iota((slots, kslots), 1)
        return jnp.sum(
            jnp.where(mine, dot_exact(spread.astype(F32), table), 0.0), axis=1, keepdims=True
        )

    def gather(scalars, *values):
        feat, pos, _ = scalars
        enc, dec = values[-2:]
        own = feat * poses + pos
        rows = []
        lists = []
        for k in range(poses):
            prompt = lax.rem(pos + k, poses)
            blocks = [block_of(values[:-2], own, a, prompt) for a in range(feats)]
            lists.append(
                (
                    jnp.concatenate([b[:tiles] for b in blocks], axis=0),
                    jnp.concatenate([b[tiles:] for b in blocks], axis=0),
                )
            )
            rows.append((as_row(lists[k][0]), as_row(lists[k][1])))
        hits = [floor_div(ids, table_rows) == own.astype(F32) for ids, _ in rows]
        earlier = (iota((slots, slots), 0) < iota((slots, slots), 1)).astype(BF16)
        ranks = dot(jnp.concatenate([h.astype(BF16) for h in hits], axis=0), earlier)
        picks, gains, ids_of = [], [], []
        for k in range(poses):
            chosen = jnp.where(
                hits[k] & (ranks[k : k + 1] == iota((listed, slots), 0)), 1.0, 0.0
            )
            ids = jnp.sum(chosen * rows[k][0], axis=1, keepdims=True)
            ids_of.append(ids)
            gains.append(jnp.sum(chosen * rows[k][1], axis=1, keepdims=True))
            live = jnp.sum(chosen, axis=1, keepdims=True) > 0.0
            local = jnp.where(live, ids - own.astype(F32) * table_rows, -1.0)
            picks.append((local == iota((listed, table_rows), 1)).astype(BF16))
        picks = jnp.concatenate(picks, axis=0)
        gains = jnp.concatenate(gains, axis=0)
        ids_of = jnp.concatenate(ids_of, axis=0)
        layer = ids_of - floor_div(ids_of, layers) * layers
        enc_rows = dot(picks, enc).astype(BF16)
        dec_rows = []
        for l in range(depth):
            gain = jnp.where(layer <= l, gains, 0.0)
            dec_rows.append((dot(picks, dec[l]) * gain).astype(BF16))
        out = [enc_rows[k * listed : (k + 1) * listed] for k in range(poses)]
        out += [
            jnp.stack([d[k * listed : (k + 1) * listed] for d in dec_rows], axis=0)
            for k in range(poses)
        ]
        return out + [lists[0][0]]

    outs = [shape(listed, width, dtype=BF16)] * poses
    outs += [shape(depth, listed, width, dtype=BF16)] * poses + [shape(feats * tiles, kslots)]
    gathered = on_core(
        gather,
        scalars,
        list(pieces) + [encoder, jnp.transpose(decoder, (1, 0, 2))],
        outs,
        kernel=holders <= DIRECT,
    )
    enc_rows, dec_rows, my_list = gathered[:poses], gathered[poses : 2 * poses], gathered[-1]

    enc_rows = [enc_rows[0]] + [rotate(enc_rows[k], "pos", k) for k in range(1, poses)]
    dec_rows = [dec_rows[0]] + [rotate(dec_rows[k], "pos", k) for k in range(1, poses)]
    ring = [enc_rows]
    for _ in range(1, feats):
        ring.append([rotate(rows, "feat", 1) for rows in ring[-1]])
    enc_shards = [rows for step in ring for rows in step]

    def places(scalars, ids_list, pattern):
        feat, pos, rep = scalars
        ids_row = as_row(ids_list)
        owner_row = floor_div(ids_row, table_rows)
        owner = floor_div(as_col(ids_list), table_rows)
        same = (owner == owner_row) & (iota((slots, slots), 1) < iota((slots, slots), 0))
        rank = jnp.sum(jnp.where(same, 1.0, 0.0), axis=1, keepdims=True)
        feat_of = floor_div(owner, poses)
        step = feat.astype(F32) - feat_of
        step = jnp.where(step < 0.0, step + feats, step)
        turn = pos.astype(F32) - (owner - feat_of * poses)
        turn = jnp.where(turn < 0.0, turn + poses, turn)
        place = (step * poses + turn) * listed + rank
        placing = (place == iota((slots, holders * listed), 1)).astype(BF16)
        layer_row = ids_row - floor_div(ids_row, layers) * layers
        allowed = jnp.where(pattern[0] == 1, 1.0, 0.0).astype(BF16)

        def in_block(slot, dim, extent):
            wide = (extent, feats) if dim == 0 else (feats, extent)
            return (floor_div(slot, block_rows) == iota(wide, 1 - dim)).astype(BF16)

        sources = in_block(iota((slots, 1), 0), 0, slots)
        across = dot(sources, allowed, NT).astype(BF16)
        mask = dot(across, in_block(iota((1, slots), 1), 1, slots))
        causal = floor_div(iota((slots, slots), 0), kslots) <= floor_div(
            iota((slots, slots), 1), kslots
        )
        mask = jnp.where(causal, mask, 0.0).astype(BF16)
        first = (feat * reps + rep).astype(F32) * result_rows
        own_slot = first + iota((result_rows, 1), 0)
        own_mask = dot(in_block(own_slot, 0, result_rows), allowed).astype(BF16)
        own_mask = dot(own_mask, in_block(iota((1, slots), 1), 1, slots))
        own_causal = floor_div(iota((result_rows, slots), 1), kslots) <= floor_div(
            first + iota((result_rows, slots), 0), kslots
        )
        own_mask = jnp.where(own_causal, own_mask, 0.0)
        return placing, layer_row, mask, own_mask

    placing, layer_row, mask, own_mask = on_core(
        places,
        scalars,
        [my_list, block_pattern],
        [
            shape(slots, holders * listed, dtype=BF16),
            shape(1, slots),
            shape(slots, slots, dtype=BF16),
            shape(result_rows, slots),
        ],
        kernel=small,
    )

    def products(scalars, placing, layer_row, *values):
        rep = scalars[2]
        enc = jnp.concatenate(values[: feats * poses], axis=0)
        targets = dot(placing, enc).astype(BF16)
        dec = values[feats * poses :]
        raw = jnp.zeros((column, slots), F32)
        for l in range(depth):
            rows = jnp.concatenate([d[l] for d in dec], axis=0)
            raw = raw + jnp.where(layer_row == l + 1.0, dot(rows, targets, NT), 0.0)
        first = rep == 0
        return (
            jnp.where(first, raw[:half], raw[half:]),
            jnp.where(first, raw[half:], raw[:half]),
        )

    keep, send = on_core(
        products,
        scalars,
        [placing, layer_row] + enc_shards + list(dec_rows),
        [shape(half, slots)] * 2,
        kernel=small,
    )
    own_edges = (keep + rotate(send, "rep", 1)).astype(BF16)
    shards = [own_edges] + [rotate(own_edges, "feat", k) for k in range(1, feats)]
    others = [rotate(shard, "rep", 1) for shard in shards]

    def finish(scalars, placing, mask, own_mask, targets, *values):
        feat, _, rep = scalars
        first = rep == 0
        parts = []
        for mine, other in zip(values[:feats], values[feats:]):
            parts += [jnp.where(first, mine, other), jnp.where(first, other, mine)]
        padded = jnp.concatenate(parts, axis=0)
        magnitude = jnp.abs(dot(placing, padded) * mask.astype(F32))
        total = jnp.maximum(jnp.sum(magnitude, axis=0, keepdims=True), 1.0)
        magnitude = magnitude.astype(BF16)
        diagonal = iota((slots, slots), 0) == iota((slots, slots), 1)
        scale = 1.0 / jnp.sum(jnp.where(diagonal, total, 0.0), axis=1, keepdims=True)
        current = (iota((slots, panel), 0) == targets.astype(F32)).astype(F32)
        accum = jnp.zeros((slots, panel), F32)
        for _ in range(ITERS):
            scaled = current * scale
            high = scaled.astype(BF16)
            low = (scaled - high.astype(F32)).astype(BF16)
            both = dot(magnitude, jnp.concatenate([high, low], axis=1))
            current = both[:, :panel] + both[:, panel:]
            accum = accum + current
        index = feat * reps + rep
        influence = accum[:result_rows]
        for w in range(1, feats * reps):
            influence = jnp.where(
                index == w, accum[w * result_rows : (w + 1) * result_rows], influence
            )
        start = (index * result_rows).astype(F32)
        own = start + iota((result_rows, slots), 0) == iota((result_rows, slots), 1)
        rows = dot(own.astype(BF16), padded, NT).astype(BF16)
        edges = (dot(rows, placing, NT) * own_mask).astype(BF16)
        return edges[None], (influence * float(slots))[None]

    edges, influence = on_core(
        finish,
        scalars,
        [placing, mask, own_mask, target_slots] + shards + others,
        [shape(1, result_rows, slots, dtype=BF16), shape(1, result_rows, panel)],
        kernel=small,
    )
    return edges, influence


def solution(mesh):
    return jax.shard_map(
        per_device,
        mesh=mesh,
        in_specs=(
            P(("grp", "pos"), "feat", None),
            P(("grp", "pos"), "feat", None),
            P(("grp", "pos"), None, None),
            P(("grp", "pos"), None),
            P(("feat", "pos"), "rep"),
            P(("feat", "pos"), None, "rep"),
        ),
        out_specs=(
            P(("grp", "pos"), ("feat", "rep"), None),
            P(("grp", "pos"), ("feat", "rep"), None),
        ),
        check_vma=False,
    )
```

```python
import jax
import jax.numpy as jnp
from jax import lax
from jax.experimental import pallas as pl
from jax.experimental.pallas import tpu as pltpu
from jax.sharding import PartitionSpec as P

ITERS = 3
F32 = jnp.float32
BF16 = jnp.bfloat16
NN = (((1,), (0,)), ((), ()))
NT = (((1,), (1,)), ((), ()))
LANES = 128
KERNEL_SLOTS = 1024


def dot(a, b, dims=NN):
    return lax.dot_general(a, b, dims, preferred_element_type=F32)


def dot_exact(a, b):
    return lax.dot_general(a, b, NN, precision=lax.Precision.HIGHEST, preferred_element_type=F32)


def iota(shape, dim):
    return lax.broadcasted_iota(jnp.int32, shape, dim).astype(F32)


def floor_div(x, n):
    return jnp.floor((x + 0.5) * (1.0 / n))


def on_core(fn, args, outs, kernel=True, after=(), cost=None):
    if not kernel:
        return fn(*args)
    count = len(args)

    def body(*refs):
        results = fn(*[ref[...] for ref in refs[:count]])
        for ref, value in zip(refs[count + len(after) :], results):
            ref[...] = value

    estimate = None
    if cost is not None:
        estimate = pl.CostEstimate(flops=cost[0], bytes_accessed=cost[1], transcendentals=0)
    return pl.pallas_call(
        body,
        out_shape=outs,
        in_specs=[pl.BlockSpec(memory_space=pltpu.VMEM)] * count
        + [pl.BlockSpec(memory_space=pl.ANY)] * len(after),
        out_specs=[pl.BlockSpec(memory_space=pltpu.VMEM)] * len(outs),
        compiler_params=pltpu.CompilerParams(vmem_limit_bytes=56 * 1024 * 1024),
        cost_estimate=estimate,
    )(*args, *after)


def rotate(x, axis, step):
    count = lax.axis_size(axis)
    return lax.ppermute(x, axis, [(i, (i + step) % count) for i in range(count)])


def ring_place(index, count):
    low = floor_div(index, 2)
    return jnp.where(index > 2 * low, count - 1 - low, low)


def ring_next(x, axis):
    count = lax.axis_size(axis)
    order = list(range(0, count, 2)) + list(range(1, count, 2))[::-1]
    return lax.ppermute(x, axis, [(order[i], order[(i + 1) % count]) for i in range(count)])


def ring_spread(x, axis):
    count = lax.axis_size(axis)
    order = list(range(0, count, 2)) + list(range(1, count, 2))[::-1]
    return [x] + [
        lax.ppermute(x, axis, [(order[i], order[(i + k) % count]) for i in range(count)])
        for k in range(1, count)
    ]


def part(x, kernel):
    return x.astype(BF16) if kernel else lax.reduce_precision(x, 8, 7).astype(BF16)


def shape(*dims, dtype=F32):
    return jax.ShapeDtypeStruct(dims, dtype)


def per_device(active_ids, active_vals, block_pattern, target_slots, encoder, decoder):
    feats = lax.axis_size("feat")
    poses = lax.axis_size("pos")
    reps = lax.axis_size("rep")
    holders = feats * poses
    table_rows, width = encoder.shape
    depth = decoder.shape[1]
    layers = depth + 1
    positions, kslots = active_ids.shape[1:]
    block_rows = positions * kslots
    slots = block_rows * feats
    capacity = max(2, (10 * block_rows + 7 * holders - 1) // (7 * holders))
    listed = capacity * feats
    column = poses * listed
    half = column // reps
    result_rows = block_rows // reps
    panel = target_slots.shape[1]
    small = slots <= KERNEL_SLOTS

    def place():
        feat, pos = lax.axis_index("feat"), lax.axis_index("pos")
        return feat.astype(F32), pos.astype(F32), lax.axis_index("rep").astype(F32)

    def pack(ids, vals):
        one = jnp.concatenate([ids[0].astype(F32), vals[0]], axis=0)
        one = jnp.concatenate([one, jnp.zeros((2 * positions, LANES - kslots), F32)], axis=1)
        return (jnp.broadcast_to(one, (holders,) + one.shape),)

    (packed,) = on_core(
        pack, [active_ids, active_vals], [shape(holders, 2 * positions, LANES)]
    )
    lists = lax.all_to_all(packed, ("feat", "pos"), split_axis=0, concat_axis=0, tiled=True)

    def list_of(values, prompt):
        blocks = []
        for a in range(feats):
            block = values[a * poses]
            for q in range(1, poses):
                block = jnp.where(prompt == q, values[a * poses + q], block)
            blocks.append(block)
        return jnp.concatenate(blocks, axis=0)[:, :kslots]

    def list_row(slot):
        place = floor_div(slot, kslots)
        return place + floor_div(place, positions) * positions

    def slot_entry(slot):
        return slot - floor_div(slot, kslots) * kslots

    def as_rows(table):
        spread = (iota((kslots, slots), 0) == slot_entry(iota((kslots, slots), 1))).astype(F32)
        wide = dot_exact(table, spread)
        row = iota(wide.shape, 0) - list_row(iota(wide.shape, 1))
        ids = jnp.sum(jnp.where(row == 0, wide, 0.0), axis=0, keepdims=True)
        return ids, jnp.sum(jnp.where(row == positions, wide, 0.0), axis=0, keepdims=True)

    def as_col(table):
        wide = (slots, table.shape[0])
        spread = (list_row(iota(wide, 0)) == iota(wide, 1)).astype(F32)
        mine = slot_entry(iota((slots, kslots), 0)) == iota((slots, kslots), 1)
        return jnp.sum(jnp.where(mine, dot_exact(spread, table), 0.0), axis=1, keepdims=True)

    def choose(values, enc):
        feat, pos, _ = place()
        own = feat * poses + pos
        tables = []
        rows = []
        for k in range(poses):
            prompt = jnp.where(pos + k >= poses, pos + k - poses, pos + k)
            tables.append(list_of(values, prompt))
            rows.append(as_rows(tables[k]))
        hits = [floor_div(ids, table_rows) == own for ids, _ in rows]
        earlier = (iota((slots, slots), 0) < iota((slots, slots), 1)).astype(BF16)
        ranks = dot(jnp.concatenate([h.astype(BF16) for h in hits], axis=0), earlier)
        picks, gains, ids_of = [], [], []
        for k in range(poses):
            chosen = jnp.where(
                hits[k] & (ranks[k : k + 1] == iota((listed, slots), 0)), 1.0, 0.0
            )
            ids = jnp.sum(chosen * rows[k][0], axis=1, keepdims=True)
            ids_of.append(ids)
            gains.append(jnp.sum(chosen * rows[k][1], axis=1, keepdims=True))
            live = jnp.sum(chosen, axis=1, keepdims=True) > 0.0
            local = jnp.where(live, ids - own * table_rows, -1.0)
            picks.append((local == iota((listed, table_rows), 1)).astype(BF16))
        picks = jnp.concatenate(picks, axis=0)
        gains = jnp.concatenate(gains, axis=0)
        ids_of = jnp.concatenate(ids_of, axis=0)
        layer = ids_of - floor_div(ids_of, layers) * layers
        gains = jnp.concatenate([jnp.where(layer <= l, gains, 0.0) for l in range(depth)], axis=1)
        enc_rows = dot(picks, enc).astype(BF16)
        enc_rows = [enc_rows[k * listed : (k + 1) * listed] for k in range(poses)]
        return enc_rows + [picks, gains, tables[0]]

    outs = [shape(listed, width, dtype=BF16)] * poses
    outs += [shape(column, table_rows, dtype=BF16), shape(column, depth)]
    outs += [shape(2 * positions * feats, kslots)]
    chosen = on_core(choose, [lists, encoder], outs, small)
    enc_rows, (picks, gains, my_list) = chosen[:poses], chosen[poses:]

    enc_rows = [enc_rows[0]] + [rotate(enc_rows[k], "pos", k) for k in range(1, poses)]
    ring = [enc_rows]
    for _ in range(1, feats):
        ring.append([ring_next(rows, "feat") for rows in ring[-1]])

    def decode(picks, gains, dec):
        rows = [(dot(picks, dec[l]) * gains[:, l : l + 1]).astype(BF16) for l in range(depth)]
        return [
            jnp.stack([row[k * listed : (k + 1) * listed] for row in rows], axis=0)
            for k in range(poses)
        ]

    dec_rows = on_core(
        decode,
        [picks, gains, jnp.transpose(decoder, (1, 0, 2))],
        [shape(depth, listed, width, dtype=BF16)] * poses,
        small,
        after=enc_rows[1:],
        cost=(2 * column * table_rows * depth * width, 2 * table_rows * depth * width),
    )
    dec_rows = [dec_rows[0]] + [rotate(dec_rows[k], "pos", k) for k in range(1, poses)]

    def places(table, pattern):
        feat, pos, rep = place()

        def padded(owner, rank):
            feat_of = floor_div(owner, poses)
            step = ring_place(feat, feats) - ring_place(feat_of, feats)
            step = jnp.where(step < 0.0, step + feats, step)
            turn = pos - (owner - feat_of * poses)
            turn = jnp.where(turn < 0.0, turn + poses, turn)
            return (step * poses + turn) * listed + rank

        ids_row = as_rows(table)[0]
        ids_col = as_col(table)
        owner_row = floor_div(ids_row, table_rows)
        owner_col = floor_div(ids_col, table_rows)
        same = owner_col == owner_row
        down, across = iota((slots, slots), 0), iota((slots, slots), 1)
        rank_col = jnp.sum(jnp.where(same & (across < down), 1.0, 0.0), axis=1, keepdims=True)
        rank_row = jnp.sum(jnp.where(same & (down < across), 1.0, 0.0), axis=0, keepdims=True)
        total = holders * listed
        placing = padded(owner_col, rank_col) == iota((slots, total), 1)
        placing_t = padded(owner_row, rank_row) == iota((total, slots), 0)
        layer = ids_col - floor_div(ids_col, layers) * layers
        layer_row = jnp.sum(jnp.where(placing, layer, 0.0), axis=0, keepdims=True)
        allowed = jnp.where(pattern[0] == 1, 1.0, 0.0).astype(BF16)

        def in_block(slot, dim, extent):
            wide = (extent, feats) if dim == 0 else (feats, extent)
            return (floor_div(slot, block_rows) == iota(wide, 1 - dim)).astype(BF16)

        sources = in_block(iota((slots, 1), 0), 0, slots)
        targets = in_block(iota((1, slots), 1), 1, slots)
        mask = dot(dot(sources, allowed, NT).astype(BF16), targets)
        mask = jnp.where(floor_div(down, kslots) <= floor_div(across, kslots), mask, 0.0)
        first = (feat * reps + rep) * result_rows
        own_slot = first + iota((result_rows, 1), 0)
        own_mask = dot(in_block(own_slot, 0, result_rows), allowed).astype(BF16)
        own_mask = dot(own_mask, targets)
        own_causal = floor_div(iota((result_rows, slots), 1), kslots) <= floor_div(
            first + iota((result_rows, slots), 0), kslots
        )
        own_mask = jnp.where(own_causal, own_mask, 0.0)
        return placing.astype(BF16), placing_t.astype(BF16), layer_row, mask.astype(BF16), own_mask

    placing, placing_t, layer_row, mask, own_mask = on_core(
        places,
        [my_list, block_pattern],
        [
            shape(slots, holders * listed, dtype=BF16),
            shape(holders * listed, slots, dtype=BF16),
            shape(1, holders * listed),
            shape(slots, slots, dtype=BF16),
            shape(result_rows, slots),
        ],
        small,
        cost=(4 * slots * slots * slots, 4 * slots * slots),
    )

    def products(first, count, layer_row, placing_t, *values):
        enc = jnp.concatenate(values[: count * poses], axis=0)
        dec = values[count * poses : count * poses + poses]
        dec = jnp.concatenate([d[l] for l in range(depth) for d in dec], axis=0)
        every = dot(dec, enc, NT)
        lanes = slice(first * column, (first + count) * column)
        raw = jnp.zeros((column, count * column), F32)
        for l in range(depth):
            rows = every[l * column : (l + 1) * column]
            raw = raw + jnp.where(layer_row[:, lanes] == l + 1.0, rows, 0.0)
        high = part(raw, small)
        rest = raw - high.astype(F32)
        middle = part(rest, small)
        low = part(rest - middle.astype(F32), small)
        split = dot(jnp.concatenate([high, middle, low], axis=0), placing_t[lanes])
        return split[:column] + split[column : 2 * column] + split[2 * column :]

    def early(*values):
        return (products(0, feats - 1, *values),)

    def late(so_far, *values):
        raw = so_far + products(feats - 1, 1, *values)
        first = place()[2] == 0.0
        return (
            jnp.where(first, raw[:half], raw[half:]),
            jnp.where(first, raw[half:], raw[:half]),
        )

    early_enc = [rows for step in ring[:-1] for rows in step]
    (so_far,) = on_core(
        early,
        [layer_row, placing_t] + early_enc + list(dec_rows),
        [shape(column, slots)],
        small,
        cost=(8 * column * slots * width, 8 * column * width),
    )
    keep, send = on_core(
        late,
        [so_far, layer_row, placing_t] + list(ring[-1]) + list(dec_rows),
        [shape(half, slots)] * 2,
        small,
    )
    own_edges = (keep + rotate(send, "rep", 1)).astype(BF16)
    shards = ring_spread(own_edges, "feat")
    others = [rotate(shard, "rep", 1) for shard in shards]

    def finish(placing, mask, own_mask, targets, *values):
        feat, _, rep = place()
        first = rep == 0.0
        parts = []
        for mine, other in zip(values[:feats], values[feats:]):
            parts += [jnp.where(first, mine, other), jnp.where(first, other, mine)]
        padded = jnp.concatenate(parts, axis=0)
        magnitude = jnp.abs(dot(placing, padded) * mask.astype(F32))
        total = jnp.maximum(jnp.sum(magnitude, axis=0, keepdims=True), 1.0)
        magnitude = magnitude.astype(BF16)
        diagonal = iota((slots, slots), 0) == iota((slots, slots), 1)
        scale = 1.0 / jnp.sum(jnp.where(diagonal, total, 0.0), axis=1, keepdims=True)
        current = (iota((slots, panel), 0) == targets.astype(F32)).astype(F32)
        accum = jnp.zeros((slots, panel), F32)
        for _ in range(ITERS):
            scaled = current * scale
            high = part(scaled, small)
            low = part(scaled - high.astype(F32), small)
            both = dot(magnitude, jnp.concatenate([high, low], axis=1))
            current = both[:, :panel] + both[:, panel:]
            accum = accum + current
        index = feat * reps + rep
        influence = accum[:result_rows]
        for w in range(1, feats * reps):
            influence = jnp.where(
                index == w, accum[w * result_rows : (w + 1) * result_rows], influence
            )
        start = index * result_rows
        own = start + iota((result_rows, slots), 0) == iota((result_rows, slots), 1)
        rows = dot(own.astype(BF16), padded, NT).astype(BF16)
        edges = (dot(rows, placing, NT) * own_mask).astype(BF16)
        return edges[None], (influence * float(slots))[None]

    edges, influence = on_core(
        finish,
        [placing, mask, own_mask, target_slots] + shards + others,
        [shape(1, result_rows, slots, dtype=BF16), shape(1, result_rows, panel)],
        small,
    )
    return edges, influence


def solution(mesh):
    return jax.shard_map(
        per_device,
        mesh=mesh,
        in_specs=(
            P(("grp", "pos"), "feat", None),
            P(("grp", "pos"), "feat", None),
            P(("grp", "pos"), None, None),
            P(("grp", "pos"), None),
            P(("feat", "pos"), "rep"),
            P(("feat", "pos"), None, "rep"),
        ),
        out_specs=(
            P(("grp", "pos"), ("feat", "rep"), None),
            P(("grp", "pos"), ("feat", "rep"), None),
        ),
        check_vma=False,
    )
```

```python
import jax
import jax.numpy as jnp
from jax import lax
from jax.experimental import pallas as pl
from jax.experimental.pallas import tpu as pltpu
from jax.sharding import PartitionSpec as P

ITERS = 3
F32 = jnp.float32
BF16 = jnp.bfloat16
NN = (((1,), (0,)), ((), ()))
NT = (((1,), (1,)), ((), ()))
LANES = 128
KERNEL_SLOTS = 1024


def dot(a, b, dims=NN):
    return lax.dot_general(a, b, dims, preferred_element_type=F32)


def dot_exact(a, b):
    return lax.dot_general(a, b, NN, precision=lax.Precision.HIGHEST, preferred_element_type=F32)


def iota(shape, dim):
    return lax.broadcasted_iota(jnp.int32, shape, dim).astype(F32)


def floor_div(x, n):
    return jnp.floor((x + 0.5) * (1.0 / n))


def on_core(fn, args, outs, kernel=True, through=(), streams=(), cost=None):
    if not kernel:
        loads = [lambda i, x=x: x[i] for x in streams]
        return list(fn(*args, *loads)) + list(through)
    count, passed, streamed = len(args), len(through), len(streams)

    def body(*refs):
        sources = refs[count : count + streamed]
        results = refs[count + streamed + passed :][: len(outs)]
        scratch = refs[len(refs) - 2 * streamed :]
        copies = []
        for n in range(streamed):
            copies.append(
                [
                    pltpu.make_async_copy(
                        sources[n].at[i], scratch[2 * n].at[i], scratch[2 * n + 1].at[i]
                    )
                    for i in range(streams[n].shape[0])
                ]
            )
            for copy in copies[-1]:
                copy.start()

        def load(n):
            def wait(i):
                copies[n][i].wait()
                return scratch[2 * n][i]

            return wait

        values = fn(*[ref[...] for ref in refs[:count]], *[load(n) for n in range(streamed)])
        for ref, value in zip(results, values):
            ref[...] = value

    estimate = None
    if cost is not None:
        estimate = pl.CostEstimate(flops=cost[0], bytes_accessed=cost[1], transcendentals=0)
    in_vmem = pl.BlockSpec(memory_space=pltpu.VMEM)
    anywhere = pl.BlockSpec(memory_space=pl.ANY)
    scratch = []
    for x in streams:
        scratch += [pltpu.VMEM(x.shape, x.dtype), pltpu.SemaphoreType.DMA((x.shape[0],))]
    call = pl.pallas_call(
        body,
        out_shape=list(outs) + [jax.ShapeDtypeStruct(x.shape, x.dtype) for x in through],
        in_specs=[in_vmem] * count + [anywhere] * (streamed + passed),
        out_specs=[in_vmem] * len(outs) + [anywhere] * passed,
        scratch_shapes=scratch,
        input_output_aliases={count + streamed + i: len(outs) + i for i in range(passed)},
        compiler_params=pltpu.CompilerParams(vmem_limit_bytes=56 * 1024 * 1024),
        cost_estimate=estimate,
    )
    return list(call(*args, *streams, *through))


def rotate(x, axis, step):
    count = lax.axis_size(axis)
    return lax.ppermute(x, axis, [(i, (i + step) % count) for i in range(count)])


def ring_place(index, count):
    low = floor_div(index, 2)
    return jnp.where(index > 2 * low, count - 1 - low, low)


def ring_next(x, axis, across=None, turn=0):
    count = lax.axis_size(axis)
    order = list(range(0, count, 2)) + list(range(1, count, 2))[::-1]
    steps = [(order[i], order[(i + 1) % count]) for i in range(count)]
    if across is None:
        return lax.ppermute(x, axis, steps)
    wide = lax.axis_size(across)
    pairs = [(a * wide + i, b * wide + (i + turn) % wide) for a, b in steps for i in range(wide)]
    return lax.ppermute(x, (axis, across), pairs)


def ring_spread(x, axis):
    count = lax.axis_size(axis)
    order = list(range(0, count, 2)) + list(range(1, count, 2))[::-1]
    return [x] + [
        lax.ppermute(x, axis, [(order[i], order[(i + k) % count]) for i in range(count)])
        for k in range(1, count)
    ]


def part(x, kernel):
    return x.astype(BF16) if kernel else lax.reduce_precision(x, 8, 7).astype(BF16)


def shape(*dims, dtype=F32):
    return jax.ShapeDtypeStruct(dims, dtype)


def per_device(active_ids, active_vals, block_pattern, target_slots, encoder, decoder):
    feats = lax.axis_size("feat")
    poses = lax.axis_size("pos")
    reps = lax.axis_size("rep")
    holders = feats * poses
    table_rows, width = encoder.shape
    depth = decoder.shape[1]
    layers = depth + 1
    positions, kslots = active_ids.shape[1:]
    block_rows = positions * kslots
    slots = block_rows * feats
    capacity = max(2, (10 * block_rows + 7 * holders - 1) // (7 * holders))
    listed = capacity * feats
    column = poses * listed
    half = column // reps
    result_rows = block_rows // reps
    panel = target_slots.shape[1]
    small = slots <= KERNEL_SLOTS

    def place():
        feat, pos = lax.axis_index("feat"), lax.axis_index("pos")
        return feat.astype(F32), pos.astype(F32), lax.axis_index("rep").astype(F32)

    def pack(ids, vals):
        one = jnp.concatenate([ids[0].astype(F32), vals[0]], axis=0)
        one = jnp.concatenate([one, jnp.zeros((2 * positions, LANES - kslots), F32)], axis=1)
        return (jnp.broadcast_to(one, (holders,) + one.shape),)

    (packed,) = on_core(
        pack, [active_ids, active_vals], [shape(holders, 2 * positions, LANES)]
    )
    lists = lax.all_to_all(packed, ("feat", "pos"), split_axis=0, concat_axis=0, tiled=True)

    def list_of(values, prompt):
        blocks = []
        for a in range(feats):
            block = values[a * poses]
            for q in range(1, poses):
                block = jnp.where(prompt == q, values[a * poses + q], block)
            blocks.append(block)
        return jnp.concatenate(blocks, axis=0)[:, :kslots]

    def list_row(slot):
        place = floor_div(slot, kslots)
        return place + floor_div(place, positions) * positions

    def slot_entry(slot):
        return slot - floor_div(slot, kslots) * kslots

    def as_rows(table):
        spread = (iota((kslots, slots), 0) == slot_entry(iota((kslots, slots), 1))).astype(F32)
        wide = dot_exact(table, spread)
        row = iota(wide.shape, 0) - list_row(iota(wide.shape, 1))
        ids = jnp.sum(jnp.where(row == 0, wide, 0.0), axis=0, keepdims=True)
        return ids, jnp.sum(jnp.where(row == positions, wide, 0.0), axis=0, keepdims=True)

    def as_col(table):
        wide = (slots, table.shape[0])
        spread = (list_row(iota(wide, 0)) == iota(wide, 1)).astype(F32)
        mine = slot_entry(iota((slots, kslots), 0)) == iota((slots, kslots), 1)
        return jnp.sum(jnp.where(mine, dot_exact(spread, table), 0.0), axis=1, keepdims=True)

    def choose(values, enc, dec):
        feat, pos, _ = place()
        own = feat * poses + pos
        tables = []
        rows = []
        for k in range(poses):
            prompt = jnp.where(pos + k >= poses, pos + k - poses, pos + k)
            tables.append(list_of(values, prompt))
            rows.append(as_rows(tables[k]))
        hits = [floor_div(ids, table_rows) == own for ids, _ in rows]
        earlier = (iota((slots, slots), 0) < iota((slots, slots), 1)).astype(BF16)
        ranks = dot(jnp.concatenate([h.astype(BF16) for h in hits], axis=0), earlier)
        picks, gains, ids_of = [], [], []
        for k in range(poses):
            chosen = jnp.where(
                hits[k] & (ranks[k : k + 1] == iota((listed, slots), 0)), 1.0, 0.0
            )
            ids = jnp.sum(chosen * rows[k][0], axis=1, keepdims=True)
            ids_of.append(ids)
            gains.append(jnp.sum(chosen * rows[k][1], axis=1, keepdims=True))
            live = jnp.sum(chosen, axis=1, keepdims=True) > 0.0
            local = jnp.where(live, ids - own * table_rows, -1.0)
            picks.append((local == iota((listed, table_rows), 1)).astype(BF16))
        picks = jnp.concatenate(picks, axis=0)
        gains = jnp.concatenate(gains, axis=0)
        ids_of = jnp.concatenate(ids_of, axis=0)
        layer = ids_of - floor_div(ids_of, layers) * layers
        enc_rows = dot(picks, enc(0)).astype(BF16)
        dec_rows = [
            (dot(picks, dec(l)) * jnp.where(layer <= l, gains, 0.0)).astype(BF16)
            for l in range(depth)
        ]
        out = []
        for k in range(poses):
            rows = slice(k * listed, (k + 1) * listed)
            out += [enc_rows[rows], jnp.stack([d[rows] for d in dec_rows], axis=0)]
        return out + [tables[0]]

    outs = [shape(listed, width, dtype=BF16), shape(depth, listed, width, dtype=BF16)] * poses
    *chosen, my_list = on_core(
        choose,
        [lists],
        outs + [shape(2 * positions * feats, kslots)],
        small,
        streams=[encoder[None], jnp.transpose(decoder, (1, 0, 2))],
    )
    enc_rows, dec_rows = chosen[::2], chosen[1::2]

    ring = [[enc_rows[0]] + [rotate(enc_rows[k], "pos", k) for k in range(1, poses)]]
    ring.append([ring_next(enc_rows[k], "feat", "pos", k) for k in range(poses)])
    dec_rows = [dec_rows[0]] + [rotate(dec_rows[k], "pos", k) for k in range(1, poses)]

    def places(table, pattern):
        feat, pos, rep = place()

        def padded(owner, rank):
            feat_of = floor_div(owner, poses)
            step = ring_place(feat, feats) - ring_place(feat_of, feats)
            step = jnp.where(step < 0.0, step + feats, step)
            turn = pos - (owner - feat_of * poses)
            turn = jnp.where(turn < 0.0, turn + poses, turn)
            return (step * poses + turn) * listed + rank

        ids_row = as_rows(table)[0]
        ids_col = as_col(table)
        owner_row = floor_div(ids_row, table_rows)
        owner_col = floor_div(ids_col, table_rows)
        same = owner_col == owner_row
        down, across = iota((slots, slots), 0), iota((slots, slots), 1)
        rank_col = jnp.sum(jnp.where(same & (across < down), 1.0, 0.0), axis=1, keepdims=True)
        rank_row = jnp.sum(jnp.where(same & (down < across), 1.0, 0.0), axis=0, keepdims=True)
        total = holders * listed
        placing = padded(owner_col, rank_col) == iota((slots, total), 1)
        placing_t = padded(owner_row, rank_row) == iota((total, slots), 0)
        layer = ids_col - floor_div(ids_col, layers) * layers
        layer_row = jnp.sum(jnp.where(placing, layer, 0.0), axis=0, keepdims=True)
        allowed = jnp.where(pattern[0] == 1, 1.0, 0.0).astype(BF16)

        def in_block(slot, dim, extent):
            wide = (extent, feats) if dim == 0 else (feats, extent)
            return (floor_div(slot, block_rows) == iota(wide, 1 - dim)).astype(BF16)

        sources = in_block(iota((slots, 1), 0), 0, slots)
        targets = in_block(iota((1, slots), 1), 1, slots)
        mask = dot(dot(sources, allowed, NT).astype(BF16), targets)
        mask = jnp.where(floor_div(down, kslots) <= floor_div(across, kslots), mask, 0.0)
        first = (feat * reps + rep) * result_rows
        own_slot = first + iota((result_rows, 1), 0)
        own_mask = dot(in_block(own_slot, 0, result_rows), allowed).astype(BF16)
        own_mask = dot(own_mask, targets)
        own_causal = floor_div(iota((result_rows, slots), 1), kslots) <= floor_div(
            first + iota((result_rows, slots), 0), kslots
        )
        own_mask = jnp.where(own_causal, own_mask, 0.0)
        return placing.astype(BF16), placing_t.astype(BF16), layer_row, mask.astype(BF16), own_mask

    placing, placing_t, layer_row, mask, own_mask, *ring[1][-1:] = on_core(
        places,
        [my_list, block_pattern],
        [
            shape(slots, holders * listed, dtype=BF16),
            shape(holders * listed, slots, dtype=BF16),
            shape(1, holders * listed),
            shape(slots, slots, dtype=BF16),
            shape(result_rows, slots),
        ],
        small,
        through=ring[1][-1:],
        cost=(4 * slots * slots * slots, 4 * slots * slots),
    )
    for _ in range(2, feats):
        ring.append([ring_next(rows, "feat") for rows in ring[-1]])

    def products(first, count, layer_row, placing_t, *values):
        enc = jnp.concatenate(values[: count * poses], axis=0)
        dec = values[count * poses : count * poses + poses]
        dec = jnp.concatenate([d[l] for l in range(depth) for d in dec], axis=0)
        every = dot(dec, enc, NT)
        lanes = slice(first * column, (first + count) * column)
        raw = jnp.zeros((column, count * column), F32)
        for l in range(depth):
            rows = every[l * column : (l + 1) * column]
            raw = raw + jnp.where(layer_row[:, lanes] == l + 1.0, rows, 0.0)
        high = part(raw, small)
        rest = raw - high.astype(F32)
        middle = part(rest, small)
        low = part(rest - middle.astype(F32), small)
        split = dot(jnp.concatenate([high, middle, low], axis=0), placing_t[lanes])
        return split[:column] + split[column : 2 * column] + split[2 * column :]

    def early(*values):
        return (products(0, feats - 1, *values),)

    def late(so_far, *values):
        raw = so_far + products(feats - 1, 1, *values)
        first = place()[2] == 0.0
        return (
            jnp.where(first, raw[:half], raw[half:]),
            jnp.where(first, raw[half:], raw[:half]),
        )

    early_enc = [rows for step in ring[:-1] for rows in step]
    (so_far,) = on_core(
        early,
        [layer_row, placing_t] + early_enc + list(dec_rows),
        [shape(column, slots)],
        small,
        cost=(8 * column * slots * width, 8 * column * width),
    )
    keep, send = on_core(
        late,
        [so_far, layer_row, placing_t] + list(ring[-1]) + list(dec_rows),
        [shape(half, slots)] * 2,
        small,
    )
    own_edges = (keep + rotate(send, "rep", 1)).astype(BF16)
    shards = ring_spread(own_edges, "feat")
    others = [rotate(shard, "rep", 1) for shard in shards]

    def finish(placing, mask, own_mask, targets, *values):
        feat, _, rep = place()
        first = rep == 0.0
        parts = []
        for mine, other in zip(values[:feats], values[feats:]):
            parts += [jnp.where(first, mine, other), jnp.where(first, other, mine)]
        padded = jnp.concatenate(parts, axis=0)
        magnitude = jnp.abs(dot(placing, padded) * mask.astype(F32))
        total = jnp.maximum(jnp.sum(magnitude, axis=0, keepdims=True), 1.0)
        magnitude = magnitude.astype(BF16)
        diagonal = iota((slots, slots), 0) == iota((slots, slots), 1)
        scale = 1.0 / jnp.sum(jnp.where(diagonal, total, 0.0), axis=1, keepdims=True)
        current = (iota((slots, panel), 0) == targets.astype(F32)).astype(F32)
        accum = jnp.zeros((slots, panel), F32)
        for _ in range(ITERS):
            scaled = current * scale
            high = part(scaled, small)
            low = part(scaled - high.astype(F32), small)
            both = dot(magnitude, jnp.concatenate([high, low], axis=1))
            current = both[:, :panel] + both[:, panel:]
            accum = accum + current
        index = feat * reps + rep
        influence = accum[:result_rows]
        for w in range(1, feats * reps):
            influence = jnp.where(
                index == w, accum[w * result_rows : (w + 1) * result_rows], influence
            )
        start = index * result_rows
        own = start + iota((result_rows, slots), 0) == iota((result_rows, slots), 1)
        rows = dot(own.astype(BF16), padded, NT).astype(BF16)
        edges = (dot(rows, placing, NT) * own_mask).astype(BF16)
        return edges[None], (influence * float(slots))[None]

    edges, influence = on_core(
        finish,
        [placing, mask, own_mask, target_slots] + shards + others,
        [shape(1, result_rows, slots, dtype=BF16), shape(1, result_rows, panel)],
        small,
    )
    return edges, influence


def solution(mesh):
    return jax.shard_map(
        per_device,
        mesh=mesh,
        in_specs=(
            P(("grp", "pos"), "feat", None),
            P(("grp", "pos"), "feat", None),
            P(("grp", "pos"), None, None),
            P(("grp", "pos"), None),
            P(("feat", "pos"), "rep"),
            P(("feat", "pos"), None, "rep"),
        ),
        out_specs=(
            P(("grp", "pos"), ("feat", "rep"), None),
            P(("grp", "pos"), ("feat", "rep"), None),
        ),
        check_vma=False,
    )
```

```python
import jax
import jax.numpy as jnp
from jax import lax
from jax.experimental import pallas as pl
from jax.experimental.pallas import tpu as pltpu
from jax.sharding import PartitionSpec as P

ITERS = 3
F32 = jnp.float32
BF16 = jnp.bfloat16
NN = (((1,), (0,)), ((), ()))
NT = (((1,), (1,)), ((), ()))
LANES = 128
KERNEL_SLOTS = 1024


def dot(a, b, dims=NN):
    return lax.dot_general(a, b, dims, preferred_element_type=F32)


def iota(shape, dim):
    return lax.broadcasted_iota(jnp.int32, shape, dim).astype(F32)


def floor_div(x, n):
    return jnp.floor((x + 0.5) * (1.0 / n))


def on_core(fn, args, outs, kernel=True, through=(), streams=(), cost=None, room=24):
    if not kernel:
        loads = [lambda i, x=x: x[i] for x in streams]
        return list(fn(*args, *loads)) + list(through)
    count, passed, streamed = len(args), len(through), len(streams)

    def body(*refs):
        sources = refs[count : count + streamed]
        results = refs[count + streamed + passed :][: len(outs)]
        scratch = refs[len(refs) - 2 * streamed :]
        copies = []
        for n in range(streamed):
            copies.append(
                [
                    pltpu.make_async_copy(
                        sources[n].at[i], scratch[2 * n].at[i], scratch[2 * n + 1].at[i]
                    )
                    for i in range(streams[n].shape[0])
                ]
            )
            for copy in copies[-1]:
                copy.start()

        def load(n):
            def wait(i):
                copies[n][i].wait()
                return scratch[2 * n][i]

            return wait

        values = fn(*[ref[...] for ref in refs[:count]], *[load(n) for n in range(streamed)])
        for ref, value in zip(results, values):
            ref[...] = value

    estimate = None
    if cost is not None:
        estimate = pl.CostEstimate(flops=cost[0], bytes_accessed=cost[1], transcendentals=0)
    in_vmem = pl.BlockSpec(memory_space=pltpu.VMEM)
    anywhere = pl.BlockSpec(memory_space=pl.ANY)
    scratch = []
    for x in streams:
        scratch += [pltpu.VMEM(x.shape, x.dtype), pltpu.SemaphoreType.DMA((x.shape[0],))]
    call = pl.pallas_call(
        body,
        out_shape=list(outs) + [jax.ShapeDtypeStruct(x.shape, x.dtype) for x in through],
        in_specs=[in_vmem] * count
        + [pl.BlockSpec(memory_space=pltpu.HBM)] * streamed
        + [anywhere] * passed,
        out_specs=[in_vmem] * len(outs) + [anywhere] * passed,
        scratch_shapes=scratch,
        input_output_aliases={count + streamed + i: len(outs) + i for i in range(passed)},
        compiler_params=pltpu.CompilerParams(vmem_limit_bytes=room * 1024 * 1024),
        cost_estimate=estimate,
    )
    return list(call(*args, *streams, *through))


def rotate(x, axis, step):
    count = lax.axis_size(axis)
    return lax.ppermute(x, axis, [(i, (i + step) % count) for i in range(count)])


def ring_place(index, count):
    low = floor_div(index, 2)
    return jnp.where(index > 2 * low, count - 1 - low, low)


def ring_next(x, axis, across=None, turn=0):
    count = lax.axis_size(axis)
    order = list(range(0, count, 2)) + list(range(1, count, 2))[::-1]
    steps = [(order[i], order[(i + 1) % count]) for i in range(count)]
    if across is None:
        return lax.ppermute(x, axis, steps)
    wide = lax.axis_size(across)
    pairs = [(a * wide + i, b * wide + (i + turn) % wide) for a, b in steps for i in range(wide)]
    return lax.ppermute(x, (axis, across), pairs)


def ring_spread(x, axis):
    count = lax.axis_size(axis)
    order = list(range(0, count, 2)) + list(range(1, count, 2))[::-1]
    return [x] + [
        lax.ppermute(x, axis, [(order[i], order[(i + k) % count]) for i in range(count)])
        for k in range(1, count)
    ]


def part(x, kernel):
    return x.astype(BF16) if kernel else lax.reduce_precision(x, 8, 7).astype(BF16)


def shape(*dims, dtype=F32):
    return jax.ShapeDtypeStruct(dims, dtype)


def per_device(active_ids, active_vals, block_pattern, target_slots, encoder, decoder):
    feats = lax.axis_size("feat")
    poses = lax.axis_size("pos")
    reps = lax.axis_size("rep")
    holders = feats * poses
    table_rows, width = encoder.shape
    depth = decoder.shape[1]
    layers = depth + 1
    positions, kslots = active_ids.shape[1:]
    block_rows = positions * kslots
    slots = block_rows * feats
    capacity = max(2, (10 * block_rows + 7 * holders - 1) // (7 * holders))
    listed = capacity * feats
    column = poses * listed
    half = column // reps
    result_rows = block_rows // reps
    panel = target_slots.shape[1]
    small = slots <= KERNEL_SLOTS

    def place():
        feat, pos = lax.axis_index("feat"), lax.axis_index("pos")
        return feat.astype(F32), pos.astype(F32), lax.axis_index("rep").astype(F32)

    def pack(ids, vals):
        one = jnp.concatenate([ids(0).astype(F32), vals(0)], axis=0)
        one = jnp.concatenate([one, jnp.zeros((2 * positions, LANES - kslots), F32)], axis=1)
        return (jnp.broadcast_to(one, (holders,) + one.shape),)

    (packed,) = on_core(
        pack,
        [],
        [shape(holders, 2 * positions, LANES)],
        streams=[active_ids, active_vals],
        room=60,
    )
    lists = lax.all_to_all(packed, ("feat", "pos"), split_axis=0, concat_axis=0, tiled=True)

    def list_of(values, prompt):
        blocks = []
        for a in range(feats):
            block = values[a * poses]
            for q in range(1, poses):
                block = jnp.where(prompt == q, values[a * poses + q], block)
            blocks.append(block)
        return jnp.concatenate(blocks, axis=0)[:, :kslots]

    def list_row(slot):
        place = floor_div(slot, kslots)
        return place + floor_div(place, positions) * positions

    def slot_entry(slot):
        return slot - floor_div(slot, kslots) * kslots

    def pieces(table):
        high = part(table, small)
        rest = table - high.astype(F32)
        middle = part(rest, small)
        return [high, middle, part(rest - middle.astype(F32), small)]

    def as_rows(table):
        spread = (iota((kslots, slots), 0) == slot_entry(iota((kslots, slots), 1))).astype(BF16)
        wide = dot(jnp.concatenate(pieces(table), axis=0), spread)
        count = table.shape[0]
        wide = wide[:count] + (wide[count : 2 * count] + wide[2 * count :])
        row = iota(wide.shape, 0) - list_row(iota(wide.shape, 1))
        ids = jnp.sum(jnp.where(row == 0, wide, 0.0), axis=0, keepdims=True)
        return ids, jnp.sum(jnp.where(row == positions, wide, 0.0), axis=0, keepdims=True)

    def as_col(table):
        wide = (slots, table.shape[0])
        spread = (list_row(iota(wide, 0)) == iota(wide, 1)).astype(BF16)
        every = dot(spread, jnp.concatenate(pieces(table), axis=1))
        every = every[:, :kslots] + (every[:, kslots : 2 * kslots] + every[:, 2 * kslots :])
        mine = slot_entry(iota((slots, kslots), 0)) == iota((slots, kslots), 1)
        return jnp.sum(jnp.where(mine, every, 0.0), axis=1, keepdims=True)

    def choose(values, enc, dec):
        feat, pos, _ = place()
        own = feat * poses + pos
        tables = []
        rows = []
        for k in range(poses):
            prompt = jnp.where(pos + k >= poses, pos + k - poses, pos + k)
            tables.append(list_of(values, prompt))
            rows.append(as_rows(tables[k]))
        hits = [floor_div(ids, table_rows) == own for ids, _ in rows]
        earlier = (iota((slots, slots), 0) < iota((slots, slots), 1)).astype(BF16)
        ranks = dot(jnp.concatenate([h.astype(BF16) for h in hits], axis=0), earlier)
        picks, gains, ids_of = [], [], []
        for k in range(poses):
            chosen = jnp.where(
                hits[k] & (ranks[k : k + 1] == iota((listed, slots), 0)), 1.0, 0.0
            )
            ids = jnp.sum(chosen * rows[k][0], axis=1, keepdims=True)
            ids_of.append(ids)
            gains.append(jnp.sum(chosen * rows[k][1], axis=1, keepdims=True))
            live = jnp.sum(chosen, axis=1, keepdims=True) > 0.0
            local = jnp.where(live, ids - own * table_rows, -1.0)
            picks.append((local == iota((listed, table_rows), 1)).astype(BF16))
        picks = jnp.concatenate(picks, axis=0)
        gains = jnp.concatenate(gains, axis=0)
        ids_of = jnp.concatenate(ids_of, axis=0)
        layer = ids_of - floor_div(ids_of, layers) * layers
        enc_rows = dot(picks, enc(0)).astype(BF16)
        dec_rows = [
            (dot(picks, dec(l)) * jnp.where(layer <= l, gains, 0.0)).astype(BF16)
            for l in range(depth)
        ]
        out = []
        for k in range(poses):
            rows = slice(k * listed, (k + 1) * listed)
            out += [enc_rows[rows], jnp.stack([d[rows] for d in dec_rows], axis=0)]
        return out + [tables[0]]

    outs = [shape(listed, width, dtype=BF16), shape(depth, listed, width, dtype=BF16)] * poses
    *chosen, my_list = on_core(
        choose,
        [lists],
        outs + [shape(2 * positions * feats, kslots)],
        small,
        streams=[encoder[None], jnp.transpose(decoder, (1, 0, 2))],
        room=60,
    )
    enc_rows, dec_rows = chosen[::2], chosen[1::2]

    ring = [[enc_rows[0]] + [rotate(enc_rows[k], "pos", k) for k in range(1, poses)]]
    ring.append([ring_next(enc_rows[k], "feat", "pos", k) for k in range(poses)])
    dec_rows = [dec_rows[0]] + [rotate(dec_rows[k], "pos", k) for k in range(1, poses)]

    def places(table, pattern):
        feat, pos, rep = place()

        def padded(owner, rank):
            feat_of = floor_div(owner, poses)
            step = ring_place(feat, feats) - ring_place(feat_of, feats)
            step = jnp.where(step < 0.0, step + feats, step)
            turn = pos - (owner - feat_of * poses)
            turn = jnp.where(turn < 0.0, turn + poses, turn)
            return (step * poses + turn) * listed + rank

        ids_row = as_rows(table)[0]
        ids_col = as_col(table)
        owner_row = floor_div(ids_row, table_rows)
        owner_col = floor_div(ids_col, table_rows)
        same = owner_col == owner_row
        down, across = iota((slots, slots), 0), iota((slots, slots), 1)
        rank_col = jnp.sum(jnp.where(same & (across < down), 1.0, 0.0), axis=1, keepdims=True)
        rank_row = jnp.sum(jnp.where(same & (down < across), 1.0, 0.0), axis=0, keepdims=True)
        total = holders * listed
        placing = padded(owner_col, rank_col) == iota((slots, total), 1)
        placing_t = padded(owner_row, rank_row) == iota((total, slots), 0)
        layer = ids_col - floor_div(ids_col, layers) * layers
        layer_row = jnp.sum(jnp.where(placing, layer, 0.0), axis=0, keepdims=True)
        allowed = jnp.where(pattern[0] == 1, 1.0, 0.0).astype(BF16)

        def in_block(slot, dim, extent):
            wide = (extent, feats) if dim == 0 else (feats, extent)
            return (floor_div(slot, block_rows) == iota(wide, 1 - dim)).astype(BF16)

        sources = in_block(iota((slots, 1), 0), 0, slots)
        targets = in_block(iota((1, slots), 1), 1, slots)
        mask = dot(dot(sources, allowed, NT).astype(BF16), targets)
        mask = jnp.where(floor_div(down, kslots) <= floor_div(across, kslots), mask, 0.0)
        first = (feat * reps + rep) * result_rows
        own_slot = first + iota((result_rows, 1), 0)
        own_mask = dot(in_block(own_slot, 0, result_rows), allowed).astype(BF16)
        own_mask = dot(own_mask, targets)
        own_causal = floor_div(iota((result_rows, slots), 1), kslots) <= floor_div(
            first + iota((result_rows, slots), 0), kslots
        )
        own_mask = jnp.where(own_causal, own_mask, 0.0)
        return placing.astype(BF16), placing_t.astype(BF16), layer_row, mask.astype(BF16), own_mask

    placing, placing_t, layer_row, mask, own_mask, *ring[1][:1] = on_core(
        places,
        [my_list, block_pattern],
        [
            shape(slots, holders * listed, dtype=BF16),
            shape(holders * listed, slots, dtype=BF16),
            shape(1, holders * listed),
            shape(slots, slots, dtype=BF16),
            shape(result_rows, slots),
        ],
        small,
        through=ring[1][:1],
        cost=(4 * slots * slots * slots, 4 * slots * slots),
    )
    for _ in range(2, feats):
        ring.append([ring_next(rows, "feat") for rows in ring[-1]])

    def products(first, count, layer_row, placing_t, *values):
        enc = jnp.concatenate(values[: count * poses], axis=0)
        dec = values[count * poses : count * poses + poses]
        dec = jnp.concatenate([d[l] for l in range(depth) for d in dec], axis=0)
        every = dot(dec, enc, NT)
        lanes = slice(first * column, (first + count) * column)
        raw = jnp.zeros((column, count * column), F32)
        for l in range(depth):
            rows = every[l * column : (l + 1) * column]
            raw = raw + jnp.where(layer_row[:, lanes] == l + 1.0, rows, 0.0)
        split = dot(jnp.concatenate(pieces(raw), axis=0), placing_t[lanes])
        return split[:column] + (split[column : 2 * column] + split[2 * column :])

    def early(*values):
        return (products(0, feats - 1, *values),)

    def late(so_far, *values):
        raw = so_far + products(feats - 1, 1, *values)
        first = place()[2] == 0.0
        return (
            jnp.where(first, raw[:half], raw[half:]),
            jnp.where(first, raw[half:], raw[:half]),
        )

    early_enc = [rows for step in ring[:-1] for rows in step]
    (so_far,) = on_core(
        early,
        [layer_row, placing_t] + early_enc + list(dec_rows),
        [shape(column, slots)],
        small,
        cost=(8 * column * slots * width, 8 * column * width),
    )
    keep, send = on_core(
        late,
        [so_far, layer_row, placing_t] + list(ring[-1]) + list(dec_rows),
        [shape(half, slots)] * 2,
        small,
    )
    own_edges = (keep + rotate(send, "rep", 1)).astype(BF16)
    shards = ring_spread(own_edges, "feat")
    others = [rotate(shard, "rep", 1) for shard in shards]

    def finish(placing, mask, own_mask, targets, *values):
        feat, _, rep = place()
        first = rep == 0.0
        parts = []
        for mine, other in zip(values[:feats], values[feats:]):
            parts += [jnp.where(first, mine, other), jnp.where(first, other, mine)]
        padded = jnp.concatenate(parts, axis=0)
        magnitude = jnp.abs(dot(placing, padded) * mask.astype(F32))
        total = jnp.maximum(jnp.sum(magnitude, axis=0, keepdims=True), 1.0)
        magnitude = magnitude.astype(BF16)
        diagonal = iota((slots, slots), 0) == iota((slots, slots), 1)
        scale = 1.0 / jnp.sum(jnp.where(diagonal, total, 0.0), axis=1, keepdims=True)
        current = (iota((slots, panel), 0) == targets.astype(F32)).astype(F32)
        accum = jnp.zeros((slots, panel), F32)
        for _ in range(ITERS):
            scaled = current * scale
            high = part(scaled, small)
            low = part(scaled - high.astype(F32), small)
            both = dot(magnitude, jnp.concatenate([high, low], axis=1))
            current = both[:, :panel] + both[:, panel:]
            accum = accum + current
        index = feat * reps + rep
        influence = accum[:result_rows]
        for w in range(1, feats * reps):
            influence = jnp.where(
                index == w, accum[w * result_rows : (w + 1) * result_rows], influence
            )
        start = index * result_rows
        own = start + iota((result_rows, slots), 0) == iota((result_rows, slots), 1)
        rows = dot(own.astype(BF16), padded, NT).astype(BF16)
        edges = (dot(rows, placing, NT) * own_mask).astype(BF16)
        return edges[None], (influence * float(slots))[None]

    edges, influence = on_core(
        finish,
        [placing, mask, own_mask, target_slots] + shards + others,
        [shape(1, result_rows, slots, dtype=BF16), shape(1, result_rows, panel)],
        small,
    )
    return edges, influence


def solution(mesh):
    return jax.shard_map(
        per_device,
        mesh=mesh,
        in_specs=(
            P(("grp", "pos"), "feat", None),
            P(("grp", "pos"), "feat", None),
            P(("grp", "pos"), None, None),
            P(("grp", "pos"), None),
            P(("feat", "pos"), "rep"),
            P(("feat", "pos"), None, "rep"),
        ),
        out_specs=(
            P(("grp", "pos"), ("feat", "rep"), None),
            P(("grp", "pos"), ("feat", "rep"), None),
        ),
        check_vma=False,
    )
```

```python
import jax
import jax.numpy as jnp
from jax import lax
from jax.experimental import pallas as pl
from jax.experimental.pallas import tpu as pltpu
from jax.sharding import PartitionSpec as P

ITERS = 3
F32 = jnp.float32
BF16 = jnp.bfloat16
NN = (((1,), (0,)), ((), ()))
NT = (((1,), (1,)), ((), ()))
LANES = 128
KERNEL_SLOTS = 1024


def dot(a, b, dims=NN):
    return lax.dot_general(a, b, dims, preferred_element_type=F32)


def iota(shape, dim):
    return lax.broadcasted_iota(jnp.int32, shape, dim).astype(F32)


def floor_div(x, n):
    return jnp.floor((x + 0.5) * (1.0 / n))


def on_core(fn, args, outs, kernel=True, through=(), streams=(), cost=None, room=24):
    if not kernel:
        loads = [lambda i, x=x: x[i] for x in streams]
        return list(fn(*args, *loads)) + list(through)
    count, passed, streamed = len(args), len(through), len(streams)

    def body(*refs):
        sources = refs[count : count + streamed]
        results = refs[count + streamed + passed :][: len(outs)]
        scratch = refs[len(refs) - 2 * streamed :]
        copies = []
        for n in range(streamed):
            copies.append(
                [
                    pltpu.make_async_copy(
                        sources[n].at[i], scratch[2 * n].at[i], scratch[2 * n + 1].at[i]
                    )
                    for i in range(streams[n].shape[0])
                ]
            )
            for copy in copies[-1]:
                copy.start()

        def load(n):
            def wait(i):
                copies[n][i].wait()
                return scratch[2 * n][i]

            return wait

        values = fn(*[ref[...] for ref in refs[:count]], *[load(n) for n in range(streamed)])
        for ref, value in zip(results, values):
            ref[...] = value

    estimate = None
    if cost is not None:
        estimate = pl.CostEstimate(flops=cost[0], bytes_accessed=cost[1], transcendentals=0)
    in_vmem = pl.BlockSpec(memory_space=pltpu.VMEM)
    anywhere = pl.BlockSpec(memory_space=pl.ANY)
    scratch = []
    for x in streams:
        scratch += [pltpu.VMEM(x.shape, x.dtype), pltpu.SemaphoreType.DMA((x.shape[0],))]
    call = pl.pallas_call(
        body,
        out_shape=list(outs) + [jax.ShapeDtypeStruct(x.shape, x.dtype) for x in through],
        in_specs=[in_vmem] * count
        + [pl.BlockSpec(memory_space=pltpu.HBM)] * streamed
        + [anywhere] * passed,
        out_specs=[in_vmem] * len(outs) + [anywhere] * passed,
        scratch_shapes=scratch,
        input_output_aliases={count + streamed + i: len(outs) + i for i in range(passed)},
        compiler_params=pltpu.CompilerParams(vmem_limit_bytes=room * 1024 * 1024),
        cost_estimate=estimate,
    )
    return list(call(*args, *streams, *through))


def rotate(x, axis, step):
    count = lax.axis_size(axis)
    return lax.ppermute(x, axis, [(i, (i + step) % count) for i in range(count)])


def ring_place(index, count):
    low = floor_div(index, 2)
    return jnp.where(index > 2 * low, count - 1 - low, low)


def ring_next(x, axis, across=None, turn=0):
    count = lax.axis_size(axis)
    order = list(range(0, count, 2)) + list(range(1, count, 2))[::-1]
    steps = [(order[i], order[(i + 1) % count]) for i in range(count)]
    if across is None:
        return lax.ppermute(x, axis, steps)
    wide = lax.axis_size(across)
    pairs = [(a * wide + i, b * wide + (i + turn) % wide) for a, b in steps for i in range(wide)]
    return lax.ppermute(x, (axis, across), pairs)


def ring_spread(x, axis):
    count = lax.axis_size(axis)
    order = list(range(0, count, 2)) + list(range(1, count, 2))[::-1]
    return [x] + [
        lax.ppermute(x, axis, [(order[i], order[(i + k) % count]) for i in range(count)])
        for k in range(1, count)
    ]


def part(x, kernel):
    return x.astype(BF16) if kernel else lax.reduce_precision(x, 8, 7).astype(BF16)


def shape(*dims, dtype=F32):
    return jax.ShapeDtypeStruct(dims, dtype)


def per_device(active_ids, active_vals, block_pattern, target_slots, encoder, decoder):
    feats = lax.axis_size("feat")
    poses = lax.axis_size("pos")
    reps = lax.axis_size("rep")
    holders = feats * poses
    table_rows, width = encoder.shape
    depth = decoder.shape[1]
    layers = depth + 1
    positions, kslots = active_ids.shape[1:]
    block_rows = positions * kslots
    slots = block_rows * feats
    capacity = max(2, (10 * block_rows + 7 * holders - 1) // (7 * holders))
    listed = capacity * feats
    column = poses * listed
    half = column // reps
    result_rows = block_rows // reps
    panel = target_slots.shape[1]
    small = slots <= KERNEL_SLOTS

    def place():
        feat, pos = lax.axis_index("feat"), lax.axis_index("pos")
        return feat.astype(F32), pos.astype(F32), lax.axis_index("rep").astype(F32)

    def pack(ids, vals):
        one = jnp.concatenate([ids(0).astype(F32), vals(0)], axis=0)
        one = jnp.concatenate([one, jnp.zeros((2 * positions, LANES - kslots), F32)], axis=1)
        return (jnp.broadcast_to(one, (holders,) + one.shape),)

    (packed,) = on_core(
        pack,
        [],
        [shape(holders, 2 * positions, LANES)],
        streams=[active_ids, active_vals],
        room=60,
    )
    lists = lax.all_to_all(packed, ("feat", "pos"), split_axis=0, concat_axis=0, tiled=True)

    def list_of(values, prompt):
        blocks = []
        for a in range(feats):
            block = values[a * poses]
            for q in range(1, poses):
                block = jnp.where(prompt == q, values[a * poses + q], block)
            blocks.append(block)
        return jnp.concatenate(blocks, axis=0)[:, :kslots]

    def list_row(slot):
        place = floor_div(slot, kslots)
        return place + floor_div(place, positions) * positions

    def slot_entry(slot):
        return slot - floor_div(slot, kslots) * kslots

    def pieces(table):
        high = part(table, small)
        rest = table - high.astype(F32)
        middle = part(rest, small)
        return [high, middle, part(rest - middle.astype(F32), small)]

    def as_rows(table):
        spread = (iota((kslots, slots), 0) == slot_entry(iota((kslots, slots), 1))).astype(BF16)
        wide = dot(jnp.concatenate(pieces(table), axis=0), spread)
        count = table.shape[0]
        wide = wide[:count] + (wide[count : 2 * count] + wide[2 * count :])
        row = iota(wide.shape, 0) - list_row(iota(wide.shape, 1))
        ids = jnp.sum(jnp.where(row == 0, wide, 0.0), axis=0, keepdims=True)
        return ids, jnp.sum(jnp.where(row == positions, wide, 0.0), axis=0, keepdims=True)

    def as_col(table):
        wide = (slots, table.shape[0])
        spread = (list_row(iota(wide, 0)) == iota(wide, 1)).astype(BF16)
        every = dot(spread, jnp.concatenate(pieces(table), axis=1))
        every = every[:, :kslots] + (every[:, kslots : 2 * kslots] + every[:, 2 * kslots :])
        mine = slot_entry(iota((slots, kslots), 0)) == iota((slots, kslots), 1)
        return jnp.sum(jnp.where(mine, every, 0.0), axis=1, keepdims=True)

    def choose(values):
        feat, pos, _ = place()
        own = feat * poses + pos
        tables = []
        rows = []
        for k in range(poses):
            prompt = jnp.where(pos + k >= poses, pos + k - poses, pos + k)
            tables.append(list_of(values, prompt))
            rows.append(as_rows(tables[k]))
        hits = [floor_div(ids, table_rows) == own for ids, _ in rows]
        earlier = (iota((slots, slots), 0) < iota((slots, slots), 1)).astype(BF16)
        ranks = dot(jnp.concatenate([h.astype(BF16) for h in hits], axis=0), earlier)
        picks, gains, ids_of = [], [], []
        for k in range(poses):
            chosen = jnp.where(
                hits[k] & (ranks[k : k + 1] == iota((listed, slots), 0)), 1.0, 0.0
            )
            ids = jnp.sum(chosen * rows[k][0], axis=1, keepdims=True)
            ids_of.append(ids)
            gains.append(jnp.sum(chosen * rows[k][1], axis=1, keepdims=True))
            live = jnp.sum(chosen, axis=1, keepdims=True) > 0.0
            local = jnp.where(live, ids - own * table_rows, -1.0)
            picks.append((local == iota((listed, table_rows), 1)).astype(BF16))
        picks = jnp.concatenate(picks, axis=0)
        gains = jnp.concatenate(gains, axis=0)
        ids_of = jnp.concatenate(ids_of, axis=0)
        layer = ids_of - floor_div(ids_of, layers) * layers
        gains = jnp.concatenate([jnp.where(layer <= l, gains, 0.0) for l in range(depth)], axis=1)
        return picks, gains, tables[0]

    picks, gains, my_list = on_core(
        choose,
        [lists],
        [
            shape(column, table_rows, dtype=BF16),
            shape(column, depth),
            shape(2 * positions * feats, kslots),
        ],
        small,
    )

    def encode(picks, enc):
        rows = dot(picks, enc).astype(BF16)
        return [rows[k * listed : (k + 1) * listed] for k in range(poses)]

    enc_rows = on_core(
        encode, [picks, encoder], [shape(listed, width, dtype=BF16)] * poses, small
    )

    ring = [[enc_rows[0]] + [rotate(enc_rows[k], "pos", k) for k in range(1, poses)]]
    ring.append([ring_next(enc_rows[k], "feat", "pos", k) for k in range(poses)])

    def decode(picks, gains, dec):
        rows = [(dot(picks, dec[l]) * gains[:, l : l + 1]).astype(BF16) for l in range(depth)]
        return [
            jnp.stack([row[k * listed : (k + 1) * listed] for row in rows], axis=0)
            for k in range(poses)
        ]

    dec_rows = on_core(
        decode,
        [picks, gains, jnp.transpose(decoder, (1, 0, 2))],
        [shape(depth, listed, width, dtype=BF16)] * poses,
        small,
        cost=(1, 1),
    )
    dec_rows = [dec_rows[0]] + [rotate(dec_rows[k], "pos", k) for k in range(1, poses)]

    def places(table, pattern):
        feat, pos, rep = place()

        def padded(owner, rank):
            feat_of = floor_div(owner, poses)
            step = ring_place(feat, feats) - ring_place(feat_of, feats)
            step = jnp.where(step < 0.0, step + feats, step)
            turn = pos - (owner - feat_of * poses)
            turn = jnp.where(turn < 0.0, turn + poses, turn)
            return (step * poses + turn) * listed + rank

        ids_row = as_rows(table)[0]
        ids_col = as_col(table)
        owner_row = floor_div(ids_row, table_rows)
        owner_col = floor_div(ids_col, table_rows)
        same = owner_col == owner_row
        down, across = iota((slots, slots), 0), iota((slots, slots), 1)
        rank_col = jnp.sum(jnp.where(same & (across < down), 1.0, 0.0), axis=1, keepdims=True)
        rank_row = jnp.sum(jnp.where(same & (down < across), 1.0, 0.0), axis=0, keepdims=True)
        total = holders * listed
        placing = padded(owner_col, rank_col) == iota((slots, total), 1)
        placing_t = padded(owner_row, rank_row) == iota((total, slots), 0)
        layer = ids_col - floor_div(ids_col, layers) * layers
        layer_row = jnp.sum(jnp.where(placing, layer, 0.0), axis=0, keepdims=True)
        allowed = jnp.where(pattern[0] == 1, 1.0, 0.0).astype(BF16)

        def in_block(slot, dim, extent):
            wide = (extent, feats) if dim == 0 else (feats, extent)
            return (floor_div(slot, block_rows) == iota(wide, 1 - dim)).astype(BF16)

        sources = in_block(iota((slots, 1), 0), 0, slots)
        targets = in_block(iota((1, slots), 1), 1, slots)
        mask = dot(dot(sources, allowed, NT).astype(BF16), targets)
        mask = jnp.where(floor_div(down, kslots) <= floor_div(across, kslots), mask, 0.0)
        first = (feat * reps + rep) * result_rows
        own_slot = first + iota((result_rows, 1), 0)
        own_mask = dot(in_block(own_slot, 0, result_rows), allowed).astype(BF16)
        own_mask = dot(own_mask, targets)
        own_causal = floor_div(iota((result_rows, slots), 1), kslots) <= floor_div(
            first + iota((result_rows, slots), 0), kslots
        )
        own_mask = jnp.where(own_causal, own_mask, 0.0)
        return placing.astype(BF16), placing_t.astype(BF16), layer_row, mask.astype(BF16), own_mask

    placing, placing_t, layer_row, mask, own_mask, ring[1][-1] = on_core(
        places,
        [my_list, block_pattern],
        [
            shape(slots, holders * listed, dtype=BF16),
            shape(holders * listed, slots, dtype=BF16),
            shape(1, holders * listed),
            shape(slots, slots, dtype=BF16),
            shape(result_rows, slots),
        ],
        small,
        through=ring[1][-1:],
        cost=(1, 1),
    )
    for _ in range(2, feats):
        ring.append([ring_next(rows, "feat") for rows in ring[-1]])

    def products(first, count, layer_row, placing_t, *values):
        enc = jnp.concatenate(values[: count * poses], axis=0)
        dec = values[count * poses : count * poses + poses]
        dec = jnp.concatenate([d[l] for l in range(depth) for d in dec], axis=0)
        every = dot(dec, enc, NT)
        lanes = slice(first * column, (first + count) * column)
        raw = jnp.zeros((column, count * column), F32)
        for l in range(depth):
            rows = every[l * column : (l + 1) * column]
            raw = raw + jnp.where(layer_row[:, lanes] == l + 1.0, rows, 0.0)
        split = dot(jnp.concatenate(pieces(raw), axis=0), placing_t[lanes])
        return split[:column] + (split[column : 2 * column] + split[2 * column :])

    def early(*values):
        return (products(0, feats - 1, *values),)

    def late(so_far, *values):
        raw = so_far + products(feats - 1, 1, *values)
        first = place()[2] == 0.0
        return (
            jnp.where(first, raw[:half], raw[half:]),
            jnp.where(first, raw[half:], raw[:half]),
        )

    early_enc = [rows for step in ring[:-1] for rows in step]
    (so_far,) = on_core(
        early,
        [layer_row, placing_t] + early_enc + list(dec_rows),
        [shape(column, slots)],
        small,
        cost=(1, 1),
    )
    keep, send = on_core(
        late,
        [so_far, layer_row, placing_t] + list(ring[-1]) + list(dec_rows),
        [shape(half, slots)] * 2,
        small,
    )
    own_edges = (keep + rotate(send, "rep", 1)).astype(BF16)
    shards = ring_spread(own_edges, "feat")
    others = [rotate(shard, "rep", 1) for shard in shards]

    def finish(placing, mask, own_mask, targets, *values):
        feat, _, rep = place()
        first = rep == 0.0
        parts = []
        for mine, other in zip(values[:feats], values[feats:]):
            parts += [jnp.where(first, mine, other), jnp.where(first, other, mine)]
        padded = jnp.concatenate(parts, axis=0)
        magnitude = jnp.abs(dot(placing, padded) * mask.astype(F32))
        total = jnp.maximum(jnp.sum(magnitude, axis=0, keepdims=True), 1.0)
        magnitude = magnitude.astype(BF16)
        diagonal = iota((slots, slots), 0) == iota((slots, slots), 1)
        scale = 1.0 / jnp.sum(jnp.where(diagonal, total, 0.0), axis=1, keepdims=True)
        current = (iota((slots, panel), 0) == targets.astype(F32)).astype(F32)
        accum = jnp.zeros((slots, panel), F32)
        for _ in range(ITERS):
            scaled = current * scale
            high = part(scaled, small)
            low = part(scaled - high.astype(F32), small)
            both = dot(magnitude, jnp.concatenate([high, low], axis=1))
            current = both[:, :panel] + both[:, panel:]
            accum = accum + current
        index = feat * reps + rep
        influence = accum[:result_rows]
        for w in range(1, feats * reps):
            influence = jnp.where(
                index == w, accum[w * result_rows : (w + 1) * result_rows], influence
            )
        start = index * result_rows
        own = start + iota((result_rows, slots), 0) == iota((result_rows, slots), 1)
        rows = dot(own.astype(BF16), padded, NT).astype(BF16)
        edges = (dot(rows, placing, NT) * own_mask).astype(BF16)
        return edges[None], (influence * float(slots))[None]

    edges, influence = on_core(
        finish,
        [placing, mask, own_mask, target_slots] + shards + others,
        [shape(1, result_rows, slots, dtype=BF16), shape(1, result_rows, panel)],
        small,
    )
    return edges, influence


def solution(mesh):
    return jax.shard_map(
        per_device,
        mesh=mesh,
        in_specs=(
            P(("grp", "pos"), "feat", None),
            P(("grp", "pos"), "feat", None),
            P(("grp", "pos"), None, None),
            P(("grp", "pos"), None),
            P(("feat", "pos"), "rep"),
            P(("feat", "pos"), None, "rep"),
        ),
        out_specs=(
            P(("grp", "pos"), ("feat", "rep"), None),
            P(("grp", "pos"), ("feat", "rep"), None),
        ),
        check_vma=False,
    )
```

```python
import jax
import jax.numpy as jnp
from jax import lax
from jax.experimental import pallas as pl
from jax.experimental.pallas import tpu as pltpu
from jax.sharding import PartitionSpec as P

ITERS = 3
F32 = jnp.float32
BF16 = jnp.bfloat16
NN = (((1,), (0,)), ((), ()))
NT = (((1,), (1,)), ((), ()))
LANES = 128
KERNEL_SLOTS = 1024


def dot(a, b, dims=NN):
    return lax.dot_general(a, b, dims, preferred_element_type=F32)


def iota(shape, dim):
    return lax.broadcasted_iota(jnp.int32, shape, dim).astype(F32)


def floor_div(x, n):
    return jnp.floor((x + 0.5) * (1.0 / n))


def on_core(fn, args, outs, kernel=True, through=(), streams=(), cost=None, room=24):
    if not kernel:
        loads = [lambda i, x=x: x[i] for x in streams]
        return list(fn(*args, *loads)) + list(through)
    count, passed, streamed = len(args), len(through), len(streams)

    def body(*refs):
        sources = refs[count : count + streamed]
        results = refs[count + streamed + passed :][: len(outs)]
        scratch = refs[len(refs) - 2 * streamed :]
        copies = []
        for n in range(streamed):
            copies.append(
                [
                    pltpu.make_async_copy(
                        sources[n].at[i], scratch[2 * n].at[i], scratch[2 * n + 1].at[i]
                    )
                    for i in range(streams[n].shape[0])
                ]
            )
            for copy in copies[-1]:
                copy.start()

        def load(n):
            def wait(i):
                copies[n][i].wait()
                return scratch[2 * n][i]

            return wait

        values = fn(*[ref[...] for ref in refs[:count]], *[load(n) for n in range(streamed)])
        for ref, value in zip(results, values):
            ref[...] = value

    estimate = None
    if cost is not None:
        estimate = pl.CostEstimate(flops=cost[0], bytes_accessed=cost[1], transcendentals=0)
    in_vmem = pl.BlockSpec(memory_space=pltpu.VMEM)
    anywhere = pl.BlockSpec(memory_space=pl.ANY)
    scratch = []
    for x in streams:
        scratch += [pltpu.VMEM(x.shape, x.dtype), pltpu.SemaphoreType.DMA((x.shape[0],))]
    call = pl.pallas_call(
        body,
        out_shape=list(outs) + [jax.ShapeDtypeStruct(x.shape, x.dtype) for x in through],
        in_specs=[in_vmem] * count
        + [pl.BlockSpec(memory_space=pltpu.HBM)] * streamed
        + [anywhere] * passed,
        out_specs=[in_vmem] * len(outs) + [anywhere] * passed,
        scratch_shapes=scratch,
        input_output_aliases={count + streamed + i: len(outs) + i for i in range(passed)},
        compiler_params=pltpu.CompilerParams(vmem_limit_bytes=room * 1024 * 1024),
        cost_estimate=estimate,
    )
    return list(call(*args, *streams, *through))


def rotate(x, axis, step):
    count = lax.axis_size(axis)
    return lax.ppermute(x, axis, [(i, (i + step) % count) for i in range(count)])


def swap(x, axis, bit):
    return lax.ppermute(x, axis, [(i, i ^ bit) for i in range(lax.axis_size(axis))])


def ring_place(index, count):
    low = floor_div(index, 2)
    return jnp.where(index > 2 * low, count - 1 - low, low)


def ring_next(x, axis, across=None, turn=0):
    count = lax.axis_size(axis)
    order = list(range(0, count, 2)) + list(range(1, count, 2))[::-1]
    steps = [(order[i], order[(i + 1) % count]) for i in range(count)]
    if across is None:
        return lax.ppermute(x, axis, steps)
    wide = lax.axis_size(across)
    pairs = [(a * wide + i, b * wide + (i + turn) % wide) for a, b in steps for i in range(wide)]
    return lax.ppermute(x, (axis, across), pairs)


def ring_spread(x, axis):
    count = lax.axis_size(axis)
    order = list(range(0, count, 2)) + list(range(1, count, 2))[::-1]
    return [x] + [
        lax.ppermute(x, axis, [(order[i], order[(i + k) % count]) for i in range(count)])
        for k in range(1, count)
    ]


def part(x, kernel):
    return x.astype(BF16) if kernel else lax.reduce_precision(x, 8, 7).astype(BF16)


def shape(*dims, dtype=F32):
    return jax.ShapeDtypeStruct(dims, dtype)


def per_device(active_ids, active_vals, block_pattern, target_slots, encoder, decoder):
    feats = lax.axis_size("feat")
    poses = lax.axis_size("pos")
    reps = lax.axis_size("rep")
    holders = feats * poses
    table_rows, width = encoder.shape
    depth = decoder.shape[1]
    layers = depth + 1
    positions, kslots = active_ids.shape[1:]
    block_rows = positions * kslots
    slots = block_rows * feats
    capacity = max(2, (10 * block_rows + 7 * holders - 1) // (7 * holders))
    listed = capacity * feats
    column = poses * listed
    half = column // reps
    result_rows = block_rows // reps
    panel = target_slots.shape[1]
    small = slots <= KERNEL_SLOTS

    def place():
        feat, pos = lax.axis_index("feat"), lax.axis_index("pos")
        return feat.astype(F32), pos.astype(F32), lax.axis_index("rep").astype(F32)

    def pack(ids, vals):
        one = jnp.concatenate([ids[0].astype(F32), vals[0]], axis=0)
        return jnp.concatenate([one, jnp.zeros((2 * positions, LANES - kslots), F32)], axis=1)[None]

    def joined(mine, other, upper):
        first = jnp.where(upper, other, mine)
        return jnp.concatenate([first, jnp.where(upper, mine, other)], axis=0)

    def upper(axis, bit):
        return lax.rem(lax.axis_index(axis) // bit, 2) == 1

    steps = [("pos", 1 << i) for i in range(poses.bit_length() - 1)]
    steps += [("feat", 1 << i) for i in range(feats.bit_length() - 1)]
    axis, bit = steps[0]
    arrived = [swap(x, axis, bit) for x in (active_ids, active_vals)]
    lists = on_core(
        lambda a, b, c, d: (joined(pack(a, b), pack(c, d), upper("pos", 1)),),
        [active_ids, active_vals] + arrived,
        [shape(2, 2 * positions, LANES)],
    )[0]
    for axis, bit in steps[1:-1]:
        lists = on_core(
            lambda a, b: (joined(a, b, upper(axis, bit)),),
            [lists, swap(lists, axis, bit)],
            [shape(2 * lists.shape[0], 2 * positions, LANES)],
        )[0]
    last = steps[-1]
    lists = [lists, swap(lists, *last)]

    def list_of(values, prompt):
        blocks = []
        for a in range(feats):
            block = values[a * poses]
            for q in range(1, poses):
                block = jnp.where(prompt == q, values[a * poses + q], block)
            blocks.append(block)
        return jnp.concatenate(blocks, axis=0)[:, :kslots]

    def list_row(slot):
        place = floor_div(slot, kslots)
        return place + floor_div(place, positions) * positions

    def slot_entry(slot):
        return slot - floor_div(slot, kslots) * kslots

    def pieces(table):
        high = part(table, small)
        rest = table - high.astype(F32)
        middle = part(rest, small)
        return [high, middle, part(rest - middle.astype(F32), small)]

    def as_rows(table):
        spread = (iota((kslots, slots), 0) == slot_entry(iota((kslots, slots), 1))).astype(BF16)
        wide = dot(jnp.concatenate(pieces(table), axis=0), spread)
        count = table.shape[0]
        wide = wide[:count] + (wide[count : 2 * count] + wide[2 * count :])
        row = iota(wide.shape, 0) - list_row(iota(wide.shape, 1))
        ids = jnp.sum(jnp.where(row == 0, wide, 0.0), axis=0, keepdims=True)
        return ids, jnp.sum(jnp.where(row == positions, wide, 0.0), axis=0, keepdims=True)

    def as_col(table):
        wide = (slots, table.shape[0])
        spread = (list_row(iota(wide, 0)) == iota(wide, 1)).astype(BF16)
        every = dot(spread, jnp.concatenate(pieces(table), axis=1))
        every = every[:, :kslots] + (every[:, kslots : 2 * kslots] + every[:, 2 * kslots :])
        mine = slot_entry(iota((slots, kslots), 0)) == iota((slots, kslots), 1)
        return jnp.sum(jnp.where(mine, every, 0.0), axis=1, keepdims=True)

    def choose(mine, other):
        values = joined(mine, other, upper(*last))
        feat, pos, _ = place()
        own = feat * poses + pos
        tables = []
        rows = []
        for k in range(poses):
            prompt = jnp.where(pos + k >= poses, pos + k - poses, pos + k)
            tables.append(list_of(values, prompt))
            rows.append(as_rows(tables[k]))
        hits = [floor_div(ids, table_rows) == own for ids, _ in rows]
        earlier = (iota((slots, slots), 0) < iota((slots, slots), 1)).astype(BF16)
        ranks = dot(jnp.concatenate([h.astype(BF16) for h in hits], axis=0), earlier)
        picks, gains, ids_of = [], [], []
        for k in range(poses):
            chosen = jnp.where(
                hits[k] & (ranks[k : k + 1] == iota((listed, slots), 0)), 1.0, 0.0
            )
            ids = jnp.sum(chosen * rows[k][0], axis=1, keepdims=True)
            ids_of.append(ids)
            gains.append(jnp.sum(chosen * rows[k][1], axis=1, keepdims=True))
            live = jnp.sum(chosen, axis=1, keepdims=True) > 0.0
            local = jnp.where(live, ids - own * table_rows, -1.0)
            picks.append((local == iota((listed, table_rows), 1)).astype(BF16))
        picks = jnp.concatenate(picks, axis=0)
        gains = jnp.concatenate(gains, axis=0)
        ids_of = jnp.concatenate(ids_of, axis=0)
        layer = ids_of - floor_div(ids_of, layers) * layers
        gains = jnp.concatenate([jnp.where(layer <= l, gains, 0.0) for l in range(depth)], axis=1)
        return picks, gains, tables[0]

    picks, gains, my_list = on_core(
        choose,
        lists,
        [
            shape(column, table_rows, dtype=BF16),
            shape(column, depth),
            shape(2 * positions * feats, kslots),
        ],
        small,
    )

    def encode(picks, enc):
        rows = dot(picks, enc).astype(BF16)
        return [rows[k * listed : (k + 1) * listed] for k in range(poses)]

    enc_rows = on_core(
        encode, [picks, encoder], [shape(listed, width, dtype=BF16)] * poses, small
    )

    ring = [[enc_rows[0]] + [rotate(enc_rows[k], "pos", k) for k in range(1, poses)]]
    ring.append([ring_next(enc_rows[k], "feat", "pos", k) for k in range(poses)])

    def decode(picks, gains, dec):
        rows = [(dot(picks, dec[l]) * gains[:, l : l + 1]).astype(BF16) for l in range(depth)]
        return [
            jnp.stack([row[k * listed : (k + 1) * listed] for row in rows], axis=0)
            for k in range(poses)
        ]

    dec_rows = on_core(
        decode,
        [picks, gains, jnp.transpose(decoder, (1, 0, 2))],
        [shape(depth, listed, width, dtype=BF16)] * poses,
        small,
        cost=(1, 1),
    )
    dec_rows = [dec_rows[0]] + [rotate(dec_rows[k], "pos", k) for k in range(1, poses)]

    def places(table, pattern):
        feat, pos, rep = place()

        def padded(owner, rank):
            feat_of = floor_div(owner, poses)
            step = ring_place(feat, feats) - ring_place(feat_of, feats)
            step = jnp.where(step < 0.0, step + feats, step)
            turn = pos - (owner - feat_of * poses)
            turn = jnp.where(turn < 0.0, turn + poses, turn)
            return (step * poses + turn) * listed + rank

        ids_row = as_rows(table)[0]
        ids_col = as_col(table)
        owner_row = floor_div(ids_row, table_rows)
        owner_col = floor_div(ids_col, table_rows)
        same = owner_col == owner_row
        down, across = iota((slots, slots), 0), iota((slots, slots), 1)
        rank_col = jnp.sum(jnp.where(same & (across < down), 1.0, 0.0), axis=1, keepdims=True)
        rank_row = jnp.sum(jnp.where(same & (down < across), 1.0, 0.0), axis=0, keepdims=True)
        total = holders * listed
        placing = padded(owner_col, rank_col) == iota((slots, total), 1)
        placing_t = padded(owner_row, rank_row) == iota((total, slots), 0)
        layer = ids_col - floor_div(ids_col, layers) * layers
        layer_row = jnp.sum(jnp.where(placing, layer, 0.0), axis=0, keepdims=True)
        allowed = jnp.where(pattern[0] == 1, 1.0, 0.0).astype(BF16)

        def in_block(slot, dim, extent):
            wide = (extent, feats) if dim == 0 else (feats, extent)
            return (floor_div(slot, block_rows) == iota(wide, 1 - dim)).astype(BF16)

        sources = in_block(iota((slots, 1), 0), 0, slots)
        targets = in_block(iota((1, slots), 1), 1, slots)
        mask = dot(dot(sources, allowed, NT).astype(BF16), targets)
        mask = jnp.where(floor_div(down, kslots) <= floor_div(across, kslots), mask, 0.0)
        first = (feat * reps + rep) * result_rows
        own_slot = first + iota((result_rows, 1), 0)
        own_mask = dot(in_block(own_slot, 0, result_rows), allowed).astype(BF16)
        own_mask = dot(own_mask, targets)
        own_causal = floor_div(iota((result_rows, slots), 1), kslots) <= floor_div(
            first + iota((result_rows, slots), 0), kslots
        )
        own_mask = jnp.where(own_causal, own_mask, 0.0)
        return placing.astype(BF16), placing_t.astype(BF16), layer_row, mask.astype(BF16), own_mask

    placing, placing_t, layer_row, mask, own_mask, ring[1][0] = on_core(
        places,
        [my_list, block_pattern],
        [
            shape(slots, holders * listed, dtype=BF16),
            shape(holders * listed, slots, dtype=BF16),
            shape(1, holders * listed),
            shape(slots, slots, dtype=BF16),
            shape(result_rows, slots),
        ],
        small,
        through=ring[1][:1],
        cost=(1, 1),
    )
    for _ in range(2, feats):
        ring.append([ring_next(rows, "feat") for rows in ring[-1]])

    def products(first, count, layer_row, placing_t, *values):
        enc = jnp.concatenate(values[: count * poses], axis=0)
        dec = values[count * poses : count * poses + poses]
        dec = jnp.concatenate([d[l] for l in range(depth) for d in dec], axis=0)
        every = dot(dec, enc, NT)
        lanes = slice(first * column, (first + count) * column)
        raw = jnp.zeros((column, count * column), F32)
        for l in range(depth):
            rows = every[l * column : (l + 1) * column]
            raw = raw + jnp.where(layer_row[:, lanes] == l + 1.0, rows, 0.0)
        split = dot(jnp.concatenate(pieces(raw), axis=0), placing_t[lanes])
        return split[:column] + (split[column : 2 * column] + split[2 * column :])

    def early(*values):
        return (products(0, feats - 1, *values),)

    def late(so_far, *values):
        raw = so_far + products(feats - 1, 1, *values)
        first = place()[2] == 0.0
        return (
            jnp.where(first, raw[:half], raw[half:]),
            jnp.where(first, raw[half:], raw[:half]),
        )

    early_enc = [rows for step in ring[:-1] for rows in step]
    (so_far,) = on_core(
        early,
        [layer_row, placing_t] + early_enc + list(dec_rows),
        [shape(column, slots)],
        small,
        cost=(1, 1),
    )
    keep, send = on_core(
        late,
        [so_far, layer_row, placing_t] + list(ring[-1]) + list(dec_rows),
        [shape(half, slots)] * 2,
        small,
    )
    own_edges = (keep + rotate(send, "rep", 1)).astype(BF16)
    shards = ring_spread(own_edges, "feat")
    others = [rotate(shard, "rep", 1) for shard in shards]

    def finish(placing, mask, own_mask, targets, *values):
        feat, _, rep = place()
        first = rep == 0.0
        parts = []
        for mine, other in zip(values[:feats], values[feats:]):
            parts += [jnp.where(first, mine, other), jnp.where(first, other, mine)]
        padded = jnp.concatenate(parts, axis=0)
        magnitude = jnp.abs(dot(placing, padded) * mask.astype(F32))
        total = jnp.maximum(jnp.sum(magnitude, axis=0, keepdims=True), 1.0)
        magnitude = magnitude.astype(BF16)
        diagonal = iota((slots, slots), 0) == iota((slots, slots), 1)
        scale = 1.0 / jnp.sum(jnp.where(diagonal, total, 0.0), axis=1, keepdims=True)
        current = (iota((slots, panel), 0) == targets.astype(F32)).astype(F32)
        accum = jnp.zeros((slots, panel), F32)
        for _ in range(ITERS):
            scaled = current * scale
            high = part(scaled, small)
            low = part(scaled - high.astype(F32), small)
            both = dot(magnitude, jnp.concatenate([high, low], axis=1))
            current = both[:, :panel] + both[:, panel:]
            accum = accum + current
        index = feat * reps + rep
        influence = accum[:result_rows]
        for w in range(1, feats * reps):
            influence = jnp.where(
                index == w, accum[w * result_rows : (w + 1) * result_rows], influence
            )
        start = index * result_rows
        own = start + iota((result_rows, slots), 0) == iota((result_rows, slots), 1)
        rows = dot(own.astype(BF16), padded, NT).astype(BF16)
        edges = (dot(rows, placing, NT) * own_mask).astype(BF16)
        return edges[None], (influence * float(slots))[None]

    edges, influence = on_core(
        finish,
        [placing, mask, own_mask, target_slots] + shards + others,
        [shape(1, result_rows, slots, dtype=BF16), shape(1, result_rows, panel)],
        small,
    )
    return edges, influence


def solution(mesh):
    return jax.shard_map(
        per_device,
        mesh=mesh,
        in_specs=(
            P(("grp", "pos"), "feat", None),
            P(("grp", "pos"), "feat", None),
            P(("grp", "pos"), None, None),
            P(("grp", "pos"), None),
            P(("feat", "pos"), "rep"),
            P(("feat", "pos"), None, "rep"),
        ),
        out_specs=(
            P(("grp", "pos"), ("feat", "rep"), None),
            P(("grp", "pos"), ("feat", "rep"), None),
        ),
        check_vma=False,
    )
```

```python
import jax
import jax.numpy as jnp
from jax import lax
from jax.experimental import pallas as pl
from jax.experimental.pallas import tpu as pltpu
from jax.sharding import PartitionSpec as P

ITERS = 3
F32 = jnp.float32
BF16 = jnp.bfloat16
NN = (((1,), (0,)), ((), ()))
NT = (((1,), (1,)), ((), ()))
LANES = 128
KERNEL_SLOTS = 1024


def dot(a, b, dims=NN):
    return lax.dot_general(a, b, dims, preferred_element_type=F32)


def iota(shape, dim):
    return lax.broadcasted_iota(jnp.int32, shape, dim).astype(F32)


def floor_div(x, n):
    return jnp.floor((x + 0.5) * (1.0 / n))


def on_core(fn, args, outs, kernel=True, through=(), streams=(), cost=None, room=24):
    if not kernel:
        loads = [lambda i, x=x: x[i] for x in streams]
        return list(fn(*args, *loads)) + list(through)
    count, passed, streamed = len(args), len(through), len(streams)

    def body(*refs):
        sources = refs[count : count + streamed]
        results = refs[count + streamed + passed :][: len(outs)]
        scratch = refs[len(refs) - 2 * streamed :]
        copies = []
        for n in range(streamed):
            copies.append(
                [
                    pltpu.make_async_copy(
                        sources[n].at[i], scratch[2 * n].at[i], scratch[2 * n + 1].at[i]
                    )
                    for i in range(streams[n].shape[0])
                ]
            )
            for copy in copies[-1]:
                copy.start()

        def load(n):
            def wait(i):
                copies[n][i].wait()
                return scratch[2 * n][i]

            return wait

        values = fn(*[ref[...] for ref in refs[:count]], *[load(n) for n in range(streamed)])
        for ref, value in zip(results, values):
            ref[...] = value

    estimate = None
    if cost is not None:
        estimate = pl.CostEstimate(flops=cost[0], bytes_accessed=cost[1], transcendentals=0)
    in_vmem = pl.BlockSpec(memory_space=pltpu.VMEM)
    anywhere = pl.BlockSpec(memory_space=pl.ANY)
    scratch = []
    for x in streams:
        scratch += [pltpu.VMEM(x.shape, x.dtype), pltpu.SemaphoreType.DMA((x.shape[0],))]
    call = pl.pallas_call(
        body,
        out_shape=list(outs) + [jax.ShapeDtypeStruct(x.shape, x.dtype) for x in through],
        in_specs=[in_vmem] * count
        + [pl.BlockSpec(memory_space=pltpu.HBM)] * streamed
        + [anywhere] * passed,
        out_specs=[in_vmem] * len(outs) + [anywhere] * passed,
        scratch_shapes=scratch,
        input_output_aliases={count + streamed + i: len(outs) + i for i in range(passed)},
        compiler_params=pltpu.CompilerParams(vmem_limit_bytes=room * 1024 * 1024),
        cost_estimate=estimate,
    )
    return list(call(*args, *streams, *through))


def rotate(x, axis, step):
    count = lax.axis_size(axis)
    return lax.ppermute(x, axis, [(i, (i + step) % count) for i in range(count)])


def ring_place(index, count):
    low = floor_div(index, 2)
    return jnp.where(index > 2 * low, count - 1 - low, low)


def ring_next(x, axis, across=None, turn=0):
    count = lax.axis_size(axis)
    order = list(range(0, count, 2)) + list(range(1, count, 2))[::-1]
    steps = [(order[i], order[(i + 1) % count]) for i in range(count)]
    if across is None:
        return lax.ppermute(x, axis, steps)
    wide = lax.axis_size(across)
    pairs = [(a * wide + i, b * wide + (i + turn) % wide) for a, b in steps for i in range(wide)]
    return lax.ppermute(x, (axis, across), pairs)


def ring_spread(x, axis):
    count = lax.axis_size(axis)
    order = list(range(0, count, 2)) + list(range(1, count, 2))[::-1]
    return [x] + [
        lax.ppermute(x, axis, [(order[i], order[(i + k) % count]) for i in range(count)])
        for k in range(1, count)
    ]


def part(x, kernel):
    return x.astype(BF16) if kernel else lax.reduce_precision(x, 8, 7).astype(BF16)


def shape(*dims, dtype=F32):
    return jax.ShapeDtypeStruct(dims, dtype)


def per_device(active_ids, active_vals, block_pattern, target_slots, encoder, decoder):
    feats = lax.axis_size("feat")
    poses = lax.axis_size("pos")
    reps = lax.axis_size("rep")
    holders = feats * poses
    table_rows, width = encoder.shape
    depth = decoder.shape[1]
    layers = depth + 1
    positions, kslots = active_ids.shape[1:]
    block_rows = positions * kslots
    slots = block_rows * feats
    capacity = max(2, (10 * block_rows + 7 * holders - 1) // (7 * holders))
    listed = capacity * feats
    column = poses * listed
    half = column // reps
    result_rows = block_rows // reps
    panel = target_slots.shape[1]
    small = slots <= KERNEL_SLOTS

    def place():
        feat, pos = lax.axis_index("feat"), lax.axis_index("pos")
        return feat.astype(F32), pos.astype(F32), lax.axis_index("rep").astype(F32)

    def pack(ids, vals):
        one = jnp.concatenate([ids(0).astype(F32), vals(0)], axis=0)
        one = jnp.concatenate([one, jnp.zeros((2 * positions, LANES - kslots), F32)], axis=1)
        return (jnp.broadcast_to(one, (holders,) + one.shape),)

    (packed,) = on_core(
        pack,
        [],
        [shape(holders, 2 * positions, LANES)],
        streams=[active_ids, active_vals],
        room=60,
    )
    lists = lax.all_to_all(packed, ("feat", "pos"), split_axis=0, concat_axis=0, tiled=True)

    def list_of(values, prompt):
        blocks = []
        for a in range(feats):
            block = values[a * poses]
            for q in range(1, poses):
                block = jnp.where(prompt == q, values[a * poses + q], block)
            blocks.append(block)
        return jnp.concatenate(blocks, axis=0)[:, :kslots]

    def list_row(slot):
        place = floor_div(slot, kslots)
        return place + floor_div(place, positions) * positions

    def slot_entry(slot):
        return slot - floor_div(slot, kslots) * kslots

    def pieces(table):
        high = part(table, small)
        rest = table - high.astype(F32)
        middle = part(rest, small)
        return [high, middle, part(rest - middle.astype(F32), small)]

    def as_rows(table):
        spread = (iota((kslots, slots), 0) == slot_entry(iota((kslots, slots), 1))).astype(BF16)
        wide = dot(jnp.concatenate(pieces(table), axis=0), spread)
        count = table.shape[0]
        wide = wide[:count] + (wide[count : 2 * count] + wide[2 * count :])
        row = iota(wide.shape, 0) - list_row(iota(wide.shape, 1))
        ids = jnp.sum(jnp.where(row == 0, wide, 0.0), axis=0, keepdims=True)
        return ids, jnp.sum(jnp.where(row == positions, wide, 0.0), axis=0, keepdims=True)

    def as_col(table):
        wide = (slots, table.shape[0])
        spread = (list_row(iota(wide, 0)) == iota(wide, 1)).astype(BF16)
        every = dot(spread, jnp.concatenate(pieces(table), axis=1))
        every = every[:, :kslots] + (every[:, kslots : 2 * kslots] + every[:, 2 * kslots :])
        mine = slot_entry(iota((slots, kslots), 0)) == iota((slots, kslots), 1)
        return jnp.sum(jnp.where(mine, every, 0.0), axis=1, keepdims=True)

    def choose(values):
        feat, pos, _ = place()
        own = feat * poses + pos
        tables = []
        rows = []
        for k in range(poses):
            prompt = jnp.where(pos + k >= poses, pos + k - poses, pos + k)
            tables.append(list_of(values, prompt))
            rows.append(as_rows(tables[k]))
        hits = [floor_div(ids, table_rows) == own for ids, _ in rows]
        earlier = (iota((slots, slots), 0) < iota((slots, slots), 1)).astype(BF16)
        ranks = dot(jnp.concatenate([h.astype(BF16) for h in hits], axis=0), earlier)
        picks, gains, ids_of = [], [], []
        for k in range(poses):
            chosen = jnp.where(
                hits[k] & (ranks[k : k + 1] == iota((listed, slots), 0)), 1.0, 0.0
            )
            ids = jnp.sum(chosen * rows[k][0], axis=1, keepdims=True)
            ids_of.append(ids)
            gains.append(jnp.sum(chosen * rows[k][1], axis=1, keepdims=True))
            live = jnp.sum(chosen, axis=1, keepdims=True) > 0.0
            local = jnp.where(live, ids - own * table_rows, -1.0)
            picks.append((local == iota((listed, table_rows), 1)).astype(BF16))
        picks = jnp.concatenate(picks, axis=0)
        gains = jnp.concatenate(gains, axis=0)
        ids_of = jnp.concatenate(ids_of, axis=0)
        layer = ids_of - floor_div(ids_of, layers) * layers
        gains = jnp.concatenate([jnp.where(layer <= l, gains, 0.0) for l in range(depth)], axis=1)
        return picks, gains, tables[0]

    picks, gains, my_list = on_core(
        choose,
        [lists],
        [
            shape(column, table_rows, dtype=BF16),
            shape(column, depth),
            shape(2 * positions * feats, kslots),
        ],
        small,
    )

    enc_rows = dot(picks, encoder).astype(BF16)
    enc_rows = [enc_rows[k * listed : (k + 1) * listed] for k in range(poses)]

    ring = [[enc_rows[0]] + [rotate(enc_rows[k], "pos", k) for k in range(1, poses)]]
    ring.append([ring_next(enc_rows[k], "feat", "pos", k) for k in range(poses)])

    dec_rows = lax.dot_general(
        picks, decoder, (((1,), (0,)), ((), ())), preferred_element_type=F32
    )
    dec_rows = (jnp.transpose(dec_rows, (1, 0, 2)) * gains.T[:, :, None]).astype(BF16)
    dec_rows = [dec_rows[:, k * listed : (k + 1) * listed] for k in range(poses)]
    dec_rows = [dec_rows[0]] + [rotate(dec_rows[k], "pos", k) for k in range(1, poses)]

    def places(table, pattern):
        feat, pos, rep = place()

        def padded(owner, rank):
            feat_of = floor_div(owner, poses)
            step = ring_place(feat, feats) - ring_place(feat_of, feats)
            step = jnp.where(step < 0.0, step + feats, step)
            turn = pos - (owner - feat_of * poses)
            turn = jnp.where(turn < 0.0, turn + poses, turn)
            return (step * poses + turn) * listed + rank

        ids_row = as_rows(table)[0]
        ids_col = as_col(table)
        owner_row = floor_div(ids_row, table_rows)
        owner_col = floor_div(ids_col, table_rows)
        same = owner_col == owner_row
        down, across = iota((slots, slots), 0), iota((slots, slots), 1)
        rank_col = jnp.sum(jnp.where(same & (across < down), 1.0, 0.0), axis=1, keepdims=True)
        rank_row = jnp.sum(jnp.where(same & (down < across), 1.0, 0.0), axis=0, keepdims=True)
        total = holders * listed
        placing = padded(owner_col, rank_col) == iota((slots, total), 1)
        placing_t = padded(owner_row, rank_row) == iota((total, slots), 0)
        layer = ids_col - floor_div(ids_col, layers) * layers
        layer_row = jnp.sum(jnp.where(placing, layer, 0.0), axis=0, keepdims=True)
        allowed = jnp.where(pattern[0] == 1, 1.0, 0.0).astype(BF16)

        def in_block(slot, dim, extent):
            wide = (extent, feats) if dim == 0 else (feats, extent)
            return (floor_div(slot, block_rows) == iota(wide, 1 - dim)).astype(BF16)

        sources = in_block(iota((slots, 1), 0), 0, slots)
        targets = in_block(iota((1, slots), 1), 1, slots)
        mask = dot(dot(sources, allowed, NT).astype(BF16), targets)
        mask = jnp.where(floor_div(down, kslots) <= floor_div(across, kslots), mask, 0.0)
        first = (feat * reps + rep) * result_rows
        own_slot = first + iota((result_rows, 1), 0)
        own_mask = dot(in_block(own_slot, 0, result_rows), allowed).astype(BF16)
        own_mask = dot(own_mask, targets)
        own_causal = floor_div(iota((result_rows, slots), 1), kslots) <= floor_div(
            first + iota((result_rows, slots), 0), kslots
        )
        own_mask = jnp.where(own_causal, own_mask, 0.0)
        return placing.astype(BF16), placing_t.astype(BF16), layer_row, mask.astype(BF16), own_mask

    placing, placing_t, layer_row, mask, own_mask, ring[1][-1] = on_core(
        places,
        [my_list, block_pattern],
        [
            shape(slots, holders * listed, dtype=BF16),
            shape(holders * listed, slots, dtype=BF16),
            shape(1, holders * listed),
            shape(slots, slots, dtype=BF16),
            shape(result_rows, slots),
        ],
        small,
        through=ring[1][-1:],
        cost=(1, 1),
    )
    for _ in range(2, feats):
        ring.append([ring_next(rows, "feat") for rows in ring[-1]])

    def products(first, count, layer_row, placing_t, *values):
        enc = jnp.concatenate(values[: count * poses], axis=0)
        dec = values[count * poses : count * poses + poses]
        dec = jnp.concatenate([d[l] for l in range(depth) for d in dec], axis=0)
        every = dot(dec, enc, NT)
        lanes = slice(first * column, (first + count) * column)
        raw = jnp.zeros((column, count * column), F32)
        for l in range(depth):
            rows = every[l * column : (l + 1) * column]
            raw = raw + jnp.where(layer_row[:, lanes] == l + 1.0, rows, 0.0)
        split = dot(jnp.concatenate(pieces(raw), axis=0), placing_t[lanes])
        return split[:column] + (split[column : 2 * column] + split[2 * column :])

    def early(*values):
        return (products(0, feats - 1, *values),)

    def late(so_far, *values):
        raw = so_far + products(feats - 1, 1, *values)
        first = place()[2] == 0.0
        return (
            jnp.where(first, raw[:half], raw[half:]),
            jnp.where(first, raw[half:], raw[:half]),
        )

    early_enc = [rows for step in ring[:-1] for rows in step]
    (so_far,) = on_core(
        early,
        [layer_row, placing_t] + early_enc + list(dec_rows),
        [shape(column, slots)],
        small,
        cost=(1, 1),
    )
    keep, send = on_core(
        late,
        [so_far, layer_row, placing_t] + list(ring[-1]) + list(dec_rows),
        [shape(half, slots)] * 2,
        small,
    )
    own_edges = (keep + rotate(send, "rep", 1)).astype(BF16)
    shards = ring_spread(own_edges, "feat")
    others = [rotate(shard, "rep", 1) for shard in shards]

    def finish(placing, mask, own_mask, targets, *values):
        feat, _, rep = place()
        first = rep == 0.0
        parts = []
        for mine, other in zip(values[:feats], values[feats:]):
            parts += [jnp.where(first, mine, other), jnp.where(first, other, mine)]
        padded = jnp.concatenate(parts, axis=0)
        magnitude = jnp.abs(dot(placing, padded) * mask.astype(F32))
        total = jnp.maximum(jnp.sum(magnitude, axis=0, keepdims=True), 1.0)
        magnitude = magnitude.astype(BF16)
        diagonal = iota((slots, slots), 0) == iota((slots, slots), 1)
        scale = 1.0 / jnp.sum(jnp.where(diagonal, total, 0.0), axis=1, keepdims=True)
        current = (iota((slots, panel), 0) == targets.astype(F32)).astype(F32)
        accum = jnp.zeros((slots, panel), F32)
        for _ in range(ITERS):
            scaled = current * scale
            high = part(scaled, small)
            low = part(scaled - high.astype(F32), small)
            both = dot(magnitude, jnp.concatenate([high, low], axis=1))
            current = both[:, :panel] + both[:, panel:]
            accum = accum + current
        index = feat * reps + rep
        influence = accum[:result_rows]
        for w in range(1, feats * reps):
            influence = jnp.where(
                index == w, accum[w * result_rows : (w + 1) * result_rows], influence
            )
        start = index * result_rows
        own = start + iota((result_rows, slots), 0) == iota((result_rows, slots), 1)
        rows = dot(own.astype(BF16), padded, NT).astype(BF16)
        edges = (dot(rows, placing, NT) * own_mask).astype(BF16)
        return edges[None], (influence * float(slots))[None]

    edges, influence = on_core(
        finish,
        [placing, mask, own_mask, target_slots] + shards + others,
        [shape(1, result_rows, slots, dtype=BF16), shape(1, result_rows, panel)],
        small,
    )
    return edges, influence


def solution(mesh):
    return jax.shard_map(
        per_device,
        mesh=mesh,
        in_specs=(
            P(("grp", "pos"), "feat", None),
            P(("grp", "pos"), "feat", None),
            P(("grp", "pos"), None, None),
            P(("grp", "pos"), None),
            P(("feat", "pos"), "rep"),
            P(("feat", "pos"), None, "rep"),
        ),
        out_specs=(
            P(("grp", "pos"), ("feat", "rep"), None),
            P(("grp", "pos"), ("feat", "rep"), None),
        ),
        check_vma=False,
    )
```

```python
import jax
import jax.numpy as jnp
from jax import lax
from jax.experimental import pallas as pl
from jax.experimental.pallas import tpu as pltpu
from jax.sharding import PartitionSpec as P

ITERS = 3
F32 = jnp.float32
BF16 = jnp.bfloat16
NN = (((1,), (0,)), ((), ()))
NT = (((1,), (1,)), ((), ()))
LANES = 128
KERNEL_SLOTS = 1024


def dot(a, b, dims=NN):
    return lax.dot_general(a, b, dims, preferred_element_type=F32)


def iota(shape, dim):
    return lax.broadcasted_iota(jnp.int32, shape, dim).astype(F32)


def floor_div(x, n):
    return jnp.floor((x + 0.5) * (1.0 / n))


def on_core(fn, args, outs, kernel=True, through=(), streams=(), cost=None, room=24):
    if not kernel:
        loads = [lambda i, x=x: x[i] for x in streams]
        return list(fn(*args, *loads)) + list(through)
    count, passed, streamed = len(args), len(through), len(streams)

    def body(*refs):
        sources = refs[count : count + streamed]
        results = refs[count + streamed + passed :][: len(outs)]
        scratch = refs[len(refs) - 2 * streamed :]
        copies = []
        for n in range(streamed):
            copies.append(
                [
                    pltpu.make_async_copy(
                        sources[n].at[i], scratch[2 * n].at[i], scratch[2 * n + 1].at[i]
                    )
                    for i in range(streams[n].shape[0])
                ]
            )
            for copy in copies[-1]:
                copy.start()

        def load(n):
            def wait(i):
                copies[n][i].wait()
                return scratch[2 * n][i]

            return wait

        values = fn(*[ref[...] for ref in refs[:count]], *[load(n) for n in range(streamed)])
        for ref, value in zip(results, values):
            ref[...] = value

    estimate = None
    if cost is not None:
        estimate = pl.CostEstimate(flops=cost[0], bytes_accessed=cost[1], transcendentals=0)
    in_vmem = pl.BlockSpec(memory_space=pltpu.VMEM)
    anywhere = pl.BlockSpec(memory_space=pl.ANY)
    scratch = []
    for x in streams:
        scratch += [pltpu.VMEM(x.shape, x.dtype), pltpu.SemaphoreType.DMA((x.shape[0],))]
    call = pl.pallas_call(
        body,
        out_shape=list(outs) + [jax.ShapeDtypeStruct(x.shape, x.dtype) for x in through],
        in_specs=[in_vmem] * count
        + [pl.BlockSpec(memory_space=pltpu.HBM)] * streamed
        + [anywhere] * passed,
        out_specs=[in_vmem] * len(outs) + [anywhere] * passed,
        scratch_shapes=scratch,
        input_output_aliases={count + streamed + i: len(outs) + i for i in range(passed)},
        compiler_params=pltpu.CompilerParams(vmem_limit_bytes=room * 1024 * 1024),
        cost_estimate=estimate,
    )
    return list(call(*args, *streams, *through))


def rotate(x, axis, step):
    count = lax.axis_size(axis)
    return lax.ppermute(x, axis, [(i, (i + step) % count) for i in range(count)])


def ring_place(index, count):
    low = floor_div(index, 2)
    return jnp.where(index > 2 * low, count - 1 - low, low)


def ring_next(x, axis, across=None, turn=0):
    count = lax.axis_size(axis)
    order = list(range(0, count, 2)) + list(range(1, count, 2))[::-1]
    steps = [(order[i], order[(i + 1) % count]) for i in range(count)]
    if across is None:
        return lax.ppermute(x, axis, steps)
    wide = lax.axis_size(across)
    pairs = [(a * wide + i, b * wide + (i + turn) % wide) for a, b in steps for i in range(wide)]
    return lax.ppermute(x, (axis, across), pairs)


def ring_spread(x, axis):
    count = lax.axis_size(axis)
    order = list(range(0, count, 2)) + list(range(1, count, 2))[::-1]
    return [x] + [
        lax.ppermute(x, axis, [(order[i], order[(i + k) % count]) for i in range(count)])
        for k in range(1, count)
    ]


def part(x, kernel):
    return x.astype(BF16) if kernel else lax.reduce_precision(x, 8, 7).astype(BF16)


def shape(*dims, dtype=F32):
    return jax.ShapeDtypeStruct(dims, dtype)


def per_device(active_ids, active_vals, block_pattern, target_slots, encoder, decoder):
    feats = lax.axis_size("feat")
    poses = lax.axis_size("pos")
    reps = lax.axis_size("rep")
    holders = feats * poses
    table_rows, width = encoder.shape
    depth = decoder.shape[1]
    layers = depth + 1
    positions, kslots = active_ids.shape[1:]
    block_rows = positions * kslots
    slots = block_rows * feats
    capacity = max(2, (10 * block_rows + 7 * holders - 1) // (7 * holders))
    listed = capacity * feats
    column = poses * listed
    half = column // reps
    result_rows = block_rows // reps
    panel = target_slots.shape[1]
    small = slots <= KERNEL_SLOTS

    def place():
        feat, pos = lax.axis_index("feat"), lax.axis_index("pos")
        return feat.astype(F32), pos.astype(F32), lax.axis_index("rep").astype(F32)

    def pack(ids, vals):
        one = jnp.concatenate([ids(0).astype(F32), vals(0)], axis=0)
        one = jnp.concatenate([one, jnp.zeros((2 * positions, LANES - kslots), F32)], axis=1)
        return (jnp.broadcast_to(one, (holders,) + one.shape),)

    (packed,) = on_core(
        pack,
        [],
        [shape(holders, 2 * positions, LANES)],
        streams=[active_ids, active_vals],
        room=60,
    )
    lists = lax.all_to_all(packed, ("feat", "pos"), split_axis=0, concat_axis=0, tiled=True)

    def list_of(values, prompt):
        blocks = []
        for a in range(feats):
            block = values[a * poses]
            for q in range(1, poses):
                block = jnp.where(prompt == q, values[a * poses + q], block)
            blocks.append(block)
        return jnp.concatenate(blocks, axis=0)[:, :kslots]

    def list_row(slot):
        place = floor_div(slot, kslots)
        return place + floor_div(place, positions) * positions

    def slot_entry(slot):
        return slot - floor_div(slot, kslots) * kslots

    def pieces(table):
        high = part(table, small)
        rest = table - high.astype(F32)
        middle = part(rest, small)
        return [high, middle, part(rest - middle.astype(F32), small)]

    def as_rows(table):
        spread = (iota((kslots, slots), 0) == slot_entry(iota((kslots, slots), 1))).astype(BF16)
        wide = dot(jnp.concatenate(pieces(table), axis=0), spread)
        count = table.shape[0]
        wide = wide[:count] + (wide[count : 2 * count] + wide[2 * count :])
        row = iota(wide.shape, 0) - list_row(iota(wide.shape, 1))
        ids = jnp.sum(jnp.where(row == 0, wide, 0.0), axis=0, keepdims=True)
        return ids, jnp.sum(jnp.where(row == positions, wide, 0.0), axis=0, keepdims=True)

    def as_col(table):
        wide = (slots, table.shape[0])
        spread = (list_row(iota(wide, 0)) == iota(wide, 1)).astype(BF16)
        every = dot(spread, jnp.concatenate(pieces(table), axis=1))
        every = every[:, :kslots] + (every[:, kslots : 2 * kslots] + every[:, 2 * kslots :])
        mine = slot_entry(iota((slots, kslots), 0)) == iota((slots, kslots), 1)
        return jnp.sum(jnp.where(mine, every, 0.0), axis=1, keepdims=True)

    def choose(values):
        feat, pos, _ = place()
        own = feat * poses + pos
        tables = []
        rows = []
        for k in range(poses):
            prompt = jnp.where(pos + k >= poses, pos + k - poses, pos + k)
            tables.append(list_of(values, prompt))
            rows.append(as_rows(tables[k])[0])
        hits = [floor_div(ids, table_rows) == own for ids in rows]
        earlier = (iota((slots, slots), 0) < iota((slots, slots), 1)).astype(BF16)
        ranks = dot(jnp.concatenate([h.astype(BF16) for h in hits], axis=0), earlier)
        picks = []
        for k in range(poses):
            chosen = jnp.where(
                hits[k] & (ranks[k : k + 1] == iota((listed, slots), 0)), 1.0, 0.0
            )
            local = jnp.sum(chosen * (rows[k] - own * table_rows + 1.0), axis=1, keepdims=True)
            picks.append((local - 1.0 == iota((listed, table_rows), 1)).astype(BF16))
        return jnp.concatenate(picks, axis=0), tables[0]

    picks, my_list = on_core(
        choose,
        [lists],
        [shape(column, table_rows, dtype=BF16), shape(2 * positions * feats, kslots)],
        small,
    )

    def encode(picks, enc):
        rows = dot(picks, enc).astype(BF16)
        return [rows[k * listed : (k + 1) * listed] for k in range(poses)] + [picks]

    *enc_rows, picks = on_core(
        encode,
        [picks, encoder],
        [shape(listed, width, dtype=BF16)] * poses + [shape(column, table_rows, dtype=BF16)],
        small,
    )

    ring = [[enc_rows[0]] + [rotate(enc_rows[k], "pos", k) for k in range(1, poses)]]
    ring.append([ring_next(enc_rows[k], "feat", "pos", k) for k in range(poses)])

    dec_rows = lax.dot_general(
        picks, decoder, (((1,), (0,)), ((), ())), preferred_element_type=F32
    )
    dec_rows = jnp.transpose(dec_rows, (1, 0, 2)).astype(BF16)
    dec_rows = [dec_rows[:, k * listed : (k + 1) * listed] for k in range(poses)]
    dec_rows = [dec_rows[0]] + [rotate(dec_rows[k], "pos", k) for k in range(1, poses)]

    def places(table, pattern):
        feat, pos, rep = place()

        def padded(owner, rank):
            feat_of = floor_div(owner, poses)
            step = ring_place(feat, feats) - ring_place(feat_of, feats)
            step = jnp.where(step < 0.0, step + feats, step)
            turn = pos - (owner - feat_of * poses)
            turn = jnp.where(turn < 0.0, turn + poses, turn)
            return (step * poses + turn) * listed + rank

        ids_row, vals_row = as_rows(table)
        ids_col = as_col(table)
        owner_row = floor_div(ids_row, table_rows)
        owner_col = floor_div(ids_col, table_rows)
        same = owner_col == owner_row
        down, across = iota((slots, slots), 0), iota((slots, slots), 1)
        rank_col = jnp.sum(jnp.where(same & (across < down), 1.0, 0.0), axis=1, keepdims=True)
        rank_row = jnp.sum(jnp.where(same & (down < across), 1.0, 0.0), axis=0, keepdims=True)
        total = holders * listed
        placing = padded(owner_col, rank_col) == iota((slots, total), 1)
        placing_t = padded(owner_row, rank_row) == iota((total, slots), 0)
        layer = ids_col - floor_div(ids_col, layers) * layers
        layer_row = jnp.sum(jnp.where(placing, layer, 0.0), axis=0, keepdims=True)
        mine = placing_t[:column]
        gain = jnp.sum(jnp.where(mine, vals_row, 0.0), axis=1, keepdims=True)
        source_layer = ids_row - floor_div(ids_row, layers) * layers
        source_layer = jnp.sum(jnp.where(mine, source_layer, 0.0), axis=1, keepdims=True)
        gains = jnp.concatenate(
            [jnp.where(source_layer <= l, gain, 0.0) for l in range(depth)], axis=0
        )
        allowed = jnp.where(pattern[0] == 1, 1.0, 0.0).astype(BF16)

        def in_block(slot, dim, extent):
            wide = (extent, feats) if dim == 0 else (feats, extent)
            return (floor_div(slot, block_rows) == iota(wide, 1 - dim)).astype(BF16)

        sources = in_block(iota((slots, 1), 0), 0, slots)
        targets = in_block(iota((1, slots), 1), 1, slots)
        mask = dot(dot(sources, allowed, NT).astype(BF16), targets)
        mask = jnp.where(floor_div(down, kslots) <= floor_div(across, kslots), mask, 0.0)
        first = (feat * reps + rep) * result_rows
        own_slot = first + iota((result_rows, 1), 0)
        own_mask = dot(in_block(own_slot, 0, result_rows), allowed).astype(BF16)
        own_mask = dot(own_mask, targets)
        own_causal = floor_div(iota((result_rows, slots), 1), kslots) <= floor_div(
            first + iota((result_rows, slots), 0), kslots
        )
        own_mask = jnp.where(own_causal, own_mask, 0.0)
        placing, placing_t = placing.astype(BF16), placing_t.astype(BF16)
        return placing, placing_t, layer_row, gains, mask.astype(BF16), own_mask

    placing, placing_t, layer_row, gains, mask, own_mask, ring[1][-1] = on_core(
        places,
        [my_list, block_pattern],
        [
            shape(slots, holders * listed, dtype=BF16),
            shape(holders * listed, slots, dtype=BF16),
            shape(1, holders * listed),
            shape(depth * column, 1),
            shape(slots, slots, dtype=BF16),
            shape(result_rows, slots),
        ],
        small,
        through=ring[1][-1:],
        cost=(1, 1),
    )
    for _ in range(2, feats):
        ring.append([ring_next(rows, "feat") for rows in ring[-1]])

    def products(first, enc, dec, layer_row, placing_t):
        count = len(enc) // poses
        every = dot(dec, jnp.concatenate(enc, axis=0), NT)
        lanes = slice(first * column, (first + count) * column)
        raw = jnp.zeros((column, count * column), F32)
        for l in range(depth):
            rows = every[l * column : (l + 1) * column]
            raw = raw + jnp.where(layer_row[:, lanes] == l + 1.0, rows, 0.0)
        split = dot(jnp.concatenate(pieces(raw), axis=0), placing_t[lanes])
        return split[:column] + (split[column : 2 * column] + split[2 * column :])

    def early(layer_row, placing_t, gains, *values):
        dec = jnp.concatenate([d[l] for l in range(depth) for d in values[:poses]], axis=0)
        dec = (dec.astype(F32) * gains).astype(BF16)
        return products(0, values[poses:], dec, layer_row, placing_t), dec

    def late(layer_row, placing_t, so_far, dec, *values):
        raw = so_far + products(feats - 1, values, dec, layer_row, placing_t)
        first = place()[2] == 0.0
        return (
            jnp.where(first, raw[:half], raw[half:]),
            jnp.where(first, raw[half:], raw[:half]),
        )

    so_far, scaled = on_core(
        early,
        [layer_row, placing_t, gains] + dec_rows + [rows for step in ring[:-1] for rows in step],
        [shape(column, slots), shape(depth * column, width, dtype=BF16)],
        small,
        cost=(1, 1),
    )
    keep, send = on_core(
        late,
        [layer_row, placing_t, so_far, scaled] + ring[-1],
        [shape(half, slots)] * 2,
        small,
    )
    own_edges = (keep + rotate(send, "rep", 1)).astype(BF16)
    shards = ring_spread(own_edges, "feat")
    others = [rotate(shard, "rep", 1) for shard in shards]

    def finish(placing, mask, own_mask, targets, *values):
        feat, _, rep = place()
        first = rep == 0.0
        parts = []
        for mine, other in zip(values[:feats], values[feats:]):
            parts += [jnp.where(first, mine, other), jnp.where(first, other, mine)]
        padded = jnp.concatenate(parts, axis=0)
        magnitude = jnp.abs(dot(placing, padded) * mask.astype(F32))
        total = jnp.maximum(jnp.sum(magnitude, axis=0, keepdims=True), 1.0)
        magnitude = magnitude.astype(BF16)
        diagonal = iota((slots, slots), 0) == iota((slots, slots), 1)
        scale = 1.0 / jnp.sum(jnp.where(diagonal, total, 0.0), axis=1, keepdims=True)
        current = (iota((slots, panel), 0) == targets.astype(F32)).astype(F32)
        accum = jnp.zeros((slots, panel), F32)
        for _ in range(ITERS):
            scaled = current * scale
            high = part(scaled, small)
            low = part(scaled - high.astype(F32), small)
            both = dot(magnitude, jnp.concatenate([high, low], axis=1))
            current = both[:, :panel] + both[:, panel:]
            accum = accum + current
        index = feat * reps + rep
        influence = accum[:result_rows]
        for w in range(1, feats * reps):
            influence = jnp.where(
                index == w, accum[w * result_rows : (w + 1) * result_rows], influence
            )
        start = index * result_rows
        own = start + iota((result_rows, slots), 0) == iota((result_rows, slots), 1)
        rows = dot(own.astype(BF16), padded, NT).astype(BF16)
        edges = (dot(rows, placing, NT) * own_mask).astype(BF16)
        return edges[None], (influence * float(slots))[None]

    edges, influence = on_core(
        finish,
        [placing, mask, own_mask, target_slots] + shards + others,
        [shape(1, result_rows, slots, dtype=BF16), shape(1, result_rows, panel)],
        small,
    )
    return edges, influence


def solution(mesh):
    return jax.shard_map(
        per_device,
        mesh=mesh,
        in_specs=(
            P(("grp", "pos"), "feat", None),
            P(("grp", "pos"), "feat", None),
            P(("grp", "pos"), None, None),
            P(("grp", "pos"), None),
            P(("feat", "pos"), "rep"),
            P(("feat", "pos"), None, "rep"),
        ),
        out_specs=(
            P(("grp", "pos"), ("feat", "rep"), None),
            P(("grp", "pos"), ("feat", "rep"), None),
        ),
        check_vma=False,
    )
```

```python
import jax
import jax.numpy as jnp
from jax import lax
from jax.experimental import pallas as pl
from jax.experimental.pallas import tpu as pltpu
from jax.sharding import PartitionSpec as P

ITERS = 3
F32 = jnp.float32
BF16 = jnp.bfloat16
NN = (((1,), (0,)), ((), ()))
NT = (((1,), (1,)), ((), ()))
LANES = 128
KERNEL_SLOTS = 1024


def dot(a, b, dims=NN):
    return lax.dot_general(a, b, dims, preferred_element_type=F32)


def iota(shape, dim):
    return lax.broadcasted_iota(jnp.int32, shape, dim).astype(F32)


def floor_div(x, n):
    return jnp.floor((x + 0.5) * (1.0 / n))


def on_core(fn, args, outs, kernel=True, through=(), streams=(), cost=None, room=24):
    if not kernel:
        loads = [lambda i, x=x: x[i] for x in streams]
        return list(fn(*args, *loads)) + list(through)
    count, passed, streamed = len(args), len(through), len(streams)

    def body(*refs):
        sources = refs[count : count + streamed]
        results = refs[count + streamed + passed :][: len(outs)]
        scratch = refs[len(refs) - 2 * streamed :]
        copies = []
        for n in range(streamed):
            copies.append(
                [
                    pltpu.make_async_copy(
                        sources[n].at[i], scratch[2 * n].at[i], scratch[2 * n + 1].at[i]
                    )
                    for i in range(streams[n].shape[0])
                ]
            )
            for copy in copies[-1]:
                copy.start()

        def load(n):
            def wait(i):
                copies[n][i].wait()
                return scratch[2 * n][i]

            return wait

        values = fn(*[ref[...] for ref in refs[:count]], *[load(n) for n in range(streamed)])
        for ref, value in zip(results, values):
            ref[...] = value

    estimate = None
    if cost is not None:
        estimate = pl.CostEstimate(flops=cost[0], bytes_accessed=cost[1], transcendentals=0)
    in_vmem = pl.BlockSpec(memory_space=pltpu.VMEM)
    anywhere = pl.BlockSpec(memory_space=pl.ANY)
    scratch = []
    for x in streams:
        scratch += [pltpu.VMEM(x.shape, x.dtype), pltpu.SemaphoreType.DMA((x.shape[0],))]
    call = pl.pallas_call(
        body,
        out_shape=list(outs) + [jax.ShapeDtypeStruct(x.shape, x.dtype) for x in through],
        in_specs=[in_vmem] * count
        + [pl.BlockSpec(memory_space=pltpu.HBM)] * streamed
        + [anywhere] * passed,
        out_specs=[in_vmem] * len(outs) + [anywhere] * passed,
        scratch_shapes=scratch,
        input_output_aliases={count + streamed + i: len(outs) + i for i in range(passed)},
        compiler_params=pltpu.CompilerParams(vmem_limit_bytes=room * 1024 * 1024),
        cost_estimate=estimate,
    )
    return list(call(*args, *streams, *through))


def rotate(x, axis, step):
    count = lax.axis_size(axis)
    return lax.ppermute(x, axis, [(i, (i + step) % count) for i in range(count)])


def swap(x, axis, bits):
    return lax.ppermute(x, axis, [(i, i ^ bits) for i in range(lax.axis_size(axis))])


def part(x, kernel):
    return x.astype(BF16) if kernel else lax.reduce_precision(x, 8, 7).astype(BF16)


def shape(*dims, dtype=F32):
    return jax.ShapeDtypeStruct(dims, dtype)


def per_device(active_ids, active_vals, block_pattern, target_slots, encoder, decoder):
    feats = lax.axis_size("feat")
    poses = lax.axis_size("pos")
    reps = lax.axis_size("rep")
    holders = feats * poses
    table_rows, width = encoder.shape
    depth = decoder.shape[1]
    layers = depth + 1
    positions, kslots = active_ids.shape[1:]
    block_rows = positions * kslots
    slots = block_rows * feats
    capacity = max(2, (10 * block_rows + 7 * holders - 1) // (7 * holders))
    listed = capacity * feats
    column = poses * listed
    half = column // reps
    result_rows = block_rows // reps
    panel = target_slots.shape[1]
    small = slots <= KERNEL_SLOTS

    def place():
        feat, pos = lax.axis_index("feat"), lax.axis_index("pos")
        return feat.astype(F32), pos.astype(F32), lax.axis_index("rep").astype(F32)

    def pack(ids, vals):
        one = jnp.concatenate([ids(0).astype(F32), vals(0)], axis=0)
        one = jnp.concatenate([one, jnp.zeros((2 * positions, LANES - kslots), F32)], axis=1)
        return (jnp.broadcast_to(one, (holders,) + one.shape),)

    (packed,) = on_core(
        pack,
        [],
        [shape(holders, 2 * positions, LANES)],
        streams=[active_ids, active_vals],
        room=60,
    )
    lists = lax.all_to_all(packed, ("feat", "pos"), split_axis=0, concat_axis=0, tiled=True)

    def list_of(values, prompt):
        blocks = []
        for a in range(feats):
            block = values[a * poses]
            for q in range(1, poses):
                block = jnp.where(prompt == q, values[a * poses + q], block)
            blocks.append(block)
        return jnp.concatenate(blocks, axis=0)[:, :kslots]

    def list_row(slot):
        place = floor_div(slot, kslots)
        return place + floor_div(place, positions) * positions

    def slot_entry(slot):
        return slot - floor_div(slot, kslots) * kslots

    def pieces(table):
        high = part(table, small)
        rest = table - high.astype(F32)
        middle = part(rest, small)
        return [high, middle, part(rest - middle.astype(F32), small)]

    def as_rows(table):
        spread = (iota((kslots, slots), 0) == slot_entry(iota((kslots, slots), 1))).astype(BF16)
        wide = dot(jnp.concatenate(pieces(table), axis=0), spread)
        count = table.shape[0]
        wide = wide[:count] + (wide[count : 2 * count] + wide[2 * count :])
        row = iota(wide.shape, 0) - list_row(iota(wide.shape, 1))
        ids = jnp.sum(jnp.where(row == 0, wide, 0.0), axis=0, keepdims=True)
        return ids, jnp.sum(jnp.where(row == positions, wide, 0.0), axis=0, keepdims=True)

    def as_col(table):
        wide = (slots, table.shape[0])
        spread = (list_row(iota(wide, 0)) == iota(wide, 1)).astype(BF16)
        every = dot(spread, jnp.concatenate(pieces(table), axis=1))
        every = every[:, :kslots] + (every[:, kslots : 2 * kslots] + every[:, 2 * kslots :])
        mine = slot_entry(iota((slots, kslots), 0)) == iota((slots, kslots), 1)
        return jnp.sum(jnp.where(mine, every, 0.0), axis=1, keepdims=True)

    def choose(values):
        feat, pos, _ = place()
        own = feat * poses + pos
        tables = []
        rows = []
        for k in range(poses):
            prompt = jnp.where(pos + k >= poses, pos + k - poses, pos + k)
            tables.append(list_of(values, prompt))
            rows.append(as_rows(tables[k])[0])
        hits = [floor_div(ids, table_rows) == own for ids in rows]
        earlier = (iota((slots, slots), 0) < iota((slots, slots), 1)).astype(BF16)
        ranks = dot(jnp.concatenate([h.astype(BF16) for h in hits], axis=0), earlier)
        picks = []
        for k in range(poses):
            chosen = jnp.where(
                hits[k] & (ranks[k : k + 1] == iota((listed, slots), 0)), 1.0, 0.0
            )
            local = jnp.sum(chosen * (rows[k] - own * table_rows + 1.0), axis=1, keepdims=True)
            picks.append((local - 1.0 == iota((listed, table_rows), 1)).astype(BF16))
        return jnp.concatenate(picks, axis=0), tables[0]

    picks, my_list = on_core(
        choose,
        [lists],
        [shape(column, table_rows, dtype=BF16), shape(2 * positions * feats, kslots)],
        small,
    )

    def encode(picks, enc):
        rows = dot(picks, enc).astype(BF16)
        return [rows[k * listed : (k + 1) * listed] for k in range(poses)] + [picks]

    *enc_rows, picks = on_core(
        encode,
        [picks, encoder],
        [shape(listed, width, dtype=BF16)] * poses + [shape(column, table_rows, dtype=BF16)],
        small,
    )

    enc_rows = [enc_rows[0]] + [rotate(enc_rows[k], "pos", k) for k in range(1, poses)]
    far = [swap(rows, "feat", feats // 2) for rows in enc_rows]

    dec_rows = lax.dot_general(
        picks, decoder, (((1,), (0,)), ((), ())), preferred_element_type=F32
    )
    dec_rows = jnp.transpose(dec_rows, (1, 0, 2)).astype(BF16)
    dec_rows = [dec_rows[:, k * listed : (k + 1) * listed] for k in range(poses)]
    dec_rows = [dec_rows[0]] + [rotate(dec_rows[k], "pos", k) for k in range(1, poses)]

    def places(table, pattern):
        feat, pos, rep = place()

        def padded(owner, rank):
            feat_of = floor_div(owner, poses)
            step = (feat.astype(jnp.int32) ^ feat_of.astype(jnp.int32)).astype(F32)
            turn = pos - (owner - feat_of * poses)
            turn = jnp.where(turn < 0.0, turn + poses, turn)
            return (step * poses + turn) * listed + rank

        ids_row, vals_row = as_rows(table)
        ids_col = as_col(table)
        owner_row = floor_div(ids_row, table_rows)
        owner_col = floor_div(ids_col, table_rows)
        same = owner_col == owner_row
        down, across = iota((slots, slots), 0), iota((slots, slots), 1)
        rank_col = jnp.sum(jnp.where(same & (across < down), 1.0, 0.0), axis=1, keepdims=True)
        rank_row = jnp.sum(jnp.where(same & (down < across), 1.0, 0.0), axis=0, keepdims=True)
        total = holders * listed
        placing = padded(owner_col, rank_col) == iota((slots, total), 1)
        placing_t = padded(owner_row, rank_row) == iota((total, slots), 0)
        layer = ids_col - floor_div(ids_col, layers) * layers
        layer_row = jnp.sum(jnp.where(placing, layer, 0.0), axis=0, keepdims=True)
        mine = placing_t[:column]
        gain = jnp.sum(jnp.where(mine, vals_row, 0.0), axis=1, keepdims=True)
        source_layer = ids_row - floor_div(ids_row, layers) * layers
        source_layer = jnp.sum(jnp.where(mine, source_layer, 0.0), axis=1, keepdims=True)
        gains = jnp.concatenate(
            [jnp.where(source_layer <= l, gain, 0.0) for l in range(depth)], axis=0
        )
        allowed = jnp.where(pattern[0] == 1, 1.0, 0.0).astype(BF16)

        def in_block(slot, dim, extent):
            wide = (extent, feats) if dim == 0 else (feats, extent)
            return (floor_div(slot, block_rows) == iota(wide, 1 - dim)).astype(BF16)

        sources = in_block(iota((slots, 1), 0), 0, slots)
        targets = in_block(iota((1, slots), 1), 1, slots)
        mask = dot(dot(sources, allowed, NT).astype(BF16), targets)
        mask = jnp.where(floor_div(down, kslots) <= floor_div(across, kslots), mask, 0.0)
        first = (feat * reps + rep) * result_rows
        own_slot = first + iota((result_rows, 1), 0)
        own_mask = dot(in_block(own_slot, 0, result_rows), allowed).astype(BF16)
        own_mask = dot(own_mask, targets)
        own_causal = floor_div(iota((result_rows, slots), 1), kslots) <= floor_div(
            first + iota((result_rows, slots), 0), kslots
        )
        own_mask = jnp.where(own_causal, own_mask, 0.0)
        placing, placing_t = placing.astype(BF16), placing_t.astype(BF16)
        return placing, placing_t, layer_row, gains, mask.astype(BF16), own_mask

    placing, placing_t, layer_row, gains, mask, own_mask, far[0] = on_core(
        places,
        [my_list, block_pattern],
        [
            shape(slots, holders * listed, dtype=BF16),
            shape(holders * listed, slots, dtype=BF16),
            shape(1, holders * listed),
            shape(depth * column, 1),
            shape(slots, slots, dtype=BF16),
            shape(result_rows, slots),
        ],
        small,
        through=far[:1],
        cost=(1, 1),
    )
    shards = []
    for m in range(feats):
        if m == 0 or m == feats // 2:
            shards.append(far if m else enc_rows)
        elif feats == 4 and m == 3:
            inner = [lax.ppermute(rows, "feat", [(1, 2), (2, 1)]) for rows in enc_rows]
            outer = [lax.ppermute(rows, "feat", [(2, 3), (1, 0)]) for rows in far]
            shards.append(inner + outer)
        else:
            shards.append([swap(rows, "feat", m) for rows in enc_rows])

    def products(first, enc, dec, layer_row, placing_t):
        enc = jnp.concatenate(enc, axis=0)
        count = enc.shape[0] // column
        every = dot(dec, enc, NT)
        lanes = slice(first * column, (first + count) * column)
        raw = jnp.zeros((column, count * column), F32)
        for l in range(depth):
            rows = every[l * column : (l + 1) * column]
            raw = raw + jnp.where(layer_row[:, lanes] == l + 1.0, rows, 0.0)
        split = dot(jnp.concatenate(pieces(raw), axis=0), placing_t[lanes])
        return split[:column] + (split[column : 2 * column] + split[2 * column :])

    def early(layer_row, placing_t, gains, *values):
        dec = jnp.concatenate([d[l] for l in range(depth) for d in values[:poses]], axis=0)
        dec = (dec.astype(F32) * gains).astype(BF16)
        return products(0, values[poses:], dec, layer_row, placing_t), dec

    def late(layer_row, placing_t, so_far, dec, *values):
        if len(values) > poses:
            values = [a + b for a, b in zip(values[:poses], values[poses:])]
        raw = so_far + products(feats - 1, values, dec, layer_row, placing_t)
        first = place()[2] == 0.0
        return (
            jnp.where(first, raw[:half], raw[half:]),
            jnp.where(first, raw[half:], raw[:half]),
        )

    so_far, scaled = on_core(
        early,
        [layer_row, placing_t, gains] + dec_rows + [rows for step in shards[:-1] for rows in step],
        [shape(column, slots), shape(depth * column, width, dtype=BF16)],
        small,
        cost=(1, 1),
    )
    keep, send = on_core(
        late,
        [layer_row, placing_t, so_far, scaled] + shards[-1],
        [shape(half, slots)] * 2,
        small,
    )
    own_edges = (keep + rotate(send, "rep", 1)).astype(BF16)
    edges = [own_edges] + [swap(own_edges, "feat", m) for m in range(1, feats)]
    others = [rotate(shard, "rep", 1) for shard in edges]

    def finish(placing, mask, own_mask, targets, *values):
        feat, _, rep = place()
        first = rep == 0.0
        parts = []
        for mine, other in zip(values[:feats], values[feats:]):
            parts += [jnp.where(first, mine, other), jnp.where(first, other, mine)]
        padded = jnp.concatenate(parts, axis=0)
        magnitude = jnp.abs(dot(placing, padded) * mask.astype(F32))
        total = jnp.maximum(jnp.sum(magnitude, axis=0, keepdims=True), 1.0)
        magnitude = magnitude.astype(BF16)
        diagonal = iota((slots, slots), 0) == iota((slots, slots), 1)
        scale = 1.0 / jnp.sum(jnp.where(diagonal, total, 0.0), axis=1, keepdims=True)
        current = (iota((slots, panel), 0) == targets.astype(F32)).astype(F32)
        accum = jnp.zeros((slots, panel), F32)
        for _ in range(ITERS):
            scaled = current * scale
            high = part(scaled, small)
            low = part(scaled - high.astype(F32), small)
            both = dot(magnitude, jnp.concatenate([high, low], axis=1))
            current = both[:, :panel] + both[:, panel:]
            accum = accum + current
        index = feat * reps + rep
        influence = accum[:result_rows]
        for w in range(1, feats * reps):
            influence = jnp.where(
                index == w, accum[w * result_rows : (w + 1) * result_rows], influence
            )
        start = index * result_rows
        own = start + iota((result_rows, slots), 0) == iota((result_rows, slots), 1)
        rows = dot(own.astype(BF16), padded, NT).astype(BF16)
        edges = (dot(rows, placing, NT) * own_mask).astype(BF16)
        return edges[None], (influence * float(slots))[None]

    edges, influence = on_core(
        finish,
        [placing, mask, own_mask, target_slots] + edges + others,
        [shape(1, result_rows, slots, dtype=BF16), shape(1, result_rows, panel)],
        small,
    )
    return edges, influence


def solution(mesh):
    return jax.shard_map(
        per_device,
        mesh=mesh,
        in_specs=(
            P(("grp", "pos"), "feat", None),
            P(("grp", "pos"), "feat", None),
            P(("grp", "pos"), None, None),
            P(("grp", "pos"), None),
            P(("feat", "pos"), "rep"),
            P(("feat", "pos"), None, "rep"),
        ),
        out_specs=(
            P(("grp", "pos"), ("feat", "rep"), None),
            P(("grp", "pos"), ("feat", "rep"), None),
        ),
        check_vma=False,
    )
```

```python
import jax
import jax.numpy as jnp
from jax import lax
from jax.experimental import pallas as pl
from jax.experimental.pallas import tpu as pltpu
from jax.sharding import PartitionSpec as P

ITERS = 3
F32 = jnp.float32
BF16 = jnp.bfloat16
NN = (((1,), (0,)), ((), ()))
NT = (((1,), (1,)), ((), ()))
LANES = 128
KERNEL_SLOTS = 1024


def dot(a, b, dims=NN):
    return lax.dot_general(a, b, dims, preferred_element_type=F32)


def iota(shape, dim):
    return lax.broadcasted_iota(jnp.int32, shape, dim).astype(F32)


def floor_div(x, n):
    return jnp.floor((x + 0.5) * (1.0 / n))


def on_core(fn, args, outs, kernel=True, through=(), streams=(), cost=None, room=24):
    if not kernel:
        loads = [lambda i, x=x: x[i] for x in streams]
        return list(fn(*args, *loads)) + list(through)
    count, passed, streamed = len(args), len(through), len(streams)

    def body(*refs):
        sources = refs[count : count + streamed]
        results = refs[count + streamed + passed :][: len(outs)]
        scratch = refs[len(refs) - 2 * streamed :]
        copies = []
        for n in range(streamed):
            copies.append(
                [
                    pltpu.make_async_copy(
                        sources[n].at[i], scratch[2 * n].at[i], scratch[2 * n + 1].at[i]
                    )
                    for i in range(streams[n].shape[0])
                ]
            )
            for copy in copies[-1]:
                copy.start()

        def load(n):
            def wait(i):
                copies[n][i].wait()
                return scratch[2 * n][i]

            return wait

        values = fn(*[ref[...] for ref in refs[:count]], *[load(n) for n in range(streamed)])
        for ref, value in zip(results, values):
            ref[...] = value

    estimate = None
    if cost is not None:
        estimate = pl.CostEstimate(flops=cost[0], bytes_accessed=cost[1], transcendentals=0)
    in_vmem = pl.BlockSpec(memory_space=pltpu.VMEM)
    anywhere = pl.BlockSpec(memory_space=pl.ANY)
    scratch = []
    for x in streams:
        scratch += [pltpu.VMEM(x.shape, x.dtype), pltpu.SemaphoreType.DMA((x.shape[0],))]
    call = pl.pallas_call(
        body,
        out_shape=list(outs) + [jax.ShapeDtypeStruct(x.shape, x.dtype) for x in through],
        in_specs=[in_vmem] * count
        + [pl.BlockSpec(memory_space=pltpu.HBM)] * streamed
        + [anywhere] * passed,
        out_specs=[in_vmem] * len(outs) + [anywhere] * passed,
        scratch_shapes=scratch,
        input_output_aliases={count + streamed + i: len(outs) + i for i in range(passed)},
        compiler_params=pltpu.CompilerParams(vmem_limit_bytes=room * 1024 * 1024),
        cost_estimate=estimate,
    )
    return list(call(*args, *streams, *through))


def rotate(x, axis, step):
    count = lax.axis_size(axis)
    return lax.ppermute(x, axis, [(i, (i + step) % count) for i in range(count)])


def swap(x, axis, bits):
    return lax.ppermute(x, axis, [(i, i ^ bits) for i in range(lax.axis_size(axis))])


def part(x, kernel):
    return x.astype(BF16) if kernel else lax.reduce_precision(x, 8, 7).astype(BF16)


def shape(*dims, dtype=F32):
    return jax.ShapeDtypeStruct(dims, dtype)


def per_device(active_ids, active_vals, block_pattern, target_slots, encoder, decoder):
    feats = lax.axis_size("feat")
    poses = lax.axis_size("pos")
    reps = lax.axis_size("rep")
    holders = feats * poses
    table_rows, width = encoder.shape
    depth = decoder.shape[1]
    layers = depth + 1
    positions, kslots = active_ids.shape[1:]
    block_rows = positions * kslots
    slots = block_rows * feats
    capacity = max(2, (10 * block_rows + 7 * holders - 1) // (7 * holders))
    listed = capacity * feats
    column = poses * listed
    half = column // reps
    result_rows = block_rows // reps
    panel = target_slots.shape[1]
    small = slots <= KERNEL_SLOTS

    def place():
        feat, pos = lax.axis_index("feat"), lax.axis_index("pos")
        return feat.astype(F32), pos.astype(F32), lax.axis_index("rep").astype(F32)

    def pack(ids, vals):
        one = jnp.concatenate([ids(0).astype(F32), vals(0)], axis=0)
        one = jnp.concatenate([one, jnp.zeros((2 * positions, LANES - kslots), F32)], axis=1)
        return (jnp.broadcast_to(one, (holders,) + one.shape),)

    (packed,) = on_core(
        pack,
        [],
        [shape(holders, 2 * positions, LANES)],
        streams=[active_ids, active_vals],
        room=60,
    )
    lists = lax.all_to_all(packed, ("feat", "pos"), split_axis=0, concat_axis=0, tiled=True)

    def list_of(values, prompt):
        blocks = []
        for a in range(feats):
            block = values[a * poses]
            for q in range(1, poses):
                block = jnp.where(prompt == q, values[a * poses + q], block)
            blocks.append(block)
        return jnp.concatenate(blocks, axis=0)[:, :kslots]

    def list_row(slot):
        place = floor_div(slot, kslots)
        return place + floor_div(place, positions) * positions

    def slot_entry(slot):
        return slot - floor_div(slot, kslots) * kslots

    def pieces(table):
        high = part(table, small)
        rest = table - high.astype(F32)
        middle = part(rest, small)
        return [high, middle, part(rest - middle.astype(F32), small)]

    def as_rows(table):
        spread = (iota((kslots, slots), 0) == slot_entry(iota((kslots, slots), 1))).astype(BF16)
        wide = dot(jnp.concatenate(pieces(table), axis=0), spread)
        count = table.shape[0]
        wide = wide[:count] + (wide[count : 2 * count] + wide[2 * count :])
        row = iota(wide.shape, 0) - list_row(iota(wide.shape, 1))
        ids = jnp.sum(jnp.where(row == 0, wide, 0.0), axis=0, keepdims=True)
        return ids, jnp.sum(jnp.where(row == positions, wide, 0.0), axis=0, keepdims=True)

    def as_col(table):
        wide = (slots, table.shape[0])
        spread = (list_row(iota(wide, 0)) == iota(wide, 1)).astype(BF16)
        every = dot(spread, jnp.concatenate(pieces(table), axis=1))
        every = every[:, :kslots] + (every[:, kslots : 2 * kslots] + every[:, 2 * kslots :])
        mine = slot_entry(iota((slots, kslots), 0)) == iota((slots, kslots), 1)
        return jnp.sum(jnp.where(mine, every, 0.0), axis=1, keepdims=True)

    def choose(values):
        feat, pos, _ = place()
        own = feat * poses + pos
        tables = []
        rows = []
        for k in range(poses):
            prompt = jnp.where(pos + k >= poses, pos + k - poses, pos + k)
            tables.append(list_of(values, prompt))
            rows.append(as_rows(tables[k])[0])
        hits = [floor_div(ids, table_rows) == own for ids in rows]
        earlier = (iota((slots, slots), 0) < iota((slots, slots), 1)).astype(BF16)
        ranks = dot(jnp.concatenate([h.astype(BF16) for h in hits], axis=0), earlier)
        picks = []
        for k in range(poses):
            chosen = jnp.where(
                hits[k] & (ranks[k : k + 1] == iota((listed, slots), 0)), 1.0, 0.0
            )
            local = jnp.sum(chosen * (rows[k] - own * table_rows + 1.0), axis=1, keepdims=True)
            picks.append((local - 1.0 == iota((listed, table_rows), 1)).astype(BF16))
        return jnp.concatenate(picks, axis=0), tables[0]

    picks, my_list = on_core(
        choose,
        [lists],
        [shape(column, table_rows, dtype=BF16), shape(2 * positions * feats, kslots)],
        small,
    )

    def encode(picks, enc):
        rows = dot(picks, enc).astype(BF16)
        return [rows[k * listed : (k + 1) * listed] for k in range(poses)] + [picks]

    *enc_rows, picks = on_core(
        encode,
        [picks, encoder],
        [shape(listed, width, dtype=BF16)] * poses + [shape(column, table_rows, dtype=BF16)],
        small,
    )

    enc_rows = [enc_rows[0]] + [rotate(enc_rows[k], "pos", k) for k in range(1, poses)]
    far = [swap(enc_rows[0], "feat", feats // 2)]

    dec_rows = lax.dot_general(
        picks, decoder, (((1,), (0,)), ((), ())), preferred_element_type=F32
    )
    dec_rows = jnp.transpose(dec_rows, (1, 0, 2)).astype(BF16)
    dec_rows = [dec_rows[:, k * listed : (k + 1) * listed] for k in range(poses)]
    near = [swap(enc_rows[0], "feat", 1)]
    *dec_rows, enc_rows[-1], near[0], far[0] = lax.optimization_barrier(
        (*dec_rows, enc_rows[-1], near[0], far[0])
    )
    dec_rows = [dec_rows[0]] + [rotate(dec_rows[k], "pos", k) for k in range(1, poses)]

    far += [swap(rows, "feat", feats // 2) for rows in enc_rows[1:]]

    def places(table, pattern):
        feat, pos, rep = place()

        def padded(owner, rank):
            feat_of = floor_div(owner, poses)
            step = (feat.astype(jnp.int32) ^ feat_of.astype(jnp.int32)).astype(F32)
            turn = pos - (owner - feat_of * poses)
            turn = jnp.where(turn < 0.0, turn + poses, turn)
            return (step * poses + turn) * listed + rank

        ids_row, vals_row = as_rows(table)
        ids_col = as_col(table)
        owner_row = floor_div(ids_row, table_rows)
        owner_col = floor_div(ids_col, table_rows)
        same = owner_col == owner_row
        down, across = iota((slots, slots), 0), iota((slots, slots), 1)
        rank_col = jnp.sum(jnp.where(same & (across < down), 1.0, 0.0), axis=1, keepdims=True)
        rank_row = jnp.sum(jnp.where(same & (down < across), 1.0, 0.0), axis=0, keepdims=True)
        total = holders * listed
        placing = padded(owner_col, rank_col) == iota((slots, total), 1)
        placing_t = padded(owner_row, rank_row) == iota((total, slots), 0)
        layer = ids_col - floor_div(ids_col, layers) * layers
        layer_row = jnp.sum(jnp.where(placing, layer, 0.0), axis=0, keepdims=True)
        mine = placing_t[:column]
        gain = jnp.sum(jnp.where(mine, vals_row, 0.0), axis=1, keepdims=True)
        source_layer = ids_row - floor_div(ids_row, layers) * layers
        source_layer = jnp.sum(jnp.where(mine, source_layer, 0.0), axis=1, keepdims=True)
        gains = jnp.concatenate(
            [jnp.where(source_layer <= l, gain, 0.0) for l in range(depth)], axis=0
        )
        allowed = jnp.where(pattern[0] == 1, 1.0, 0.0).astype(BF16)

        def in_block(slot, dim, extent):
            wide = (extent, feats) if dim == 0 else (feats, extent)
            return (floor_div(slot, block_rows) == iota(wide, 1 - dim)).astype(BF16)

        sources = in_block(iota((slots, 1), 0), 0, slots)
        targets = in_block(iota((1, slots), 1), 1, slots)
        mask = dot(dot(sources, allowed, NT).astype(BF16), targets)
        mask = jnp.where(floor_div(down, kslots) <= floor_div(across, kslots), mask, 0.0)
        first = (feat * reps + rep) * result_rows
        own_slot = first + iota((result_rows, 1), 0)
        own_mask = dot(in_block(own_slot, 0, result_rows), allowed).astype(BF16)
        own_mask = dot(own_mask, targets)
        own_causal = floor_div(iota((result_rows, slots), 1), kslots) <= floor_div(
            first + iota((result_rows, slots), 0), kslots
        )
        own_mask = jnp.where(own_causal, own_mask, 0.0)
        placing, placing_t = placing.astype(BF16), placing_t.astype(BF16)
        return placing, placing_t, layer_row, gains, mask.astype(BF16), own_mask

    placing, placing_t, layer_row, gains, mask, own_mask, far[0] = on_core(
        places,
        [my_list, block_pattern],
        [
            shape(slots, holders * listed, dtype=BF16),
            shape(holders * listed, slots, dtype=BF16),
            shape(1, holders * listed),
            shape(depth * column, 1),
            shape(slots, slots, dtype=BF16),
            shape(result_rows, slots),
        ],
        small,
        through=far[:1],
        cost=(1, 1),
    )
    shards = []
    for m in range(feats):
        if m == 0 or m == feats // 2:
            shards.append(far if m else enc_rows)
        elif feats == 4 and m == 3:
            inner = [lax.ppermute(rows, "feat", [(1, 2), (2, 1)]) for rows in enc_rows]
            outer = [lax.ppermute(rows, "feat", [(2, 3), (1, 0)]) for rows in far]
            shards.append(inner + outer)
        else:
            shards.append([swap(rows, "feat", m) for rows in enc_rows])
        if m == 1:
            shards[1][0] = near[0]

    def products(first, enc, dec, layer_row, placing_t):
        enc = jnp.concatenate(enc, axis=0)
        count = enc.shape[0] // column
        every = dot(dec, enc, NT)
        lanes = slice(first * column, (first + count) * column)
        raw = jnp.zeros((column, count * column), F32)
        for l in range(depth):
            rows = every[l * column : (l + 1) * column]
            raw = raw + jnp.where(layer_row[:, lanes] == l + 1.0, rows, 0.0)
        split = dot(jnp.concatenate(pieces(raw), axis=0), placing_t[lanes])
        return split[:column] + (split[column : 2 * column] + split[2 * column :])

    def early(layer_row, placing_t, gains, *values):
        dec = jnp.concatenate([d[l] for l in range(depth) for d in values[:poses]], axis=0)
        dec = (dec.astype(F32) * gains).astype(BF16)
        return products(0, values[poses:], dec, layer_row, placing_t), dec

    def late(layer_row, placing_t, so_far, dec, *values):
        if len(values) > poses:
            values = [a + b for a, b in zip(values[:poses], values[poses:])]
        raw = so_far + products(feats - 1, values, dec, layer_row, placing_t)
        first = place()[2] == 0.0
        return (
            jnp.where(first, raw[:half], raw[half:]),
            jnp.where(first, raw[half:], raw[:half]),
        )

    so_far, scaled = on_core(
        early,
        [layer_row, placing_t, gains] + dec_rows + [rows for step in shards[:-1] for rows in step],
        [shape(column, slots), shape(depth * column, width, dtype=BF16)],
        small,
        cost=(1, 1),
    )
    keep, send = on_core(
        late,
        [layer_row, placing_t, so_far, scaled] + shards[-1],
        [shape(half, slots)] * 2,
        small,
    )
    own_edges = (keep + rotate(send, "rep", 1)).astype(BF16)
    edges = [own_edges] + [swap(own_edges, "feat", m) for m in range(1, feats)]
    others = [rotate(shard, "rep", 1) for shard in edges]

    def finish(placing, mask, own_mask, targets, *values):
        feat, _, rep = place()
        first = rep == 0.0
        parts = []
        for mine, other in zip(values[:feats], values[feats:]):
            parts += [jnp.where(first, mine, other), jnp.where(first, other, mine)]
        padded = jnp.concatenate(parts, axis=0)
        magnitude = jnp.abs(dot(placing, padded) * mask.astype(F32))
        total = jnp.maximum(jnp.sum(magnitude, axis=0, keepdims=True), 1.0)
        magnitude = magnitude.astype(BF16)
        diagonal = iota((slots, slots), 0) == iota((slots, slots), 1)
        scale = 1.0 / jnp.sum(jnp.where(diagonal, total, 0.0), axis=1, keepdims=True)
        current = (iota((slots, panel), 0) == targets.astype(F32)).astype(F32)
        accum = jnp.zeros((slots, panel), F32)
        for _ in range(ITERS):
            scaled = current * scale
            high = part(scaled, small)
            low = part(scaled - high.astype(F32), small)
            both = dot(magnitude, jnp.concatenate([high, low], axis=1))
            current = both[:, :panel] + both[:, panel:]
            accum = accum + current
        index = feat * reps + rep
        influence = accum[:result_rows]
        for w in range(1, feats * reps):
            influence = jnp.where(
                index == w, accum[w * result_rows : (w + 1) * result_rows], influence
            )
        start = index * result_rows
        own = start + iota((result_rows, slots), 0) == iota((result_rows, slots), 1)
        rows = dot(own.astype(BF16), padded, NT).astype(BF16)
        edges = (dot(rows, placing, NT) * own_mask).astype(BF16)
        return edges[None], (influence * float(slots))[None]

    edges, influence = on_core(
        finish,
        [placing, mask, own_mask, target_slots] + edges + others,
        [shape(1, result_rows, slots, dtype=BF16), shape(1, result_rows, panel)],
        small,
    )
    return edges, influence


def solution(mesh):
    return jax.shard_map(
        per_device,
        mesh=mesh,
        in_specs=(
            P(("grp", "pos"), "feat", None),
            P(("grp", "pos"), "feat", None),
            P(("grp", "pos"), None, None),
            P(("grp", "pos"), None),
            P(("feat", "pos"), "rep"),
            P(("feat", "pos"), None, "rep"),
        ),
        out_specs=(
            P(("grp", "pos"), ("feat", "rep"), None),
            P(("grp", "pos"), ("feat", "rep"), None),
        ),
        check_vma=False,
    )
```

```python
import jax
import jax.numpy as jnp
from jax import lax
from jax.experimental import pallas as pl
from jax.experimental.pallas import tpu as pltpu
from jax.sharding import PartitionSpec as P

ITERS = 3
F32 = jnp.float32
BF16 = jnp.bfloat16
NN = (((1,), (0,)), ((), ()))
NT = (((1,), (1,)), ((), ()))
LANES = 128
KERNEL_SLOTS = 1024


def dot(a, b, dims=NN):
    return lax.dot_general(a, b, dims, preferred_element_type=F32)


def iota(shape, dim):
    return lax.broadcasted_iota(jnp.int32, shape, dim).astype(F32)


def floor_div(x, n):
    return jnp.floor((x + 0.5) * (1.0 / n))


def on_core(fn, args, outs, kernel=True, through=(), streams=(), cost=None, room=24):
    if not kernel:
        loads = [lambda i, x=x: x[i] for x in streams]
        return list(fn(*args, *loads)) + list(through)
    count, passed, streamed = len(args), len(through), len(streams)

    def body(*refs):
        sources = refs[count : count + streamed]
        results = refs[count + streamed + passed :][: len(outs)]
        scratch = refs[len(refs) - 2 * streamed :]
        copies = []
        for n in range(streamed):
            copies.append(
                [
                    pltpu.make_async_copy(
                        sources[n].at[i], scratch[2 * n].at[i], scratch[2 * n + 1].at[i]
                    )
                    for i in range(streams[n].shape[0])
                ]
            )
            for copy in copies[-1]:
                copy.start()

        def load(n):
            def wait(i):
                copies[n][i].wait()
                return scratch[2 * n][i]

            return wait

        values = fn(*[ref[...] for ref in refs[:count]], *[load(n) for n in range(streamed)])
        for ref, value in zip(results, values):
            ref[...] = value

    estimate = None
    if cost is not None:
        estimate = pl.CostEstimate(flops=cost[0], bytes_accessed=cost[1], transcendentals=0)
    in_vmem = pl.BlockSpec(memory_space=pltpu.VMEM)
    anywhere = pl.BlockSpec(memory_space=pl.ANY)
    scratch = []
    for x in streams:
        scratch += [pltpu.VMEM(x.shape, x.dtype), pltpu.SemaphoreType.DMA((x.shape[0],))]
    call = pl.pallas_call(
        body,
        out_shape=list(outs) + [jax.ShapeDtypeStruct(x.shape, x.dtype) for x in through],
        in_specs=[in_vmem] * count
        + [pl.BlockSpec(memory_space=pltpu.HBM)] * streamed
        + [anywhere] * passed,
        out_specs=[in_vmem] * len(outs) + [anywhere] * passed,
        scratch_shapes=scratch,
        input_output_aliases={count + streamed + i: len(outs) + i for i in range(passed)},
        compiler_params=pltpu.CompilerParams(vmem_limit_bytes=room * 1024 * 1024),
        cost_estimate=estimate,
    )
    return list(call(*args, *streams, *through))


def rotate(x, axis, step):
    count = lax.axis_size(axis)
    return lax.ppermute(x, axis, [(i, (i + step) % count) for i in range(count)])


def ring_place(index, count):
    low = floor_div(index, 2)
    return jnp.where(index > 2 * low, count - 1 - low, low)


def ring_next(x, axis, across=None, turn=0):
    count = lax.axis_size(axis)
    order = list(range(0, count, 2)) + list(range(1, count, 2))[::-1]
    steps = [(order[i], order[(i + 1) % count]) for i in range(count)]
    if across is None:
        return lax.ppermute(x, axis, steps)
    wide = lax.axis_size(across)
    pairs = [(a * wide + i, b * wide + (i + turn) % wide) for a, b in steps for i in range(wide)]
    return lax.ppermute(x, (axis, across), pairs)


def ring_spread(x, axis):
    count = lax.axis_size(axis)
    order = list(range(0, count, 2)) + list(range(1, count, 2))[::-1]
    return [x] + [
        lax.ppermute(x, axis, [(order[i], order[(i + k) % count]) for i in range(count)])
        for k in range(1, count)
    ]


def part(x, kernel):
    return x.astype(BF16) if kernel else lax.reduce_precision(x, 8, 7).astype(BF16)


def shape(*dims, dtype=F32):
    return jax.ShapeDtypeStruct(dims, dtype)


def per_device(active_ids, active_vals, block_pattern, target_slots, encoder, decoder):
    feats = lax.axis_size("feat")
    poses = lax.axis_size("pos")
    reps = lax.axis_size("rep")
    holders = feats * poses
    table_rows, width = encoder.shape
    depth = decoder.shape[1]
    layers = depth + 1
    positions, kslots = active_ids.shape[1:]
    block_rows = positions * kslots
    slots = block_rows * feats
    capacity = max(2, (10 * block_rows + 7 * holders - 1) // (7 * holders))
    listed = capacity * feats
    column = poses * listed
    half = column // reps
    result_rows = block_rows // reps
    panel = target_slots.shape[1]
    small = slots <= KERNEL_SLOTS

    def place():
        feat, pos = lax.axis_index("feat"), lax.axis_index("pos")
        return feat.astype(F32), pos.astype(F32), lax.axis_index("rep").astype(F32)

    def pack(ids, vals):
        one = jnp.concatenate([ids(0).astype(F32), vals(0)], axis=0)
        one = jnp.concatenate([one, jnp.zeros((2 * positions, LANES - kslots), F32)], axis=1)
        return (jnp.broadcast_to(one, (holders,) + one.shape),)

    (packed,) = on_core(
        pack,
        [],
        [shape(holders, 2 * positions, LANES)],
        streams=[active_ids, active_vals],
        room=60,
    )
    lists = lax.all_to_all(packed, ("feat", "pos"), split_axis=0, concat_axis=0, tiled=True)

    def list_of(values, prompt):
        blocks = []
        for a in range(feats):
            block = values[a * poses]
            for q in range(1, poses):
                block = jnp.where(prompt == q, values[a * poses + q], block)
            blocks.append(block)
        return jnp.concatenate(blocks, axis=0)[:, :kslots]

    def list_row(slot):
        place = floor_div(slot, kslots)
        return place + floor_div(place, positions) * positions

    def slot_entry(slot):
        return slot - floor_div(slot, kslots) * kslots

    def pieces(table):
        high = part(table, small)
        rest = table - high.astype(F32)
        middle = part(rest, small)
        return [high, middle, part(rest - middle.astype(F32), small)]

    def as_rows(table):
        spread = (iota((kslots, slots), 0) == slot_entry(iota((kslots, slots), 1))).astype(BF16)
        wide = dot(jnp.concatenate(pieces(table), axis=0), spread)
        count = table.shape[0]
        wide = wide[:count] + (wide[count : 2 * count] + wide[2 * count :])
        row = iota(wide.shape, 0) - list_row(iota(wide.shape, 1))
        ids = jnp.sum(jnp.where(row == 0, wide, 0.0), axis=0, keepdims=True)
        return ids, jnp.sum(jnp.where(row == positions, wide, 0.0), axis=0, keepdims=True)

    def as_col(table):
        wide = (slots, table.shape[0])
        spread = (list_row(iota(wide, 0)) == iota(wide, 1)).astype(BF16)
        every = dot(spread, jnp.concatenate(pieces(table), axis=1))
        every = every[:, :kslots] + (every[:, kslots : 2 * kslots] + every[:, 2 * kslots :])
        mine = slot_entry(iota((slots, kslots), 0)) == iota((slots, kslots), 1)
        return jnp.sum(jnp.where(mine, every, 0.0), axis=1, keepdims=True)

    def choose(values):
        feat, pos, _ = place()
        own = feat * poses + pos
        tables = []
        rows = []
        for k in range(poses):
            prompt = jnp.where(pos + k >= poses, pos + k - poses, pos + k)
            tables.append(list_of(values, prompt))
            rows.append(as_rows(tables[k])[0])
        hits = [floor_div(ids, table_rows) == own for ids in rows]
        earlier = (iota((slots, slots), 0) < iota((slots, slots), 1)).astype(BF16)
        ranks = dot(jnp.concatenate([h.astype(BF16) for h in hits], axis=0), earlier)
        picks = []
        for k in range(poses):
            chosen = jnp.where(
                hits[k] & (ranks[k : k + 1] == iota((listed, slots), 0)), 1.0, 0.0
            )
            local = jnp.sum(chosen * (rows[k] - own * table_rows + 1.0), axis=1, keepdims=True)
            picks.append((local - 1.0 == iota((listed, table_rows), 1)).astype(BF16))
        return jnp.concatenate(picks, axis=0), tables[0]

    picks, my_list = on_core(
        choose,
        [lists],
        [shape(column, table_rows, dtype=BF16), shape(2 * positions * feats, kslots)],
        small,
        cost=(10**9, 10**7),
    )

    def encode(picks, enc):
        rows = dot(picks, enc).astype(BF16)
        return [rows[k * listed : (k + 1) * listed] for k in range(poses)] + [picks]

    *enc_rows, picks = on_core(
        encode,
        [picks, encoder],
        [shape(listed, width, dtype=BF16)] * poses + [shape(column, table_rows, dtype=BF16)],
        small,
    )

    ring = [[enc_rows[0]] + [rotate(enc_rows[k], "pos", k) for k in range(1, poses)]]
    ring.append([ring_next(enc_rows[k], "feat", "pos", k) for k in range(poses)])

    dec_rows = lax.dot_general(
        picks, decoder, (((1,), (0,)), ((), ())), preferred_element_type=F32
    )
    dec_rows = jnp.transpose(dec_rows, (1, 0, 2)).astype(BF16)
    dec_rows = [dec_rows[:, k * listed : (k + 1) * listed] for k in range(poses)]
    *dec_rows, ring[1][-1] = lax.optimization_barrier((*dec_rows, ring[1][-1]))
    dec_rows = [dec_rows[0]] + [rotate(dec_rows[k], "pos", k) for k in range(1, poses)]

    ring.append([ring_next(rows, "feat") for rows in ring[-1]])

    order = [(0, 0)] + [(k, q) for k in range(1, feats - 1) for q in range(poses)]
    soon = len(order)
    order += [(0, q) for q in range(1, poses)] + [(feats - 1, q) for q in range(poses)]
    own_lists = [order.index((0, q)) for q in range(poses)]

    def places(table, pattern):
        feat, pos, rep = place()

        def padded(owner, rank):
            feat_of = floor_div(owner, poses)
            step = ring_place(feat, feats) - ring_place(feat_of, feats)
            step = jnp.where(step < 0.0, step + feats, step)
            turn = pos - (owner - feat_of * poses)
            turn = jnp.where(turn < 0.0, turn + poses, turn)
            at = step * poses + turn
            at = jnp.where(step < feats - 1.0, at - (poses - 1), at)
            at = jnp.where(step == 0.0, turn + (feats - 2) * poses, at)
            at = jnp.where((step == 0.0) & (turn == 0.0), 0.0, at)
            return at * listed + rank

        ids_row, vals_row = as_rows(table)
        ids_col = as_col(table)
        owner_row = floor_div(ids_row, table_rows)
        owner_col = floor_div(ids_col, table_rows)
        same = owner_col == owner_row
        down, across = iota((slots, slots), 0), iota((slots, slots), 1)
        rank_col = jnp.sum(jnp.where(same & (across < down), 1.0, 0.0), axis=1, keepdims=True)
        rank_row = jnp.sum(jnp.where(same & (down < across), 1.0, 0.0), axis=0, keepdims=True)
        total = holders * listed
        placing = padded(owner_col, rank_col) == iota((slots, total), 1)
        placing_t = padded(owner_row, rank_row) == iota((total, slots), 0)
        layer = ids_col - floor_div(ids_col, layers) * layers
        layer_row = jnp.sum(jnp.where(placing, layer, 0.0), axis=0, keepdims=True)
        mine = [placing_t[at * listed : (at + 1) * listed] for at in own_lists]
        mine = jnp.concatenate(mine, axis=0)
        gain = jnp.sum(jnp.where(mine, vals_row, 0.0), axis=1, keepdims=True)
        source_layer = ids_row - floor_div(ids_row, layers) * layers
        source_layer = jnp.sum(jnp.where(mine, source_layer, 0.0), axis=1, keepdims=True)
        gains = jnp.concatenate(
            [jnp.where(source_layer <= l, gain, 0.0) for l in range(depth)], axis=0
        )
        allowed = jnp.where(pattern[0] == 1, 1.0, 0.0).astype(BF16)

        def in_block(slot, dim, extent):
            wide = (extent, feats) if dim == 0 else (feats, extent)
            return (floor_div(slot, block_rows) == iota(wide, 1 - dim)).astype(BF16)

        sources = in_block(iota((slots, 1), 0), 0, slots)
        targets = in_block(iota((1, slots), 1), 1, slots)
        mask = dot(dot(sources, allowed, NT).astype(BF16), targets)
        mask = jnp.where(floor_div(down, kslots) <= floor_div(across, kslots), mask, 0.0)
        first = (feat * reps + rep) * result_rows
        own_slot = first + iota((result_rows, 1), 0)
        own_mask = dot(in_block(own_slot, 0, result_rows), allowed).astype(BF16)
        own_mask = dot(own_mask, targets)
        own_causal = floor_div(iota((result_rows, slots), 1), kslots) <= floor_div(
            first + iota((result_rows, slots), 0), kslots
        )
        own_mask = jnp.where(own_causal, own_mask, 0.0)
        placing, placing_t = placing.astype(BF16), placing_t.astype(BF16)
        return placing, placing_t, layer_row, gains, mask.astype(BF16), own_mask

    placing, placing_t, layer_row, gains, mask, own_mask, ring[2][0] = on_core(
        places,
        [my_list, block_pattern],
        [
            shape(slots, holders * listed, dtype=BF16),
            shape(holders * listed, slots, dtype=BF16),
            shape(1, holders * listed),
            shape(depth * column, 1),
            shape(slots, slots, dtype=BF16),
            shape(result_rows, slots),
        ],
        small,
        through=[ring[2][0]],
        cost=(1, 1),
    )
    for _ in range(3, feats):
        ring.append([ring_next(rows, "feat") for rows in ring[-1]])

    def products(first, enc, dec, layer_row, placing_t):
        enc = jnp.concatenate(enc, axis=0)
        every = dot(dec, enc, NT)
        lanes = slice(first * listed, first * listed + enc.shape[0])
        raw = jnp.zeros((column, enc.shape[0]), F32)
        for l in range(depth):
            rows = every[l * column : (l + 1) * column]
            raw = raw + jnp.where(layer_row[:, lanes] == l + 1.0, rows, 0.0)
        split = dot(jnp.concatenate(pieces(raw), axis=0), placing_t[lanes])
        return split[:column] + (split[column : 2 * column] + split[2 * column :])

    def early(layer_row, placing_t, gains, *values):
        dec = jnp.concatenate([d[l] for l in range(depth) for d in values[:poses]], axis=0)
        dec = (dec.astype(F32) * gains).astype(BF16)
        return products(0, values[poses:], dec, layer_row, placing_t), dec

    def late(layer_row, placing_t, so_far, dec, *values):
        raw = so_far + products(soon, values, dec, layer_row, placing_t)
        first = place()[2] == 0.0
        return (
            jnp.where(first, raw[:half], raw[half:]),
            jnp.where(first, raw[half:], raw[:half]),
        )

    so_far, scaled = on_core(
        early,
        [layer_row, placing_t, gains] + dec_rows + [ring[k][q] for k, q in order[:soon]],
        [shape(column, slots), shape(depth * column, width, dtype=BF16)],
        small,
        cost=(1, 1),
    )
    keep, send = on_core(
        late,
        [layer_row, placing_t, so_far, scaled] + [ring[k][q] for k, q in order[soon:]],
        [shape(half, slots)] * 2,
        small,
    )
    own_edges = (keep + rotate(send, "rep", 1)).astype(BF16)
    shards = ring_spread(own_edges, "feat")
    others = [rotate(shard, "rep", 1) for shard in shards]

    def finish(placing, mask, own_mask, targets, *values):
        feat, _, rep = place()
        first = rep == 0.0
        chips = []
        for mine, other in zip(values[:feats], values[feats:]):
            chips.append((jnp.where(first, mine, other), jnp.where(first, other, mine)))
        chips = [jnp.concatenate(chip, axis=0) for chip in chips]
        padded = [chips[k][q * listed : (q + 1) * listed] for k, q in order]
        padded = jnp.concatenate(padded, axis=0)
        magnitude = jnp.abs(dot(placing, padded) * mask.astype(F32))
        total = jnp.maximum(jnp.sum(magnitude, axis=0, keepdims=True), 1.0)
        magnitude = magnitude.astype(BF16)
        diagonal = iota((slots, slots), 0) == iota((slots, slots), 1)
        scale = 1.0 / jnp.sum(jnp.where(diagonal, total, 0.0), axis=1, keepdims=True)
        current = (iota((slots, panel), 0) == targets.astype(F32)).astype(F32)
        accum = jnp.zeros((slots, panel), F32)
        for _ in range(ITERS):
            scaled = current * scale
            high = part(scaled, small)
            low = part(scaled - high.astype(F32), small)
            both = dot(magnitude, jnp.concatenate([high, low], axis=1))
            current = both[:, :panel] + both[:, panel:]
            accum = accum + current
        index = feat * reps + rep
        influence = accum[:result_rows]
        for w in range(1, feats * reps):
            influence = jnp.where(
                index == w, accum[w * result_rows : (w + 1) * result_rows], influence
            )
        start = index * result_rows
        own = start + iota((result_rows, slots), 0) == iota((result_rows, slots), 1)
        rows = dot(own.astype(BF16), padded, NT).astype(BF16)
        edges = (dot(rows, placing, NT) * own_mask).astype(BF16)
        return edges[None], (influence * float(slots))[None]

    edges, influence = on_core(
        finish,
        [placing, mask, own_mask, target_slots] + shards + others,
        [shape(1, result_rows, slots, dtype=BF16), shape(1, result_rows, panel)],
        small,
    )
    return edges, influence


def solution(mesh):
    return jax.shard_map(
        per_device,
        mesh=mesh,
        in_specs=(
            P(("grp", "pos"), "feat", None),
            P(("grp", "pos"), "feat", None),
            P(("grp", "pos"), None, None),
            P(("grp", "pos"), None),
            P(("feat", "pos"), "rep"),
            P(("feat", "pos"), None, "rep"),
        ),
        out_specs=(
            P(("grp", "pos"), ("feat", "rep"), None),
            P(("grp", "pos"), ("feat", "rep"), None),
        ),
        check_vma=False,
    )
```

```python
import jax
import jax.numpy as jnp
from jax import lax
from jax.experimental import pallas as pl
from jax.experimental.pallas import tpu as pltpu
from jax.sharding import PartitionSpec as P

ITERS = 3
F32 = jnp.float32
BF16 = jnp.bfloat16
NN = (((1,), (0,)), ((), ()))
NT = (((1,), (1,)), ((), ()))
LANES = 128
GROUP = 8
KERNEL_SLOTS = 1024


def dot(a, b, dims=NN):
    return lax.dot_general(a, b, dims, preferred_element_type=F32)


def iota(shape, dim):
    return lax.broadcasted_iota(jnp.int32, shape, dim).astype(F32)


def floor_div(x, n):
    return jnp.floor((x + 0.5) * (1.0 / n))


def on_core(fn, args, outs, kernel=True, through=(), streams=(), cost=None, room=24):
    if not kernel:
        loads = [lambda i, x=x: x[i] for x in streams]
        return list(fn(*args, *loads)) + list(through)
    count, passed, streamed = len(args), len(through), len(streams)

    def body(*refs):
        sources = refs[count : count + streamed]
        results = refs[count + streamed + passed :][: len(outs)]
        scratch = refs[len(refs) - 2 * streamed :]
        copies = []
        for n in range(streamed):
            copies.append(
                [
                    pltpu.make_async_copy(
                        sources[n].at[i], scratch[2 * n].at[i], scratch[2 * n + 1].at[i]
                    )
                    for i in range(streams[n].shape[0])
                ]
            )
            for copy in copies[-1]:
                copy.start()

        def load(n):
            def wait(i):
                copies[n][i].wait()
                return scratch[2 * n][i]

            return wait

        values = fn(*[ref[...] for ref in refs[:count]], *[load(n) for n in range(streamed)])
        for ref, value in zip(results, values):
            ref[...] = value

    estimate = None
    if cost is not None:
        estimate = pl.CostEstimate(flops=cost[0], bytes_accessed=cost[1], transcendentals=0)
    in_vmem = pl.BlockSpec(memory_space=pltpu.VMEM)
    anywhere = pl.BlockSpec(memory_space=pl.ANY)
    scratch = []
    for x in streams:
        scratch += [pltpu.VMEM(x.shape, x.dtype), pltpu.SemaphoreType.DMA((x.shape[0],))]
    call = pl.pallas_call(
        body,
        out_shape=list(outs) + [jax.ShapeDtypeStruct(x.shape, x.dtype) for x in through],
        in_specs=[in_vmem] * count
        + [pl.BlockSpec(memory_space=pltpu.HBM)] * streamed
        + [anywhere] * passed,
        out_specs=[in_vmem] * len(outs) + [anywhere] * passed,
        scratch_shapes=scratch,
        input_output_aliases={count + streamed + i: len(outs) + i for i in range(passed)},
        compiler_params=pltpu.CompilerParams(vmem_limit_bytes=room * 1024 * 1024),
        cost_estimate=estimate,
    )
    return list(call(*args, *streams, *through))


def rotate(x, axis, step):
    count = lax.axis_size(axis)
    return lax.ppermute(x, axis, [(i, (i + step) % count) for i in range(count)])


def ring_place(index, count):
    low = floor_div(index, 2)
    return jnp.where(index > 2 * low, count - 1 - low, low)


def ring_next(x, axis, across=None, turn=0):
    count = lax.axis_size(axis)
    order = list(range(0, count, 2)) + list(range(1, count, 2))[::-1]
    steps = [(order[i], order[(i + 1) % count]) for i in range(count)]
    if across is None:
        return lax.ppermute(x, axis, steps)
    wide = lax.axis_size(across)
    pairs = [(a * wide + i, b * wide + (i + turn) % wide) for a, b in steps for i in range(wide)]
    return lax.ppermute(x, (axis, across), pairs)


def ring_spread(x, axis):
    count = lax.axis_size(axis)
    order = list(range(0, count, 2)) + list(range(1, count, 2))[::-1]
    return [x] + [
        lax.ppermute(x, axis, [(order[i], order[(i + k) % count]) for i in range(count)])
        for k in range(1, count)
    ]


def part(x, kernel):
    return x.astype(BF16) if kernel else lax.reduce_precision(x, 8, 7).astype(BF16)


def shape(*dims, dtype=F32):
    return jax.ShapeDtypeStruct(dims, dtype)


def per_device(active_ids, active_vals, block_pattern, target_slots, encoder, decoder):
    feats = lax.axis_size("feat")
    poses = lax.axis_size("pos")
    reps = lax.axis_size("rep")
    holders = feats * poses
    table_rows, width = encoder.shape
    depth = decoder.shape[1]
    layers = depth + 1
    positions, kslots = active_ids.shape[1:]
    block_rows = positions * kslots
    slots = block_rows * feats
    capacity = max(2, (10 * block_rows + 7 * holders - 1) // (7 * holders))
    listed = capacity * feats
    column = poses * listed
    half = column // reps
    result_rows = block_rows // reps
    panel = target_slots.shape[1]
    small = slots <= KERNEL_SLOTS
    span = -(-block_rows // LANES) * LANES if small else block_rows
    wide = feats * span

    rests = []
    for row in range(0, half, GROUP):
        rests.append((row, row % listed // capacity))
    bins = []
    for rest in sorted(rests, key=lambda rest: rest[1]):
        for row in bins:
            if sum(feats - block for _, block in row) + feats - rest[1] <= feats:
                row.append(rest)
                break
        else:
            bins.append([rest])

    def pack_rests(x):
        rows = []
        for row in bins:
            parts = [x[at : at + GROUP, block * span :] for at, block in row]
            empty = wide - sum(part.shape[1] for part in parts)
            parts += [jnp.zeros((GROUP, empty), x.dtype)] if empty else []
            rows.append(jnp.concatenate(parts, axis=1) if len(parts) > 1 else parts[0])
        return jnp.concatenate(rows, axis=0)

    def unpack_rests(x):
        x = x.astype(F32) if small else x
        found = {}
        for n, row in enumerate(bins):
            lane = 0
            for at, block in row:
                rest = x[n * GROUP : (n + 1) * GROUP, lane : lane + wide - block * span]
                lane += wide - block * span
                if block:
                    rest = jnp.concatenate([jnp.zeros((GROUP, block * span), x.dtype), rest], axis=1)
                found[at] = rest
        return jnp.concatenate([found[at] for at, _ in rests], axis=0).astype(BF16)

    def place():
        feat, pos = lax.axis_index("feat"), lax.axis_index("pos")
        return feat.astype(F32), pos.astype(F32), lax.axis_index("rep").astype(F32)

    def pack(ids, vals):
        one = jnp.concatenate([ids(0).astype(F32), vals(0)], axis=0)
        one = jnp.concatenate([one, jnp.zeros((2 * positions, LANES - kslots), F32)], axis=1)
        return (jnp.broadcast_to(one, (holders,) + one.shape),)

    (packed,) = on_core(
        pack,
        [],
        [shape(holders, 2 * positions, LANES)],
        streams=[active_ids, active_vals],
        room=60,
    )
    lists = lax.all_to_all(packed, ("feat", "pos"), split_axis=0, concat_axis=0, tiled=True)

    def list_of(values, prompt):
        blocks = []
        for a in range(feats):
            block = values[a * poses]
            for q in range(1, poses):
                block = jnp.where(prompt == q, values[a * poses + q], block)
            blocks.append(block)
        return jnp.concatenate(blocks, axis=0)[:, :kslots]

    def list_row(slot):
        place = floor_div(slot, kslots)
        return place + floor_div(place, positions) * positions

    def slot_entry(slot):
        return slot - floor_div(slot, kslots) * kslots

    def pieces(table):
        high = part(table, small)
        rest = table - high.astype(F32)
        middle = part(rest, small)
        return [high, middle, part(rest - middle.astype(F32), small)]

    def as_rows(table, slot_at, lanes):
        entry = slot_entry(slot_at(iota((kslots, lanes), 1)))
        spread = (iota((kslots, lanes), 0) == entry).astype(BF16)
        every = dot(jnp.concatenate(pieces(table), axis=0), spread)
        count = table.shape[0]
        every = every[:count] + (every[count : 2 * count] + every[2 * count :])
        row = iota(every.shape, 0) - list_row(slot_at(iota(every.shape, 1)))
        ids = jnp.sum(jnp.where(row == 0, every, 0.0), axis=0, keepdims=True)
        return ids, jnp.sum(jnp.where(row == positions, every, 0.0), axis=0, keepdims=True)

    def spread_slot(lane):
        block = floor_div(lane, span)
        inside = lane - block * span
        return jnp.where(inside < block_rows, block * block_rows + inside, -1.0 * slots)

    def as_col(table):
        wide = (slots, table.shape[0])
        spread = (list_row(iota(wide, 0)) == iota(wide, 1)).astype(BF16)
        every = dot(spread, jnp.concatenate(pieces(table), axis=1))
        every = every[:, :kslots] + (every[:, kslots : 2 * kslots] + every[:, 2 * kslots :])
        mine = slot_entry(iota((slots, kslots), 0)) == iota((slots, kslots), 1)
        return jnp.sum(jnp.where(mine, every, 0.0), axis=1, keepdims=True)

    def choose(values):
        feat, pos, _ = place()
        own = feat * poses + pos
        tables = []
        rows = []
        for k in range(poses):
            prompt = jnp.where(pos + k >= poses, pos + k - poses, pos + k)
            tables.append(list_of(values, prompt))
            rows.append(as_rows(tables[k], lambda lane: lane, slots)[0])
        hits = [floor_div(ids, table_rows) == own for ids in rows]
        earlier = (iota((slots, slots), 0) < iota((slots, slots), 1)).astype(BF16)
        ranks = dot(jnp.concatenate([h.astype(BF16) for h in hits], axis=0), earlier)
        picks = []
        for k in range(poses):
            chosen = jnp.where(
                hits[k] & (ranks[k : k + 1] == iota((listed, slots), 0)), 1.0, 0.0
            )
            local = jnp.sum(chosen * (rows[k] - own * table_rows + 1.0), axis=1, keepdims=True)
            picks.append((local - 1.0 == iota((listed, table_rows), 1)).astype(BF16))
        return jnp.concatenate(picks, axis=0), tables[0]

    picks, my_list = on_core(
        choose,
        [lists],
        [shape(column, table_rows, dtype=BF16), shape(2 * positions * feats, kslots)],
        small,
        cost=(10**9, 10**7),
    )

    def encode(picks, enc):
        rows = dot(picks, enc).astype(BF16)
        return [rows[k * listed : (k + 1) * listed] for k in range(poses)] + [picks]

    *enc_rows, picks = on_core(
        encode,
        [picks, encoder],
        [shape(listed, width, dtype=BF16)] * poses + [shape(column, table_rows, dtype=BF16)],
        small,
    )

    ring = [[enc_rows[0]] + [rotate(enc_rows[k], "pos", k) for k in range(1, poses)]]
    ring.append([ring_next(enc_rows[k], "feat", "pos", k) for k in range(poses)])

    dec_rows = lax.dot_general(
        picks, decoder, (((1,), (0,)), ((), ())), preferred_element_type=F32
    )
    dec_rows = jnp.transpose(dec_rows, (1, 0, 2)).astype(BF16)
    dec_rows = [dec_rows[:, k * listed : (k + 1) * listed] for k in range(poses)]
    order = [(0, 0)] + [(k, q) for k in range(1, feats - 1) for q in range(poses)]
    soon = len(order)
    order += [(0, q) for q in range(1, poses)] + [(feats - 1, q) for q in range(poses)]
    own_lists = [order.index((0, q)) for q in range(poses)]

    def places(table, pattern):
        feat, pos, rep = place()

        def padded(owner, rank):
            feat_of = floor_div(owner, poses)
            step = ring_place(feat, feats) - ring_place(feat_of, feats)
            step = jnp.where(step < 0.0, step + feats, step)
            turn = pos - (owner - feat_of * poses)
            turn = jnp.where(turn < 0.0, turn + poses, turn)
            at = step * poses + turn
            at = jnp.where(step < feats - 1.0, at - (poses - 1), at)
            at = jnp.where(step == 0.0, turn + (feats - 2) * poses, at)
            at = jnp.where((step == 0.0) & (turn == 0.0), 0.0, at)
            return at * listed + rank

        ids_row, vals_row = as_rows(table, spread_slot, wide)
        ids_col = as_col(table)
        owner_row = floor_div(ids_row, table_rows)
        owner_col = floor_div(ids_col, table_rows)
        down, across = iota((slots, slots), 0), iota((slots, slots), 1)
        same = owner_col == floor_div(as_rows(table, lambda lane: lane, slots)[0], table_rows)
        rank_col = jnp.sum(jnp.where(same & (across < down), 1.0, 0.0), axis=1, keepdims=True)
        slot = spread_slot(iota((slots, wide), 1))
        same = (owner_col == owner_row) & (iota((slots, wide), 0) < slot)
        rank_row = jnp.sum(jnp.where(same, 1.0, 0.0), axis=0, keepdims=True)
        total = holders * listed
        used = spread_slot(iota((1, wide), 1)) >= 0.0
        place_row = jnp.where(used, padded(owner_row, rank_row), -1.0)
        placing = padded(owner_col, rank_col) == iota((slots, total), 1)
        placing_t = place_row == iota((total, wide), 0)
        layer = ids_col - floor_div(ids_col, layers) * layers
        layer_row = jnp.sum(jnp.where(placing, layer, 0.0), axis=0, keepdims=True)
        mine = [placing_t[at * listed : (at + 1) * listed] for at in own_lists]
        mine = jnp.concatenate(mine, axis=0)
        gain = jnp.sum(jnp.where(mine, vals_row, 0.0), axis=1, keepdims=True)
        source_layer = ids_row - floor_div(ids_row, layers) * layers
        source_layer = jnp.sum(jnp.where(mine, source_layer, 0.0), axis=1, keepdims=True)
        gains = jnp.concatenate(
            [jnp.where(source_layer <= l, gain, 0.0) for l in range(depth)], axis=0
        )
        allowed = jnp.where(pattern[0] == 1, 1.0, 0.0).astype(BF16)

        def in_block(slot, dim, extent):
            wide = (extent, feats) if dim == 0 else (feats, extent)
            return (floor_div(slot, block_rows) == iota(wide, 1 - dim)).astype(BF16)

        sources = (floor_div(iota((wide, 1), 0), span) == iota((wide, feats), 1)).astype(BF16)
        targets = (floor_div(iota((1, wide), 1), span) == iota((feats, wide), 0)).astype(BF16)
        mask = dot(dot(sources, allowed, NT).astype(BF16), targets)
        source = floor_div(spread_slot(iota((wide, wide), 0)), kslots)
        target = floor_div(spread_slot(iota((wide, wide), 1)), kslots)
        mask = jnp.where(source <= target, mask, 0.0)
        first = (feat * reps + rep) * result_rows
        own_slot = first + iota((result_rows, 1), 0)
        own_mask = dot(in_block(own_slot, 0, result_rows), allowed).astype(BF16)
        own_mask = dot(own_mask, in_block(iota((1, slots), 1), 1, slots))
        own_causal = floor_div(iota((result_rows, slots), 1), kslots) <= floor_div(
            first + iota((result_rows, slots), 0), kslots
        )
        own_mask = jnp.where(own_causal, own_mask, 0.0)
        placing, placing_t = placing.astype(BF16), placing_t.astype(BF16)
        return placing, placing_t, layer_row, gains, mask.astype(BF16), own_mask

    placing, placing_t, layer_row, gains, mask, own_mask, *dec_rows[1:] = on_core(
        places,
        [my_list, block_pattern],
        [
            shape(slots, holders * listed, dtype=BF16),
            shape(holders * listed, wide, dtype=BF16),
            shape(1, holders * listed),
            shape(depth * column, 1),
            shape(wide, wide, dtype=BF16),
            shape(result_rows, slots),
        ],
        small,
        through=dec_rows[1:],
        cost=(1, 1),
    )
    *dec_rows, ring[1][0], ring[1][-1] = lax.optimization_barrier(
        (*dec_rows, ring[1][0], ring[1][-1])
    )
    dec_rows = [dec_rows[0]] + [rotate(dec_rows[k], "pos", k) for k in range(1, poses)]

    for _ in range(2, feats):
        ring.append([ring_next(rows, "feat") for rows in ring[-1]])

    def products(first, enc, dec, layer_row, placing_t):
        enc = jnp.concatenate(enc, axis=0)
        every = dot(dec, enc, NT)
        lanes = slice(first * listed, first * listed + enc.shape[0])
        raw = jnp.zeros((column, enc.shape[0]), F32)
        for l in range(depth):
            rows = every[l * column : (l + 1) * column]
            raw = raw + jnp.where(layer_row[:, lanes] == l + 1.0, rows, 0.0)
        split = dot(jnp.concatenate(pieces(raw), axis=0), placing_t[lanes])
        return split[:column] + (split[column : 2 * column] + split[2 * column :])

    def early(layer_row, placing_t, gains, *values):
        dec = jnp.concatenate([d[l] for l in range(depth) for d in values[:poses]], axis=0)
        dec = (dec.astype(F32) * gains).astype(BF16)
        return products(0, values[poses:], dec, layer_row, placing_t), dec

    def late(layer_row, placing_t, so_far, dec, *values):
        raw = so_far + products(soon, values, dec, layer_row, placing_t)
        first = place()[2] == 0.0
        lower, higher = pack_rests(raw[:half]), pack_rests(raw[half:])
        return jnp.where(first, lower, higher), jnp.where(first, higher, lower)

    so_far, scaled = on_core(
        early,
        [layer_row, placing_t, gains] + dec_rows + [ring[k][q] for k, q in order[:soon]],
        [shape(column, wide), shape(depth * column, width, dtype=BF16)],
        small,
        cost=(1, 1),
    )
    keep, send = on_core(
        late,
        [layer_row, placing_t, so_far, scaled] + [ring[k][q] for k, q in order[soon:]],
        [shape(len(bins) * GROUP, wide)] * 2,
        small,
    )
    own_edges = (keep + rotate(send, "rep", 1)).astype(BF16)
    shards = ring_spread(own_edges, "feat")
    others = [rotate(shard, "rep", 1) for shard in shards]

    def finish(placing, mask, own_mask, targets, *values):
        feat, _, rep = place()
        first = rep == 0.0
        chips = []
        for mine, other in zip(values[:feats], values[feats:]):
            lower, higher = jnp.where(first, mine, other), jnp.where(first, other, mine)
            chips.append(jnp.concatenate([unpack_rests(lower), unpack_rests(higher)], axis=0))
        padded = [chips[k][q * listed : (q + 1) * listed] for k, q in order]
        padded = jnp.concatenate(padded, axis=0)
        unused = [jnp.zeros((span - block_rows, holders * listed), BF16)]
        unused = unused if span > block_rows else []
        sources = []
        for f in range(feats):
            sources += [placing[f * block_rows : (f + 1) * block_rows]] + unused
        sources = jnp.concatenate(sources, axis=0)
        magnitude = jnp.abs(dot(sources, padded) * mask.astype(F32))
        total = jnp.maximum(jnp.sum(magnitude, axis=0, keepdims=True), 1.0)
        magnitude = magnitude.astype(BF16)
        diagonal = iota((wide, wide), 0) == iota((wide, wide), 1)
        scale = 1.0 / jnp.sum(jnp.where(diagonal, total, 0.0), axis=1, keepdims=True)
        targets = targets.astype(F32)
        targets = targets + floor_div(targets, block_rows) * (span - block_rows)
        current = (iota((wide, panel), 0) == targets).astype(F32)
        accum = jnp.zeros((wide, panel), F32)
        for _ in range(ITERS):
            scaled = current * scale
            high = part(scaled, small)
            low = part(scaled - high.astype(F32), small)
            both = dot(magnitude, jnp.concatenate([high, low], axis=1))
            current = both[:, :panel] + both[:, panel:]
            accum = accum + current
        influence = accum[:result_rows]
        for f in range(feats):
            for r in range(reps):
                at = f * span + r * result_rows
                mine = (feat == f) & (rep == r)
                influence = jnp.where(mine, accum[at : at + result_rows], influence)
        start = feat * span + rep * result_rows
        own = start + iota((result_rows, wide), 0) == iota((result_rows, wide), 1)
        rows = dot(own.astype(BF16), padded, NT).astype(BF16)
        edges = (dot(rows, placing, NT) * own_mask).astype(BF16)
        return edges[None], (influence * float(slots))[None]

    edges, influence = on_core(
        finish,
        [placing, mask, own_mask, target_slots] + shards + others,
        [shape(1, result_rows, slots, dtype=BF16), shape(1, result_rows, panel)],
        small,
    )
    return edges, influence


def solution(mesh):
    return jax.shard_map(
        per_device,
        mesh=mesh,
        in_specs=(
            P(("grp", "pos"), "feat", None),
            P(("grp", "pos"), "feat", None),
            P(("grp", "pos"), None, None),
            P(("grp", "pos"), None),
            P(("feat", "pos"), "rep"),
            P(("feat", "pos"), None, "rep"),
        ),
        out_specs=(
            P(("grp", "pos"), ("feat", "rep"), None),
            P(("grp", "pos"), ("feat", "rep"), None),
        ),
        check_vma=False,
    )
```

```python
import jax
import jax.numpy as jnp
from jax import lax
from jax.experimental import pallas as pl
from jax.experimental.pallas import tpu as pltpu
from jax.sharding import PartitionSpec as P

ITERS = 3
F32 = jnp.float32
BF16 = jnp.bfloat16
NN = (((1,), (0,)), ((), ()))
NT = (((1,), (1,)), ((), ()))
LANES = 128
GROUP = 8
KERNEL_SLOTS = 1024


def dot(a, b, dims=NN):
    return lax.dot_general(a, b, dims, preferred_element_type=F32)


def iota(shape, dim):
    return lax.broadcasted_iota(jnp.int32, shape, dim).astype(F32)


def floor_div(x, n):
    return jnp.floor((x + 0.5) * (1.0 / n))


def on_core(fn, args, outs, kernel=True, through=(), streams=(), cost=None, room=24):
    if not kernel:
        loads = [lambda i, x=x: x[i] for x in streams]
        return list(fn(*args, *loads)) + list(through)
    count, passed, streamed = len(args), len(through), len(streams)

    def body(*refs):
        sources = refs[count : count + streamed]
        results = refs[count + streamed + passed :][: len(outs)]
        scratch = refs[len(refs) - 2 * streamed :]
        copies = []
        for n in range(streamed):
            copies.append(
                [
                    pltpu.make_async_copy(
                        sources[n].at[i], scratch[2 * n].at[i], scratch[2 * n + 1].at[i]
                    )
                    for i in range(streams[n].shape[0])
                ]
            )
            for copy in copies[-1]:
                copy.start()

        def load(n):
            def wait(i):
                copies[n][i].wait()
                return scratch[2 * n][i]

            return wait

        values = fn(*[ref[...] for ref in refs[:count]], *[load(n) for n in range(streamed)])
        for ref, value in zip(results, values):
            ref[...] = value

    estimate = None
    if cost is not None:
        estimate = pl.CostEstimate(flops=cost[0], bytes_accessed=cost[1], transcendentals=0)
    in_vmem = pl.BlockSpec(memory_space=pltpu.VMEM)
    anywhere = pl.BlockSpec(memory_space=pl.ANY)
    scratch = []
    for x in streams:
        scratch += [pltpu.VMEM(x.shape, x.dtype), pltpu.SemaphoreType.DMA((x.shape[0],))]
    call = pl.pallas_call(
        body,
        out_shape=list(outs) + [jax.ShapeDtypeStruct(x.shape, x.dtype) for x in through],
        in_specs=[in_vmem] * count
        + [pl.BlockSpec(memory_space=pltpu.HBM)] * streamed
        + [anywhere] * passed,
        out_specs=[in_vmem] * len(outs) + [anywhere] * passed,
        scratch_shapes=scratch,
        input_output_aliases={count + streamed + i: len(outs) + i for i in range(passed)},
        compiler_params=pltpu.CompilerParams(vmem_limit_bytes=room * 1024 * 1024),
        cost_estimate=estimate,
    )
    return list(call(*args, *streams, *through))


def rotate(x, axis, step):
    count = lax.axis_size(axis)
    return lax.ppermute(x, axis, [(i, (i + step) % count) for i in range(count)])


def ring_place(index, count):
    low = floor_div(index, 2)
    return jnp.where(index > 2 * low, count - 1 - low, low)


def ring_next(x, axis, across=None, turn=0):
    count = lax.axis_size(axis)
    order = list(range(0, count, 2)) + list(range(1, count, 2))[::-1]
    steps = [(order[i], order[(i + 1) % count]) for i in range(count)]
    if across is None:
        return lax.ppermute(x, axis, steps)
    wide = lax.axis_size(across)
    pairs = [(a * wide + i, b * wide + (i + turn) % wide) for a, b in steps for i in range(wide)]
    return lax.ppermute(x, (axis, across), pairs)


def ring_spread(x, axis):
    count = lax.axis_size(axis)
    order = list(range(0, count, 2)) + list(range(1, count, 2))[::-1]
    return [x] + [
        lax.ppermute(x, axis, [(order[i], order[(i + k) % count]) for i in range(count)])
        for k in range(1, count)
    ]


def part(x, kernel):
    return x.astype(BF16) if kernel else lax.reduce_precision(x, 8, 7).astype(BF16)


def shape(*dims, dtype=F32):
    return jax.ShapeDtypeStruct(dims, dtype)


def per_device(active_ids, active_vals, block_pattern, target_slots, encoder, decoder):
    feats = lax.axis_size("feat")
    poses = lax.axis_size("pos")
    reps = lax.axis_size("rep")
    holders = feats * poses
    table_rows, width = encoder.shape
    depth = decoder.shape[1]
    layers = depth + 1
    positions, kslots = active_ids.shape[1:]
    block_rows = positions * kslots
    slots = block_rows * feats
    capacity = max(2, (10 * block_rows + 7 * holders - 1) // (7 * holders))
    listed = capacity * feats
    column = poses * listed
    half = column // reps
    result_rows = block_rows // reps
    panel = target_slots.shape[1]
    small = slots <= KERNEL_SLOTS
    span = -(-block_rows // LANES) * LANES if small else block_rows
    wide = feats * span

    rests = []
    for row in range(0, half, GROUP):
        rests.append((row, row % listed // capacity))
    bins = []
    for rest in sorted(rests, key=lambda rest: rest[1]):
        for row in bins:
            if sum(feats - block for _, block in row) + feats - rest[1] <= feats:
                row.append(rest)
                break
        else:
            bins.append([rest])

    def pack_rests(x):
        rows = []
        for row in bins:
            parts = [x[at : at + GROUP, block * span :] for at, block in row]
            empty = wide - sum(part.shape[1] for part in parts)
            parts += [jnp.zeros((GROUP, empty), x.dtype)] if empty else []
            rows.append(jnp.concatenate(parts, axis=1) if len(parts) > 1 else parts[0])
        return jnp.concatenate(rows, axis=0)

    def unpack_rests(x):
        x = x.astype(F32) if small else x
        found = {}
        for n, row in enumerate(bins):
            lane = 0
            for at, block in row:
                rest = x[n * GROUP : (n + 1) * GROUP, lane : lane + wide - block * span]
                lane += wide - block * span
                if block:
                    rest = jnp.concatenate([jnp.zeros((GROUP, block * span), x.dtype), rest], axis=1)
                found[at] = rest
        return jnp.concatenate([found[at] for at, _ in rests], axis=0).astype(BF16)

    def place():
        feat, pos = lax.axis_index("feat"), lax.axis_index("pos")
        return feat.astype(F32), pos.astype(F32), lax.axis_index("rep").astype(F32)

    def pack(ids, vals):
        one = jnp.concatenate([ids(0).astype(F32), vals(0)], axis=0)
        one = jnp.concatenate([one, jnp.zeros((2 * positions, LANES - kslots), F32)], axis=1)
        return (jnp.broadcast_to(one, (holders,) + one.shape),)

    (packed,) = on_core(
        pack,
        [],
        [shape(holders, 2 * positions, LANES)],
        streams=[active_ids, active_vals],
        room=60,
    )
    lists = lax.all_to_all(packed, ("feat", "pos"), split_axis=0, concat_axis=0, tiled=True)

    def list_of(values, prompt):
        blocks = []
        for a in range(feats):
            block = values[a * poses]
            for q in range(1, poses):
                block = jnp.where(prompt == q, values[a * poses + q], block)
            blocks.append(block)
        return jnp.concatenate(blocks, axis=0)[:, :kslots]

    def list_row(slot):
        place = floor_div(slot, kslots)
        return place + floor_div(place, positions) * positions

    def slot_entry(slot):
        return slot - floor_div(slot, kslots) * kslots

    def pieces(table):
        high = part(table, small)
        rest = table - high.astype(F32)
        middle = part(rest, small)
        return [high, middle, part(rest - middle.astype(F32), small)]

    def as_rows(table, slot_at, lanes):
        entry = slot_entry(slot_at(iota((kslots, lanes), 1)))
        spread = (iota((kslots, lanes), 0) == entry).astype(BF16)
        every = dot(jnp.concatenate(pieces(table), axis=0), spread)
        count = table.shape[0]
        every = every[:count] + (every[count : 2 * count] + every[2 * count :])
        row = iota(every.shape, 0) - list_row(slot_at(iota(every.shape, 1)))
        ids = jnp.sum(jnp.where(row == 0, every, 0.0), axis=0, keepdims=True)
        return ids, jnp.sum(jnp.where(row == positions, every, 0.0), axis=0, keepdims=True)

    def spread_slot(lane):
        block = floor_div(lane, span)
        inside = lane - block * span
        return jnp.where(inside < block_rows, block * block_rows + inside, -1.0 * slots)

    def as_col(table):
        wide = (slots, table.shape[0])
        spread = (list_row(iota(wide, 0)) == iota(wide, 1)).astype(BF16)
        every = dot(spread, jnp.concatenate(pieces(table), axis=1))
        every = every[:, :kslots] + (every[:, kslots : 2 * kslots] + every[:, 2 * kslots :])
        mine = slot_entry(iota((slots, kslots), 0)) == iota((slots, kslots), 1)
        return jnp.sum(jnp.where(mine, every, 0.0), axis=1, keepdims=True)

    def choose(values):
        feat, pos, _ = place()
        own = feat * poses + pos
        tables = []
        rows = []
        for k in range(poses):
            prompt = jnp.where(pos + k >= poses, pos + k - poses, pos + k)
            tables.append(list_of(values, prompt))
            rows.append(as_rows(tables[k], lambda lane: lane, slots)[0])
        hits = [floor_div(ids, table_rows) == own for ids in rows]
        earlier = (iota((slots, slots), 0) < iota((slots, slots), 1)).astype(BF16)
        ranks = dot(jnp.concatenate([h.astype(BF16) for h in hits], axis=0), earlier)
        picks = []
        for k in range(poses):
            chosen = jnp.where(
                hits[k] & (ranks[k : k + 1] == iota((listed, slots), 0)), 1.0, 0.0
            )
            local = jnp.sum(chosen * (rows[k] - own * table_rows + 1.0), axis=1, keepdims=True)
            picks.append((local - 1.0 == iota((listed, table_rows), 1)).astype(BF16))
        return jnp.concatenate(picks, axis=0), tables[0]

    picks, my_list = on_core(
        choose,
        [lists],
        [shape(column, table_rows, dtype=BF16), shape(2 * positions * feats, kslots)],
        small,
        cost=(10**9, 10**7),
    )

    def encode(picks, enc):
        rows = dot(picks, enc).astype(BF16)
        return [rows[k * listed : (k + 1) * listed] for k in range(poses)] + [picks]

    *enc_rows, picks = on_core(
        encode,
        [picks, encoder],
        [shape(listed, width, dtype=BF16)] * poses + [shape(column, table_rows, dtype=BF16)],
        small,
    )

    ring = [[enc_rows[0]] + [rotate(enc_rows[k], "pos", k) for k in range(1, poses)]]
    ring.append([ring_next(enc_rows[k], "feat", "pos", k) for k in range(poses)])

    dec_rows = lax.dot_general(
        picks, decoder, (((1,), (0,)), ((), ())), preferred_element_type=F32
    )
    dec_rows = jnp.transpose(dec_rows, (1, 0, 2)).astype(BF16)
    dec_rows = [
        [dec_rows[l, k * listed : (k + 1) * listed] for l in range(depth)] for k in range(poses)
    ]
    away = [rows for k in range(1, poses) for rows in dec_rows[k]]
    order = [(0, 0)] + [(k, q) for k in range(1, feats - 1) for q in range(poses)]
    soon = len(order)
    order += [(0, q) for q in range(1, poses)] + [(feats - 1, q) for q in range(poses)]
    own_lists = [order.index((0, q)) for q in range(poses)]

    def places(table, pattern):
        feat, pos, rep = place()

        def padded(owner, rank):
            feat_of = floor_div(owner, poses)
            step = ring_place(feat, feats) - ring_place(feat_of, feats)
            step = jnp.where(step < 0.0, step + feats, step)
            turn = pos - (owner - feat_of * poses)
            turn = jnp.where(turn < 0.0, turn + poses, turn)
            at = step * poses + turn
            at = jnp.where(step < feats - 1.0, at - (poses - 1), at)
            at = jnp.where(step == 0.0, turn + (feats - 2) * poses, at)
            at = jnp.where((step == 0.0) & (turn == 0.0), 0.0, at)
            return at * listed + rank

        ids_row, vals_row = as_rows(table, spread_slot, wide)
        ids_col = as_col(table)
        owner_row = floor_div(ids_row, table_rows)
        owner_col = floor_div(ids_col, table_rows)
        down, across = iota((slots, slots), 0), iota((slots, slots), 1)
        same = owner_col == floor_div(as_rows(table, lambda lane: lane, slots)[0], table_rows)
        rank_col = jnp.sum(jnp.where(same & (across < down), 1.0, 0.0), axis=1, keepdims=True)
        slot = spread_slot(iota((slots, wide), 1))
        same = (owner_col == owner_row) & (iota((slots, wide), 0) < slot)
        rank_row = jnp.sum(jnp.where(same, 1.0, 0.0), axis=0, keepdims=True)
        total = holders * listed
        used = spread_slot(iota((1, wide), 1)) >= 0.0
        place_row = jnp.where(used, padded(owner_row, rank_row), -1.0)
        placing = padded(owner_col, rank_col) == iota((slots, total), 1)
        placing_t = place_row == iota((total, wide), 0)
        layer = ids_col - floor_div(ids_col, layers) * layers
        layer_row = jnp.sum(jnp.where(placing, layer, 0.0), axis=0, keepdims=True)
        mine = [placing_t[at * listed : (at + 1) * listed] for at in own_lists]
        mine = jnp.concatenate(mine, axis=0)
        gain = jnp.sum(jnp.where(mine, vals_row, 0.0), axis=1, keepdims=True)
        source_layer = ids_row - floor_div(ids_row, layers) * layers
        source_layer = jnp.sum(jnp.where(mine, source_layer, 0.0), axis=1, keepdims=True)
        gains = jnp.concatenate(
            [jnp.where(source_layer <= l, gain, 0.0) for l in range(depth)], axis=0
        )
        allowed = jnp.where(pattern[0] == 1, 1.0, 0.0).astype(BF16)

        def in_block(slot, dim, extent):
            wide = (extent, feats) if dim == 0 else (feats, extent)
            return (floor_div(slot, block_rows) == iota(wide, 1 - dim)).astype(BF16)

        sources = (floor_div(iota((wide, 1), 0), span) == iota((wide, feats), 1)).astype(BF16)
        targets = (floor_div(iota((1, wide), 1), span) == iota((feats, wide), 0)).astype(BF16)
        mask = dot(dot(sources, allowed, NT).astype(BF16), targets)
        source = floor_div(spread_slot(iota((wide, wide), 0)), kslots)
        target = floor_div(spread_slot(iota((wide, wide), 1)), kslots)
        mask = jnp.where(source <= target, mask, 0.0)
        first = (feat * reps + rep) * result_rows
        own_slot = first + iota((result_rows, 1), 0)
        own_mask = dot(in_block(own_slot, 0, result_rows), allowed).astype(BF16)
        own_mask = dot(own_mask, in_block(iota((1, slots), 1), 1, slots))
        own_causal = floor_div(iota((result_rows, slots), 1), kslots) <= floor_div(
            first + iota((result_rows, slots), 0), kslots
        )
        own_mask = jnp.where(own_causal, own_mask, 0.0)
        placing, placing_t = placing.astype(BF16), placing_t.astype(BF16)
        return placing, placing_t, layer_row, gains, mask.astype(BF16), own_mask

    placing, placing_t, layer_row, gains, mask, own_mask, *away = on_core(
        places,
        [my_list, block_pattern],
        [
            shape(slots, holders * listed, dtype=BF16),
            shape(holders * listed, wide, dtype=BF16),
            shape(1, holders * listed),
            shape(depth * column, 1),
            shape(wide, wide, dtype=BF16),
            shape(result_rows, slots),
        ],
        small,
        through=away,
        cost=(1, 1),
    )
    *away, ring[1][0], ring[1][-1] = lax.optimization_barrier((*away, ring[1][0], ring[1][-1]))
    for k in range(1, poses):
        rows = away[(k - 1) * depth : k * depth]
        dec_rows[k] = [rotate(row, "pos", k) for row in rows]
    dec_rows = [dec_rows[k][l] for l in range(depth) for k in range(poses)]

    for _ in range(2, feats):
        ring.append([ring_next(rows, "feat") for rows in ring[-1]])

    def products(first, enc, dec, layer_row, placing_t):
        enc = jnp.concatenate(enc, axis=0)
        every = dot(dec, enc, NT)
        lanes = slice(first * listed, first * listed + enc.shape[0])
        raw = jnp.zeros((column, enc.shape[0]), F32)
        for l in range(depth):
            rows = every[l * column : (l + 1) * column]
            raw = raw + jnp.where(layer_row[:, lanes] == l + 1.0, rows, 0.0)
        split = dot(jnp.concatenate(pieces(raw), axis=0), placing_t[lanes])
        return split[:column] + (split[column : 2 * column] + split[2 * column :])

    def early(layer_row, placing_t, gains, *values):
        dec = jnp.concatenate(values[: depth * poses], axis=0)
        dec = (dec.astype(F32) * gains).astype(BF16)
        return products(0, values[depth * poses :], dec, layer_row, placing_t), dec

    def late(layer_row, placing_t, so_far, dec, *values):
        raw = so_far + products(soon, values, dec, layer_row, placing_t)
        first = place()[2] == 0.0
        lower, higher = pack_rests(raw[:half]), pack_rests(raw[half:])
        return jnp.where(first, lower, higher), jnp.where(first, higher, lower)

    so_far, scaled = on_core(
        early,
        [layer_row, placing_t, gains] + dec_rows + [ring[k][q] for k, q in order[:soon]],
        [shape(column, wide), shape(depth * column, width, dtype=BF16)],
        small,
        cost=(1, 1),
    )
    keep, send = on_core(
        late,
        [layer_row, placing_t, so_far, scaled] + [ring[k][q] for k, q in order[soon:]],
        [shape(len(bins) * GROUP, wide)] * 2,
        small,
    )
    own_edges = (keep + rotate(send, "rep", 1)).astype(BF16)
    shards = ring_spread(own_edges, "feat")
    others = [rotate(shard, "rep", 1) for shard in shards]

    def finish(placing, mask, own_mask, targets, *values):
        feat, _, rep = place()
        first = rep == 0.0
        chips = []
        for mine, other in zip(values[:feats], values[feats:]):
            lower, higher = jnp.where(first, mine, other), jnp.where(first, other, mine)
            chips.append(jnp.concatenate([unpack_rests(lower), unpack_rests(higher)], axis=0))
        padded = [chips[k][q * listed : (q + 1) * listed] for k, q in order]
        padded = jnp.concatenate(padded, axis=0)
        unused = [jnp.zeros((span - block_rows, holders * listed), BF16)]
        unused = unused if span > block_rows else []
        sources = []
        for f in range(feats):
            sources += [placing[f * block_rows : (f + 1) * block_rows]] + unused
        sources = jnp.concatenate(sources, axis=0)
        magnitude = jnp.abs(dot(sources, padded) * mask.astype(F32))
        total = jnp.maximum(jnp.sum(magnitude, axis=0, keepdims=True), 1.0)
        magnitude = magnitude.astype(BF16)
        diagonal = iota((wide, wide), 0) == iota((wide, wide), 1)
        scale = 1.0 / jnp.sum(jnp.where(diagonal, total, 0.0), axis=1, keepdims=True)
        targets = targets.astype(F32)
        targets = targets + floor_div(targets, block_rows) * (span - block_rows)
        current = (iota((wide, panel), 0) == targets).astype(F32)
        accum = jnp.zeros((wide, panel), F32)
        for _ in range(ITERS):
            scaled = current * scale
            high = part(scaled, small)
            low = part(scaled - high.astype(F32), small)
            both = dot(magnitude, jnp.concatenate([high, low], axis=1))
            current = both[:, :panel] + both[:, panel:]
            accum = accum + current
        influence = accum[:result_rows]
        for f in range(feats):
            for r in range(reps):
                at = f * span + r * result_rows
                mine = (feat == f) & (rep == r)
                influence = jnp.where(mine, accum[at : at + result_rows], influence)
        start = feat * span + rep * result_rows
        own = start + iota((result_rows, wide), 0) == iota((result_rows, wide), 1)
        rows = dot(own.astype(BF16), padded, NT).astype(BF16)
        edges = (dot(rows, placing, NT) * own_mask).astype(BF16)
        return edges[None], (influence * float(slots))[None]

    edges, influence = on_core(
        finish,
        [placing, mask, own_mask, target_slots] + shards + others,
        [shape(1, result_rows, slots, dtype=BF16), shape(1, result_rows, panel)],
        small,
    )
    return edges, influence


def solution(mesh):
    return jax.shard_map(
        per_device,
        mesh=mesh,
        in_specs=(
            P(("grp", "pos"), "feat", None),
            P(("grp", "pos"), "feat", None),
            P(("grp", "pos"), None, None),
            P(("grp", "pos"), None),
            P(("feat", "pos"), "rep"),
            P(("feat", "pos"), None, "rep"),
        ),
        out_specs=(
            P(("grp", "pos"), ("feat", "rep"), None),
            P(("grp", "pos"), ("feat", "rep"), None),
        ),
        check_vma=False,
    )
```

```python
import jax
import jax.numpy as jnp
from jax import lax
from jax.experimental import pallas as pl
from jax.experimental.pallas import tpu as pltpu
from jax.sharding import PartitionSpec as P

ITERS = 3
F32 = jnp.float32
BF16 = jnp.bfloat16
NN = (((1,), (0,)), ((), ()))
NT = (((1,), (1,)), ((), ()))
LANES = 128
GROUP = 8
KERNEL_SLOTS = 1024


def dot(a, b, dims=NN):
    return lax.dot_general(a, b, dims, preferred_element_type=F32)


def iota(shape, dim):
    return lax.broadcasted_iota(jnp.int32, shape, dim).astype(F32)


def floor_div(x, n):
    return jnp.floor((x + 0.5) * (1.0 / n))


def on_core(fn, args, outs, kernel=True, through=(), streams=(), cost=None, room=24):
    if not kernel:
        loads = [lambda i, x=x: x[i] for x in streams]
        return list(fn(*args, *loads)) + list(through)
    count, passed, streamed = len(args), len(through), len(streams)

    def body(*refs):
        sources = refs[count : count + streamed]
        results = refs[count + streamed + passed :][: len(outs)]
        scratch = refs[len(refs) - 2 * streamed :]
        copies = []
        for n in range(streamed):
            copies.append(
                [
                    pltpu.make_async_copy(
                        sources[n].at[i], scratch[2 * n].at[i], scratch[2 * n + 1].at[i]
                    )
                    for i in range(streams[n].shape[0])
                ]
            )
            for copy in copies[-1]:
                copy.start()

        def load(n):
            def wait(i):
                copies[n][i].wait()
                return scratch[2 * n][i]

            return wait

        values = fn(*[ref[...] for ref in refs[:count]], *[load(n) for n in range(streamed)])
        for ref, value in zip(results, values):
            ref[...] = value

    estimate = None
    if cost is not None:
        estimate = pl.CostEstimate(flops=cost[0], bytes_accessed=cost[1], transcendentals=0)
    in_vmem = pl.BlockSpec(memory_space=pltpu.VMEM)
    anywhere = pl.BlockSpec(memory_space=pl.ANY)
    scratch = []
    for x in streams:
        scratch += [pltpu.VMEM(x.shape, x.dtype), pltpu.SemaphoreType.DMA((x.shape[0],))]
    call = pl.pallas_call(
        body,
        out_shape=list(outs) + [jax.ShapeDtypeStruct(x.shape, x.dtype) for x in through],
        in_specs=[in_vmem] * count
        + [pl.BlockSpec(memory_space=pltpu.HBM)] * streamed
        + [anywhere] * passed,
        out_specs=[in_vmem] * len(outs) + [anywhere] * passed,
        scratch_shapes=scratch,
        input_output_aliases={count + streamed + i: len(outs) + i for i in range(passed)},
        compiler_params=pltpu.CompilerParams(vmem_limit_bytes=room * 1024 * 1024),
        cost_estimate=estimate,
    )
    return list(call(*args, *streams, *through))


def rotate(x, axis, step):
    count = lax.axis_size(axis)
    return lax.ppermute(x, axis, [(i, (i + step) % count) for i in range(count)])


def ring_place(index, count):
    low = floor_div(index, 2)
    return jnp.where(index > 2 * low, count - 1 - low, low)


def ring_next(x, axis, across=None, turn=0):
    count = lax.axis_size(axis)
    order = list(range(0, count, 2)) + list(range(1, count, 2))[::-1]
    steps = [(order[i], order[(i + 1) % count]) for i in range(count)]
    if across is None:
        return lax.ppermute(x, axis, steps)
    wide = lax.axis_size(across)
    pairs = [(a * wide + i, b * wide + (i + turn) % wide) for a, b in steps for i in range(wide)]
    return lax.ppermute(x, (axis, across), pairs)


def spread(x, axis):
    count = lax.axis_size(axis)
    return [x] + [
        lax.ppermute(x, axis, [(i, i ^ bits) for i in range(count)]) for bits in range(1, count)
    ]


def part(x, kernel):
    return x.astype(BF16) if kernel else lax.reduce_precision(x, 8, 7).astype(BF16)


def shape(*dims, dtype=F32):
    return jax.ShapeDtypeStruct(dims, dtype)


def per_device(active_ids, active_vals, block_pattern, target_slots, encoder, decoder):
    feats = lax.axis_size("feat")
    poses = lax.axis_size("pos")
    reps = lax.axis_size("rep")
    holders = feats * poses
    table_rows, width = encoder.shape
    depth = decoder.shape[1]
    layers = depth + 1
    positions, kslots = active_ids.shape[1:]
    block_rows = positions * kslots
    slots = block_rows * feats
    capacity = max(2, (10 * block_rows + 7 * holders - 1) // (7 * holders))
    listed = capacity * feats
    column = poses * listed
    half = column // reps
    result_rows = block_rows // reps
    panel = target_slots.shape[1]
    small = slots <= KERNEL_SLOTS
    span = -(-block_rows // LANES) * LANES if small else block_rows
    wide = feats * span

    rests = []
    for row in range(0, half, GROUP):
        rests.append((row, row % listed // capacity))
    bins = []
    for rest in sorted(rests, key=lambda rest: rest[1]):
        for row in bins:
            if sum(feats - block for _, block in row) + feats - rest[1] <= feats:
                row.append(rest)
                break
        else:
            bins.append([rest])

    def pack_rests(x):
        rows = []
        for row in bins:
            parts = [x[at : at + GROUP, block * span :] for at, block in row]
            empty = wide - sum(part.shape[1] for part in parts)
            parts += [jnp.zeros((GROUP, empty), x.dtype)] if empty else []
            rows.append(jnp.concatenate(parts, axis=1) if len(parts) > 1 else parts[0])
        return jnp.concatenate(rows, axis=0)

    def unpack_rests(x):
        x = x.astype(F32) if small else x
        found = {}
        for n, row in enumerate(bins):
            lane = 0
            for at, block in row:
                rest = x[n * GROUP : (n + 1) * GROUP, lane : lane + wide - block * span]
                lane += wide - block * span
                if block:
                    rest = jnp.concatenate([jnp.zeros((GROUP, block * span), x.dtype), rest], axis=1)
                found[at] = rest
        return jnp.concatenate([found[at] for at, _ in rests], axis=0).astype(BF16)

    def place():
        feat, pos = lax.axis_index("feat"), lax.axis_index("pos")
        return feat.astype(F32), pos.astype(F32), lax.axis_index("rep").astype(F32)

    def pack(ids, vals):
        one = jnp.concatenate([ids(0).astype(F32), vals(0)], axis=0)
        one = jnp.concatenate([one, jnp.zeros((2 * positions, LANES - kslots), F32)], axis=1)
        return (jnp.broadcast_to(one, (holders,) + one.shape),)

    (packed,) = on_core(
        pack,
        [],
        [shape(holders, 2 * positions, LANES)],
        streams=[active_ids, active_vals],
        room=60,
    )
    lists = lax.all_to_all(packed, ("feat", "pos"), split_axis=0, concat_axis=0, tiled=True)

    def list_of(values, prompt):
        blocks = []
        for a in range(feats):
            block = values[a * poses]
            for q in range(1, poses):
                block = jnp.where(prompt == q, values[a * poses + q], block)
            blocks.append(block)
        return jnp.concatenate(blocks, axis=0)[:, :kslots]

    def list_row(slot):
        place = floor_div(slot, kslots)
        return place + floor_div(place, positions) * positions

    def slot_entry(slot):
        return slot - floor_div(slot, kslots) * kslots

    def pieces(table):
        high = part(table, small)
        rest = table - high.astype(F32)
        middle = part(rest, small)
        return [high, middle, part(rest - middle.astype(F32), small)]

    def as_rows(table, slot_at, lanes):
        entry = slot_entry(slot_at(iota((kslots, lanes), 1)))
        spread = (iota((kslots, lanes), 0) == entry).astype(BF16)
        every = dot(jnp.concatenate(pieces(table), axis=0), spread)
        count = table.shape[0]
        every = every[:count] + (every[count : 2 * count] + every[2 * count :])
        row = iota(every.shape, 0) - list_row(slot_at(iota(every.shape, 1)))
        ids = jnp.sum(jnp.where(row == 0, every, 0.0), axis=0, keepdims=True)
        return ids, jnp.sum(jnp.where(row == positions, every, 0.0), axis=0, keepdims=True)

    def spread_slot(lane):
        block = floor_div(lane, span)
        inside = lane - block * span
        return jnp.where(inside < block_rows, block * block_rows + inside, -1.0 * slots)

    def as_col(table):
        wide = (slots, table.shape[0])
        spread = (list_row(iota(wide, 0)) == iota(wide, 1)).astype(BF16)
        every = dot(spread, jnp.concatenate(pieces(table), axis=1))
        every = every[:, :kslots] + (every[:, kslots : 2 * kslots] + every[:, 2 * kslots :])
        mine = slot_entry(iota((slots, kslots), 0)) == iota((slots, kslots), 1)
        return jnp.sum(jnp.where(mine, every, 0.0), axis=1, keepdims=True)

    def choose(values):
        feat, pos, _ = place()
        own = feat * poses + pos
        tables = []
        rows = []
        for k in range(poses):
            prompt = jnp.where(pos + k >= poses, pos + k - poses, pos + k)
            tables.append(list_of(values, prompt))
            rows.append(as_rows(tables[k], lambda lane: lane, slots)[0])
        hits = [floor_div(ids, table_rows) == own for ids in rows]
        earlier = (iota((slots, slots), 0) < iota((slots, slots), 1)).astype(BF16)
        ranks = dot(jnp.concatenate([h.astype(BF16) for h in hits], axis=0), earlier)
        picks = []
        for k in range(poses):
            chosen = jnp.where(
                hits[k] & (ranks[k : k + 1] == iota((listed, slots), 0)), 1.0, 0.0
            )
            local = jnp.sum(chosen * (rows[k] - own * table_rows + 1.0), axis=1, keepdims=True)
            picks.append((local - 1.0 == iota((listed, table_rows), 1)).astype(BF16))
        return jnp.concatenate(picks, axis=0), tables[0]

    picks, my_list = on_core(
        choose,
        [lists],
        [shape(column, table_rows, dtype=BF16), shape(2 * positions * feats, kslots)],
        small,
        cost=(10**9, 10**7),
    )

    def encode(picks, enc):
        rows = dot(picks, enc).astype(BF16)
        return [rows[k * listed : (k + 1) * listed] for k in range(poses)] + [picks]

    *enc_rows, picks = on_core(
        encode,
        [picks, encoder],
        [shape(listed, width, dtype=BF16)] * poses + [shape(column, table_rows, dtype=BF16)],
        small,
    )

    ring = [[enc_rows[0]] + [rotate(enc_rows[k], "pos", k) for k in range(1, poses)]]
    ring.append([ring_next(enc_rows[k], "feat", "pos", k) for k in range(poses)])

    dec_rows = lax.dot_general(
        picks, decoder, (((1,), (0,)), ((), ())), preferred_element_type=F32
    )
    dec_rows = jnp.transpose(dec_rows, (1, 0, 2)).astype(BF16)
    dec_rows = [dec_rows[:, k * listed : (k + 1) * listed] for k in range(poses)]
    order = [(0, 0)] + [(k, q) for k in range(1, feats - 1) for q in range(poses)]
    soon = len(order)
    order += [(0, q) for q in range(1, poses)] + [(feats - 1, q) for q in range(poses)]
    own_lists = [order.index((0, q)) for q in range(poses)]

    def places(table, pattern):
        feat, pos, rep = place()

        def turned(owner):
            turn = pos - (owner - floor_div(owner, poses) * poses)
            return jnp.where(turn < 0.0, turn + poses, turn)

        def spread_place(owner, rank):
            feat_of = floor_div(owner, poses).astype(jnp.int32)
            bits = (feat.astype(jnp.int32) ^ feat_of).astype(F32)
            return (bits * poses + turned(owner)) * listed + rank

        def padded(owner, rank):
            feat_of = floor_div(owner, poses)
            turn = turned(owner)
            step = ring_place(feat, feats) - ring_place(feat_of, feats)
            step = jnp.where(step < 0.0, step + feats, step)
            at = step * poses + turn
            at = jnp.where(step < feats - 1.0, at - (poses - 1), at)
            at = jnp.where(step == 0.0, turn + (feats - 2) * poses, at)
            at = jnp.where((step == 0.0) & (turn == 0.0), 0.0, at)
            return at * listed + rank

        ids_row, vals_row = as_rows(table, spread_slot, wide)
        ids_col = as_col(table)
        owner_row = floor_div(ids_row, table_rows)
        owner_col = floor_div(ids_col, table_rows)
        down, across = iota((slots, slots), 0), iota((slots, slots), 1)
        same = owner_col == floor_div(as_rows(table, lambda lane: lane, slots)[0], table_rows)
        rank_col = jnp.sum(jnp.where(same & (across < down), 1.0, 0.0), axis=1, keepdims=True)
        slot = spread_slot(iota((slots, wide), 1))
        same = (owner_col == owner_row) & (iota((slots, wide), 0) < slot)
        rank_row = jnp.sum(jnp.where(same, 1.0, 0.0), axis=0, keepdims=True)
        total = holders * listed
        used = spread_slot(iota((1, wide), 1)) >= 0.0
        place_row = jnp.where(used, padded(owner_row, rank_row), -1.0)
        placing = spread_place(owner_col, rank_col) == iota((slots, total), 1)
        entry = padded(owner_col, rank_col) == iota((slots, total), 1)
        placing_t = place_row == iota((total, wide), 0)
        layer = ids_col - floor_div(ids_col, layers) * layers
        layer_row = jnp.sum(jnp.where(entry, layer, 0.0), axis=0, keepdims=True)
        mine = [placing_t[at * listed : (at + 1) * listed] for at in own_lists]
        mine = jnp.concatenate(mine, axis=0)
        gain = jnp.sum(jnp.where(mine, vals_row, 0.0), axis=1, keepdims=True)
        source_layer = ids_row - floor_div(ids_row, layers) * layers
        source_layer = jnp.sum(jnp.where(mine, source_layer, 0.0), axis=1, keepdims=True)
        gains = jnp.concatenate(
            [jnp.where(source_layer <= l, gain, 0.0) for l in range(depth)], axis=0
        )
        allowed = jnp.where(pattern[0] == 1, 1.0, 0.0).astype(BF16)

        sources = (floor_div(iota((wide, 1), 0), span) == iota((wide, feats), 1)).astype(BF16)
        targets = (floor_div(iota((1, wide), 1), span) == iota((feats, wide), 0)).astype(BF16)
        mask = dot(dot(sources, allowed, NT).astype(BF16), targets)
        source = floor_div(spread_slot(iota((wide, wide), 0)), kslots)
        target = floor_div(spread_slot(iota((wide, wide), 1)), kslots)
        mask = jnp.where(source <= target, mask, 0.0)
        squeeze = spread_slot(iota((wide, slots), 0)) == iota((wide, slots), 1)
        placing, placing_t = placing.astype(BF16), placing_t.astype(BF16)
        return placing, placing_t, layer_row, gains, mask.astype(BF16), squeeze.astype(BF16)

    placing, placing_t, layer_row, gains, mask, squeeze, *dec_rows[1:] = on_core(
        places,
        [my_list, block_pattern],
        [
            shape(slots, holders * listed, dtype=BF16),
            shape(holders * listed, wide, dtype=BF16),
            shape(1, holders * listed),
            shape(depth * column, 1),
            shape(wide, wide, dtype=BF16),
            shape(wide, slots, dtype=BF16),
        ],
        small,
        through=dec_rows[1:],
        cost=(1, 1),
    )
    *dec_rows, ring[1][0], ring[1][-1] = lax.optimization_barrier(
        (*dec_rows, ring[1][0], ring[1][-1])
    )
    dec_rows = [dec_rows[0]] + [rotate(dec_rows[k], "pos", k) for k in range(1, poses)]

    for _ in range(2, feats):
        ring.append([ring_next(rows, "feat") for rows in ring[-1]])

    def products(first, enc, dec, layer_row, placing_t):
        enc = jnp.concatenate(enc, axis=0)
        every = dot(dec, enc, NT)
        lanes = slice(first * listed, first * listed + enc.shape[0])
        raw = jnp.zeros((column, enc.shape[0]), F32)
        for l in range(depth):
            rows = every[l * column : (l + 1) * column]
            raw = raw + jnp.where(layer_row[:, lanes] == l + 1.0, rows, 0.0)
        split = dot(jnp.concatenate(pieces(raw), axis=0), placing_t[lanes])
        return split[:column] + (split[column : 2 * column] + split[2 * column :])

    def early(layer_row, placing_t, gains, *values):
        dec = jnp.concatenate([d[l] for l in range(depth) for d in values[:poses]], axis=0)
        dec = (dec.astype(F32) * gains).astype(BF16)
        return products(0, values[poses:], dec, layer_row, placing_t), dec

    def late(layer_row, placing_t, so_far, dec, *values):
        raw = so_far + products(soon, values, dec, layer_row, placing_t)
        first = place()[2] == 0.0
        lower, higher = pack_rests(raw[:half]), pack_rests(raw[half:])
        return jnp.where(first, lower, higher), jnp.where(first, higher, lower)

    so_far, scaled = on_core(
        early,
        [layer_row, placing_t, gains] + dec_rows + [ring[k][q] for k, q in order[:soon]],
        [shape(column, wide), shape(depth * column, width, dtype=BF16)],
        small,
        cost=(1, 1),
    )
    keep, send = on_core(
        late,
        [layer_row, placing_t, so_far, scaled] + [ring[k][q] for k, q in order[soon:]],
        [shape(len(bins) * GROUP, wide)] * 2,
        small,
    )
    own_edges = (keep + rotate(send, "rep", 1)).astype(BF16)
    shards = spread(own_edges, "feat")
    others = [rotate(shard, "rep", 1) for shard in shards]

    def finish(placing, mask, squeeze, targets, *values):
        feat, _, rep = place()
        first = rep == 0.0
        chips = []
        for mine, other in zip(values[:feats], values[feats:]):
            lower, higher = jnp.where(first, mine, other), jnp.where(first, other, mine)
            chips.append(jnp.concatenate([unpack_rests(lower), unpack_rests(higher)], axis=0))
        padded = jnp.concatenate(chips, axis=0)
        unused = [jnp.zeros((span - block_rows, holders * listed), BF16)]
        unused = unused if span > block_rows else []
        sources = []
        for f in range(feats):
            sources += [placing[f * block_rows : (f + 1) * block_rows]] + unused
        sources = jnp.concatenate(sources, axis=0)
        edges = dot(sources, padded) * mask.astype(F32)
        magnitude = jnp.abs(edges)
        total = jnp.maximum(jnp.sum(magnitude, axis=0, keepdims=True), 1.0)
        magnitude = magnitude.astype(BF16)
        diagonal = iota((wide, wide), 0) == iota((wide, wide), 1)
        scale = 1.0 / jnp.sum(jnp.where(diagonal, total, 0.0), axis=1, keepdims=True)
        targets = targets.astype(F32)
        targets = targets + floor_div(targets, block_rows) * (span - block_rows)
        current = (iota((wide, panel), 0) == targets).astype(F32)
        accum = jnp.zeros((wide, panel), F32)
        for _ in range(ITERS):
            scaled = current * scale
            high = part(scaled, small)
            low = part(scaled - high.astype(F32), small)
            both = dot(magnitude, jnp.concatenate([high, low], axis=1))
            current = both[:, :panel] + both[:, panel:]
            accum = accum + current
        influence = accum[:result_rows]
        for f in range(feats):
            for r in range(reps):
                at = f * span + r * result_rows
                mine = (feat == f) & (rep == r)
                influence = jnp.where(mine, accum[at : at + result_rows], influence)
        start = feat * span + rep * result_rows
        own = start + iota((result_rows, wide), 0) == iota((result_rows, wide), 1)
        rows = dot(own.astype(BF16), edges.astype(BF16), NT).astype(BF16)
        edges = dot(rows, squeeze).astype(BF16)
        return edges[None], (influence * float(slots))[None]

    edges, influence = on_core(
        finish,
        [placing, mask, squeeze, target_slots] + shards + others,
        [shape(1, result_rows, slots, dtype=BF16), shape(1, result_rows, panel)],
        small,
    )
    return edges, influence


def solution(mesh):
    return jax.shard_map(
        per_device,
        mesh=mesh,
        in_specs=(
            P(("grp", "pos"), "feat", None),
            P(("grp", "pos"), "feat", None),
            P(("grp", "pos"), None, None),
            P(("grp", "pos"), None),
            P(("feat", "pos"), "rep"),
            P(("feat", "pos"), None, "rep"),
        ),
        out_specs=(
            P(("grp", "pos"), ("feat", "rep"), None),
            P(("grp", "pos"), ("feat", "rep"), None),
        ),
        check_vma=False,
    )
```

```python
import jax
import jax.numpy as jnp
from jax import lax
from jax.experimental import pallas as pl
from jax.experimental.pallas import tpu as pltpu
from jax.sharding import PartitionSpec as P

ITERS = 3
F32 = jnp.float32
BF16 = jnp.bfloat16
NN = (((1,), (0,)), ((), ()))
NT = (((1,), (1,)), ((), ()))
LANES = 128
GROUP = 8
KERNEL_SLOTS = 1024


def dot(a, b, dims=NN):
    return lax.dot_general(a, b, dims, preferred_element_type=F32)


def iota(shape, dim):
    return lax.broadcasted_iota(jnp.int32, shape, dim).astype(F32)


def floor_div(x, n):
    return jnp.floor((x + 0.5) * (1.0 / n))


def on_core(fn, args, outs, kernel=True, through=(), streams=(), cost=None, room=24):
    if not kernel:
        loads = [lambda i, x=x: x[i] for x in streams]
        return list(fn(*args, *loads)) + list(through)
    count, passed, streamed = len(args), len(through), len(streams)

    def body(*refs):
        sources = refs[count : count + streamed]
        results = refs[count + streamed + passed :][: len(outs)]
        scratch = refs[len(refs) - 2 * streamed :]
        copies = []
        for n in range(streamed):
            copies.append(
                [
                    pltpu.make_async_copy(
                        sources[n].at[i], scratch[2 * n].at[i], scratch[2 * n + 1].at[i]
                    )
                    for i in range(streams[n].shape[0])
                ]
            )
            for copy in copies[-1]:
                copy.start()

        def load(n):
            def wait(i):
                copies[n][i].wait()
                return scratch[2 * n][i]

            return wait

        values = fn(*[ref[...] for ref in refs[:count]], *[load(n) for n in range(streamed)])
        for ref, value in zip(results, values):
            ref[...] = value

    estimate = None
    if cost is not None:
        estimate = pl.CostEstimate(flops=cost[0], bytes_accessed=cost[1], transcendentals=0)
    in_vmem = pl.BlockSpec(memory_space=pltpu.VMEM)
    anywhere = pl.BlockSpec(memory_space=pl.ANY)
    scratch = []
    for x in streams:
        scratch += [pltpu.VMEM(x.shape, x.dtype), pltpu.SemaphoreType.DMA((x.shape[0],))]
    call = pl.pallas_call(
        body,
        out_shape=list(outs) + [jax.ShapeDtypeStruct(x.shape, x.dtype) for x in through],
        in_specs=[in_vmem] * count
        + [pl.BlockSpec(memory_space=pltpu.HBM)] * streamed
        + [anywhere] * passed,
        out_specs=[in_vmem] * len(outs) + [anywhere] * passed,
        scratch_shapes=scratch,
        input_output_aliases={count + streamed + i: len(outs) + i for i in range(passed)},
        compiler_params=pltpu.CompilerParams(vmem_limit_bytes=room * 1024 * 1024),
        cost_estimate=estimate,
    )
    return list(call(*args, *streams, *through))


def rotate(x, axis, step):
    count = lax.axis_size(axis)
    return lax.ppermute(x, axis, [(i, (i + step) % count) for i in range(count)])


def ring_place(index, count):
    low = floor_div(index, 2)
    return jnp.where(index > 2 * low, count - 1 - low, low)


def ring_next(x, axis, across=None, turn=0):
    count = lax.axis_size(axis)
    order = list(range(0, count, 2)) + list(range(1, count, 2))[::-1]
    steps = [(order[i], order[(i + 1) % count]) for i in range(count)]
    if across is None:
        return lax.ppermute(x, axis, steps)
    wide = lax.axis_size(across)
    pairs = [(a * wide + i, b * wide + (i + turn) % wide) for a, b in steps for i in range(wide)]
    return lax.ppermute(x, (axis, across), pairs)


def spread(x, axis):
    count = lax.axis_size(axis)
    found = {0: x}
    for bits in sorted(range(1, count), key=lambda bits: bits < count // 2):
        found[bits] = lax.ppermute(x, axis, [(i, i ^ bits) for i in range(count)])
    return list(found.items())


def part(x, kernel):
    return x.astype(BF16) if kernel else lax.reduce_precision(x, 8, 7).astype(BF16)


def shape(*dims, dtype=F32):
    return jax.ShapeDtypeStruct(dims, dtype)


def per_device(active_ids, active_vals, block_pattern, target_slots, encoder, decoder):
    feats = lax.axis_size("feat")
    poses = lax.axis_size("pos")
    reps = lax.axis_size("rep")
    holders = feats * poses
    table_rows, width = encoder.shape
    depth = decoder.shape[1]
    layers = depth + 1
    positions, kslots = active_ids.shape[1:]
    block_rows = positions * kslots
    slots = block_rows * feats
    capacity = max(2, (10 * block_rows + 7 * holders - 1) // (7 * holders))
    listed = capacity * feats
    column = poses * listed
    half = column // reps
    result_rows = block_rows // reps
    panel = target_slots.shape[1]
    small = slots <= KERNEL_SLOTS
    span = -(-block_rows // LANES) * LANES if small else block_rows
    wide = feats * span

    rests = []
    for row in range(0, half, GROUP):
        rests.append((row, row % listed // capacity))
    bins = []
    for rest in sorted(rests, key=lambda rest: rest[1]):
        for row in bins:
            if sum(feats - block for _, block in row) + feats - rest[1] <= feats:
                row.append(rest)
                break
        else:
            bins.append([rest])

    def pack_rests(x):
        rows = []
        for row in bins:
            parts = [x[at : at + GROUP, block * span :] for at, block in row]
            empty = wide - sum(part.shape[1] for part in parts)
            parts += [jnp.zeros((GROUP, empty), x.dtype)] if empty else []
            rows.append(jnp.concatenate(parts, axis=1) if len(parts) > 1 else parts[0])
        return jnp.concatenate(rows, axis=0)

    def unpack_rests(x):
        x = x.astype(F32) if small else x
        found = {}
        for n, row in enumerate(bins):
            lane = 0
            for at, block in row:
                rest = x[n * GROUP : (n + 1) * GROUP, lane : lane + wide - block * span]
                lane += wide - block * span
                if block:
                    rest = jnp.concatenate([jnp.zeros((GROUP, block * span), x.dtype), rest], axis=1)
                found[at] = rest
        return jnp.concatenate([found[at] for at, _ in rests], axis=0).astype(BF16)

    def place():
        feat, pos = lax.axis_index("feat"), lax.axis_index("pos")
        return feat.astype(F32), pos.astype(F32), lax.axis_index("rep").astype(F32)

    def pack(ids, vals):
        one = jnp.concatenate([ids(0).astype(F32), vals(0)], axis=0)
        one = jnp.concatenate([one, jnp.zeros((2 * positions, LANES - kslots), F32)], axis=1)
        return (jnp.broadcast_to(one, (holders,) + one.shape),)

    (packed,) = on_core(
        pack,
        [],
        [shape(holders, 2 * positions, LANES)],
        streams=[active_ids, active_vals],
        room=60,
    )
    lists = lax.all_to_all(packed, ("feat", "pos"), split_axis=0, concat_axis=0, tiled=True)

    def list_of(values, prompt):
        blocks = []
        for a in range(feats):
            block = values[a * poses]
            for q in range(1, poses):
                block = jnp.where(prompt == q, values[a * poses + q], block)
            blocks.append(block)
        return jnp.concatenate(blocks, axis=0)[:, :kslots]

    def list_row(slot):
        place = floor_div(slot, kslots)
        return place + floor_div(place, positions) * positions

    def slot_entry(slot):
        return slot - floor_div(slot, kslots) * kslots

    def pieces(table):
        high = part(table, small)
        rest = table - high.astype(F32)
        middle = part(rest, small)
        return [high, middle, part(rest - middle.astype(F32), small)]

    def as_rows(table, slot_at, lanes):
        entry = slot_entry(slot_at(iota((kslots, lanes), 1)))
        spread = (iota((kslots, lanes), 0) == entry).astype(BF16)
        every = dot(jnp.concatenate(pieces(table), axis=0), spread)
        count = table.shape[0]
        every = every[:count] + (every[count : 2 * count] + every[2 * count :])
        row = iota(every.shape, 0) - list_row(slot_at(iota(every.shape, 1)))
        ids = jnp.sum(jnp.where(row == 0, every, 0.0), axis=0, keepdims=True)
        return ids, jnp.sum(jnp.where(row == positions, every, 0.0), axis=0, keepdims=True)

    def spread_slot(lane):
        block = floor_div(lane, span)
        inside = lane - block * span
        return jnp.where(inside < block_rows, block * block_rows + inside, -1.0 * slots)

    def as_col(table):
        wide = (slots, table.shape[0])
        spread = (list_row(iota(wide, 0)) == iota(wide, 1)).astype(BF16)
        every = dot(spread, jnp.concatenate(pieces(table), axis=1))
        every = every[:, :kslots] + (every[:, kslots : 2 * kslots] + every[:, 2 * kslots :])
        mine = slot_entry(iota((slots, kslots), 0)) == iota((slots, kslots), 1)
        return jnp.sum(jnp.where(mine, every, 0.0), axis=1, keepdims=True)

    def choose(values):
        feat, pos, _ = place()
        own = feat * poses + pos
        tables = []
        rows = []
        for k in range(poses):
            prompt = jnp.where(pos + k >= poses, pos + k - poses, pos + k)
            tables.append(list_of(values, prompt))
            rows.append(as_rows(tables[k], lambda lane: lane, slots)[0])
        hits = [floor_div(ids, table_rows) == own for ids in rows]
        earlier = (iota((slots, slots), 0) < iota((slots, slots), 1)).astype(BF16)
        ranks = dot(jnp.concatenate([h.astype(BF16) for h in hits], axis=0), earlier)
        picks = []
        for k in range(poses):
            chosen = jnp.where(
                hits[k] & (ranks[k : k + 1] == iota((listed, slots), 0)), 1.0, 0.0
            )
            local = jnp.sum(chosen * (rows[k] - own * table_rows + 1.0), axis=1, keepdims=True)
            picks.append((local - 1.0 == iota((listed, table_rows), 1)).astype(BF16))
        return jnp.concatenate(picks, axis=0), tables[0]

    picks, my_list = on_core(
        choose,
        [lists],
        [shape(column, table_rows, dtype=BF16), shape(2 * positions * feats, kslots)],
        small,
        cost=(10**9, 10**7),
    )

    def encode(picks, enc):
        rows = dot(picks, enc).astype(BF16)
        return [rows[k * listed : (k + 1) * listed] for k in range(poses)] + [picks]

    *enc_rows, picks = on_core(
        encode,
        [picks, encoder],
        [shape(listed, width, dtype=BF16)] * poses + [shape(column, table_rows, dtype=BF16)],
        small,
    )

    ring = [[enc_rows[0]] + [rotate(enc_rows[k], "pos", k) for k in range(1, poses)]]
    ring.append([ring_next(enc_rows[k], "feat", "pos", k) for k in range(poses)])

    dec_rows = lax.dot_general(
        picks, decoder, (((1,), (0,)), ((), ())), preferred_element_type=F32
    )
    dec_rows = jnp.transpose(dec_rows, (1, 0, 2)).astype(BF16)
    dec_rows = [
        [dec_rows[l, k * listed : (k + 1) * listed] for l in range(depth)] for k in range(poses)
    ]
    away = [rows for k in range(1, poses) for rows in dec_rows[k]]
    order = [(0, 0)] + [(k, q) for k in range(1, feats - 1) for q in range(poses)]
    soon = len(order)
    order += [(0, q) for q in range(1, poses)] + [(feats - 1, q) for q in range(poses)]
    own_lists = [order.index((0, q)) for q in range(poses)]

    def places(table, pattern):
        feat, pos, rep = place()

        def turned(owner):
            turn = pos - (owner - floor_div(owner, poses) * poses)
            return jnp.where(turn < 0.0, turn + poses, turn)

        def spread_place(owner, rank):
            feat_of = floor_div(owner, poses).astype(jnp.int32)
            bits = (feat.astype(jnp.int32) ^ feat_of).astype(F32)
            return (bits * poses + turned(owner)) * listed + rank

        def padded(owner, rank):
            feat_of = floor_div(owner, poses)
            turn = turned(owner)
            step = ring_place(feat, feats) - ring_place(feat_of, feats)
            step = jnp.where(step < 0.0, step + feats, step)
            at = step * poses + turn
            at = jnp.where(step < feats - 1.0, at - (poses - 1), at)
            at = jnp.where(step == 0.0, turn + (feats - 2) * poses, at)
            at = jnp.where((step == 0.0) & (turn == 0.0), 0.0, at)
            return at * listed + rank

        ids_row, vals_row = as_rows(table, spread_slot, wide)
        ids_col = as_col(table)
        owner_row = floor_div(ids_row, table_rows)
        owner_col = floor_div(ids_col, table_rows)
        down, across = iota((slots, slots), 0), iota((slots, slots), 1)
        same = owner_col == floor_div(as_rows(table, lambda lane: lane, slots)[0], table_rows)
        rank_col = jnp.sum(jnp.where(same & (across < down), 1.0, 0.0), axis=1, keepdims=True)
        slot = spread_slot(iota((slots, wide), 1))
        same = (owner_col == owner_row) & (iota((slots, wide), 0) < slot)
        rank_row = jnp.sum(jnp.where(same, 1.0, 0.0), axis=0, keepdims=True)
        total = holders * listed
        used = spread_slot(iota((1, wide), 1)) >= 0.0
        place_row = jnp.where(used, padded(owner_row, rank_row), -1.0)
        placing = spread_place(owner_col, rank_col) == iota((slots, total), 1)
        entry = padded(owner_col, rank_col) == iota((slots, total), 1)
        placing_t = place_row == iota((total, wide), 0)
        layer = ids_col - floor_div(ids_col, layers) * layers
        layer_row = jnp.sum(jnp.where(entry, layer, 0.0), axis=0, keepdims=True)
        mine = [placing_t[at * listed : (at + 1) * listed] for at in own_lists]
        mine = jnp.concatenate(mine, axis=0)
        gain = jnp.sum(jnp.where(mine, vals_row, 0.0), axis=1, keepdims=True)
        source_layer = ids_row - floor_div(ids_row, layers) * layers
        source_layer = jnp.sum(jnp.where(mine, source_layer, 0.0), axis=1, keepdims=True)
        gains = jnp.concatenate(
            [jnp.where(source_layer <= l, gain, 0.0) for l in range(depth)], axis=0
        )
        allowed = jnp.where(pattern[0] == 1, 1.0, 0.0).astype(BF16)

        sources = (floor_div(iota((wide, 1), 0), span) == iota((wide, feats), 1)).astype(BF16)
        targets = (floor_div(iota((1, wide), 1), span) == iota((feats, wide), 0)).astype(BF16)
        mask = dot(dot(sources, allowed, NT).astype(BF16), targets)
        source = floor_div(spread_slot(iota((wide, wide), 0)), kslots)
        target = floor_div(spread_slot(iota((wide, wide), 1)), kslots)
        mask = jnp.where(source <= target, mask, 0.0)
        squeeze = spread_slot(iota((wide, slots), 0)) == iota((wide, slots), 1)
        placing, placing_t = placing.astype(BF16), placing_t.astype(BF16)
        return placing, placing_t, layer_row, gains, mask.astype(BF16), squeeze.astype(BF16)

    placing, placing_t, layer_row, gains, mask, squeeze, *away = on_core(
        places,
        [my_list, block_pattern],
        [
            shape(slots, holders * listed, dtype=BF16),
            shape(holders * listed, wide, dtype=BF16),
            shape(1, holders * listed),
            shape(depth * column, 1),
            shape(wide, wide, dtype=BF16),
            shape(wide, slots, dtype=BF16),
        ],
        small,
        through=away,
        cost=(1, 1),
    )
    for k in range(1, poses):
        rows = away[(k - 1) * depth : k * depth]
        dec_rows[k] = [rotate(row, "pos", k) for row in rows]
    dec_rows = [dec_rows[k][l] for l in range(depth) for k in range(poses)]

    for _ in range(2, feats):
        ring.append([ring_next(rows, "feat") for rows in ring[-1]])

    def products(first, enc, dec, layer_row, placing_t):
        enc = jnp.concatenate(enc, axis=0)
        every = dot(dec, enc, NT)
        lanes = slice(first * listed, first * listed + enc.shape[0])
        raw = jnp.zeros((column, enc.shape[0]), F32)
        for l in range(depth):
            rows = every[l * column : (l + 1) * column]
            raw = raw + jnp.where(layer_row[:, lanes] == l + 1.0, rows, 0.0)
        split = dot(jnp.concatenate(pieces(raw), axis=0), placing_t[lanes])
        return split[:column] + (split[column : 2 * column] + split[2 * column :])

    def early(layer_row, placing_t, gains, *values):
        count = depth * poses
        dec = jnp.concatenate(values[-count:], axis=0)
        dec = (dec.astype(F32) * gains).astype(BF16)
        return products(0, values[:-count], dec, layer_row, placing_t), dec

    def late(layer_row, placing_t, so_far, dec, *values):
        raw = so_far + products(soon, values, dec, layer_row, placing_t)
        first = place()[2] == 0.0
        lower, higher = pack_rests(raw[:half]), pack_rests(raw[half:])
        return jnp.where(first, lower, higher), jnp.where(first, higher, lower)

    so_far, scaled = on_core(
        early,
        [layer_row, placing_t, gains] + [ring[k][q] for k, q in order[:soon]] + dec_rows,
        [shape(column, wide), shape(depth * column, width, dtype=BF16)],
        small,
        cost=(1, 1),
    )
    keep, send = on_core(
        late,
        [layer_row, placing_t, so_far, scaled] + [ring[k][q] for k, q in order[soon:]],
        [shape(len(bins) * GROUP, wide)] * 2,
        small,
    )
    own_edges = (keep + rotate(send, "rep", 1)).astype(BF16)
    found = spread(own_edges, "feat")
    arrival = [bits for bits, _ in found]
    shards = [shard for _, shard in found]
    others = [rotate(shard, "rep", 1) for shard in shards]

    def finish(placing, mask, squeeze, targets, *values):
        feat, _, rep = place()
        first = rep == 0.0
        chips = []
        for mine, other in zip(values[:feats], values[feats:]):
            lower, higher = jnp.where(first, mine, other), jnp.where(first, other, mine)
            chips.append(jnp.concatenate([unpack_rests(lower), unpack_rests(higher)], axis=0))
        padded = jnp.concatenate([chips[arrival.index(m)] for m in range(feats)], axis=0)
        unused = [jnp.zeros((span - block_rows, holders * listed), BF16)]
        unused = unused if span > block_rows else []
        sources = []
        for f in range(feats):
            sources += [placing[f * block_rows : (f + 1) * block_rows]] + unused
        sources = jnp.concatenate(sources, axis=0)
        edges = dot(sources, padded) * mask.astype(F32)
        magnitude = jnp.abs(edges)
        total = jnp.maximum(jnp.sum(magnitude, axis=0, keepdims=True), 1.0)
        magnitude = magnitude.astype(BF16)
        diagonal = iota((wide, wide), 0) == iota((wide, wide), 1)
        scale = 1.0 / jnp.sum(jnp.where(diagonal, total, 0.0), axis=1, keepdims=True)
        targets = targets.astype(F32)
        targets = targets + floor_div(targets, block_rows) * (span - block_rows)
        current = (iota((wide, panel), 0) == targets).astype(F32)
        accum = jnp.zeros((wide, panel), F32)
        for _ in range(ITERS):
            scaled = current * scale
            high = part(scaled, small)
            low = part(scaled - high.astype(F32), small)
            both = dot(magnitude, jnp.concatenate([high, low], axis=1))
            current = both[:, :panel] + both[:, panel:]
            accum = accum + current
        influence = accum[:result_rows]
        for f in range(feats):
            for r in range(reps):
                at = f * span + r * result_rows
                mine = (feat == f) & (rep == r)
                influence = jnp.where(mine, accum[at : at + result_rows], influence)
        start = feat * span + rep * result_rows
        own = start + iota((result_rows, wide), 0) == iota((result_rows, wide), 1)
        rows = dot(own.astype(BF16), edges.astype(BF16), NT).astype(BF16)
        edges = dot(rows, squeeze).astype(BF16)
        return edges[None], (influence * float(slots))[None]

    edges, influence = on_core(
        finish,
        [placing, mask, squeeze, target_slots] + shards + others,
        [shape(1, result_rows, slots, dtype=BF16), shape(1, result_rows, panel)],
        small,
    )
    return edges, influence


def solution(mesh):
    return jax.shard_map(
        per_device,
        mesh=mesh,
        in_specs=(
            P(("grp", "pos"), "feat", None),
            P(("grp", "pos"), "feat", None),
            P(("grp", "pos"), None, None),
            P(("grp", "pos"), None),
            P(("feat", "pos"), "rep"),
            P(("feat", "pos"), None, "rep"),
        ),
        out_specs=(
            P(("grp", "pos"), ("feat", "rep"), None),
            P(("grp", "pos"), ("feat", "rep"), None),
        ),
        check_vma=False,
    )
```

```python
import jax
import jax.numpy as jnp
from jax import lax
from jax.experimental import pallas as pl
from jax.experimental.pallas import tpu as pltpu
from jax.sharding import PartitionSpec as P

ITERS = 3
F32 = jnp.float32
BF16 = jnp.bfloat16
NN = (((1,), (0,)), ((), ()))
NT = (((1,), (1,)), ((), ()))
LANES = 128
GROUP = 8
KERNEL_SLOTS = 1024


def dot(a, b, dims=NN):
    return lax.dot_general(a, b, dims, preferred_element_type=F32)


def iota(shape, dim):
    return lax.broadcasted_iota(jnp.int32, shape, dim).astype(F32)


def floor_div(x, n):
    return jnp.floor((x + 0.5) * (1.0 / n))


def on_core(fn, args, outs, kernel=True, through=(), streams=(), cost=None, room=24):
    if not kernel:
        loads = [lambda i, x=x: x[i] for x in streams]
        return list(fn(*args, *loads)) + list(through)
    count, passed, streamed = len(args), len(through), len(streams)

    def body(*refs):
        sources = refs[count : count + streamed]
        results = refs[count + streamed + passed :][: len(outs)]
        scratch = refs[len(refs) - 2 * streamed :]
        copies = []
        for n in range(streamed):
            copies.append(
                [
                    pltpu.make_async_copy(
                        sources[n].at[i], scratch[2 * n].at[i], scratch[2 * n + 1].at[i]
                    )
                    for i in range(streams[n].shape[0])
                ]
            )
            for copy in copies[-1]:
                copy.start()

        def load(n):
            def wait(i):
                copies[n][i].wait()
                return scratch[2 * n][i]

            return wait

        values = fn(*[ref[...] for ref in refs[:count]], *[load(n) for n in range(streamed)])
        for ref, value in zip(results, values):
            ref[...] = value

    estimate = None
    if cost is not None:
        estimate = pl.CostEstimate(flops=cost[0], bytes_accessed=cost[1], transcendentals=0)
    in_vmem = pl.BlockSpec(memory_space=pltpu.VMEM)
    anywhere = pl.BlockSpec(memory_space=pl.ANY)
    scratch = []
    for x in streams:
        scratch += [pltpu.VMEM(x.shape, x.dtype), pltpu.SemaphoreType.DMA((x.shape[0],))]
    call = pl.pallas_call(
        body,
        out_shape=list(outs) + [jax.ShapeDtypeStruct(x.shape, x.dtype) for x in through],
        in_specs=[in_vmem] * count
        + [pl.BlockSpec(memory_space=pltpu.HBM)] * streamed
        + [anywhere] * passed,
        out_specs=[in_vmem] * len(outs) + [anywhere] * passed,
        scratch_shapes=scratch,
        input_output_aliases={count + streamed + i: len(outs) + i for i in range(passed)},
        compiler_params=pltpu.CompilerParams(vmem_limit_bytes=room * 1024 * 1024),
        cost_estimate=estimate,
    )
    return list(call(*args, *streams, *through))


def rotate(x, axis, step):
    count = lax.axis_size(axis)
    return lax.ppermute(x, axis, [(i, (i + step) % count) for i in range(count)])


def ring_place(index, count):
    low = floor_div(index, 2)
    return jnp.where(index > 2 * low, count - 1 - low, low)


def ring_next(x, axis, across=None, turn=0):
    count = lax.axis_size(axis)
    order = list(range(0, count, 2)) + list(range(1, count, 2))[::-1]
    steps = [(order[i], order[(i + 1) % count]) for i in range(count)]
    if across is None:
        return lax.ppermute(x, axis, steps)
    wide = lax.axis_size(across)
    pairs = [(a * wide + i, b * wide + (i + turn) % wide) for a, b in steps for i in range(wide)]
    return lax.ppermute(x, (axis, across), pairs)


def part(x, kernel):
    return x.astype(BF16) if kernel else lax.reduce_precision(x, 8, 7).astype(BF16)


def shape(*dims, dtype=F32):
    return jax.ShapeDtypeStruct(dims, dtype)


def per_device(active_ids, active_vals, block_pattern, target_slots, encoder, decoder):
    feats = lax.axis_size("feat")
    poses = lax.axis_size("pos")
    reps = lax.axis_size("rep")
    holders = feats * poses
    table_rows, width = encoder.shape
    depth = decoder.shape[1]
    layers = depth + 1
    positions, kslots = active_ids.shape[1:]
    block_rows = positions * kslots
    slots = block_rows * feats
    capacity = max(2, (10 * block_rows + 7 * holders - 1) // (7 * holders))
    listed = capacity * feats
    column = poses * listed
    half = column // reps
    result_rows = block_rows // reps
    panel = target_slots.shape[1]
    small = slots <= KERNEL_SLOTS
    span = -(-block_rows // LANES) * LANES if small else block_rows
    wide = feats * span

    rests = []
    for row in range(0, half, GROUP):
        rests.append((row, row % listed // capacity))
    bins = []
    for rest in sorted(rests, key=lambda rest: rest[1]):
        for row in bins:
            if sum(feats - block for _, block in row) + feats - rest[1] <= feats:
                row.append(rest)
                break
        else:
            bins.append([rest])

    def pack_rests(x):
        rows = []
        for row in bins:
            parts = [x[at : at + GROUP, block * span :] for at, block in row]
            empty = wide - sum(part.shape[1] for part in parts)
            parts += [jnp.zeros((GROUP, empty), x.dtype)] if empty else []
            rows.append(jnp.concatenate(parts, axis=1) if len(parts) > 1 else parts[0])
        return jnp.concatenate(rows, axis=0)

    def unpack_rests(x, first):
        found = {}
        for n, row in enumerate(bins):
            lane = 0
            for at, block in row:
                at_row = (first + n) * GROUP
                rest = x[at_row : at_row + GROUP, lane : lane + wide - block * span]
                lane += wide - block * span
                if block:
                    rest = jnp.concatenate([jnp.zeros((GROUP, block * span), x.dtype), rest], axis=1)
                found[at] = rest
        return jnp.concatenate([found[at] for at, _ in rests], axis=0).astype(BF16)

    def place():
        feat, pos = lax.axis_index("feat"), lax.axis_index("pos")
        return feat.astype(F32), pos.astype(F32), lax.axis_index("rep").astype(F32)

    def pack(ids, vals):
        one = jnp.concatenate([ids(0).astype(F32), vals(0)], axis=0)
        one = jnp.concatenate([one, jnp.zeros((2 * positions, LANES - kslots), F32)], axis=1)
        return (jnp.broadcast_to(one, (holders,) + one.shape),)

    (packed,) = on_core(
        pack,
        [],
        [shape(holders, 2 * positions, LANES)],
        streams=[active_ids, active_vals],
        room=60,
    )
    lists = lax.all_to_all(packed, ("feat", "pos"), split_axis=0, concat_axis=0, tiled=True)

    def list_of(values, prompt):
        blocks = []
        for a in range(feats):
            block = values[a * poses]
            for q in range(1, poses):
                block = jnp.where(prompt == q, values[a * poses + q], block)
            blocks.append(block)
        return jnp.concatenate(blocks, axis=0)[:, :kslots]

    def list_row(slot):
        place = floor_div(slot, kslots)
        return place + floor_div(place, positions) * positions

    def slot_entry(slot):
        return slot - floor_div(slot, kslots) * kslots

    def pieces(table):
        high = part(table, small)
        rest = table - high.astype(F32)
        middle = part(rest, small)
        return [high, middle, part(rest - middle.astype(F32), small)]

    def as_rows(table, slot_at, lanes):
        entry = slot_entry(slot_at(iota((kslots, lanes), 1)))
        spread = (iota((kslots, lanes), 0) == entry).astype(BF16)
        every = dot(jnp.concatenate(pieces(table), axis=0), spread)
        count = table.shape[0]
        every = every[:count] + (every[count : 2 * count] + every[2 * count :])
        row = iota(every.shape, 0) - list_row(slot_at(iota(every.shape, 1)))
        ids = jnp.sum(jnp.where(row == 0, every, 0.0), axis=0, keepdims=True)
        return ids, jnp.sum(jnp.where(row == positions, every, 0.0), axis=0, keepdims=True)

    def spread_slot(lane):
        block = floor_div(lane, span)
        inside = lane - block * span
        return jnp.where(inside < block_rows, block * block_rows + inside, -1.0 * slots)

    def as_col(table):
        wide = (slots, table.shape[0])
        spread = (list_row(iota(wide, 0)) == iota(wide, 1)).astype(BF16)
        every = dot(spread, jnp.concatenate(pieces(table), axis=1))
        every = every[:, :kslots] + (every[:, kslots : 2 * kslots] + every[:, 2 * kslots :])
        mine = slot_entry(iota((slots, kslots), 0)) == iota((slots, kslots), 1)
        return jnp.sum(jnp.where(mine, every, 0.0), axis=1, keepdims=True)

    def choose(values):
        feat, pos, _ = place()
        own = feat * poses + pos
        tables = []
        rows = []
        for k in range(poses):
            prompt = jnp.where(pos + k >= poses, pos + k - poses, pos + k)
            tables.append(list_of(values, prompt))
            rows.append(as_rows(tables[k], lambda lane: lane, slots)[0])
        hits = [floor_div(ids, table_rows) == own for ids in rows]
        earlier = (iota((slots, slots), 0) < iota((slots, slots), 1)).astype(BF16)
        ranks = dot(jnp.concatenate([h.astype(BF16) for h in hits], axis=0), earlier)
        picks = []
        for k in range(poses):
            chosen = jnp.where(
                hits[k] & (ranks[k : k + 1] == iota((listed, slots), 0)), 1.0, 0.0
            )
            local = jnp.sum(chosen * (rows[k] - own * table_rows + 1.0), axis=1, keepdims=True)
            picks.append((local - 1.0 == iota((listed, table_rows), 1)).astype(BF16))
        return jnp.concatenate(picks, axis=0), tables[0]

    picks, my_list = on_core(
        choose,
        [lists],
        [shape(column, table_rows, dtype=BF16), shape(2 * positions * feats, kslots)],
        small,
        cost=(10**9, 10**7),
    )

    def encode(picks, enc):
        rows = dot(picks, enc).astype(BF16)
        return [rows[k * listed : (k + 1) * listed] for k in range(poses)] + [picks]

    *enc_rows, picks = on_core(
        encode,
        [picks, encoder],
        [shape(listed, width, dtype=BF16)] * poses + [shape(column, table_rows, dtype=BF16)],
        small,
    )

    ring = [[enc_rows[0]] + [rotate(enc_rows[k], "pos", k) for k in range(1, poses)]]
    ring.append([ring_next(enc_rows[k], "feat", "pos", k) for k in range(poses)])

    dec_rows = lax.dot_general(
        picks, decoder, (((1,), (0,)), ((), ())), preferred_element_type=F32
    )
    dec_rows = jnp.transpose(dec_rows, (1, 0, 2)).astype(BF16)
    dec_rows = [
        [dec_rows[l, k * listed : (k + 1) * listed] for l in range(depth)] for k in range(poses)
    ]
    away = [rows for k in range(1, poses) for rows in dec_rows[k]]
    order = [(0, 0)] + [(k, q) for k in range(1, feats - 1) for q in range(poses)]
    soon = len(order)
    order += [(0, q) for q in range(1, poses)] + [(feats - 1, q) for q in range(poses)]
    own_lists = [order.index((0, q)) for q in range(poses)]

    def places(table, pattern):
        feat, pos, rep = place()

        def turned(owner):
            turn = pos - (owner - floor_div(owner, poses) * poses)
            return jnp.where(turn < 0.0, turn + poses, turn)

        def spread_place(owner, rank):
            feat_of = floor_div(owner, poses).astype(jnp.int32)
            bits = (feat.astype(jnp.int32) ^ feat_of).astype(F32)
            return (bits * poses + turned(owner)) * listed + rank

        def padded(owner, rank):
            feat_of = floor_div(owner, poses)
            turn = turned(owner)
            step = ring_place(feat, feats) - ring_place(feat_of, feats)
            step = jnp.where(step < 0.0, step + feats, step)
            at = step * poses + turn
            at = jnp.where(step < feats - 1.0, at - (poses - 1), at)
            at = jnp.where(step == 0.0, turn + (feats - 2) * poses, at)
            at = jnp.where((step == 0.0) & (turn == 0.0), 0.0, at)
            return at * listed + rank

        ids_row, vals_row = as_rows(table, spread_slot, wide)
        ids_col = as_col(table)
        owner_row = floor_div(ids_row, table_rows)
        owner_col = floor_div(ids_col, table_rows)
        down, across = iota((slots, slots), 0), iota((slots, slots), 1)
        same = owner_col == floor_div(as_rows(table, lambda lane: lane, slots)[0], table_rows)
        rank_col = jnp.sum(jnp.where(same & (across < down), 1.0, 0.0), axis=1, keepdims=True)
        slot = spread_slot(iota((slots, wide), 1))
        same = (owner_col == owner_row) & (iota((slots, wide), 0) < slot)
        rank_row = jnp.sum(jnp.where(same, 1.0, 0.0), axis=0, keepdims=True)
        total = holders * listed
        used = spread_slot(iota((1, wide), 1)) >= 0.0
        place_row = jnp.where(used, padded(owner_row, rank_row), -1.0)
        placing = spread_place(owner_col, rank_col) == iota((slots, total), 1)
        entry = padded(owner_col, rank_col) == iota((slots, total), 1)
        placing_t = place_row == iota((total, wide), 0)
        layer = ids_col - floor_div(ids_col, layers) * layers
        layer_row = jnp.sum(jnp.where(entry, layer, 0.0), axis=0, keepdims=True)
        mine = [placing_t[at * listed : (at + 1) * listed] for at in own_lists]
        mine = jnp.concatenate(mine, axis=0)
        gain = jnp.sum(jnp.where(mine, vals_row, 0.0), axis=1, keepdims=True)
        source_layer = ids_row - floor_div(ids_row, layers) * layers
        source_layer = jnp.sum(jnp.where(mine, source_layer, 0.0), axis=1, keepdims=True)
        gains = jnp.concatenate(
            [jnp.where(source_layer <= l, gain, 0.0) for l in range(depth)], axis=0
        )
        allowed = jnp.where(pattern[0] == 1, 1.0, 0.0).astype(BF16)

        sources = (floor_div(iota((wide, 1), 0), span) == iota((wide, feats), 1)).astype(BF16)
        targets = (floor_div(iota((1, wide), 1), span) == iota((feats, wide), 0)).astype(BF16)
        mask = dot(dot(sources, allowed, NT).astype(BF16), targets)
        source = floor_div(spread_slot(iota((wide, wide), 0)), kslots)
        target = floor_div(spread_slot(iota((wide, wide), 1)), kslots)
        mask = jnp.where(source <= target, mask, 0.0)
        squeeze = spread_slot(iota((wide, slots), 0)) == iota((wide, slots), 1)
        placing, placing_t = placing.astype(BF16), placing_t.astype(BF16)
        return placing, placing_t, layer_row, gains, mask.astype(BF16), squeeze.astype(BF16)

    placing, placing_t, layer_row, gains, mask, squeeze, *away = on_core(
        places,
        [my_list, block_pattern],
        [
            shape(slots, holders * listed, dtype=BF16),
            shape(holders * listed, wide, dtype=BF16),
            shape(1, holders * listed),
            shape(depth * column, 1),
            shape(wide, wide, dtype=BF16),
            shape(wide, slots, dtype=BF16),
        ],
        small,
        through=away,
        cost=(1, 1),
    )
    for k in range(1, poses):
        rows = away[(k - 1) * depth : k * depth]
        dec_rows[k] = [rotate(row, "pos", k) for row in rows]
    dec_rows = [dec_rows[k][l] for l in range(depth) for k in range(poses)]

    for _ in range(2, feats):
        ring.append([ring_next(rows, "feat") for rows in ring[-1]])

    def products(first, enc, dec, layer_row, placing_t):
        enc = jnp.concatenate(enc, axis=0)
        every = dot(dec, enc, NT)
        lanes = slice(first * listed, first * listed + enc.shape[0])
        raw = jnp.zeros((column, enc.shape[0]), F32)
        for l in range(depth):
            rows = every[l * column : (l + 1) * column]
            raw = raw + jnp.where(layer_row[:, lanes] == l + 1.0, rows, 0.0)
        split = dot(jnp.concatenate(pieces(raw), axis=0), placing_t[lanes])
        return split[:column] + (split[column : 2 * column] + split[2 * column :])

    def early(layer_row, placing_t, gains, *values):
        count = depth * poses
        dec = jnp.concatenate(values[-count:], axis=0)
        dec = (dec.astype(F32) * gains).astype(BF16)
        return products(0, values[:-count], dec, layer_row, placing_t), dec

    def late(layer_row, placing_t, so_far, dec, *values):
        raw = so_far + products(soon, values, dec, layer_row, placing_t)
        return (jnp.concatenate([pack_rests(raw[:half]), pack_rests(raw[half:])], axis=0),)

    so_far, scaled = on_core(
        early,
        [layer_row, placing_t, gains] + [ring[k][q] for k, q in order[:soon]] + dec_rows,
        [shape(column, wide), shape(depth * column, width, dtype=BF16)],
        small,
        cost=(1, 1),
    )
    (partial,) = on_core(
        late,
        [layer_row, placing_t, so_far, scaled] + [ring[k][q] for k, q in order[soon:]],
        [shape(reps * len(bins) * GROUP, wide)],
        small,
    )
    columns = (partial + rotate(partial, "rep", 1)).astype(BF16)

    far = []
    for bits in range(2, feats, 2):
        pairs = [
            (f * reps + r, (f ^ (bits + r)) * reps + r) for f in range(feats) for r in range(reps)
        ]
        far.append(lax.ppermute(columns, ("feat", "rep"), pairs))
    near = lax.ppermute(columns, "feat", [(f, f ^ 1) for f in range(feats)])
    across = [rotate(shard, "rep", 1) for shard in far]

    def finish(placing, mask, squeeze, targets, *values):
        feat, _, rep = place()
        first = rep == 0.0
        chips = [values[0], values[len(far) + 1]]
        for mine, other in zip(values[1 : len(far) + 1], values[len(far) + 2 :]):
            chips += [jnp.where(first, mine, other), jnp.where(first, other, mine)]
        padded = []
        for chip in chips:
            chip = chip.astype(F32) if small else chip
            padded += [unpack_rests(chip, r * len(bins)) for r in range(reps)]
        padded = jnp.concatenate(padded, axis=0)
        unused = [jnp.zeros((span - block_rows, holders * listed), BF16)]
        unused = unused if span > block_rows else []
        sources = []
        for f in range(feats):
            sources += [placing[f * block_rows : (f + 1) * block_rows]] + unused
        sources = jnp.concatenate(sources, axis=0)
        edges = dot(sources, padded) * mask.astype(F32)
        magnitude = jnp.abs(edges)
        total = jnp.maximum(jnp.sum(magnitude, axis=0, keepdims=True), 1.0)
        magnitude = magnitude.astype(BF16)
        diagonal = iota((wide, wide), 0) == iota((wide, wide), 1)
        scale = 1.0 / jnp.sum(jnp.where(diagonal, total, 0.0), axis=1, keepdims=True)
        targets = targets.astype(F32)
        targets = targets + floor_div(targets, block_rows) * (span - block_rows)
        current = (iota((wide, panel), 0) == targets).astype(F32)
        accum = jnp.zeros((wide, panel), F32)
        for _ in range(ITERS):
            scaled = current * scale
            high = part(scaled, small)
            low = part(scaled - high.astype(F32), small)
            both = dot(magnitude, jnp.concatenate([high, low], axis=1))
            current = both[:, :panel] + both[:, panel:]
            accum = accum + current
        influence = accum[:result_rows]
        for f in range(feats):
            for r in range(reps):
                at = f * span + r * result_rows
                mine = (feat == f) & (rep == r)
                influence = jnp.where(mine, accum[at : at + result_rows], influence)
        start = feat * span + rep * result_rows
        own = start + iota((result_rows, wide), 0) == iota((result_rows, wide), 1)
        rows = dot(own.astype(BF16), edges.astype(BF16), NT).astype(BF16)
        edges = dot(rows, squeeze).astype(BF16)
        return edges[None], (influence * float(slots))[None]

    edges, influence = on_core(
        finish,
        [placing, mask, squeeze, target_slots, columns] + far + [near] + across,
        [shape(1, result_rows, slots, dtype=BF16), shape(1, result_rows, panel)],
        small,
    )
    return edges, influence


def solution(mesh):
    return jax.shard_map(
        per_device,
        mesh=mesh,
        in_specs=(
            P(("grp", "pos"), "feat", None),
            P(("grp", "pos"), "feat", None),
            P(("grp", "pos"), None, None),
            P(("grp", "pos"), None),
            P(("feat", "pos"), "rep"),
            P(("feat", "pos"), None, "rep"),
        ),
        out_specs=(
            P(("grp", "pos"), ("feat", "rep"), None),
            P(("grp", "pos"), ("feat", "rep"), None),
        ),
        check_vma=False,
    )
```

```python
import jax
import jax.numpy as jnp
from jax import lax
from jax.experimental import pallas as pl
from jax.experimental.pallas import tpu as pltpu
from jax.sharding import PartitionSpec as P

ITERS = 3
F32 = jnp.float32
BF16 = jnp.bfloat16
NN = (((1,), (0,)), ((), ()))
NT = (((1,), (1,)), ((), ()))
LANES = 128
GROUP = 8
KERNEL_SLOTS = 1024


def dot(a, b, dims=NN):
    return lax.dot_general(a, b, dims, preferred_element_type=F32)


def iota(shape, dim):
    return lax.broadcasted_iota(jnp.int32, shape, dim).astype(F32)


def floor_div(x, n):
    return jnp.floor((x + 0.5) * (1.0 / n))


def on_core(fn, args, outs, kernel=True, through=(), streams=(), cost=None, room=24):
    if not kernel:
        loads = [lambda i, x=x: x[i] for x in streams]
        return list(fn(*args, *loads)) + list(through)
    count, passed, streamed = len(args), len(through), len(streams)

    def body(*refs):
        sources = refs[count : count + streamed]
        results = refs[count + streamed + passed :][: len(outs)]
        scratch = refs[len(refs) - 2 * streamed :]
        copies = []
        for n in range(streamed):
            copies.append(
                [
                    pltpu.make_async_copy(
                        sources[n].at[i], scratch[2 * n].at[i], scratch[2 * n + 1].at[i]
                    )
                    for i in range(streams[n].shape[0])
                ]
            )
            for copy in copies[-1]:
                copy.start()

        def load(n):
            def wait(i):
                copies[n][i].wait()
                return scratch[2 * n][i]

            return wait

        values = fn(*[ref[...] for ref in refs[:count]], *[load(n) for n in range(streamed)])
        for ref, value in zip(results, values):
            ref[...] = value

    estimate = None
    if cost is not None:
        estimate = pl.CostEstimate(flops=cost[0], bytes_accessed=cost[1], transcendentals=0)
    in_vmem = pl.BlockSpec(memory_space=pltpu.VMEM)
    anywhere = pl.BlockSpec(memory_space=pl.ANY)
    scratch = []
    for x in streams:
        scratch += [pltpu.VMEM(x.shape, x.dtype), pltpu.SemaphoreType.DMA((x.shape[0],))]
    call = pl.pallas_call(
        body,
        out_shape=list(outs) + [jax.ShapeDtypeStruct(x.shape, x.dtype) for x in through],
        in_specs=[in_vmem] * count
        + [pl.BlockSpec(memory_space=pltpu.HBM)] * streamed
        + [anywhere] * passed,
        out_specs=[in_vmem] * len(outs) + [anywhere] * passed,
        scratch_shapes=scratch,
        input_output_aliases={count + streamed + i: len(outs) + i for i in range(passed)},
        compiler_params=pltpu.CompilerParams(vmem_limit_bytes=room * 1024 * 1024),
        cost_estimate=estimate,
    )
    return list(call(*args, *streams, *through))


def rotate(x, axis, step):
    count = lax.axis_size(axis)
    return lax.ppermute(x, axis, [(i, (i + step) % count) for i in range(count)])


def ring_place(index, count):
    low = floor_div(index, 2)
    return jnp.where(index > 2 * low, count - 1 - low, low)


def ring_next(x, axis, across=None, turn=0):
    count = lax.axis_size(axis)
    order = list(range(0, count, 2)) + list(range(1, count, 2))[::-1]
    steps = [(order[i], order[(i + 1) % count]) for i in range(count)]
    if across is None:
        return lax.ppermute(x, axis, steps)
    wide = lax.axis_size(across)
    pairs = [(a * wide + i, b * wide + (i + turn) % wide) for a, b in steps for i in range(wide)]
    return lax.ppermute(x, (axis, across), pairs)


def part(x, kernel):
    return x.astype(BF16) if kernel else lax.reduce_precision(x, 8, 7).astype(BF16)


def shape(*dims, dtype=F32):
    return jax.ShapeDtypeStruct(dims, dtype)


def per_device(active_ids, active_vals, block_pattern, target_slots, encoder, decoder):
    feats = lax.axis_size("feat")
    poses = lax.axis_size("pos")
    reps = lax.axis_size("rep")
    holders = feats * poses
    table_rows, width = encoder.shape
    depth = decoder.shape[1]
    layers = depth + 1
    positions, kslots = active_ids.shape[1:]
    block_rows = positions * kslots
    slots = block_rows * feats
    capacity = max(2, (10 * block_rows + 7 * holders - 1) // (7 * holders))
    listed = capacity * feats
    column = poses * listed
    half = column // reps
    result_rows = block_rows // reps
    panel = target_slots.shape[1]
    small = slots <= KERNEL_SLOTS
    span = -(-block_rows // LANES) * LANES if small else block_rows
    wide = feats * span

    rests = []
    for row in range(0, half, GROUP):
        rests.append((row, row % listed // capacity))
    bins = []
    for rest in sorted(rests, key=lambda rest: rest[1]):
        for row in bins:
            if sum(feats - block for _, block in row) + feats - rest[1] <= feats:
                row.append(rest)
                break
        else:
            bins.append([rest])

    def pack_rests(x):
        rows = []
        for row in bins:
            parts = [x[at : at + GROUP, block * span :] for at, block in row]
            empty = wide - sum(part.shape[1] for part in parts)
            parts += [jnp.zeros((GROUP, empty), x.dtype)] if empty else []
            rows.append(jnp.concatenate(parts, axis=1) if len(parts) > 1 else parts[0])
        return jnp.concatenate(rows, axis=0)

    def unpack_rests(x, first):
        found = {}
        for n, row in enumerate(bins):
            lane = 0
            for at, block in row:
                at_row = (first + n) * GROUP
                rest = x[at_row : at_row + GROUP, lane : lane + wide - block * span]
                lane += wide - block * span
                if block:
                    rest = jnp.concatenate([jnp.zeros((GROUP, block * span), x.dtype), rest], axis=1)
                found[at] = rest
        return jnp.concatenate([found[at] for at, _ in rests], axis=0).astype(BF16)

    def place():
        feat, pos = lax.axis_index("feat"), lax.axis_index("pos")
        return feat.astype(F32), pos.astype(F32), lax.axis_index("rep").astype(F32)

    def pack(ids, vals):
        one = jnp.concatenate([ids(0).astype(F32), vals(0)], axis=0)
        one = jnp.concatenate([one, jnp.zeros((2 * positions, LANES - kslots), F32)], axis=1)
        return (jnp.broadcast_to(one, (holders,) + one.shape),)

    (packed,) = on_core(
        pack,
        [],
        [shape(holders, 2 * positions, LANES)],
        streams=[active_ids, active_vals],
        room=60,
    )
    lists = lax.all_to_all(packed, ("feat", "pos"), split_axis=0, concat_axis=0, tiled=True)

    def list_of(values, prompt):
        blocks = []
        for a in range(feats):
            block = values[a * poses]
            for q in range(1, poses):
                block = jnp.where(prompt == q, values[a * poses + q], block)
            blocks.append(block)
        return jnp.concatenate(blocks, axis=0)[:, :kslots]

    def list_row(slot):
        place = floor_div(slot, kslots)
        return place + floor_div(place, positions) * positions

    def slot_entry(slot):
        return slot - floor_div(slot, kslots) * kslots

    def pieces(table):
        high = part(table, small)
        rest = table - high.astype(F32)
        middle = part(rest, small)
        return [high, middle, part(rest - middle.astype(F32), small)]

    def as_rows(table, slot_at, lanes):
        entry = slot_entry(slot_at(iota((kslots, lanes), 1)))
        spread = (iota((kslots, lanes), 0) == entry).astype(BF16)
        every = dot(jnp.concatenate(pieces(table), axis=0), spread)
        count = table.shape[0]
        every = every[:count] + (every[count : 2 * count] + every[2 * count :])
        row = iota(every.shape, 0) - list_row(slot_at(iota(every.shape, 1)))
        ids = jnp.sum(jnp.where(row == 0, every, 0.0), axis=0, keepdims=True)
        return ids, jnp.sum(jnp.where(row == positions, every, 0.0), axis=0, keepdims=True)

    def spread_slot(lane):
        block = floor_div(lane, span)
        inside = lane - block * span
        return jnp.where(inside < block_rows, block * block_rows + inside, -1.0 * slots)

    def as_col(table):
        wide = (slots, table.shape[0])
        spread = (list_row(iota(wide, 0)) == iota(wide, 1)).astype(BF16)
        every = dot(spread, jnp.concatenate(pieces(table), axis=1))
        every = every[:, :kslots] + (every[:, kslots : 2 * kslots] + every[:, 2 * kslots :])
        mine = slot_entry(iota((slots, kslots), 0)) == iota((slots, kslots), 1)
        return jnp.sum(jnp.where(mine, every, 0.0), axis=1, keepdims=True)

    def choose(values):
        feat, pos, _ = place()
        own = feat * poses + pos
        tables = []
        rows = []
        for k in range(poses):
            prompt = jnp.where(pos + k >= poses, pos + k - poses, pos + k)
            tables.append(list_of(values, prompt))
            rows.append(as_rows(tables[k], lambda lane: lane, slots)[0])
        hits = [floor_div(ids, table_rows) == own for ids in rows]
        earlier = (iota((slots, slots), 0) < iota((slots, slots), 1)).astype(BF16)
        ranks = dot(jnp.concatenate([h.astype(BF16) for h in hits], axis=0), earlier)
        picks = []
        for k in range(poses):
            chosen = jnp.where(
                hits[k] & (ranks[k : k + 1] == iota((listed, slots), 0)), 1.0, 0.0
            )
            local = jnp.sum(chosen * (rows[k] - own * table_rows + 1.0), axis=1, keepdims=True)
            picks.append((local - 1.0 == iota((listed, table_rows), 1)).astype(BF16))
        return jnp.concatenate(picks, axis=0), tables[0]

    picks, my_list = on_core(
        choose,
        [lists],
        [shape(column, table_rows, dtype=BF16), shape(2 * positions * feats, kslots)],
        small,
        cost=(10**9, 10**7),
    )

    def encode(picks, enc):
        rows = dot(picks, enc).astype(BF16)
        return [rows[k * listed : (k + 1) * listed] for k in range(poses)] + [picks]

    *enc_rows, picks = on_core(
        encode,
        [picks, encoder],
        [shape(listed, width, dtype=BF16)] * poses + [shape(column, table_rows, dtype=BF16)],
        small,
    )

    ring = [[enc_rows[0]] + [rotate(enc_rows[k], "pos", k) for k in range(1, poses)]]
    ring.append([ring_next(enc_rows[k], "feat", "pos", k) for k in range(poses)])

    dec_rows = lax.dot_general(
        picks, decoder, (((1,), (0,)), ((), ())), preferred_element_type=F32
    )
    dec_rows = jnp.transpose(dec_rows, (1, 0, 2)).astype(BF16)
    dec_rows = [
        [dec_rows[l, k * listed : (k + 1) * listed] for l in range(depth)] for k in range(poses)
    ]
    away = [rows for k in range(1, poses) for rows in dec_rows[k]]
    order = [(0, 0)] + [(k, q) for k in range(1, feats - 1) for q in range(poses)]
    soon = len(order)
    order += [(0, q) for q in range(1, poses)] + [(feats - 1, q) for q in range(poses)]
    own_lists = [order.index((0, q)) for q in range(poses)]

    def places(table, pattern):
        feat, pos, rep = place()

        def turned(owner):
            turn = pos - (owner - floor_div(owner, poses) * poses)
            return jnp.where(turn < 0.0, turn + poses, turn)

        def spread_place(owner, rank):
            feat_of = floor_div(owner, poses).astype(jnp.int32)
            bits = (feat.astype(jnp.int32) ^ feat_of).astype(F32)
            return (bits * poses + turned(owner)) * listed + rank

        def padded(owner, rank):
            feat_of = floor_div(owner, poses)
            turn = turned(owner)
            step = ring_place(feat, feats) - ring_place(feat_of, feats)
            step = jnp.where(step < 0.0, step + feats, step)
            at = step * poses + turn
            at = jnp.where(step < feats - 1.0, at - (poses - 1), at)
            at = jnp.where(step == 0.0, turn + (feats - 2) * poses, at)
            at = jnp.where((step == 0.0) & (turn == 0.0), 0.0, at)
            return at * listed + rank

        ids_row, vals_row = as_rows(table, spread_slot, wide)
        ids_col = as_col(table)
        owner_row = floor_div(ids_row, table_rows)
        owner_col = floor_div(ids_col, table_rows)
        down, across = iota((slots, slots), 0), iota((slots, slots), 1)
        same = owner_col == floor_div(as_rows(table, lambda lane: lane, slots)[0], table_rows)
        rank_col = jnp.sum(jnp.where(same & (across < down), 1.0, 0.0), axis=1, keepdims=True)
        slot = spread_slot(iota((slots, wide), 1))
        same = (owner_col == owner_row) & (iota((slots, wide), 0) < slot)
        rank_row = jnp.sum(jnp.where(same, 1.0, 0.0), axis=0, keepdims=True)
        total = holders * listed
        used = spread_slot(iota((1, wide), 1)) >= 0.0
        place_row = jnp.where(used, padded(owner_row, rank_row), -1.0)
        placing = spread_place(owner_col, rank_col) == iota((slots, total), 1)
        entry = padded(owner_col, rank_col) == iota((slots, total), 1)
        placing_t = place_row == iota((total, wide), 0)
        layer = ids_col - floor_div(ids_col, layers) * layers
        layer_row = jnp.sum(jnp.where(entry, layer, 0.0), axis=0, keepdims=True)
        mine = [placing_t[at * listed : (at + 1) * listed] for at in own_lists]
        mine = jnp.concatenate(mine, axis=0)
        gain = jnp.sum(jnp.where(mine, vals_row, 0.0), axis=1, keepdims=True)
        source_layer = ids_row - floor_div(ids_row, layers) * layers
        source_layer = jnp.sum(jnp.where(mine, source_layer, 0.0), axis=1, keepdims=True)
        gains = jnp.concatenate(
            [jnp.where(source_layer <= l, gain, 0.0) for l in range(depth)], axis=0
        )
        allowed = jnp.where(pattern[0] == 1, 1.0, 0.0).astype(BF16)

        sources = (floor_div(iota((wide, 1), 0), span) == iota((wide, feats), 1)).astype(BF16)
        targets = (floor_div(iota((1, wide), 1), span) == iota((feats, wide), 0)).astype(BF16)
        mask = dot(dot(sources, allowed, NT).astype(BF16), targets)
        source = floor_div(spread_slot(iota((wide, wide), 0)), kslots)
        target = floor_div(spread_slot(iota((wide, wide), 1)), kslots)
        mask = jnp.where(source <= target, mask, 0.0)
        squeeze = spread_slot(iota((wide, slots), 0)) == iota((wide, slots), 1)
        placing, placing_t = placing.astype(BF16), placing_t.astype(BF16)
        return placing, placing_t, layer_row, gains, mask.astype(BF16), squeeze.astype(BF16)

    placing, placing_t, layer_row, gains, mask, squeeze, *away = on_core(
        places,
        [my_list, block_pattern],
        [
            shape(slots, holders * listed, dtype=BF16),
            shape(holders * listed, wide, dtype=BF16),
            shape(1, holders * listed),
            shape(depth * column, 1),
            shape(wide, wide, dtype=BF16),
            shape(wide, slots, dtype=BF16),
        ],
        small,
        through=away,
        cost=(1, 1),
    )
    for k in range(1, poses):
        rows = away[(k - 1) * depth : k * depth]
        dec_rows[k] = [rotate(row, "pos", k) for row in rows]
    dec_rows = [dec_rows[k][l] for l in range(depth) for k in range(poses)]

    for _ in range(2, feats):
        ring.append([ring_next(rows, "feat") for rows in ring[-1]])

    def products(first, enc, dec, layer_row, placing_t):
        enc = jnp.concatenate(enc, axis=0)
        every = dot(dec, enc, NT)
        lanes = slice(first * listed, first * listed + enc.shape[0])
        raw = jnp.zeros((column, enc.shape[0]), F32)
        for l in range(depth):
            rows = every[l * column : (l + 1) * column]
            raw = raw + jnp.where(layer_row[:, lanes] == l + 1.0, rows, 0.0)
        split = dot(jnp.concatenate(pieces(raw), axis=0), placing_t[lanes])
        return split[:column] + (split[column : 2 * column] + split[2 * column :])

    def early(layer_row, placing_t, gains, *values):
        count = depth * poses
        dec = jnp.concatenate(values[-count:], axis=0)
        dec = (dec.astype(F32) * gains).astype(BF16)
        return products(0, values[:-count], dec, layer_row, placing_t), dec

    def late(layer_row, placing_t, so_far, dec, *values):
        raw = so_far + products(soon, values, dec, layer_row, placing_t)
        return (jnp.concatenate([pack_rests(raw[:half]), pack_rests(raw[half:])], axis=0),)

    so_far, scaled = on_core(
        early,
        [layer_row, placing_t, gains] + [ring[k][q] for k, q in order[:soon]] + dec_rows,
        [shape(column, wide), shape(depth * column, width, dtype=BF16)],
        small,
        cost=(1, 1),
    )
    (partial,) = on_core(
        late,
        [layer_row, placing_t, so_far, scaled] + [ring[k][q] for k, q in order[soon:]],
        [shape(reps * len(bins) * GROUP, wide)],
        small,
    )
    columns = (partial + rotate(partial, "rep", 1)).astype(BF16)

    far = []
    for bits in range(2, feats, 2):
        pairs = [
            (f * reps + r, (f ^ (bits + r)) * reps + r) for f in range(feats) for r in range(reps)
        ]
        far.append(lax.ppermute(columns, ("feat", "rep"), pairs))
    rows = len(bins) * GROUP
    own_half = jnp.where(lax.axis_index("rep") == 0, columns[:rows], columns[rows:])
    near = lax.ppermute(own_half, "feat", [(f, f ^ 1) for f in range(feats)])
    across = [rotate(shard, "rep", 1) for shard in far + [near]]

    def finish(placing, mask, squeeze, targets, *values):
        feat, _, rep = place()
        first = rep == 0.0
        chips = []
        for mine, other in zip(values[1 : len(far) + 2], values[len(far) + 2 :]):
            chips += [jnp.where(first, mine, other), jnp.where(first, other, mine)]
        chips = [values[0], jnp.concatenate(chips[-reps:], axis=0)] + chips[:-reps]
        padded = []
        for chip in chips:
            chip = chip.astype(F32) if small else chip
            padded += [unpack_rests(chip, r * len(bins)) for r in range(reps)]
        padded = jnp.concatenate(padded, axis=0)
        unused = [jnp.zeros((span - block_rows, holders * listed), BF16)]
        unused = unused if span > block_rows else []
        sources = []
        for f in range(feats):
            sources += [placing[f * block_rows : (f + 1) * block_rows]] + unused
        sources = jnp.concatenate(sources, axis=0)
        edges = dot(sources, padded) * mask.astype(F32)
        magnitude = jnp.abs(edges)
        total = jnp.maximum(jnp.sum(magnitude, axis=0, keepdims=True), 1.0)
        magnitude = magnitude.astype(BF16)
        diagonal = iota((wide, wide), 0) == iota((wide, wide), 1)
        scale = 1.0 / jnp.sum(jnp.where(diagonal, total, 0.0), axis=1, keepdims=True)
        targets = targets.astype(F32)
        targets = targets + floor_div(targets, block_rows) * (span - block_rows)
        current = (iota((wide, panel), 0) == targets).astype(F32)
        accum = jnp.zeros((wide, panel), F32)
        for _ in range(ITERS):
            scaled = current * scale
            high = part(scaled, small)
            low = part(scaled - high.astype(F32), small)
            both = dot(magnitude, jnp.concatenate([high, low], axis=1))
            current = both[:, :panel] + both[:, panel:]
            accum = accum + current
        influence = accum[:result_rows]
        for f in range(feats):
            for r in range(reps):
                at = f * span + r * result_rows
                mine = (feat == f) & (rep == r)
                influence = jnp.where(mine, accum[at : at + result_rows], influence)
        start = feat * span + rep * result_rows
        own = start + iota((result_rows, wide), 0) == iota((result_rows, wide), 1)
        rows = dot(own.astype(BF16), edges.astype(BF16), NT).astype(BF16)
        edges = dot(rows, squeeze).astype(BF16)
        return edges[None], (influence * float(slots))[None]

    edges, influence = on_core(
        finish,
        [placing, mask, squeeze, target_slots, columns] + far + [near] + across,
        [shape(1, result_rows, slots, dtype=BF16), shape(1, result_rows, panel)],
        small,
    )
    return edges, influence


def solution(mesh):
    return jax.shard_map(
        per_device,
        mesh=mesh,
        in_specs=(
            P(("grp", "pos"), "feat", None),
            P(("grp", "pos"), "feat", None),
            P(("grp", "pos"), None, None),
            P(("grp", "pos"), None),
            P(("feat", "pos"), "rep"),
            P(("feat", "pos"), None, "rep"),
        ),
        out_specs=(
            P(("grp", "pos"), ("feat", "rep"), None),
            P(("grp", "pos"), ("feat", "rep"), None),
        ),
        check_vma=False,
    )
```

```python
import jax
import jax.numpy as jnp
from jax import lax
from jax.experimental import pallas as pl
from jax.experimental.pallas import tpu as pltpu
from jax.sharding import PartitionSpec as P

ITERS = 3
F32 = jnp.float32
BF16 = jnp.bfloat16
NN = (((1,), (0,)), ((), ()))
NT = (((1,), (1,)), ((), ()))
LANES = 128
GROUP = 8
KERNEL_SLOTS = 1024


def dot(a, b, dims=NN):
    return lax.dot_general(a, b, dims, preferred_element_type=F32)


def iota(shape, dim):
    return lax.broadcasted_iota(jnp.int32, shape, dim).astype(F32)


def floor_div(x, n):
    return jnp.floor((x + 0.5) * (1.0 / n))


def on_core(fn, args, outs, kernel=True, through=(), streams=(), cost=None, room=24):
    if not kernel:
        loads = [lambda i, x=x: x[i] for x in streams]
        return list(fn(*args, *loads)) + list(through)
    count, passed, streamed = len(args), len(through), len(streams)

    def body(*refs):
        sources = refs[count : count + streamed]
        results = refs[count + streamed + passed :][: len(outs)]
        scratch = refs[len(refs) - 2 * streamed :]
        copies = []
        for n in range(streamed):
            copies.append(
                [
                    pltpu.make_async_copy(
                        sources[n].at[i], scratch[2 * n].at[i], scratch[2 * n + 1].at[i]
                    )
                    for i in range(streams[n].shape[0])
                ]
            )
            for copy in copies[-1]:
                copy.start()

        def load(n):
            def wait(i):
                copies[n][i].wait()
                return scratch[2 * n][i]

            return wait

        values = fn(*[ref[...] for ref in refs[:count]], *[load(n) for n in range(streamed)])
        for ref, value in zip(results, values):
            ref[...] = value

    estimate = None
    if cost is not None:
        estimate = pl.CostEstimate(flops=cost[0], bytes_accessed=cost[1], transcendentals=0)
    in_vmem = pl.BlockSpec(memory_space=pltpu.VMEM)
    anywhere = pl.BlockSpec(memory_space=pl.ANY)
    scratch = []
    for x in streams:
        scratch += [pltpu.VMEM(x.shape, x.dtype), pltpu.SemaphoreType.DMA((x.shape[0],))]
    call = pl.pallas_call(
        body,
        out_shape=list(outs) + [jax.ShapeDtypeStruct(x.shape, x.dtype) for x in through],
        in_specs=[in_vmem] * count
        + [pl.BlockSpec(memory_space=pltpu.HBM)] * streamed
        + [anywhere] * passed,
        out_specs=[in_vmem] * len(outs) + [anywhere] * passed,
        scratch_shapes=scratch,
        input_output_aliases={count + streamed + i: len(outs) + i for i in range(passed)},
        compiler_params=pltpu.CompilerParams(vmem_limit_bytes=room * 1024 * 1024),
        cost_estimate=estimate,
    )
    return list(call(*args, *streams, *through))


def rotate(x, axis, step):
    count = lax.axis_size(axis)
    return lax.ppermute(x, axis, [(i, (i + step) % count) for i in range(count)])


def ring_place(index, count):
    low = floor_div(index, 2)
    return jnp.where(index > 2 * low, count - 1 - low, low)


def ring_next(x, axis, across=None, turn=0):
    count = lax.axis_size(axis)
    order = list(range(0, count, 2)) + list(range(1, count, 2))[::-1]
    steps = [(order[i], order[(i + 1) % count]) for i in range(count)]
    if across is None:
        return lax.ppermute(x, axis, steps)
    wide = lax.axis_size(across)
    pairs = [(a * wide + i, b * wide + (i + turn) % wide) for a, b in steps for i in range(wide)]
    return lax.ppermute(x, (axis, across), pairs)


def part(x, kernel):
    return x.astype(BF16) if kernel else lax.reduce_precision(x, 8, 7).astype(BF16)


def shape(*dims, dtype=F32):
    return jax.ShapeDtypeStruct(dims, dtype)


def per_device(active_ids, active_vals, block_pattern, target_slots, encoder, decoder):
    feats = lax.axis_size("feat")
    poses = lax.axis_size("pos")
    reps = lax.axis_size("rep")
    holders = feats * poses
    table_rows, width = encoder.shape
    depth = decoder.shape[1]
    layers = depth + 1
    positions, kslots = active_ids.shape[1:]
    block_rows = positions * kslots
    slots = block_rows * feats
    capacity = max(2, (10 * block_rows + 7 * holders - 1) // (7 * holders))
    listed = capacity * feats
    column = poses * listed
    half = column // reps
    result_rows = block_rows // reps
    panel = target_slots.shape[1]
    small = slots <= KERNEL_SLOTS
    span = -(-block_rows // LANES) * LANES if small else block_rows
    wide = feats * span

    rests = []
    for row in range(0, half, GROUP):
        rests.append((row, row % listed // capacity))
    bins = []
    for rest in sorted(rests, key=lambda rest: rest[1]):
        for row in bins:
            if sum(feats - block for _, block in row) + feats - rest[1] <= feats:
                row.append(rest)
                break
        else:
            bins.append([rest])

    def pack_rests(x):
        rows = []
        for row in bins:
            parts = [x[at : at + GROUP, block * span :] for at, block in row]
            empty = wide - sum(part.shape[1] for part in parts)
            parts += [jnp.zeros((GROUP, empty), x.dtype)] if empty else []
            rows.append(jnp.concatenate(parts, axis=1) if len(parts) > 1 else parts[0])
        return jnp.concatenate(rows, axis=0)

    def unpack_rests(x, first):
        found = {}
        for n, row in enumerate(bins):
            lane = 0
            for at, block in row:
                at_row = (first + n) * GROUP
                rest = x[at_row : at_row + GROUP, lane : lane + wide - block * span]
                lane += wide - block * span
                if block:
                    rest = jnp.concatenate([jnp.zeros((GROUP, block * span), x.dtype), rest], axis=1)
                found[at] = rest
        return jnp.concatenate([found[at] for at, _ in rests], axis=0).astype(BF16)

    def place():
        feat, pos = lax.axis_index("feat"), lax.axis_index("pos")
        return feat.astype(F32), pos.astype(F32), lax.axis_index("rep").astype(F32)

    def pack(ids, vals):
        one = jnp.concatenate([ids(0).astype(F32), vals(0)], axis=0)
        one = jnp.concatenate([one, jnp.zeros((2 * positions, LANES - kslots), F32)], axis=1)
        return (jnp.broadcast_to(one, (holders,) + one.shape),)

    (packed,) = on_core(
        pack,
        [],
        [shape(holders, 2 * positions, LANES)],
        streams=[active_ids, active_vals],
        room=60,
    )
    lists = lax.all_to_all(packed, ("feat", "pos"), split_axis=0, concat_axis=0, tiled=True)

    def list_of(values, prompt):
        blocks = []
        for a in range(feats):
            block = values[a * poses]
            for q in range(1, poses):
                block = jnp.where(prompt == q, values[a * poses + q], block)
            blocks.append(block)
        return jnp.concatenate(blocks, axis=0)[:, :kslots]

    def list_row(slot):
        place = floor_div(slot, kslots)
        return place + floor_div(place, positions) * positions

    def slot_entry(slot):
        return slot - floor_div(slot, kslots) * kslots

    def pieces(table):
        high = part(table, small)
        rest = table - high.astype(F32)
        middle = part(rest, small)
        return [high, middle, part(rest - middle.astype(F32), small)]

    def as_rows(table, slot_at, lanes):
        entry = slot_entry(slot_at(iota((kslots, lanes), 1)))
        spread = (iota((kslots, lanes), 0) == entry).astype(BF16)
        every = dot(jnp.concatenate(pieces(table), axis=0), spread)
        count = table.shape[0]
        every = every[:count] + (every[count : 2 * count] + every[2 * count :])
        row = iota(every.shape, 0) - list_row(slot_at(iota(every.shape, 1)))
        ids = jnp.sum(jnp.where(row == 0, every, 0.0), axis=0, keepdims=True)
        return ids, jnp.sum(jnp.where(row == positions, every, 0.0), axis=0, keepdims=True)

    def spread_slot(lane):
        block = floor_div(lane, span)
        inside = lane - block * span
        return jnp.where(inside < block_rows, block * block_rows + inside, -1.0 * slots)

    def as_col(table):
        wide = (slots, table.shape[0])
        spread = (list_row(iota(wide, 0)) == iota(wide, 1)).astype(BF16)
        every = dot(spread, jnp.concatenate(pieces(table), axis=1))
        every = every[:, :kslots] + (every[:, kslots : 2 * kslots] + every[:, 2 * kslots :])
        mine = slot_entry(iota((slots, kslots), 0)) == iota((slots, kslots), 1)
        return jnp.sum(jnp.where(mine, every, 0.0), axis=1, keepdims=True)

    def choose(values):
        feat, pos, _ = place()
        own = feat * poses + pos
        tables = []
        rows = []
        for k in range(poses):
            prompt = jnp.where(pos + k >= poses, pos + k - poses, pos + k)
            tables.append(list_of(values, prompt))
            rows.append(as_rows(tables[k], lambda lane: lane, slots)[0])
        hits = [floor_div(ids, table_rows) == own for ids in rows]
        earlier = (iota((slots, slots), 0) < iota((slots, slots), 1)).astype(BF16)
        ranks = dot(jnp.concatenate([h.astype(BF16) for h in hits], axis=0), earlier)
        picks = []
        for k in range(poses):
            chosen = jnp.where(
                hits[k] & (ranks[k : k + 1] == iota((listed, slots), 0)), 1.0, 0.0
            )
            local = jnp.sum(chosen * (rows[k] - own * table_rows + 1.0), axis=1, keepdims=True)
            picks.append((local - 1.0 == iota((listed, table_rows), 1)).astype(BF16))
        return jnp.concatenate(picks, axis=0), tables[0]

    picks, my_list = on_core(
        choose,
        [lists],
        [shape(column, table_rows, dtype=BF16), shape(2 * positions * feats, kslots)],
        small,
        cost=(10**9, 10**7),
    )

    def encode(picks, enc):
        rows = dot(picks, enc).astype(BF16)
        return [rows[k * listed : (k + 1) * listed] for k in range(poses)] + [picks]

    *enc_rows, picks = on_core(
        encode,
        [picks, encoder],
        [shape(listed, width, dtype=BF16)] * poses + [shape(column, table_rows, dtype=BF16)],
        small,
    )

    ring = [[enc_rows[0]] + [rotate(enc_rows[k], "pos", k) for k in range(1, poses)]]
    ring.append([ring_next(enc_rows[k], "feat", "pos", k) for k in range(poses)])

    dec_rows = lax.dot_general(
        picks, decoder, (((1,), (0,)), ((), ())), preferred_element_type=F32
    )
    dec_rows = jnp.transpose(dec_rows, (1, 0, 2)).astype(BF16)
    dec_rows = [
        [dec_rows[l, k * listed : (k + 1) * listed] for l in range(depth)] for k in range(poses)
    ]
    away = [rows for k in range(1, poses) for rows in dec_rows[k]]
    order = [(0, 0)] + [(k, q) for k in range(1, feats - 1) for q in range(poses)]
    soon = len(order)
    order += [(0, q) for q in range(1, poses)] + [(feats - 1, q) for q in range(poses)]
    own_lists = [order.index((0, q)) for q in range(poses)]

    def places(table, pattern):
        feat, pos, rep = place()

        def turned(owner):
            turn = pos - (owner - floor_div(owner, poses) * poses)
            return jnp.where(turn < 0.0, turn + poses, turn)

        def spread_place(owner, rank):
            feat_of = floor_div(owner, poses).astype(jnp.int32)
            bits = (feat.astype(jnp.int32) ^ feat_of).astype(F32)
            return (bits * poses + turned(owner)) * listed + rank

        def padded(owner, rank):
            feat_of = floor_div(owner, poses)
            turn = turned(owner)
            step = ring_place(feat, feats) - ring_place(feat_of, feats)
            step = jnp.where(step < 0.0, step + feats, step)
            at = step * poses + turn
            at = jnp.where(step < feats - 1.0, at - (poses - 1), at)
            at = jnp.where(step == 0.0, turn + (feats - 2) * poses, at)
            at = jnp.where((step == 0.0) & (turn == 0.0), 0.0, at)
            return at * listed + rank

        ids_row, vals_row = as_rows(table, spread_slot, wide)
        ids_col = as_col(table)
        owner_row = floor_div(ids_row, table_rows)
        owner_col = floor_div(ids_col, table_rows)
        down, across = iota((slots, slots), 0), iota((slots, slots), 1)
        same = owner_col == floor_div(as_rows(table, lambda lane: lane, slots)[0], table_rows)
        rank_col = jnp.sum(jnp.where(same & (across < down), 1.0, 0.0), axis=1, keepdims=True)
        slot = spread_slot(iota((slots, wide), 1))
        same = (owner_col == owner_row) & (iota((slots, wide), 0) < slot)
        rank_row = jnp.sum(jnp.where(same, 1.0, 0.0), axis=0, keepdims=True)
        total = holders * listed
        used = spread_slot(iota((1, wide), 1)) >= 0.0
        place_row = jnp.where(used, padded(owner_row, rank_row), -1.0)
        placing = spread_place(owner_col, rank_col) == iota((slots, total), 1)
        entry = padded(owner_col, rank_col) == iota((slots, total), 1)
        placing_t = place_row == iota((total, wide), 0)
        layer = ids_col - floor_div(ids_col, layers) * layers
        layer_row = jnp.sum(jnp.where(entry, layer, 0.0), axis=0, keepdims=True)
        mine = [placing_t[at * listed : (at + 1) * listed] for at in own_lists]
        mine = jnp.concatenate(mine, axis=0)
        gain = jnp.sum(jnp.where(mine, vals_row, 0.0), axis=1, keepdims=True)
        source_layer = ids_row - floor_div(ids_row, layers) * layers
        source_layer = jnp.sum(jnp.where(mine, source_layer, 0.0), axis=1, keepdims=True)
        gains = jnp.concatenate(
            [jnp.where(source_layer <= l, gain, 0.0) for l in range(depth)], axis=0
        )
        allowed = jnp.where(pattern[0] == 1, 1.0, 0.0).astype(BF16)

        sources = (floor_div(iota((wide, 1), 0), span) == iota((wide, feats), 1)).astype(BF16)
        targets = (floor_div(iota((1, wide), 1), span) == iota((feats, wide), 0)).astype(BF16)
        mask = dot(dot(sources, allowed, NT).astype(BF16), targets)
        source = floor_div(spread_slot(iota((wide, wide), 0)), kslots)
        target = floor_div(spread_slot(iota((wide, wide), 1)), kslots)
        mask = jnp.where(source <= target, mask, 0.0)
        squeeze = spread_slot(iota((wide, slots), 0)) == iota((wide, slots), 1)
        placing, placing_t = placing.astype(BF16), placing_t.astype(BF16)
        return placing, placing_t, layer_row, gains, mask.astype(BF16), squeeze.astype(BF16)

    placing, placing_t, layer_row, gains, mask, squeeze, *away = on_core(
        places,
        [my_list, block_pattern],
        [
            shape(slots, holders * listed, dtype=BF16),
            shape(holders * listed, wide, dtype=BF16),
            shape(1, holders * listed),
            shape(depth * column, 1),
            shape(wide, wide, dtype=BF16),
            shape(wide, slots, dtype=BF16),
        ],
        small,
        through=away,
        cost=(1, 1),
    )
    for k in range(1, poses):
        rows = away[(k - 1) * depth : k * depth]
        dec_rows[k] = [rotate(row, "pos", k) for row in rows]
    dec_rows = [dec_rows[k][l] for l in range(depth) for k in range(poses)]

    for _ in range(2, feats):
        ring.append([ring_next(rows, "feat") for rows in ring[-1]])

    def products(first, enc, dec, layer_row, placing_t):
        enc = jnp.concatenate(enc, axis=0)
        every = dot(dec, enc, NT)
        lanes = slice(first * listed, first * listed + enc.shape[0])
        raw = jnp.zeros((column, enc.shape[0]), F32)
        for l in range(depth):
            rows = every[l * column : (l + 1) * column]
            raw = raw + jnp.where(layer_row[:, lanes] == l + 1.0, rows, 0.0)
        split = dot(jnp.concatenate(pieces(raw), axis=0), placing_t[lanes])
        return split[:column] + (split[column : 2 * column] + split[2 * column :])

    def early(layer_row, placing_t, gains, *values):
        count = depth * poses
        dec = jnp.concatenate(values[-count:], axis=0)
        dec = (dec.astype(F32) * gains).astype(BF16)
        return products(0, values[:-count], dec, layer_row, placing_t), dec

    def late(layer_row, placing_t, so_far, dec, *values):
        raw = so_far + products(soon, values, dec, layer_row, placing_t)
        return (jnp.concatenate([pack_rests(raw[:half]), pack_rests(raw[half:])], axis=0),)

    so_far, scaled = on_core(
        early,
        [layer_row, placing_t, gains] + [ring[k][q] for k, q in order[:soon]] + dec_rows,
        [shape(column, wide), shape(depth * column, width, dtype=BF16)],
        small,
        cost=(1, 1),
    )
    (partial,) = on_core(
        late,
        [layer_row, placing_t, so_far, scaled] + [ring[k][q] for k, q in order[soon:]],
        [shape(reps * len(bins) * GROUP, wide)],
        small,
    )
    rows = len(bins) * GROUP

    def summed(mine, other):
        both = mine + other
        own = jnp.where(place()[2] == 0.0, both[:rows], both[rows:])
        return both.astype(BF16), own.astype(BF16)

    columns, own_half = on_core(
        summed,
        [partial, rotate(partial, "rep", 1)],
        [shape(reps * rows, wide, dtype=BF16), shape(rows, wide, dtype=BF16)],
        small,
    )

    far = []
    for bits in range(2, feats, 2):
        pairs = [
            (f * reps + r, (f ^ (bits + r)) * reps + r) for f in range(feats) for r in range(reps)
        ]
        far.append(lax.ppermute(columns, ("feat", "rep"), pairs))
    near = lax.ppermute(own_half, "feat", [(f, f ^ 1) for f in range(feats)])
    across = [rotate(shard, "rep", 1) for shard in far + [near]]

    def finish(placing, mask, squeeze, targets, *values):
        feat, _, rep = place()
        first = rep == 0.0
        chips = []
        for mine, other in zip(values[1 : len(far) + 2], values[len(far) + 2 :]):
            chips += [jnp.where(first, mine, other), jnp.where(first, other, mine)]
        chips = [values[0], jnp.concatenate(chips[-reps:], axis=0)] + chips[:-reps]
        padded = []
        for chip in chips:
            chip = chip.astype(F32) if small else chip
            padded += [unpack_rests(chip, r * len(bins)) for r in range(reps)]
        padded = jnp.concatenate(padded, axis=0)
        unused = [jnp.zeros((span - block_rows, holders * listed), BF16)]
        unused = unused if span > block_rows else []
        sources = []
        for f in range(feats):
            sources += [placing[f * block_rows : (f + 1) * block_rows]] + unused
        sources = jnp.concatenate(sources, axis=0)
        edges = dot(sources, padded) * mask.astype(F32)
        magnitude = jnp.abs(edges)
        total = jnp.maximum(jnp.sum(magnitude, axis=0, keepdims=True), 1.0)
        magnitude = magnitude.astype(BF16)
        diagonal = iota((wide, wide), 0) == iota((wide, wide), 1)
        scale = 1.0 / jnp.sum(jnp.where(diagonal, total, 0.0), axis=1, keepdims=True)
        targets = targets.astype(F32)
        targets = targets + floor_div(targets, block_rows) * (span - block_rows)
        current = (iota((wide, panel), 0) == targets).astype(F32)
        accum = jnp.zeros((wide, panel), F32)
        for _ in range(ITERS):
            scaled = current * scale
            high = part(scaled, small)
            low = part(scaled - high.astype(F32), small)
            both = dot(magnitude, jnp.concatenate([high, low], axis=1))
            current = both[:, :panel] + both[:, panel:]
            accum = accum + current
        influence = accum[:result_rows]
        for f in range(feats):
            for r in range(reps):
                at = f * span + r * result_rows
                mine = (feat == f) & (rep == r)
                influence = jnp.where(mine, accum[at : at + result_rows], influence)
        start = feat * span + rep * result_rows
        own = start + iota((result_rows, wide), 0) == iota((result_rows, wide), 1)
        rows = dot(own.astype(BF16), edges.astype(BF16), NT).astype(BF16)
        edges = dot(rows, squeeze).astype(BF16)
        return edges[None], (influence * float(slots))[None]

    edges, influence = on_core(
        finish,
        [placing, mask, squeeze, target_slots, columns] + far + [near] + across,
        [shape(1, result_rows, slots, dtype=BF16), shape(1, result_rows, panel)],
        small,
    )
    return edges, influence


def solution(mesh):
    return jax.shard_map(
        per_device,
        mesh=mesh,
        in_specs=(
            P(("grp", "pos"), "feat", None),
            P(("grp", "pos"), "feat", None),
            P(("grp", "pos"), None, None),
            P(("grp", "pos"), None),
            P(("feat", "pos"), "rep"),
            P(("feat", "pos"), None, "rep"),
        ),
        out_specs=(
            P(("grp", "pos"), ("feat", "rep"), None),
            P(("grp", "pos"), ("feat", "rep"), None),
        ),
        check_vma=False,
    )
```

```python
import jax
import jax.numpy as jnp
from jax import lax
from jax.experimental import pallas as pl
from jax.experimental.pallas import tpu as pltpu
from jax.sharding import PartitionSpec as P

ITERS = 3
F32 = jnp.float32
BF16 = jnp.bfloat16
NN = (((1,), (0,)), ((), ()))
NT = (((1,), (1,)), ((), ()))
LANES = 128
GROUP = 8
KERNEL_SLOTS = 1024


def dot(a, b, dims=NN):
    return lax.dot_general(a, b, dims, preferred_element_type=F32)


def iota(shape, dim):
    return lax.broadcasted_iota(jnp.int32, shape, dim).astype(F32)


def floor_div(x, n):
    return jnp.floor((x + 0.5) * (1.0 / n))


def on_core(fn, args, outs, kernel=True, through=(), streams=(), cost=None, room=24):
    if not kernel:
        loads = [lambda i, x=x: x[i] for x in streams]
        return list(fn(*args, *loads)) + list(through)
    count, passed, streamed = len(args), len(through), len(streams)

    def body(*refs):
        sources = refs[count : count + streamed]
        results = refs[count + streamed + passed :][: len(outs)]
        scratch = refs[len(refs) - 2 * streamed :]
        copies = []
        for n in range(streamed):
            copies.append(
                [
                    pltpu.make_async_copy(
                        sources[n].at[i], scratch[2 * n].at[i], scratch[2 * n + 1].at[i]
                    )
                    for i in range(streams[n].shape[0])
                ]
            )
            for copy in copies[-1]:
                copy.start()

        def load(n):
            def wait(i):
                copies[n][i].wait()
                return scratch[2 * n][i]

            return wait

        values = fn(*[ref[...] for ref in refs[:count]], *[load(n) for n in range(streamed)])
        for ref, value in zip(results, values):
            ref[...] = value

    estimate = None
    if cost is not None:
        estimate = pl.CostEstimate(flops=cost[0], bytes_accessed=cost[1], transcendentals=0)
    in_vmem = pl.BlockSpec(memory_space=pltpu.VMEM)
    anywhere = pl.BlockSpec(memory_space=pl.ANY)
    scratch = []
    for x in streams:
        scratch += [pltpu.VMEM(x.shape, x.dtype), pltpu.SemaphoreType.DMA((x.shape[0],))]
    call = pl.pallas_call(
        body,
        out_shape=list(outs) + [jax.ShapeDtypeStruct(x.shape, x.dtype) for x in through],
        in_specs=[in_vmem] * count
        + [pl.BlockSpec(memory_space=pltpu.HBM)] * streamed
        + [anywhere] * passed,
        out_specs=[in_vmem] * len(outs) + [anywhere] * passed,
        scratch_shapes=scratch,
        input_output_aliases={count + streamed + i: len(outs) + i for i in range(passed)},
        compiler_params=pltpu.CompilerParams(vmem_limit_bytes=room * 1024 * 1024),
        cost_estimate=estimate,
    )
    return list(call(*args, *streams, *through))


def rotate(x, axis, step):
    count = lax.axis_size(axis)
    return lax.ppermute(x, axis, [(i, (i + step) % count) for i in range(count)])


def ring_place(index, count):
    low = floor_div(index, 2)
    return jnp.where(index > 2 * low, count - 1 - low, low)


def ring_next(x, axis, across=None, turn=0):
    count = lax.axis_size(axis)
    order = list(range(0, count, 2)) + list(range(1, count, 2))[::-1]
    steps = [(order[i], order[(i + 1) % count]) for i in range(count)]
    if across is None:
        return lax.ppermute(x, axis, steps)
    wide = lax.axis_size(across)
    pairs = [(a * wide + i, b * wide + (i + turn) % wide) for a, b in steps for i in range(wide)]
    return lax.ppermute(x, (axis, across), pairs)


def spread(x, axis):
    count = lax.axis_size(axis)
    found = {0: x}
    for bits in sorted(range(1, count), key=lambda bits: bits < count // 2):
        found[bits] = lax.ppermute(x, axis, [(i, i ^ bits) for i in range(count)])
    return list(found.items())


def part(x, kernel):
    return x.astype(BF16) if kernel else lax.reduce_precision(x, 8, 7).astype(BF16)


def shape(*dims, dtype=F32):
    return jax.ShapeDtypeStruct(dims, dtype)


def per_device(active_ids, active_vals, block_pattern, target_slots, encoder, decoder):
    feats = lax.axis_size("feat")
    poses = lax.axis_size("pos")
    reps = lax.axis_size("rep")
    holders = feats * poses
    table_rows, width = encoder.shape
    depth = decoder.shape[1]
    layers = depth + 1
    positions, kslots = active_ids.shape[1:]
    block_rows = positions * kslots
    slots = block_rows * feats
    capacity = max(2, (10 * block_rows + 7 * holders - 1) // (7 * holders))
    listed = capacity * feats
    column = poses * listed
    half = column // reps
    result_rows = block_rows // reps
    panel = target_slots.shape[1]
    small = slots <= KERNEL_SLOTS
    span = -(-block_rows // LANES) * LANES if small else block_rows
    wide = feats * span

    rests = []
    for row in range(0, half, GROUP):
        rests.append((row, row % listed // capacity))
    bins = []
    for rest in sorted(rests, key=lambda rest: rest[1]):
        for row in bins:
            if sum(feats - block for _, block in row) + feats - rest[1] <= feats:
                row.append(rest)
                break
        else:
            bins.append([rest])

    def pack_rests(x):
        rows = []
        for row in bins:
            parts = [x[at : at + GROUP, block * span :] for at, block in row]
            empty = wide - sum(part.shape[1] for part in parts)
            parts += [jnp.zeros((GROUP, empty), x.dtype)] if empty else []
            rows.append(jnp.concatenate(parts, axis=1) if len(parts) > 1 else parts[0])
        return jnp.concatenate(rows, axis=0)

    def unpack_rests(x):
        x = x.astype(F32) if small else x
        found = {}
        for n, row in enumerate(bins):
            lane = 0
            for at, block in row:
                rest = x[n * GROUP : (n + 1) * GROUP, lane : lane + wide - block * span]
                lane += wide - block * span
                if block:
                    rest = jnp.concatenate([jnp.zeros((GROUP, block * span), x.dtype), rest], axis=1)
                found[at] = rest
        return jnp.concatenate([found[at] for at, _ in rests], axis=0).astype(BF16)

    def place():
        feat, pos = lax.axis_index("feat"), lax.axis_index("pos")
        return feat.astype(F32), pos.astype(F32), lax.axis_index("rep").astype(F32)

    def pack(ids, vals):
        one = jnp.concatenate([ids(0).astype(F32), vals(0)], axis=0)
        one = jnp.concatenate([one, jnp.zeros((2 * positions, LANES - kslots), F32)], axis=1)
        return (jnp.broadcast_to(one, (holders,) + one.shape),)

    (packed,) = on_core(
        pack,
        [],
        [shape(holders, 2 * positions, LANES)],
        streams=[active_ids, active_vals],
        room=60,
    )
    lists = lax.all_to_all(packed, ("feat", "pos"), split_axis=0, concat_axis=0, tiled=True)

    def list_of(values, prompt):
        blocks = []
        for a in range(feats):
            block = values[a * poses]
            for q in range(1, poses):
                block = jnp.where(prompt == q, values[a * poses + q], block)
            blocks.append(block)
        return jnp.concatenate(blocks, axis=0)[:, :kslots]

    def list_row(slot):
        place = floor_div(slot, kslots)
        return place + floor_div(place, positions) * positions

    def slot_entry(slot):
        return slot - floor_div(slot, kslots) * kslots

    def pieces(table):
        high = part(table, small)
        rest = table - high.astype(F32)
        middle = part(rest, small)
        return [high, middle, part(rest - middle.astype(F32), small)]

    def as_rows(table, slot_at, lanes):
        entry = slot_entry(slot_at(iota((kslots, lanes), 1)))
        spread = (iota((kslots, lanes), 0) == entry).astype(BF16)
        every = dot(jnp.concatenate(pieces(table), axis=0), spread)
        count = table.shape[0]
        every = every[:count] + (every[count : 2 * count] + every[2 * count :])
        row = iota(every.shape, 0) - list_row(slot_at(iota(every.shape, 1)))
        ids = jnp.sum(jnp.where(row == 0, every, 0.0), axis=0, keepdims=True)
        return ids, jnp.sum(jnp.where(row == positions, every, 0.0), axis=0, keepdims=True)

    def spread_slot(lane):
        block = floor_div(lane, span)
        inside = lane - block * span
        return jnp.where(inside < block_rows, block * block_rows + inside, -1.0 * slots)

    def as_col(table):
        wide = (slots, table.shape[0])
        spread = (list_row(iota(wide, 0)) == iota(wide, 1)).astype(BF16)
        every = dot(spread, jnp.concatenate(pieces(table), axis=1))
        every = every[:, :kslots] + (every[:, kslots : 2 * kslots] + every[:, 2 * kslots :])
        mine = slot_entry(iota((slots, kslots), 0)) == iota((slots, kslots), 1)
        return jnp.sum(jnp.where(mine, every, 0.0), axis=1, keepdims=True)

    def choose(values):
        feat, pos, _ = place()
        own = feat * poses + pos
        tables = []
        rows = []
        for k in range(poses):
            prompt = jnp.where(pos + k >= poses, pos + k - poses, pos + k)
            tables.append(list_of(values, prompt))
            rows.append(as_rows(tables[k], lambda lane: lane, slots)[0])
        hits = [floor_div(ids, table_rows) == own for ids in rows]
        earlier = (iota((slots, slots), 0) < iota((slots, slots), 1)).astype(BF16)
        ranks = dot(jnp.concatenate([h.astype(BF16) for h in hits], axis=0), earlier)
        picks = []
        for k in range(poses):
            chosen = jnp.where(
                hits[k] & (ranks[k : k + 1] == iota((listed, slots), 0)), 1.0, 0.0
            )
            local = jnp.sum(chosen * (rows[k] - own * table_rows + 1.0), axis=1, keepdims=True)
            picks.append((local - 1.0 == iota((listed, table_rows), 1)).astype(BF16))
        return jnp.concatenate(picks, axis=0), tables[0]

    picks, my_list = on_core(
        choose,
        [lists],
        [shape(column, table_rows, dtype=BF16), shape(2 * positions * feats, kslots)],
        small,
        cost=(10**9, 10**7),
    )

    def encode(picks, enc):
        rows = dot(picks, enc).astype(BF16)
        return [rows[k * listed : (k + 1) * listed] for k in range(poses)] + [picks]

    *enc_rows, picks = on_core(
        encode,
        [picks, encoder],
        [shape(listed, width, dtype=BF16)] * poses + [shape(column, table_rows, dtype=BF16)],
        small,
    )

    ring = [[enc_rows[0]] + [rotate(enc_rows[k], "pos", k) for k in range(1, poses)]]
    ring.append([ring_next(enc_rows[k], "feat", "pos", k) for k in range(poses)])

    dec_rows = lax.dot_general(
        picks, decoder, (((1,), (0,)), ((), ())), preferred_element_type=F32
    )
    dec_rows = jnp.transpose(dec_rows, (1, 0, 2)).astype(BF16)
    dec_rows = [
        [dec_rows[l, k * listed : (k + 1) * listed] for l in range(depth)] for k in range(poses)
    ]
    away = [rows for k in range(1, poses) for rows in dec_rows[k]]
    order = [(0, 0)] + [(k, q) for k in range(1, feats - 1) for q in range(poses)]
    soon = len(order)
    order += [(0, q) for q in range(1, poses)] + [(feats - 1, q) for q in range(poses)]
    own_lists = [order.index((0, q)) for q in range(poses)]

    def places(table, pattern):
        feat, pos, rep = place()

        def turned(owner):
            turn = pos - (owner - floor_div(owner, poses) * poses)
            return jnp.where(turn < 0.0, turn + poses, turn)

        def spread_place(owner, rank):
            feat_of = floor_div(owner, poses).astype(jnp.int32)
            bits = (feat.astype(jnp.int32) ^ feat_of).astype(F32)
            return (bits * poses + turned(owner)) * listed + rank

        def padded(owner, rank):
            feat_of = floor_div(owner, poses)
            turn = turned(owner)
            step = ring_place(feat, feats) - ring_place(feat_of, feats)
            step = jnp.where(step < 0.0, step + feats, step)
            at = step * poses + turn
            at = jnp.where(step < feats - 1.0, at - (poses - 1), at)
            at = jnp.where(step == 0.0, turn + (feats - 2) * poses, at)
            at = jnp.where((step == 0.0) & (turn == 0.0), 0.0, at)
            return at * listed + rank

        ids_row, vals_row = as_rows(table, spread_slot, wide)
        ids_col = as_col(table)
        owner_row = floor_div(ids_row, table_rows)
        owner_col = floor_div(ids_col, table_rows)
        down, across = iota((slots, slots), 0), iota((slots, slots), 1)
        same = owner_col == floor_div(as_rows(table, lambda lane: lane, slots)[0], table_rows)
        rank_col = jnp.sum(jnp.where(same & (across < down), 1.0, 0.0), axis=1, keepdims=True)
        slot = spread_slot(iota((slots, wide), 1))
        same = (owner_col == owner_row) & (iota((slots, wide), 0) < slot)
        rank_row = jnp.sum(jnp.where(same, 1.0, 0.0), axis=0, keepdims=True)
        total = holders * listed
        used = spread_slot(iota((1, wide), 1)) >= 0.0
        place_row = jnp.where(used, padded(owner_row, rank_row), -1.0)
        placing = spread_place(owner_col, rank_col) == iota((slots, total), 1)
        entry = padded(owner_col, rank_col) == iota((slots, total), 1)
        placing_t = place_row == iota((total, wide), 0)
        layer = ids_col - floor_div(ids_col, layers) * layers
        layer_row = jnp.sum(jnp.where(entry, layer, 0.0), axis=0, keepdims=True)
        mine = [placing_t[at * listed : (at + 1) * listed] for at in own_lists]
        mine = jnp.concatenate(mine, axis=0)
        gain = jnp.sum(jnp.where(mine, vals_row, 0.0), axis=1, keepdims=True)
        source_layer = ids_row - floor_div(ids_row, layers) * layers
        source_layer = jnp.sum(jnp.where(mine, source_layer, 0.0), axis=1, keepdims=True)
        gains = jnp.concatenate(
            [jnp.where(source_layer <= l, gain, 0.0) for l in range(depth)], axis=0
        )
        allowed = jnp.where(pattern[0] == 1, 1.0, 0.0).astype(BF16)

        sources = (floor_div(iota((wide, 1), 0), span) == iota((wide, feats), 1)).astype(BF16)
        targets = (floor_div(iota((1, wide), 1), span) == iota((feats, wide), 0)).astype(BF16)
        mask = dot(dot(sources, allowed, NT).astype(BF16), targets)
        source = floor_div(spread_slot(iota((wide, wide), 0)), kslots)
        target = floor_div(spread_slot(iota((wide, wide), 1)), kslots)
        mask = jnp.where(source <= target, mask, 0.0)
        squeeze = spread_slot(iota((wide, slots), 0)) == iota((wide, slots), 1)
        placing, placing_t = placing.astype(BF16), placing_t.astype(BF16)
        unused = [jnp.zeros((span - block_rows, holders * listed), BF16)]
        unused = unused if span > block_rows else []
        spaced = []
        for f in range(feats):
            spaced += [placing[f * block_rows : (f + 1) * block_rows]] + unused
        placing = jnp.concatenate(spaced, axis=0)
        return placing, placing_t, layer_row, gains, mask.astype(BF16), squeeze.astype(BF16)

    placing, placing_t, layer_row, gains, mask, squeeze, *away = on_core(
        places,
        [my_list, block_pattern],
        [
            shape(wide, holders * listed, dtype=BF16),
            shape(holders * listed, wide, dtype=BF16),
            shape(1, holders * listed),
            shape(depth * column, 1),
            shape(wide, wide, dtype=BF16),
            shape(wide, slots, dtype=BF16),
        ],
        small,
        through=away,
        cost=(1, 1),
    )
    for k in range(1, poses):
        rows = away[(k - 1) * depth : k * depth]
        dec_rows[k] = [rotate(row, "pos", k) for row in rows]
    dec_rows = [dec_rows[k][l] for l in range(depth) for k in range(poses)]

    for _ in range(2, feats):
        ring.append([ring_next(rows, "feat") for rows in ring[-1]])

    def products(first, enc, dec, layer_row, placing_t):
        enc = jnp.concatenate(enc, axis=0)
        every = dot(dec, enc, NT)
        lanes = slice(first * listed, first * listed + enc.shape[0])
        raw = jnp.zeros((column, enc.shape[0]), F32)
        for l in range(depth):
            rows = every[l * column : (l + 1) * column]
            raw = raw + jnp.where(layer_row[:, lanes] == l + 1.0, rows, 0.0)
        split = dot(jnp.concatenate(pieces(raw), axis=0), placing_t[lanes])
        return split[:column] + (split[column : 2 * column] + split[2 * column :])

    def early(layer_row, placing_t, gains, *values):
        count = depth * poses
        dec = jnp.concatenate(values[-count:], axis=0)
        dec = (dec.astype(F32) * gains).astype(BF16)
        return products(0, values[:-count], dec, layer_row, placing_t), dec

    def late(layer_row, placing_t, so_far, dec, *values):
        raw = so_far + products(soon, values, dec, layer_row, placing_t)
        first = place()[2] == 0.0
        lower, higher = pack_rests(raw[:half]), pack_rests(raw[half:])
        return jnp.where(first, lower, higher), jnp.where(first, higher, lower)

    so_far, scaled = on_core(
        early,
        [layer_row, placing_t, gains] + [ring[k][q] for k, q in order[:soon]] + dec_rows,
        [shape(column, wide), shape(depth * column, width, dtype=BF16)],
        small,
        cost=(1, 1),
    )
    keep, send = on_core(
        late,
        [layer_row, placing_t, so_far, scaled] + [ring[k][q] for k, q in order[soon:]],
        [shape(len(bins) * GROUP, wide)] * 2,
        small,
    )
    own_edges = (keep + rotate(send, "rep", 1)).astype(BF16)
    found = spread(own_edges, "feat")
    arrival = [bits for bits, _ in found]
    shards = [shard for _, shard in found]
    others = [rotate(shard, "rep", 1) for shard in shards]

    def finish(placing, mask, squeeze, targets, *values):
        feat, _, rep = place()
        first = rep == 0.0
        chips = []
        for mine, other in zip(values[:feats], values[feats:]):
            lower, higher = jnp.where(first, mine, other), jnp.where(first, other, mine)
            chips.append(jnp.concatenate([unpack_rests(lower), unpack_rests(higher)], axis=0))
        padded = jnp.concatenate([chips[arrival.index(m)] for m in range(feats)], axis=0)
        edges = dot(placing, padded) * mask.astype(F32)
        magnitude = jnp.abs(edges)
        total = jnp.maximum(jnp.sum(magnitude, axis=0, keepdims=True), 1.0)
        magnitude = magnitude.astype(BF16)
        scale = 1.0 / jnp.transpose(jnp.broadcast_to(total, (GROUP, wide)))[:, :1]
        targets = targets.astype(F32)
        targets = targets + floor_div(targets, block_rows) * (span - block_rows)
        current = (iota((wide, panel), 0) == targets).astype(F32)
        accum = jnp.zeros((wide, panel), F32)
        for _ in range(ITERS):
            scaled = current * scale
            high = part(scaled, small)
            low = part(scaled - high.astype(F32), small)
            both = dot(magnitude, jnp.concatenate([high, low], axis=1))
            current = both[:, :panel] + both[:, panel:]
            accum = accum + current
        influence = accum[:result_rows]
        for f in range(feats):
            for r in range(reps):
                at = f * span + r * result_rows
                mine = (feat == f) & (rep == r)
                influence = jnp.where(mine, accum[at : at + result_rows], influence)
        start = feat * span + rep * result_rows
        own = start + iota((result_rows, wide), 0) == iota((result_rows, wide), 1)
        rows = dot(own.astype(BF16), edges.astype(BF16), NT).astype(BF16)
        edges = dot(rows, squeeze).astype(BF16)
        return edges[None], (influence * float(slots))[None]

    edges, influence = on_core(
        finish,
        [placing, mask, squeeze, target_slots] + shards + others,
        [shape(1, result_rows, slots, dtype=BF16), shape(1, result_rows, panel)],
        small,
    )
    return edges, influence


def solution(mesh):
    return jax.shard_map(
        per_device,
        mesh=mesh,
        in_specs=(
            P(("grp", "pos"), "feat", None),
            P(("grp", "pos"), "feat", None),
            P(("grp", "pos"), None, None),
            P(("grp", "pos"), None),
            P(("feat", "pos"), "rep"),
            P(("feat", "pos"), None, "rep"),
        ),
        out_specs=(
            P(("grp", "pos"), ("feat", "rep"), None),
            P(("grp", "pos"), ("feat", "rep"), None),
        ),
        check_vma=False,
    )
```

```python
import jax
import jax.numpy as jnp
from jax import lax
from jax.experimental import pallas as pl
from jax.experimental.pallas import tpu as pltpu
from jax.sharding import PartitionSpec as P

ITERS = 3
F32 = jnp.float32
BF16 = jnp.bfloat16
NN = (((1,), (0,)), ((), ()))
NT = (((1,), (1,)), ((), ()))
LANES = 128
GROUP = 8
KERNEL_SLOTS = 1024


def dot(a, b, dims=NN):
    return lax.dot_general(a, b, dims, preferred_element_type=F32)


def iota(shape, dim):
    return lax.broadcasted_iota(jnp.int32, shape, dim).astype(F32)


def floor_div(x, n):
    return jnp.floor((x + 0.5) * (1.0 / n))


def on_core(fn, args, outs, kernel=True, through=(), streams=(), cost=None, room=24):
    if not kernel:
        loads = [lambda i, x=x: x[i] for x in streams]
        return list(fn(*args, *loads)) + list(through)
    count, passed, streamed = len(args), len(through), len(streams)

    def body(*refs):
        sources = refs[count : count + streamed]
        results = refs[count + streamed + passed :][: len(outs)]
        scratch = refs[len(refs) - 2 * streamed :]
        copies = []
        for n in range(streamed):
            copies.append(
                [
                    pltpu.make_async_copy(
                        sources[n].at[i], scratch[2 * n].at[i], scratch[2 * n + 1].at[i]
                    )
                    for i in range(streams[n].shape[0])
                ]
            )
            for copy in copies[-1]:
                copy.start()

        def load(n):
            def wait(i):
                copies[n][i].wait()
                return scratch[2 * n][i]

            return wait

        values = fn(*[ref[...] for ref in refs[:count]], *[load(n) for n in range(streamed)])
        for ref, value in zip(results, values):
            ref[...] = value

    estimate = None
    if cost is not None:
        estimate = pl.CostEstimate(flops=cost[0], bytes_accessed=cost[1], transcendentals=0)
    in_vmem = pl.BlockSpec(memory_space=pltpu.VMEM)
    anywhere = pl.BlockSpec(memory_space=pl.ANY)
    scratch = []
    for x in streams:
        scratch += [pltpu.VMEM(x.shape, x.dtype), pltpu.SemaphoreType.DMA((x.shape[0],))]
    call = pl.pallas_call(
        body,
        out_shape=list(outs) + [jax.ShapeDtypeStruct(x.shape, x.dtype) for x in through],
        in_specs=[in_vmem] * count
        + [pl.BlockSpec(memory_space=pltpu.HBM)] * streamed
        + [anywhere] * passed,
        out_specs=[in_vmem] * len(outs) + [anywhere] * passed,
        scratch_shapes=scratch,
        input_output_aliases={count + streamed + i: len(outs) + i for i in range(passed)},
        compiler_params=pltpu.CompilerParams(vmem_limit_bytes=room * 1024 * 1024),
        cost_estimate=estimate,
    )
    return list(call(*args, *streams, *through))


def rotate(x, axis, step):
    count = lax.axis_size(axis)
    return lax.ppermute(x, axis, [(i, (i + step) % count) for i in range(count)])


def ring_place(index, count):
    low = floor_div(index, 2)
    return jnp.where(index > 2 * low, count - 1 - low, low)


def ring_next(x, axis, across=None, turn=0):
    count = lax.axis_size(axis)
    order = list(range(0, count, 2)) + list(range(1, count, 2))[::-1]
    steps = [(order[i], order[(i + 1) % count]) for i in range(count)]
    if across is None:
        return lax.ppermute(x, axis, steps)
    wide = lax.axis_size(across)
    pairs = [(a * wide + i, b * wide + (i + turn) % wide) for a, b in steps for i in range(wide)]
    return lax.ppermute(x, (axis, across), pairs)


def spread(x, axis):
    count = lax.axis_size(axis)
    found = {0: x}
    for bits in sorted(range(1, count), key=lambda bits: bits < count // 2):
        found[bits] = lax.ppermute(x, axis, [(i, i ^ bits) for i in range(count)])
    return list(found.items())


def part(x, kernel):
    return x.astype(BF16) if kernel else lax.reduce_precision(x, 8, 7).astype(BF16)


def shape(*dims, dtype=F32):
    return jax.ShapeDtypeStruct(dims, dtype)


def per_device(active_ids, active_vals, block_pattern, target_slots, encoder, decoder):
    feats = lax.axis_size("feat")
    poses = lax.axis_size("pos")
    reps = lax.axis_size("rep")
    holders = feats * poses
    table_rows, width = encoder.shape
    depth = decoder.shape[1]
    layers = depth + 1
    positions, kslots = active_ids.shape[1:]
    block_rows = positions * kslots
    slots = block_rows * feats
    capacity = max(2, (10 * block_rows + 7 * holders - 1) // (7 * holders))
    listed = capacity * feats
    column = poses * listed
    half = column // reps
    result_rows = block_rows // reps
    panel = target_slots.shape[1]
    small = slots <= KERNEL_SLOTS
    span = -(-block_rows // LANES) * LANES if small else block_rows
    wide = feats * span

    rests = []
    for row in range(0, half, GROUP):
        rests.append((row, row % listed // capacity))
    bins = []
    for rest in sorted(rests, key=lambda rest: rest[1]):
        for row in bins:
            if sum(feats - block for _, block in row) + feats - rest[1] <= feats:
                row.append(rest)
                break
        else:
            bins.append([rest])

    def pack_rests(x):
        rows = []
        for row in bins:
            parts = [x[at : at + GROUP, block * span :] for at, block in row]
            empty = wide - sum(part.shape[1] for part in parts)
            parts += [jnp.zeros((GROUP, empty), x.dtype)] if empty else []
            rows.append(jnp.concatenate(parts, axis=1) if len(parts) > 1 else parts[0])
        return jnp.concatenate(rows, axis=0)

    def unpack_rests(x):
        x = x.astype(F32) if small else x
        found = {}
        for n, row in enumerate(bins):
            lane = 0
            for at, block in row:
                rest = x[n * GROUP : (n + 1) * GROUP, lane : lane + wide - block * span]
                lane += wide - block * span
                if block:
                    rest = jnp.concatenate([jnp.zeros((GROUP, block * span), x.dtype), rest], axis=1)
                found[at] = rest
        return jnp.concatenate([found[at] for at, _ in rests], axis=0).astype(BF16)

    def place():
        feat, pos = lax.axis_index("feat"), lax.axis_index("pos")
        return feat.astype(F32), pos.astype(F32), lax.axis_index("rep").astype(F32)

    def pack(ids, vals):
        one = jnp.concatenate([ids[0].astype(F32), vals[0]], axis=0)
        one = jnp.concatenate([one, jnp.zeros((2 * positions, LANES - kslots), F32)], axis=1)
        return (jnp.broadcast_to(one, (holders,) + one.shape),)

    (packed,) = on_core(
        pack,
        [active_ids, active_vals],
        [shape(holders, 2 * positions, LANES)],
        room=60,
    )
    lists = lax.all_to_all(packed, ("feat", "pos"), split_axis=0, concat_axis=0, tiled=True)

    def list_of(values, prompt):
        blocks = []
        for a in range(feats):
            block = values[a * poses]
            for q in range(1, poses):
                block = jnp.where(prompt == q, values[a * poses + q], block)
            blocks.append(block)
        return jnp.concatenate(blocks, axis=0)[:, :kslots]

    def list_row(slot):
        place = floor_div(slot, kslots)
        return place + floor_div(place, positions) * positions

    def slot_entry(slot):
        return slot - floor_div(slot, kslots) * kslots

    def pieces(table):
        high = part(table, small)
        rest = table - high.astype(F32)
        middle = part(rest, small)
        return [high, middle, part(rest - middle.astype(F32), small)]

    def as_rows(table, slot_at, lanes):
        entry = slot_entry(slot_at(iota((kslots, lanes), 1)))
        spread = (iota((kslots, lanes), 0) == entry).astype(BF16)
        every = dot(jnp.concatenate(pieces(table), axis=0), spread)
        count = table.shape[0]
        every = every[:count] + (every[count : 2 * count] + every[2 * count :])
        row = iota(every.shape, 0) - list_row(slot_at(iota(every.shape, 1)))
        ids = jnp.sum(jnp.where(row == 0, every, 0.0), axis=0, keepdims=True)
        return ids, jnp.sum(jnp.where(row == positions, every, 0.0), axis=0, keepdims=True)

    def spread_slot(lane):
        block = floor_div(lane, span)
        inside = lane - block * span
        return jnp.where(inside < block_rows, block * block_rows + inside, -1.0 * slots)

    def as_col(table):
        wide = (slots, table.shape[0])
        spread = (list_row(iota(wide, 0)) == iota(wide, 1)).astype(BF16)
        every = dot(spread, jnp.concatenate(pieces(table), axis=1))
        every = every[:, :kslots] + (every[:, kslots : 2 * kslots] + every[:, 2 * kslots :])
        mine = slot_entry(iota((slots, kslots), 0)) == iota((slots, kslots), 1)
        return jnp.sum(jnp.where(mine, every, 0.0), axis=1, keepdims=True)

    def choose(values):
        feat, pos, _ = place()
        own = feat * poses + pos
        tables = []
        rows = []
        for k in range(poses):
            prompt = jnp.where(pos + k >= poses, pos + k - poses, pos + k)
            tables.append(list_of(values, prompt))
            rows.append(as_rows(tables[k], lambda lane: lane, slots)[0])
        hits = [floor_div(ids, table_rows) == own for ids in rows]
        earlier = (iota((slots, slots), 0) < iota((slots, slots), 1)).astype(BF16)
        ranks = dot(jnp.concatenate([h.astype(BF16) for h in hits], axis=0), earlier)
        picks = []
        for k in range(poses):
            chosen = jnp.where(
                hits[k] & (ranks[k : k + 1] == iota((listed, slots), 0)), 1.0, 0.0
            )
            local = jnp.sum(chosen * (rows[k] - own * table_rows + 1.0), axis=1, keepdims=True)
            picks.append((local - 1.0 == iota((listed, table_rows), 1)).astype(BF16))
        return jnp.concatenate(picks, axis=0), tables[0]

    picks, my_list = on_core(
        choose,
        [lists],
        [shape(column, table_rows, dtype=BF16), shape(2 * positions * feats, kslots)],
        small,
        cost=(10**9, 10**7),
    )

    def encode(picks, enc):
        rows = dot(picks, enc).astype(BF16)
        return [rows[k * listed : (k + 1) * listed] for k in range(poses)] + [picks]

    *enc_rows, picks = on_core(
        encode,
        [picks, encoder],
        [shape(listed, width, dtype=BF16)] * poses + [shape(column, table_rows, dtype=BF16)],
        small,
    )

    ring = [[enc_rows[0]] + [rotate(enc_rows[k], "pos", k) for k in range(1, poses)]]
    ring.append([ring_next(enc_rows[k], "feat", "pos", k) for k in range(poses)])

    dec_rows = lax.dot_general(
        picks, decoder, (((1,), (0,)), ((), ())), preferred_element_type=F32
    )
    dec_rows = jnp.transpose(dec_rows, (1, 0, 2)).astype(BF16)
    dec_rows = [
        [dec_rows[l, k * listed : (k + 1) * listed] for l in range(depth)] for k in range(poses)
    ]
    away = [rows for k in range(1, poses) for rows in dec_rows[k]]
    order = [(0, 0)] + [(k, q) for k in range(1, feats - 1) for q in range(poses)]
    soon = len(order)
    order += [(0, q) for q in range(1, poses)] + [(feats - 1, q) for q in range(poses)]
    own_lists = [order.index((0, q)) for q in range(poses)]

    def places(table, pattern):
        feat, pos, rep = place()

        def turned(owner):
            turn = pos - (owner - floor_div(owner, poses) * poses)
            return jnp.where(turn < 0.0, turn + poses, turn)

        def spread_place(owner, rank):
            feat_of = floor_div(owner, poses).astype(jnp.int32)
            bits = (feat.astype(jnp.int32) ^ feat_of).astype(F32)
            return (bits * poses + turned(owner)) * listed + rank

        def padded(owner, rank):
            feat_of = floor_div(owner, poses)
            turn = turned(owner)
            step = ring_place(feat, feats) - ring_place(feat_of, feats)
            step = jnp.where(step < 0.0, step + feats, step)
            at = step * poses + turn
            at = jnp.where(step < feats - 1.0, at - (poses - 1), at)
            at = jnp.where(step == 0.0, turn + (feats - 2) * poses, at)
            at = jnp.where((step == 0.0) & (turn == 0.0), 0.0, at)
            return at * listed + rank

        ids_row, vals_row = as_rows(table, spread_slot, wide)
        ids_col = as_col(table)
        owner_row = floor_div(ids_row, table_rows)
        owner_col = floor_div(ids_col, table_rows)
        down, across = iota((slots, slots), 0), iota((slots, slots), 1)
        same = owner_col == floor_div(as_rows(table, lambda lane: lane, slots)[0], table_rows)
        rank_col = jnp.sum(jnp.where(same & (across < down), 1.0, 0.0), axis=1, keepdims=True)
        slot = spread_slot(iota((slots, wide), 1))
        same = (owner_col == owner_row) & (iota((slots, wide), 0) < slot)
        rank_row = jnp.sum(jnp.where(same, 1.0, 0.0), axis=0, keepdims=True)
        total = holders * listed
        used = spread_slot(iota((1, wide), 1)) >= 0.0
        place_row = jnp.where(used, padded(owner_row, rank_row), -1.0)
        placing = spread_place(owner_col, rank_col) == iota((slots, total), 1)
        entry = padded(owner_col, rank_col) == iota((slots, total), 1)
        placing_t = place_row == iota((total, wide), 0)
        layer = ids_col - floor_div(ids_col, layers) * layers
        layer_row = jnp.sum(jnp.where(entry, layer, 0.0), axis=0, keepdims=True)
        mine = [placing_t[at * listed : (at + 1) * listed] for at in own_lists]
        mine = jnp.concatenate(mine, axis=0)
        gain = jnp.sum(jnp.where(mine, vals_row, 0.0), axis=1, keepdims=True)
        source_layer = ids_row - floor_div(ids_row, layers) * layers
        source_layer = jnp.sum(jnp.where(mine, source_layer, 0.0), axis=1, keepdims=True)
        gains = jnp.concatenate(
            [jnp.where(source_layer <= l, gain, 0.0) for l in range(depth)], axis=0
        )
        allowed = jnp.where(pattern[0] == 1, 1.0, 0.0).astype(BF16)

        sources = (floor_div(iota((wide, 1), 0), span) == iota((wide, feats), 1)).astype(BF16)
        targets = (floor_div(iota((1, wide), 1), span) == iota((feats, wide), 0)).astype(BF16)
        mask = dot(dot(sources, allowed, NT).astype(BF16), targets)
        source = floor_div(spread_slot(iota((wide, wide), 0)), kslots)
        target = floor_div(spread_slot(iota((wide, wide), 1)), kslots)
        mask = jnp.where(source <= target, mask, 0.0)
        squeeze = spread_slot(iota((wide, slots), 0)) == iota((wide, slots), 1)
        placing, placing_t = placing.astype(BF16), placing_t.astype(BF16)
        return placing, placing_t, layer_row, gains, mask.astype(BF16), squeeze.astype(BF16)

    placing, placing_t, layer_row, gains, mask, squeeze, *away = on_core(
        places,
        [my_list, block_pattern],
        [
            shape(slots, holders * listed, dtype=BF16),
            shape(holders * listed, wide, dtype=BF16),
            shape(1, holders * listed),
            shape(depth * column, 1),
            shape(wide, wide, dtype=BF16),
            shape(wide, slots, dtype=BF16),
        ],
        small,
        through=away,
        cost=(1, 1),
    )
    for k in range(1, poses):
        rows = away[(k - 1) * depth : k * depth]
        dec_rows[k] = [rotate(row, "pos", k) for row in rows]
    dec_rows = [dec_rows[k][l] for l in range(depth) for k in range(poses)]

    for _ in range(2, feats):
        ring.append([ring_next(rows, "feat") for rows in ring[-1]])

    def products(first, enc, dec, layer_row, placing_t):
        enc = jnp.concatenate(enc, axis=0)
        every = dot(dec, enc, NT)
        lanes = slice(first * listed, first * listed + enc.shape[0])
        raw = jnp.zeros((column, enc.shape[0]), F32)
        for l in range(depth):
            rows = every[l * column : (l + 1) * column]
            raw = raw + jnp.where(layer_row[:, lanes] == l + 1.0, rows, 0.0)
        split = dot(jnp.concatenate(pieces(raw), axis=0), placing_t[lanes])
        return split[:column] + (split[column : 2 * column] + split[2 * column :])

    def early(layer_row, placing_t, gains, *values):
        count = depth * poses
        dec = jnp.concatenate(values[-count:], axis=0)
        dec = (dec.astype(F32) * gains).astype(BF16)
        return products(0, values[:-count], dec, layer_row, placing_t), dec

    def late(layer_row, placing_t, so_far, dec, *values):
        raw = so_far + products(soon, values, dec, layer_row, placing_t)
        first = place()[2] == 0.0
        lower, higher = pack_rests(raw[:half]), pack_rests(raw[half:])
        return jnp.where(first, lower, higher), jnp.where(first, higher, lower)

    so_far, scaled = on_core(
        early,
        [layer_row, placing_t, gains] + [ring[k][q] for k, q in order[:soon]] + dec_rows,
        [shape(column, wide), shape(depth * column, width, dtype=BF16)],
        small,
        cost=(1, 1),
    )
    keep, send = on_core(
        late,
        [layer_row, placing_t, so_far, scaled] + [ring[k][q] for k, q in order[soon:]],
        [shape(len(bins) * GROUP, wide)] * 2,
        small,
    )
    own_edges = (keep + rotate(send, "rep", 1)).astype(BF16)
    found = spread(own_edges, "feat")
    arrival = [bits for bits, _ in found]
    shards = [shard for _, shard in found]
    others = [rotate(shard, "rep", 1) for shard in shards]

    def finish(placing, mask, squeeze, targets, *values):
        feat, _, rep = place()
        first = rep == 0.0
        chips = []
        for mine, other in zip(values[:feats], values[feats:]):
            lower, higher = jnp.where(first, mine, other), jnp.where(first, other, mine)
            chips.append(jnp.concatenate([unpack_rests(lower), unpack_rests(higher)], axis=0))
        padded = jnp.concatenate([chips[arrival.index(m)] for m in range(feats)], axis=0)
        unused = [jnp.zeros((span - block_rows, holders * listed), BF16)]
        unused = unused if span > block_rows else []
        sources = []
        for f in range(feats):
            sources += [placing[f * block_rows : (f + 1) * block_rows]] + unused
        sources = jnp.concatenate(sources, axis=0)
        edges = dot(sources, padded) * mask.astype(F32)
        magnitude = jnp.abs(edges)
        total = jnp.maximum(jnp.sum(magnitude, axis=0, keepdims=True), 1.0)
        magnitude = magnitude.astype(BF16)
        diagonal = iota((wide, wide), 0) == iota((wide, wide), 1)
        scale = 1.0 / jnp.sum(jnp.where(diagonal, total, 0.0), axis=1, keepdims=True)
        targets = targets.astype(F32)
        targets = targets + floor_div(targets, block_rows) * (span - block_rows)
        current = (iota((wide, panel), 0) == targets).astype(F32)
        accum = jnp.zeros((wide, panel), F32)
        for _ in range(ITERS):
            current = dot(magnitude, (current * scale).astype(BF16))
            accum = accum + current
        influence = accum[:result_rows]
        for f in range(feats):
            for r in range(reps):
                at = f * span + r * result_rows
                mine = (feat == f) & (rep == r)
                influence = jnp.where(mine, accum[at : at + result_rows], influence)
        start = feat * span + rep * result_rows
        own = start + iota((result_rows, wide), 0) == iota((result_rows, wide), 1)
        rows = dot(own.astype(BF16), edges.astype(BF16), NT).astype(BF16)
        edges = dot(rows, squeeze).astype(BF16)
        return edges[None], (influence * float(slots))[None]

    edges, influence = on_core(
        finish,
        [placing, mask, squeeze, target_slots] + shards + others,
        [shape(1, result_rows, slots, dtype=BF16), shape(1, result_rows, panel)],
        small,
    )
    return edges, influence


def solution(mesh):
    return jax.shard_map(
        per_device,
        mesh=mesh,
        in_specs=(
            P(("grp", "pos"), "feat", None),
            P(("grp", "pos"), "feat", None),
            P(("grp", "pos"), None, None),
            P(("grp", "pos"), None),
            P(("feat", "pos"), "rep"),
            P(("feat", "pos"), None, "rep"),
        ),
        out_specs=(
            P(("grp", "pos"), ("feat", "rep"), None),
            P(("grp", "pos"), ("feat", "rep"), None),
        ),
        check_vma=False,
    )
```

```python
import jax
import jax.numpy as jnp
from jax import lax
from jax.experimental import pallas as pl
from jax.experimental.pallas import tpu as pltpu
from jax.sharding import PartitionSpec as P

ITERS = 3
F32 = jnp.float32
BF16 = jnp.bfloat16
NN = (((1,), (0,)), ((), ()))
NT = (((1,), (1,)), ((), ()))
LANES = 128
GROUP = 8
KERNEL_SLOTS = 1024


def dot(a, b, dims=NN):
    return lax.dot_general(a, b, dims, preferred_element_type=F32)


def iota(shape, dim):
    return lax.broadcasted_iota(jnp.int32, shape, dim).astype(F32)


def floor_div(x, n):
    return jnp.floor((x + 0.5) * (1.0 / n))


def on_core(fn, args, outs, kernel=True, through=(), streams=(), cost=None, room=24):
    if not kernel:
        loads = [lambda i, x=x: x[i] for x in streams]
        return list(fn(*args, *loads)) + list(through)
    count, passed, streamed = len(args), len(through), len(streams)

    def body(*refs):
        sources = refs[count : count + streamed]
        results = refs[count + streamed + passed :][: len(outs)]
        scratch = refs[len(refs) - 2 * streamed :]
        copies = []
        for n in range(streamed):
            copies.append(
                [
                    pltpu.make_async_copy(
                        sources[n].at[i], scratch[2 * n].at[i], scratch[2 * n + 1].at[i]
                    )
                    for i in range(streams[n].shape[0])
                ]
            )
            for copy in copies[-1]:
                copy.start()

        def load(n):
            def wait(i):
                copies[n][i].wait()
                return scratch[2 * n][i]

            return wait

        values = fn(*[ref[...] for ref in refs[:count]], *[load(n) for n in range(streamed)])
        for ref, value in zip(results, values):
            ref[...] = value

    estimate = None
    if cost is not None:
        estimate = pl.CostEstimate(flops=cost[0], bytes_accessed=cost[1], transcendentals=0)
    in_vmem = pl.BlockSpec(memory_space=pltpu.VMEM)
    anywhere = pl.BlockSpec(memory_space=pl.ANY)
    scratch = []
    for x in streams:
        scratch += [pltpu.VMEM(x.shape, x.dtype), pltpu.SemaphoreType.DMA((x.shape[0],))]
    call = pl.pallas_call(
        body,
        out_shape=list(outs) + [jax.ShapeDtypeStruct(x.shape, x.dtype) for x in through],
        in_specs=[in_vmem] * count
        + [pl.BlockSpec(memory_space=pltpu.HBM)] * streamed
        + [anywhere] * passed,
        out_specs=[in_vmem] * len(outs) + [anywhere] * passed,
        scratch_shapes=scratch,
        input_output_aliases={count + streamed + i: len(outs) + i for i in range(passed)},
        compiler_params=pltpu.CompilerParams(vmem_limit_bytes=room * 1024 * 1024),
        cost_estimate=estimate,
    )
    return list(call(*args, *streams, *through))


def rotate(x, axis, step):
    count = lax.axis_size(axis)
    return lax.ppermute(x, axis, [(i, (i + step) % count) for i in range(count)])


def ring_place(index, count):
    low = floor_div(index, 2)
    return jnp.where(index > 2 * low, count - 1 - low, low)


def ring_next(x, axis, across=None, turn=0):
    count = lax.axis_size(axis)
    order = list(range(0, count, 2)) + list(range(1, count, 2))[::-1]
    steps = [(order[i], order[(i + 1) % count]) for i in range(count)]
    if across is None:
        return lax.ppermute(x, axis, steps)
    wide = lax.axis_size(across)
    pairs = [(a * wide + i, b * wide + (i + turn) % wide) for a, b in steps for i in range(wide)]
    return lax.ppermute(x, (axis, across), pairs)


def spread(x, axis):
    count = lax.axis_size(axis)
    found = {0: x}
    for bits in range(count - 1, 0, -1):
        found[bits] = lax.ppermute(x, axis, [(i, i ^ bits) for i in range(count)])
    return list(found.items())


def part(x, kernel):
    return x.astype(BF16) if kernel else lax.reduce_precision(x, 8, 7).astype(BF16)


def shape(*dims, dtype=F32):
    return jax.ShapeDtypeStruct(dims, dtype)


def per_device(active_ids, active_vals, block_pattern, target_slots, encoder, decoder):
    feats = lax.axis_size("feat")
    poses = lax.axis_size("pos")
    reps = lax.axis_size("rep")
    holders = feats * poses
    table_rows, width = encoder.shape
    depth = decoder.shape[1]
    layers = depth + 1
    positions, kslots = active_ids.shape[1:]
    block_rows = positions * kslots
    slots = block_rows * feats
    capacity = max(2, (10 * block_rows + 7 * holders - 1) // (7 * holders))
    listed = capacity * feats
    column = poses * listed
    half = column // reps
    result_rows = block_rows // reps
    panel = target_slots.shape[1]
    small = slots <= KERNEL_SLOTS
    span = -(-block_rows // LANES) * LANES if small else block_rows
    wide = feats * span

    rests = []
    for row in range(0, half, GROUP):
        rests.append((row, row % listed // capacity))
    bins = []
    for rest in sorted(rests, key=lambda rest: rest[1]):
        for row in bins:
            if sum(feats - block for _, block in row) + feats - rest[1] <= feats:
                row.append(rest)
                break
        else:
            bins.append([rest])

    def pack_rests(x):
        rows = []
        for row in bins:
            parts = [x[at : at + GROUP, block * span :] for at, block in row]
            empty = wide - sum(part.shape[1] for part in parts)
            parts += [jnp.zeros((GROUP, empty), x.dtype)] if empty else []
            rows.append(jnp.concatenate(parts, axis=1) if len(parts) > 1 else parts[0])
        return jnp.concatenate(rows, axis=0)

    def unpack_rests(x):
        x = x.astype(F32) if small else x
        found = {}
        for n, row in enumerate(bins):
            lane = 0
            for at, block in row:
                rest = x[n * GROUP : (n + 1) * GROUP, lane : lane + wide - block * span]
                lane += wide - block * span
                if block:
                    rest = jnp.concatenate([jnp.zeros((GROUP, block * span), x.dtype), rest], axis=1)
                found[at] = rest
        return jnp.concatenate([found[at] for at, _ in rests], axis=0).astype(BF16)

    def place():
        feat, pos = lax.axis_index("feat"), lax.axis_index("pos")
        return feat.astype(F32), pos.astype(F32), lax.axis_index("rep").astype(F32)

    def pack(ids, vals):
        one = jnp.concatenate([ids(0).astype(F32), vals(0)], axis=0)
        one = jnp.concatenate([one, jnp.zeros((2 * positions, LANES - kslots), F32)], axis=1)
        return (jnp.broadcast_to(one, (holders,) + one.shape),)

    (packed,) = on_core(
        pack,
        [],
        [shape(holders, 2 * positions, LANES)],
        streams=[active_ids, active_vals],
        room=60,
    )
    lists = lax.all_to_all(packed, ("feat", "pos"), split_axis=0, concat_axis=0, tiled=True)

    def list_of(values, prompt):
        blocks = []
        for a in range(feats):
            block = values[a * poses]
            for q in range(1, poses):
                block = jnp.where(prompt == q, values[a * poses + q], block)
            blocks.append(block)
        return jnp.concatenate(blocks, axis=0)[:, :kslots]

    def list_row(slot):
        place = floor_div(slot, kslots)
        return place + floor_div(place, positions) * positions

    def slot_entry(slot):
        return slot - floor_div(slot, kslots) * kslots

    def pieces(table):
        high = part(table, small)
        rest = table - high.astype(F32)
        middle = part(rest, small)
        return [high, middle, part(rest - middle.astype(F32), small)]

    def as_rows(table, slot_at, lanes):
        entry = slot_entry(slot_at(iota((kslots, lanes), 1)))
        spread = (iota((kslots, lanes), 0) == entry).astype(BF16)
        every = dot(jnp.concatenate(pieces(table), axis=0), spread)
        count = table.shape[0]
        every = every[:count] + (every[count : 2 * count] + every[2 * count :])
        row = iota(every.shape, 0) - list_row(slot_at(iota(every.shape, 1)))
        ids = jnp.sum(jnp.where(row == 0, every, 0.0), axis=0, keepdims=True)
        return ids, jnp.sum(jnp.where(row == positions, every, 0.0), axis=0, keepdims=True)

    def spread_slot(lane):
        block = floor_div(lane, span)
        inside = lane - block * span
        return jnp.where(inside < block_rows, block * block_rows + inside, -1.0 * slots)

    def as_col(table):
        wide = (slots, table.shape[0])
        spread = (list_row(iota(wide, 0)) == iota(wide, 1)).astype(BF16)
        every = dot(spread, jnp.concatenate(pieces(table), axis=1))
        every = every[:, :kslots] + (every[:, kslots : 2 * kslots] + every[:, 2 * kslots :])
        mine = slot_entry(iota((slots, kslots), 0)) == iota((slots, kslots), 1)
        return jnp.sum(jnp.where(mine, every, 0.0), axis=1, keepdims=True)

    def choose(values):
        feat, pos, _ = place()
        own = feat * poses + pos
        tables = []
        rows = []
        for k in range(poses):
            prompt = jnp.where(pos + k >= poses, pos + k - poses, pos + k)
            tables.append(list_of(values, prompt))
            rows.append(as_rows(tables[k], lambda lane: lane, slots)[0])
        hits = [floor_div(ids, table_rows) == own for ids in rows]
        earlier = (iota((slots, slots), 0) < iota((slots, slots), 1)).astype(BF16)
        ranks = dot(jnp.concatenate([h.astype(BF16) for h in hits], axis=0), earlier)
        picks = []
        for k in range(poses):
            chosen = jnp.where(
                hits[k] & (ranks[k : k + 1] == iota((listed, slots), 0)), 1.0, 0.0
            )
            local = jnp.sum(chosen * (rows[k] - own * table_rows + 1.0), axis=1, keepdims=True)
            picks.append((local - 1.0 == iota((listed, table_rows), 1)).astype(BF16))
        return jnp.concatenate(picks, axis=0), tables[0]

    picks, my_list = on_core(
        choose,
        [lists],
        [shape(column, table_rows, dtype=BF16), shape(2 * positions * feats, kslots)],
        small,
        cost=(10**9, 10**7),
    )

    def encode(picks, enc):
        rows = dot(picks, enc).astype(BF16)
        return [rows[k * listed : (k + 1) * listed] for k in range(poses)] + [picks]

    *enc_rows, picks = on_core(
        encode,
        [picks, encoder],
        [shape(listed, width, dtype=BF16)] * poses + [shape(column, table_rows, dtype=BF16)],
        small,
    )

    ring = [[enc_rows[0]] + [rotate(enc_rows[k], "pos", k) for k in range(1, poses)]]
    ring.append([ring_next(enc_rows[k], "feat", "pos", k) for k in range(poses)])

    dec_rows = lax.dot_general(
        picks, decoder, (((1,), (0,)), ((), ())), preferred_element_type=F32
    )
    dec_rows = jnp.transpose(dec_rows, (1, 0, 2)).astype(BF16)
    dec_rows = [
        [dec_rows[l, k * listed : (k + 1) * listed] for l in range(depth)] for k in range(poses)
    ]
    away = [rows for k in range(1, poses) for rows in dec_rows[k]]
    order = [(0, 0)] + [(k, q) for k in range(1, feats - 1) for q in range(poses)]
    soon = len(order)
    order += [(0, q) for q in range(1, poses)] + [(feats - 1, q) for q in range(poses)]
    own_lists = [order.index((0, q)) for q in range(poses)]

    def places(table, pattern):
        feat, pos, rep = place()

        def turned(owner):
            turn = pos - (owner - floor_div(owner, poses) * poses)
            return jnp.where(turn < 0.0, turn + poses, turn)

        def spread_place(owner, rank):
            feat_of = floor_div(owner, poses).astype(jnp.int32)
            bits = (feat.astype(jnp.int32) ^ feat_of).astype(F32)
            return (bits * poses + turned(owner)) * listed + rank

        def padded(owner, rank):
            feat_of = floor_div(owner, poses)
            turn = turned(owner)
            step = ring_place(feat, feats) - ring_place(feat_of, feats)
            step = jnp.where(step < 0.0, step + feats, step)
            at = step * poses + turn
            at = jnp.where(step < feats - 1.0, at - (poses - 1), at)
            at = jnp.where(step == 0.0, turn + (feats - 2) * poses, at)
            at = jnp.where((step == 0.0) & (turn == 0.0), 0.0, at)
            return at * listed + rank

        ids_row, vals_row = as_rows(table, spread_slot, wide)
        ids_col = as_col(table)
        owner_row = floor_div(ids_row, table_rows)
        owner_col = floor_div(ids_col, table_rows)
        down, across = iota((slots, slots), 0), iota((slots, slots), 1)
        same = owner_col == floor_div(as_rows(table, lambda lane: lane, slots)[0], table_rows)
        rank_col = jnp.sum(jnp.where(same & (across < down), 1.0, 0.0), axis=1, keepdims=True)
        slot = spread_slot(iota((slots, wide), 1))
        same = (owner_col == owner_row) & (iota((slots, wide), 0) < slot)
        rank_row = jnp.sum(jnp.where(same, 1.0, 0.0), axis=0, keepdims=True)
        total = holders * listed
        used = spread_slot(iota((1, wide), 1)) >= 0.0
        place_row = jnp.where(used, padded(owner_row, rank_row), -1.0)
        placing = spread_place(owner_col, rank_col) == iota((slots, total), 1)
        entry = padded(owner_col, rank_col) == iota((slots, total), 1)
        placing_t = place_row == iota((total, wide), 0)
        layer = ids_col - floor_div(ids_col, layers) * layers
        layer_row = jnp.sum(jnp.where(entry, layer, 0.0), axis=0, keepdims=True)
        mine = [placing_t[at * listed : (at + 1) * listed] for at in own_lists]
        mine = jnp.concatenate(mine, axis=0)
        gain = jnp.sum(jnp.where(mine, vals_row, 0.0), axis=1, keepdims=True)
        source_layer = ids_row - floor_div(ids_row, layers) * layers
        source_layer = jnp.sum(jnp.where(mine, source_layer, 0.0), axis=1, keepdims=True)
        gains = jnp.concatenate(
            [jnp.where(source_layer <= l, gain, 0.0) for l in range(depth)], axis=0
        )
        allowed = jnp.where(pattern[0] == 1, 1.0, 0.0).astype(BF16)

        sources = (floor_div(iota((wide, 1), 0), span) == iota((wide, feats), 1)).astype(BF16)
        targets = (floor_div(iota((1, wide), 1), span) == iota((feats, wide), 0)).astype(BF16)
        mask = dot(dot(sources, allowed, NT).astype(BF16), targets)
        source = floor_div(spread_slot(iota((wide, wide), 0)), kslots)
        target = floor_div(spread_slot(iota((wide, wide), 1)), kslots)
        mask = jnp.where(source <= target, mask, 0.0)
        squeeze = spread_slot(iota((wide, slots), 0)) == iota((wide, slots), 1)
        placing, placing_t = placing.astype(BF16), placing_t.astype(BF16)
        return placing, placing_t, layer_row, gains, mask.astype(BF16), squeeze.astype(BF16)

    placing, placing_t, layer_row, gains, mask, squeeze, *away = on_core(
        places,
        [my_list, block_pattern],
        [
            shape(slots, holders * listed, dtype=BF16),
            shape(holders * listed, wide, dtype=BF16),
            shape(1, holders * listed),
            shape(depth * column, 1),
            shape(wide, wide, dtype=BF16),
            shape(wide, slots, dtype=BF16),
        ],
        small,
        through=away,
        cost=(1, 1),
    )
    for k in range(1, poses):
        rows = away[(k - 1) * depth : k * depth]
        dec_rows[k] = [rotate(row, "pos", k) for row in rows]
    dec_rows = [dec_rows[k][l] for l in range(depth) for k in range(poses)]

    for _ in range(2, feats):
        ring.append([ring_next(rows, "feat") for rows in ring[-1]])

    def products(first, enc, dec, layer_row, placing_t):
        enc = jnp.concatenate(enc, axis=0)
        every = dot(dec, enc, NT)
        lanes = slice(first * listed, first * listed + enc.shape[0])
        raw = jnp.zeros((column, enc.shape[0]), F32)
        for l in range(depth):
            rows = every[l * column : (l + 1) * column]
            raw = raw + jnp.where(layer_row[:, lanes] == l + 1.0, rows, 0.0)
        split = dot(jnp.concatenate(pieces(raw), axis=0), placing_t[lanes])
        return split[:column] + (split[column : 2 * column] + split[2 * column :])

    def early(layer_row, placing_t, gains, *values):
        count = depth * poses
        dec = jnp.concatenate(values[-count:], axis=0)
        dec = (dec.astype(F32) * gains).astype(BF16)
        return products(0, values[:-count], dec, layer_row, placing_t), dec

    def late(layer_row, placing_t, so_far, dec, *values):
        raw = so_far + products(soon, values, dec, layer_row, placing_t)
        first = place()[2] == 0.0
        lower, higher = pack_rests(raw[:half]), pack_rests(raw[half:])
        return jnp.where(first, lower, higher), jnp.where(first, higher, lower)

    so_far, scaled = on_core(
        early,
        [layer_row, placing_t, gains] + [ring[k][q] for k, q in order[:soon]] + dec_rows,
        [shape(column, wide), shape(depth * column, width, dtype=BF16)],
        small,
        cost=(1, 1),
    )
    keep, send = on_core(
        late,
        [layer_row, placing_t, so_far, scaled] + [ring[k][q] for k, q in order[soon:]],
        [shape(len(bins) * GROUP, wide)] * 2,
        small,
    )
    own_edges = (keep + rotate(send, "rep", 1)).astype(BF16)
    found = spread(own_edges, "feat")
    arrival = [bits for bits, _ in found]
    shards = [shard for _, shard in found]
    others = [rotate(shard, "rep", 1) for shard in shards]

    def finish(placing, mask, squeeze, targets, *values):
        feat, _, rep = place()
        first = rep == 0.0
        chips = []
        for mine, other in zip(values[:feats], values[feats:]):
            lower, higher = jnp.where(first, mine, other), jnp.where(first, other, mine)
            chips.append(jnp.concatenate([unpack_rests(lower), unpack_rests(higher)], axis=0))
        padded = jnp.concatenate([chips[arrival.index(m)] for m in range(feats)], axis=0)
        unused = [jnp.zeros((span - block_rows, holders * listed), BF16)]
        unused = unused if span > block_rows else []
        sources = []
        for f in range(feats):
            sources += [placing[f * block_rows : (f + 1) * block_rows]] + unused
        sources = jnp.concatenate(sources, axis=0)
        edges = dot(sources, padded) * mask.astype(F32)
        magnitude = jnp.abs(edges)
        total = jnp.maximum(jnp.sum(magnitude, axis=0, keepdims=True), 1.0)
        magnitude = magnitude.astype(BF16)
        diagonal = iota((wide, wide), 0) == iota((wide, wide), 1)
        scale = 1.0 / jnp.sum(jnp.where(diagonal, total, 0.0), axis=1, keepdims=True)
        targets = targets.astype(F32)
        targets = targets + floor_div(targets, block_rows) * (span - block_rows)
        current = (iota((wide, panel), 0) == targets).astype(F32)
        accum = jnp.zeros((wide, panel), F32)
        for _ in range(ITERS):
            scaled = current * scale
            high = part(scaled, small)
            low = part(scaled - high.astype(F32), small)
            both = dot(magnitude, jnp.concatenate([high, low], axis=1))
            current = both[:, :panel] + both[:, panel:]
            accum = accum + current
        influence = accum[:result_rows]
        for f in range(feats):
            for r in range(reps):
                at = f * span + r * result_rows
                mine = (feat == f) & (rep == r)
                influence = jnp.where(mine, accum[at : at + result_rows], influence)
        start = feat * span + rep * result_rows
        own = start + iota((result_rows, wide), 0) == iota((result_rows, wide), 1)
        rows = dot(own.astype(BF16), edges.astype(BF16), NT).astype(BF16)
        edges = dot(rows, squeeze).astype(BF16)
        return edges[None], (influence * float(slots))[None]

    edges, influence = on_core(
        finish,
        [placing, mask, squeeze, target_slots] + shards + others,
        [shape(1, result_rows, slots, dtype=BF16), shape(1, result_rows, panel)],
        small,
    )
    return edges, influence


def solution(mesh):
    return jax.shard_map(
        per_device,
        mesh=mesh,
        in_specs=(
            P(("grp", "pos"), "feat", None),
            P(("grp", "pos"), "feat", None),
            P(("grp", "pos"), None, None),
            P(("grp", "pos"), None),
            P(("feat", "pos"), "rep"),
            P(("feat", "pos"), None, "rep"),
        ),
        out_specs=(
            P(("grp", "pos"), ("feat", "rep"), None),
            P(("grp", "pos"), ("feat", "rep"), None),
        ),
        check_vma=False,
    )
```

```python
import jax
import jax.numpy as jnp
from jax import lax
from jax.experimental import pallas as pl
from jax.experimental.pallas import tpu as pltpu
from jax.sharding import PartitionSpec as P

ITERS = 3
F32 = jnp.float32
BF16 = jnp.bfloat16
NN = (((1,), (0,)), ((), ()))
NT = (((1,), (1,)), ((), ()))
LANES = 128
GROUP = 8
KERNEL_SLOTS = 1024


def dot(a, b, dims=NN):
    return lax.dot_general(a, b, dims, preferred_element_type=F32)


def iota(shape, dim):
    return lax.broadcasted_iota(jnp.int32, shape, dim).astype(F32)


def floor_div(x, n):
    return jnp.floor((x + 0.5) * (1.0 / n))


def on_core(fn, args, outs, kernel=True, through=(), streams=(), cost=None, room=24):
    if not kernel:
        loads = [lambda i, x=x: x[i] for x in streams]
        return list(fn(*args, *loads)) + list(through)
    count, passed, streamed = len(args), len(through), len(streams)

    def body(*refs):
        sources = refs[count : count + streamed]
        results = refs[count + streamed + passed :][: len(outs)]
        scratch = refs[len(refs) - 2 * streamed :]
        copies = []
        for n in range(streamed):
            copies.append(
                [
                    pltpu.make_async_copy(
                        sources[n].at[i], scratch[2 * n].at[i], scratch[2 * n + 1].at[i]
                    )
                    for i in range(streams[n].shape[0])
                ]
            )
            for copy in copies[-1]:
                copy.start()

        def load(n):
            def wait(i):
                copies[n][i].wait()
                return scratch[2 * n][i]

            return wait

        values = fn(*[ref[...] for ref in refs[:count]], *[load(n) for n in range(streamed)])
        for ref, value in zip(results, values):
            ref[...] = value

    estimate = None
    if cost is not None:
        estimate = pl.CostEstimate(flops=cost[0], bytes_accessed=cost[1], transcendentals=0)
    in_vmem = pl.BlockSpec(memory_space=pltpu.VMEM)
    anywhere = pl.BlockSpec(memory_space=pl.ANY)
    scratch = []
    for x in streams:
        scratch += [pltpu.VMEM(x.shape, x.dtype), pltpu.SemaphoreType.DMA((x.shape[0],))]
    call = pl.pallas_call(
        body,
        out_shape=list(outs) + [jax.ShapeDtypeStruct(x.shape, x.dtype) for x in through],
        in_specs=[in_vmem] * count
        + [pl.BlockSpec(memory_space=pltpu.HBM)] * streamed
        + [anywhere] * passed,
        out_specs=[in_vmem] * len(outs) + [anywhere] * passed,
        scratch_shapes=scratch,
        input_output_aliases={count + streamed + i: len(outs) + i for i in range(passed)},
        compiler_params=pltpu.CompilerParams(vmem_limit_bytes=room * 1024 * 1024),
        cost_estimate=estimate,
    )
    return list(call(*args, *streams, *through))


def rotate(x, axis, step):
    count = lax.axis_size(axis)
    return lax.ppermute(x, axis, [(i, (i + step) % count) for i in range(count)])


def ring_place(index, count):
    low = floor_div(index, 2)
    return jnp.where(index > 2 * low, count - 1 - low, low)


def ring_next(x, axis, across=None, turn=0):
    count = lax.axis_size(axis)
    order = list(range(0, count, 2)) + list(range(1, count, 2))[::-1]
    steps = [(order[i], order[(i + 1) % count]) for i in range(count)]
    if across is None:
        return lax.ppermute(x, axis, steps)
    wide = lax.axis_size(across)
    pairs = [(a * wide + i, b * wide + (i + turn) % wide) for a, b in steps for i in range(wide)]
    return lax.ppermute(x, (axis, across), pairs)


def spread(x, axis):
    count = lax.axis_size(axis)
    found = {0: x}
    for bits in sorted(range(1, count), key=lambda bits: bits < count // 2):
        found[bits] = lax.ppermute(x, axis, [(i, i ^ bits) for i in range(count)])
    return list(found.items())


def part(x, kernel):
    return x.astype(BF16) if kernel else lax.reduce_precision(x, 8, 7).astype(BF16)


def shape(*dims, dtype=F32):
    return jax.ShapeDtypeStruct(dims, dtype)


def per_device(active_ids, active_vals, block_pattern, target_slots, encoder, decoder):
    feats = lax.axis_size("feat")
    poses = lax.axis_size("pos")
    reps = lax.axis_size("rep")
    holders = feats * poses
    table_rows, width = encoder.shape
    depth = decoder.shape[1]
    layers = depth + 1
    positions, kslots = active_ids.shape[1:]
    block_rows = positions * kslots
    slots = block_rows * feats
    capacity = max(2, (10 * block_rows + 7 * holders - 1) // (7 * holders))
    listed = capacity * feats
    column = poses * listed
    half = column // reps
    result_rows = block_rows // reps
    panel = target_slots.shape[1]
    small = slots <= KERNEL_SLOTS
    span = -(-block_rows // LANES) * LANES if small else block_rows
    wide = feats * span

    rests = []
    for row in range(0, half, GROUP):
        rests.append((row, row % listed // capacity))
    bins = []
    for rest in sorted(rests, key=lambda rest: rest[1]):
        for row in bins:
            if sum(feats - block for _, block in row) + feats - rest[1] <= feats:
                row.append(rest)
                break
        else:
            bins.append([rest])

    def pack_rests(x):
        rows = []
        for row in bins:
            parts = [x[at : at + GROUP, block * span :] for at, block in row]
            empty = wide - sum(part.shape[1] for part in parts)
            parts += [jnp.zeros((GROUP, empty), x.dtype)] if empty else []
            rows.append(jnp.concatenate(parts, axis=1) if len(parts) > 1 else parts[0])
        return jnp.concatenate(rows, axis=0)

    def unpack_rests(x):
        x = x.astype(F32) if small else x
        found = {}
        for n, row in enumerate(bins):
            lane = 0
            for at, block in row:
                rest = x[n * GROUP : (n + 1) * GROUP, lane : lane + wide - block * span]
                lane += wide - block * span
                if block:
                    rest = jnp.concatenate([jnp.zeros((GROUP, block * span), x.dtype), rest], axis=1)
                found[at] = rest
        return jnp.concatenate([found[at] for at, _ in rests], axis=0).astype(BF16)

    def place():
        feat, pos = lax.axis_index("feat"), lax.axis_index("pos")
        return feat.astype(F32), pos.astype(F32), lax.axis_index("rep").astype(F32)

    def pack(ids, vals):
        one = jnp.concatenate([ids(0).astype(F32), vals(0)], axis=0)
        one = jnp.concatenate([one, jnp.zeros((2 * positions, LANES - kslots), F32)], axis=1)
        return (jnp.broadcast_to(one, (holders,) + one.shape),)

    (packed,) = on_core(
        pack,
        [],
        [shape(holders, 2 * positions, LANES)],
        streams=[active_ids, active_vals],
        room=60,
    )
    lists = lax.all_to_all(packed, ("feat", "pos"), split_axis=0, concat_axis=0, tiled=True)

    def list_of(values, prompt):
        blocks = []
        for a in range(feats):
            block = values[a * poses]
            for q in range(1, poses):
                block = jnp.where(prompt == q, values[a * poses + q], block)
            blocks.append(block)
        return jnp.concatenate(blocks, axis=0)[:, :kslots]

    def list_row(slot):
        place = floor_div(slot, kslots)
        return place + floor_div(place, positions) * positions

    def slot_entry(slot):
        return slot - floor_div(slot, kslots) * kslots

    def pieces(table):
        high = part(table, small)
        rest = table - high.astype(F32)
        middle = part(rest, small)
        return [high, middle, part(rest - middle.astype(F32), small)]

    def as_rows(table, slot_at, lanes):
        entry = slot_entry(slot_at(iota((kslots, lanes), 1)))
        spread = (iota((kslots, lanes), 0) == entry).astype(BF16)
        every = dot(jnp.concatenate(pieces(table), axis=0), spread)
        count = table.shape[0]
        every = every[:count] + (every[count : 2 * count] + every[2 * count :])
        row = iota(every.shape, 0) - list_row(slot_at(iota(every.shape, 1)))
        ids = jnp.sum(jnp.where(row == 0, every, 0.0), axis=0, keepdims=True)
        return ids, jnp.sum(jnp.where(row == positions, every, 0.0), axis=0, keepdims=True)

    def spread_slot(lane):
        block = floor_div(lane, span)
        inside = lane - block * span
        return jnp.where(inside < block_rows, block * block_rows + inside, -1.0 * slots)

    def as_col(table):
        wide = (slots, table.shape[0])
        spread = (list_row(iota(wide, 0)) == iota(wide, 1)).astype(BF16)
        every = dot(spread, jnp.concatenate(pieces(table), axis=1))
        every = every[:, :kslots] + (every[:, kslots : 2 * kslots] + every[:, 2 * kslots :])
        mine = slot_entry(iota((slots, kslots), 0)) == iota((slots, kslots), 1)
        return jnp.sum(jnp.where(mine, every, 0.0), axis=1, keepdims=True)

    def choose(values):
        feat, pos, _ = place()
        own = feat * poses + pos
        tables = []
        rows = []
        for k in range(poses):
            prompt = jnp.where(pos + k >= poses, pos + k - poses, pos + k)
            tables.append(list_of(values, prompt))
            rows.append(as_rows(tables[k], lambda lane: lane, slots)[0])
        hits = [floor_div(ids, table_rows) == own for ids in rows]
        earlier = (iota((slots, slots), 0) < iota((slots, slots), 1)).astype(BF16)
        ranks = dot(jnp.concatenate([h.astype(BF16) for h in hits], axis=0), earlier)
        picks = []
        for k in range(poses):
            chosen = jnp.where(
                hits[k] & (ranks[k : k + 1] == iota((listed, slots), 0)), 1.0, 0.0
            )
            local = jnp.sum(chosen * (rows[k] - own * table_rows + 1.0), axis=1, keepdims=True)
            picks.append((local - 1.0 == iota((listed, table_rows), 1)).astype(BF16))
        return jnp.concatenate(picks, axis=0), tables[0]

    picks, my_list = on_core(
        choose,
        [lists],
        [shape(column, table_rows, dtype=BF16), shape(2 * positions * feats, kslots)],
        small,
        cost=(10**9, 10**7),
    )

    def encode(picks, enc):
        rows = dot(picks, enc).astype(BF16)
        return [rows[k * listed : (k + 1) * listed] for k in range(poses)] + [picks]

    *enc_rows, picks = on_core(
        encode,
        [picks, encoder],
        [shape(listed, width, dtype=BF16)] * poses + [shape(column, table_rows, dtype=BF16)],
        small,
    )

    ring = [[enc_rows[0]] + [rotate(enc_rows[k], "pos", k) for k in range(1, poses)]]
    ring.append([ring_next(enc_rows[k], "feat", "pos", k) for k in range(poses)])

    dec_rows = lax.dot_general(
        picks, decoder, (((1,), (0,)), ((), ())), preferred_element_type=F32
    )
    dec_rows = jnp.transpose(dec_rows, (1, 0, 2)).astype(BF16)
    dec_rows = [
        [dec_rows[l, k * listed : (k + 1) * listed] for l in range(depth)] for k in range(poses)
    ]
    away = [rows for k in range(1, poses) for rows in dec_rows[k]]
    order = [(0, 0)] + [(k, q) for k in range(1, feats - 1) for q in range(poses)]
    soon = len(order)
    order += [(0, q) for q in range(1, poses)] + [(feats - 1, q) for q in range(poses)]
    own_lists = [order.index((0, q)) for q in range(poses)]

    def places(table, pattern):
        feat, pos, rep = place()

        def turned(owner):
            turn = pos - (owner - floor_div(owner, poses) * poses)
            return jnp.where(turn < 0.0, turn + poses, turn)

        def spread_place(owner, rank):
            feat_of = floor_div(owner, poses).astype(jnp.int32)
            bits = (feat.astype(jnp.int32) ^ feat_of).astype(F32)
            return (bits * poses + turned(owner)) * listed + rank

        def padded(owner, rank):
            feat_of = floor_div(owner, poses)
            turn = turned(owner)
            step = ring_place(feat, feats) - ring_place(feat_of, feats)
            step = jnp.where(step < 0.0, step + feats, step)
            at = step * poses + turn
            at = jnp.where(step < feats - 1.0, at - (poses - 1), at)
            at = jnp.where(step == 0.0, turn + (feats - 2) * poses, at)
            at = jnp.where((step == 0.0) & (turn == 0.0), 0.0, at)
            return at * listed + rank

        ids_row, vals_row = as_rows(table, spread_slot, wide)
        ids_col = as_col(table)
        owner_row = floor_div(ids_row, table_rows)
        owner_col = floor_div(ids_col, table_rows)
        down, across = iota((slots, slots), 0), iota((slots, slots), 1)
        same = owner_col == floor_div(as_rows(table, lambda lane: lane, slots)[0], table_rows)
        rank_col = jnp.sum(jnp.where(same & (across < down), 1.0, 0.0), axis=1, keepdims=True)
        slot = spread_slot(iota((slots, wide), 1))
        same = (owner_col == owner_row) & (iota((slots, wide), 0) < slot)
        rank_row = jnp.sum(jnp.where(same, 1.0, 0.0), axis=0, keepdims=True)
        total = holders * listed
        used = spread_slot(iota((1, wide), 1)) >= 0.0
        place_row = jnp.where(used, padded(owner_row, rank_row), -1.0)
        placing = spread_place(owner_col, rank_col) == iota((slots, total), 1)
        entry = padded(owner_col, rank_col) == iota((slots, total), 1)
        placing_t = place_row == iota((total, wide), 0)
        layer = ids_col - floor_div(ids_col, layers) * layers
        layer_row = jnp.sum(jnp.where(entry, layer, 0.0), axis=0, keepdims=True)
        mine = [placing_t[at * listed : (at + 1) * listed] for at in own_lists]
        mine = jnp.concatenate(mine, axis=0)
        gain = jnp.sum(jnp.where(mine, vals_row, 0.0), axis=1, keepdims=True)
        source_layer = ids_row - floor_div(ids_row, layers) * layers
        source_layer = jnp.sum(jnp.where(mine, source_layer, 0.0), axis=1, keepdims=True)
        gains = jnp.concatenate(
            [jnp.where(source_layer <= l, gain, 0.0) for l in range(depth)], axis=0
        )
        allowed = jnp.where(pattern[0] == 1, 1.0, 0.0).astype(BF16)

        sources = (floor_div(iota((wide, 1), 0), span) == iota((wide, feats), 1)).astype(BF16)
        targets = (floor_div(iota((1, wide), 1), span) == iota((feats, wide), 0)).astype(BF16)
        mask = dot(dot(sources, allowed, NT).astype(BF16), targets)
        source = floor_div(spread_slot(iota((wide, wide), 0)), kslots)
        target = floor_div(spread_slot(iota((wide, wide), 1)), kslots)
        mask = jnp.where(source <= target, mask, 0.0)
        squeeze = spread_slot(iota((wide, slots), 0)) == iota((wide, slots), 1)
        placing, placing_t = placing.astype(BF16), placing_t.astype(BF16)
        return placing, placing_t, layer_row, gains, mask.astype(BF16), squeeze.astype(BF16)

    placing, placing_t, layer_row, gains, mask, squeeze, *away = on_core(
        places,
        [my_list, block_pattern],
        [
            shape(slots, holders * listed, dtype=BF16),
            shape(holders * listed, wide, dtype=BF16),
            shape(1, holders * listed),
            shape(depth * column, 1),
            shape(wide, wide, dtype=BF16),
            shape(wide, slots, dtype=BF16),
        ],
        small,
        through=away,
        cost=(1, 1),
    )
    for k in range(1, poses):
        rows = away[(k - 1) * depth : k * depth]
        dec_rows[k] = [rotate(row, "pos", k) for row in rows]
    dec_rows = [dec_rows[k][l] for l in range(depth) for k in range(poses)]

    for _ in range(2, feats):
        ring.append([ring_next(rows, "feat") for rows in ring[-1]])

    def products(first, enc, dec, layer_row, placing_t):
        enc = jnp.concatenate(enc, axis=0)
        every = dot(dec, enc, NT)
        lanes = slice(first * listed, first * listed + enc.shape[0])
        raw = jnp.zeros((column, enc.shape[0]), F32)
        for l in range(depth):
            rows = every[l * column : (l + 1) * column]
            raw = raw + jnp.where(layer_row[:, lanes] == l + 1.0, rows, 0.0)
        split = dot(jnp.concatenate(pieces(raw)[:2], axis=0), placing_t[lanes])
        return split[:column] + split[column:]

    def early(layer_row, placing_t, gains, *values):
        count = depth * poses
        dec = jnp.concatenate(values[-count:], axis=0)
        dec = (dec.astype(F32) * gains).astype(BF16)
        return products(0, values[:-count], dec, layer_row, placing_t), dec

    def late(layer_row, placing_t, so_far, dec, *values):
        raw = so_far + products(soon, values, dec, layer_row, placing_t)
        first = place()[2] == 0.0
        lower, higher = pack_rests(raw[:half]), pack_rests(raw[half:])
        return jnp.where(first, lower, higher), jnp.where(first, higher, lower)

    so_far, scaled = on_core(
        early,
        [layer_row, placing_t, gains] + [ring[k][q] for k, q in order[:soon]] + dec_rows,
        [shape(column, wide), shape(depth * column, width, dtype=BF16)],
        small,
        cost=(1, 1),
    )
    keep, send = on_core(
        late,
        [layer_row, placing_t, so_far, scaled] + [ring[k][q] for k, q in order[soon:]],
        [shape(len(bins) * GROUP, wide)] * 2,
        small,
    )
    own_edges = (keep + rotate(send, "rep", 1)).astype(BF16)
    found = spread(own_edges, "feat")
    arrival = [bits for bits, _ in found]
    shards = [shard for _, shard in found]
    others = [rotate(shard, "rep", 1) for shard in shards]

    def finish(placing, mask, squeeze, targets, *values):
        feat, _, rep = place()
        first = rep == 0.0
        chips = []
        for mine, other in zip(values[:feats], values[feats:]):
            lower, higher = jnp.where(first, mine, other), jnp.where(first, other, mine)
            chips.append(jnp.concatenate([unpack_rests(lower), unpack_rests(higher)], axis=0))
        padded = jnp.concatenate([chips[arrival.index(m)] for m in range(feats)], axis=0)
        unused = [jnp.zeros((span - block_rows, holders * listed), BF16)]
        unused = unused if span > block_rows else []
        sources = []
        for f in range(feats):
            sources += [placing[f * block_rows : (f + 1) * block_rows]] + unused
        sources = jnp.concatenate(sources, axis=0)
        edges = dot(sources, padded) * mask.astype(F32)
        magnitude = jnp.abs(edges)
        total = jnp.maximum(jnp.sum(magnitude, axis=0, keepdims=True), 1.0)
        magnitude = magnitude.astype(BF16)
        diagonal = iota((wide, wide), 0) == iota((wide, wide), 1)
        scale = 1.0 / jnp.sum(jnp.where(diagonal, total, 0.0), axis=1, keepdims=True)
        targets = targets.astype(F32)
        targets = targets + floor_div(targets, block_rows) * (span - block_rows)
        current = (iota((wide, panel), 0) == targets).astype(F32)
        accum = jnp.zeros((wide, panel), F32)
        for _ in range(ITERS):
            scaled = current * scale
            high = part(scaled, small)
            low = part(scaled - high.astype(F32), small)
            both = dot(magnitude, jnp.concatenate([high, low], axis=1))
            current = both[:, :panel] + both[:, panel:]
            accum = accum + current
        influence = accum[:result_rows]
        for f in range(feats):
            for r in range(reps):
                at = f * span + r * result_rows
                mine = (feat == f) & (rep == r)
                influence = jnp.where(mine, accum[at : at + result_rows], influence)
        start = feat * span + rep * result_rows
        own = start + iota((result_rows, wide), 0) == iota((result_rows, wide), 1)
        rows = dot(own.astype(BF16), edges.astype(BF16), NT).astype(BF16)
        edges = dot(rows, squeeze).astype(BF16)
        return edges[None], (influence * float(slots))[None]

    edges, influence = on_core(
        finish,
        [placing, mask, squeeze, target_slots] + shards + others,
        [shape(1, result_rows, slots, dtype=BF16), shape(1, result_rows, panel)],
        small,
    )
    return edges, influence


def solution(mesh):
    return jax.shard_map(
        per_device,
        mesh=mesh,
        in_specs=(
            P(("grp", "pos"), "feat", None),
            P(("grp", "pos"), "feat", None),
            P(("grp", "pos"), None, None),
            P(("grp", "pos"), None),
            P(("feat", "pos"), "rep"),
            P(("feat", "pos"), None, "rep"),
        ),
        out_specs=(
            P(("grp", "pos"), ("feat", "rep"), None),
            P(("grp", "pos"), ("feat", "rep"), None),
        ),
        check_vma=False,
    )
```
